128 devices in a mesh: batch: 2 (over x_lo), seq: 64 (over x_hi, z, y, core).
Axes of the slice: x: 4 (x_hi: 2, x_lo: 2; x = x_hi * 2 + x_lo), y: 4, z: 4, core: 2. Of those that a mesh axis runs over, the one named last changes fastest.
Arguments:
- tokens: bfloat16 [16384, 2048], P(('batch', 'seq')), may hold values from -8 to 8
- cotangent: bfloat16 [16384, 2048], P(('batch', 'seq')), may hold values from -6 to 6
- attn_gain: float32 [2048], replicated, may hold values from 0.1 to 1.9
- w_input: bfloat16 [2048, 2048], P(('batch', 'seq')), may hold values from -0.125 to 0.125
- w_forget: bfloat16 [2048, 2048], P(('batch', 'seq')), may hold values from -1 to 1
- w_outgate: bfloat16 [2048, 2048], P(('batch', 'seq')), may hold values from -0.125 to 0.125
- w_out: bfloat16 [2048, 2048], P(('batch', 'seq')), may hold values from -0.125 to 0.125
- norm_gain: float32 [2048], replicated, may hold values from 0.1 to 1.9
- mlp_gain: float32 [2048], replicated, may hold values from 0.1 to 1.9
- w_gate: bfloat16 [2048, 5632], P(('batch', 'seq')), may hold values from -0.125 to 0.125
- w_up: bfloat16 [2048, 5632], P(('batch', 'seq')), may hold values from -0.125 to 0.125
- w_down: bfloat16 [5632, 2048], P(('batch', 'seq')), may hold values from -0.078125 to 0.078125
- bound_table: float32 [24, 2048], replicated, may hold values from -4 to 4
- layer_idx: int32 [1], replicated, may hold values from 1 to 23
Outputs:
- result: bfloat16 [16384, 2048], P(('batch', 'seq'))
- grad_tokens: float32 [16384, 2048], P(('batch', 'seq'))
- grad_attn_gain: float32 [2048], replicated
- grad_w_input: float32 [2048, 2048], P(('batch', 'seq'))
- grad_w_forget: float32 [2048, 2048], P(('batch', 'seq'))
- grad_w_outgate: float32 [2048, 2048], P(('batch', 'seq'))
- grad_w_out: float32 [2048, 2048], P(('batch', 'seq'))
- grad_norm_gain: float32 [2048], replicated
- feedforward_gain_gradient: float32 [2048], replicated
- grad_w_gate: float32 [2048, 5632], P(('batch', 'seq'))
- grad_w_up: float32 [2048, 5632], P(('batch', 'seq'))
- grad_w_down: float32 [5632, 2048], P(('batch', 'seq'))
- grad_bound_table: float32 [24, 2048], replicated
The draws below stay inside these ranges and needn't reach their ends.
All inputs are finite; a program needn't handle non-finite values.
Results may differ from the reference program's by a relative error of at most 0.009.
Values may be sent and summed in bfloat16 or wider, within the bound.
A program may use at most 704 MiB of HBM per device.

```python
import jax
import jax.numpy as jnp
from jax import lax

D = 2048
FF = 5632
LAYERS = 24
LEN = 8192
TOKENS = 16384
N_BATCH = 2


def shared_direction(key):
    return jnp.where(jax.random.bernoulli(key, 0.5, (D,)), 1.0, -1.0).astype(jnp.float32)


def draw_tokens(key, part):
    direction = shared_direction(key)
    key = jax.random.fold_in(key, 11)
    key_noise, key_marks = jax.random.split(key)
    noise_portion = jax.random.truncated_normal(key_noise, -6.0, 6.0, (TOKENS, D), jnp.float32)
    token_markers = jax.random.randint(key_marks, (8,), 0, TOKENS)
    row_numbers = jnp.arange(TOKENS, dtype=jnp.int32)[:, None]
    spike_rows = jnp.any(row_numbers == token_markers[None, :], axis=1, keepdims=True)
    raised_rows = jnp.where(spike_rows, 0.0, 1.5).astype(jnp.float32)
    return (noise_portion + raised_rows * direction[None, :]).astype(jnp.bfloat16)


def draw_w_forget(key, part):
    direction = shared_direction(key)
    key = jax.random.fold_in(key, 23)
    key_noise, key_rate, key_pick = jax.random.split(key, 3)
    noise_portion = 0.3 * jax.random.truncated_normal(key_noise, -4.0, 4.0, (D, D), jnp.float32) / jnp.sqrt(1.0 * D)
    rate_draw = jax.random.uniform(key_rate, (D,), jnp.float32)
    slow_keep = jnp.log(1.0 * LEN) + rate_draw * jnp.log(4.0)
    fast_keep = jnp.log(20.0) + rate_draw * jnp.log(3.0)
    slow_mask = jax.random.bernoulli(key_pick, 0.5, (D,))
    log_keep = jnp.where(slow_mask, slow_keep, fast_keep)
    reach = 1.5 / jnp.sqrt(1.0 + 1.5 * 1.5)
    return (noise_portion + log_keep[None, :] * direction[:, None] / (D * reach)).astype(jnp.bfloat16)


def block_levels(rng, shape, cuts, smallest, high):
    def one(axis_at, blocks):
        draws = jax.random.uniform(jax.random.fold_in(jax.random.fold_in(rng, 6), axis_at), (blocks,), jnp.float32, smallest / len(cuts), high / len(cuts))
        return jnp.repeat(jnp.exp(draws), shape[axis_at] // blocks).reshape((-1,) + (1,) * (len(shape) - axis_at - 1))

    factor_of = one(*cuts[0])
    for cut in cuts[1:]:
        factor_of = factor_of * one(*cut)
    return factor_of


def scatter_about(rng, dims, spread, most, shards=(), kind=jnp.bfloat16):
    values = jax.random.normal(rng, dims, jnp.float32) * spread
    if len(shards) > 0:
        values = block_levels(rng, dims, shards, -0.22, 0.18) * values
    return jnp.clip(values, min=-most, max=most).astype(kind)


def setup_inputs(seed: int = 0) -> dict:
    key_of = jax.random.split(jax.random.key(seed), 15)
    return {
        "tokens": draw_tokens(jax.random.fold_in(key_of[14], 71), 0),
        "cotangent": scatter_about(key_of[1], (TOKENS, D), 1.0, 6.0, ((0, 128),)),
        "attn_gain": jnp.clip(1.0 + 0.18 * jax.random.normal(key_of[2], (D,), jnp.float32), 0.1, 1.9),
        "w_input": scatter_about(key_of[3], (D, D), D ** -0.5, 0.125, ((0, 128),)),
        "w_forget": draw_w_forget(jax.random.fold_in(key_of[14], 71), 0),
        "w_outgate": scatter_about(key_of[5], (D, D), D ** -0.5, 0.125, ((0, 128),)),
        "w_out": scatter_about(key_of[6], (D, D), D ** -0.5, 0.125, ((0, 128),)),
        "norm_gain": jnp.clip(1.0 + 0.18 * jax.random.normal(key_of[7], (D,), jnp.float32), 0.1, 1.9),
        "mlp_gain": jnp.clip(1.0 + 0.18 * jax.random.normal(key_of[8], (D,), jnp.float32), 0.1, 1.9),
        "w_gate": scatter_about(key_of[9], (D, FF), D ** -0.5, 0.125, ((0, 128),)),
        "w_up": scatter_about(key_of[10], (D, FF), D ** -0.5, 0.125, ((0, 128),)),
        "w_down": scatter_about(key_of[11], (FF, D), FF ** -0.5, 0.078125, ((0, 128),)),
        "bound_table": scatter_about(key_of[12], (LAYERS, D), 1.0, 4.0, (), jnp.float32),
        "layer_idx": jax.random.randint(key_of[13], (1,), 1, LAYERS).astype(jnp.int32),
    }


@jax.custom_vjp
def low(v):
    return lax.optimization_barrier(v.astype(jnp.bfloat16)).astype(jnp.float32)

@jax.custom_vjp
def low_back(v):
    return v

def low_keep(v):
    return (low(v), None)

def low_pass(kept, grad):
    return (grad,)

def back_keep(v):
    return (v, None)

def back_low(kept, grad):
    return (low(grad),)
low.defvjp(low_keep, low_pass)
low_back.defvjp(back_keep, back_low)
EPS = 1e-06

def rms_norm(field, gain_vec):
    return field * lax.rsqrt(lax.optimization_barrier(jnp.mean(field * field, axis=-1, keepdims=True)) + EPS) * gain_vec

def matmul_hi(left_side, right_side):
    return jnp.dot(left_side, right_side, precision=lax.Precision.HIGHEST, preferred_element_type=jnp.float32)

def chain_link(earlier, later):
    return (earlier[0] * later[0], later[0] * earlier[1] + later[1])

def bound_value(bound_table, layer_idx):
    probabilities = jax.nn.softmax(bound_table, axis=0)
    levels = jnp.arange(bound_table.shape[0], dtype=jnp.int32)[:, None]
    keep_mask = jnp.where((levels >= 1) & (levels <= layer_idx[0]), 1.0, 0.0).astype(jnp.float32)
    return lax.optimization_barrier(jnp.sum(probabilities * keep_mask, axis=0))

def layer_forward(tokens, attn_gain, w_input, w_forget, w_outgate, w_out, norm_gain, mlp_gain, w_gate, w_up, w_down, bound_table, layer_idx):
    first_in = low(rms_norm(tokens, attn_gain))
    proj_in = low_back(matmul_hi(first_in, w_input))
    proj_forget = low_back(matmul_hi(first_in, w_forget))
    proj_gate = low_back(matmul_hi(first_in, w_outgate))
    lower_bound = bound_value(bound_table, layer_idx)
    forget = lower_bound + (1.0 - lower_bound) * jax.nn.sigmoid(proj_forget)
    inputs = jax.nn.silu(proj_in) * (1.0 - forget)
    seq_shape = (N_BATCH, LEN, D)
    decays, states = lax.associative_scan(chain_link, (forget.reshape(seq_shape), inputs.reshape(seq_shape)), axis=1)
    states = states.reshape(tokens.shape)
    gated = low(rms_norm(states, norm_gain) * jax.nn.silu(proj_gate))
    residual_mid = tokens + low_back(matmul_hi(gated, w_out))
    second_in = low(rms_norm(residual_mid, mlp_gain))
    gate_proj = low_back(matmul_hi(second_in, w_gate))
    up_proj = low_back(matmul_hi(second_in, w_up))
    hidden = low(jax.nn.silu(gate_proj) * up_proj)
    return residual_mid + matmul_hi(hidden, w_down)

def reference(tokens, cotangent, attn_gain, w_input, w_forget, w_outgate, w_out, norm_gain, mlp_gain, w_gate, w_up, w_down, bound_table, layer_idx):
    primals = (tokens.astype(jnp.float32), attn_gain, w_input.astype(jnp.float32), w_forget.astype(jnp.float32), w_outgate.astype(jnp.float32), w_out.astype(jnp.float32), norm_gain, mlp_gain, w_gate.astype(jnp.float32), w_up.astype(jnp.float32), w_down.astype(jnp.float32), bound_table)

    def forward(*params):
        return layer_forward(*params, layer_idx)
    output, pullback = jax.vjp(forward, *primals)
    grads = pullback(cotangent.astype(jnp.float32))
    return (output.astype(jnp.bfloat16), grads[0], grads[1], grads[2], grads[3], grads[4], grads[5], grads[6], grads[7], grads[8], grads[9], grads[10], grads[11])
```

```python
import functools

import jax
import jax.numpy as jnp
from jax import lax
from jax.experimental import pallas as pl
from jax.experimental.pallas import tpu as pltpu
from jax.sharding import Mesh, PartitionSpec as P

EPS = 1e-06
BF = jnp.bfloat16
F32 = jnp.float32
AXES = ("xlo", "xhi", "z", "y", "core")
MESH = pl.DeviceIdType.MESH
ANY = pl.BlockSpec(memory_space=pl.ANY)
VMEM = pl.BlockSpec(memory_space=pltpu.VMEM)
STEPS = (1, 3, 2)
GROUP = [(a, b) for a in range(4) for b in range(2) if a or b]
CHAIN = [(a, b) for a in range(2) for b in range(4) if a or b]
PLANE = [(a, b) for a in range(4) for b in range(4) if a or b]
HIGH = lax.Precision.HIGHEST


def ax(name):
    return lax.axis_index(name)


def ring(axis, s):
    if axis == "x":
        x = lax.rem(ax("xhi") * 2 + ax("xlo") + s, 4)
        return {"xhi": lax.div(x, 2), "xlo": lax.rem(x, 2)}
    return {axis: lax.rem(ax(axis) + s, 4)}


def sibling():
    return {"core": 1 - ax("core")}


def in_group(s, t):
    return {"y": lax.rem(ax("y") + s, 4), "core": lax.rem(ax("core") + t, 2)}


def in_chain(s, t):
    return {"xhi": lax.rem(ax("xhi") + s, 2), "z": lax.rem(ax("z") + t, 4)}


def in_plane(s, t):
    return {**ring("x", s), **ring("z", t)}


def place():
    return ax("xlo") * 8 + ax("xhi") * 4 + ax("z"), ax("y") * 2 + ax("core")


def device(p, g):
    return {
        "xlo": lax.div(p, 8),
        "xhi": lax.rem(lax.div(p, 4), 2),
        "z": lax.rem(p, 4),
        "y": lax.div(g, 2),
        "core": lax.rem(g, 2),
    }


class Copies:
    def __init__(self, send, recv, near):
        self.sems = (send, recv, near)
        self.count = 0
        self.locals = 0
        self.open = []

    def remote(self, src, dst, dev):
        i = self.count
        self.count += 1
        return pltpu.make_async_remote_copy(
            src_ref=src,
            dst_ref=dst,
            send_sem=self.sems[0].at[i],
            recv_sem=self.sems[1].at[i],
            device_id=dev,
            device_id_type=MESH,
        )

    def send(self, src, dst, dev):
        copy = self.remote(src, dst, dev)
        copy.start()
        self.open.append(copy)
        return copy

    def local(self, src, dst):
        copy = pltpu.make_async_copy(src, dst, self.sems[2].at[self.locals])
        self.locals += 1
        copy.start()
        return copy

    def finish(self):
        for copy in self.open:
            copy.wait_send()


def greet(peers, shuffle=None):
    bar = pltpu.get_barrier_semaphore()
    for dev in peers:
        pl.semaphore_signal(bar, inc=1, device_id=dev, device_id_type=MESH)
    count = len(peers)
    if shuffle is not None:
        source, from_me, to_me = shuffle

        @pl.when(jnp.logical_not(from_me))
        def _():
            pl.semaphore_signal(bar, inc=1, device_id=source, device_id_type=MESH)

        count = count + jnp.where(to_me, 0, 1)
    pl.semaphore_wait(bar, count)


def rings():
    return [ring("x", s) for s in STEPS] + [ring("z", s) for s in STEPS]


def ys():
    return [ring("y", s) for s in STEPS] + [sibling()]


def run(chains, order):
    for i in order:
        next(chains[i], None)
    for chain in chains:
        for _ in chain:
            pass


def rows_of(i, n=16):
    return pl.ds(pl.multiple_of(i * n, n), n)


def group_gather(cp, src, full):
    g = place()[1]
    own = cp.local(src, full.at[g])
    moved = {s: cp.send(src, full.at[g], ring("y", s)) for s in STEPS}
    near = [cp.send(src, full.at[g], sibling())]
    yield
    for s in STEPS:
        moved[s].wait_recv()
        k = 2 * lax.rem(ax("y") + 4 - s, 4) + ax("core")
        near.append(cp.send(full.at[k], full.at[k], sibling()))
    yield
    for copy in near:
        copy.wait_recv()
    own.wait()


def group_sum(cp, part, mine, near, far, out):
    c = ax("core")
    block = {s: 2 * lax.rem(ax("y") + s, 4) for s in range(4)}
    sent = {s: cp.send(part.at[block[s] + 1 - c], near.at[s], sibling()) for s in (2, 1, 3, 0)}
    own = {s: cp.local(part.at[block[s] + c], mine.at[s]) for s in (2, 1, 3, 0)}
    yield
    moved = {}
    for s in (2, 1, 3):
        own[s].wait()
        sent[s].wait_recv()

        def add(i, carry, s=s):
            r = rows_of(i)
            mine[s, r, :] = (mine[s, r, :].astype(F32) + near[s, r, :].astype(F32)).astype(BF)
            return carry

        lax.fori_loop(0, mine.shape[1] // 16, add, 0)
        moved[s] = cp.send(mine.at[s], far.at[s - 1], ring("y", s))
    own[0].wait()
    sent[0].wait_recv()
    yield
    for s in (1, 3, 2):
        moved[s].wait_recv()

    def total(r):
        acc = mine[0, r, :].astype(F32) + near[0, r, :].astype(F32)
        for s in range(3):
            acc = acc + far[s, r, :].astype(F32)
        return acc

    out.append(total)


def group_sum_scratch(rows, width):
    return [
        pltpu.VMEM((4, rows, width), BF),
        pltpu.VMEM((4, rows, width), BF),
        pltpu.VMEM((3, rows, width), BF),
    ]


def plane_gather(cp, buf, halves):
    me = (ax("xlo"), ax("xhi"), ax("z"))

    def view(h, *at):
        return buf.at[at + halves[h]]

    first = []
    for s in STEPS:
        first.append(cp.send(view(0, *me), view(0, *me), ring("z", s)))
        first.append(cp.send(view(1, *me), view(1, *me), ring("x", s)))
    yield
    for copy in first:
        copy.wait_recv()
    column = view(0, me[0], me[1], pl.ds(0, 4))
    row = view(1, pl.ds(0, 2), pl.ds(0, 2), me[2])
    wide = {}
    for s in (1, 3):
        wide["x", s] = cp.send(column, column, ring("x", s))
        wide["z", s] = cp.send(row, row, ring("z", s))
    yield
    last = []
    for s in (1, 3):
        back = ring("x", 4 - s)
        wide["x", s].wait_recv()
        v = view(0, back["xlo"], back["xhi"], pl.ds(0 if s == 1 else 2, 2))
        last.append(cp.send(v, v, ring("x", s)))
        back = ring("z", 4 - s)
        wide["z", s].wait_recv()
        v = view(1, 0 if s == 1 else 1, pl.ds(0, 2), back["z"])
        last.append(cp.send(v, v, ring("z", s)))
    yield
    for copy in last:
        copy.wait_recv()


def half_shapes(halves):
    return [tuple(d.size for d in h) for h in halves]


def plane_sum_scratch(halves):
    a, b = half_shapes(halves)
    return [
        pltpu.VMEM((4,) + a, BF),
        pltpu.VMEM((3, 4) + a, BF),
        pltpu.VMEM((3,) + a, BF),
        pltpu.VMEM((2, 2) + b, BF),
        pltpu.VMEM((3, 2, 2) + b, BF),
        pltpu.VMEM((3,) + b, BF),
    ]


def plane_sum(cp, part, halves, own_a, far_a, last_a, own_b, far_b, last_b, out):
    me = (ax("xlo"), ax("xhi"), ax("z"))
    shape_a, shape_b = half_shapes(halves)

    def view(h, *at):
        return part.at[at + halves[h]]

    near_a = cp.local(view(0, me[0], me[1], pl.ds(0, 4)), own_a)
    near_b = cp.local(view(1, pl.ds(0, 2), pl.ds(0, 2), me[2]), own_b)
    first_a, first_b = [], []
    for j, s in enumerate(STEPS):
        d = ring("x", s)
        first_a.append(cp.send(view(0, d["xlo"], d["xhi"], pl.ds(0, 4)), far_a.at[j], d))
        d = ring("z", s)
        first_b.append(cp.send(view(1, pl.ds(0, 2), pl.ds(0, 2), d["z"]), far_b.at[j], d))
    yield
    near_a.wait()
    for copy in first_a:
        copy.wait_recv()
    for k in range(4):

        def add(i, carry, k=k):
            r = rows_of(i)
            acc = own_a[k, r, :].astype(F32)
            for j in range(3):
                acc = acc + far_a[j, k, r, :].astype(F32)
            own_a[k, r, :] = acc.astype(BF)
            return carry

        lax.fori_loop(0, shape_a[0] // 16, add, 0)
    second = []
    for j, s in enumerate(STEPS):
        d = ring("z", s)
        second.append(cp.send(own_a.at[d["z"]], last_a.at[j], d))
    near_b.wait()
    for copy in first_b:
        copy.wait_recv()
    for k in range(4):

        def add(i, carry, k=k):
            r = rows_of(i)
            acc = own_b[k // 2, k % 2, r, :].astype(F32)
            for j in range(3):
                acc = acc + far_b[j, k // 2, k % 2, r, :].astype(F32)
            own_b[k // 2, k % 2, r, :] = acc.astype(BF)
            return carry

        lax.fori_loop(0, shape_b[0] // 16, add, 0)
    for j, s in enumerate(STEPS):
        d = ring("x", s)
        second.append(cp.send(own_b.at[d["xlo"], d["xhi"]], last_b.at[j], d))
    yield
    for copy in second:
        copy.wait_recv()

    def end_a(i, carry):
        r = rows_of(i)
        acc = own_a[me[2], r, :].astype(F32)
        for j in range(3):
            acc = acc + last_a[j, r, :].astype(F32)
        at = rows_of(i) if halves[0][0].start == 0 else pl.ds(halves[0][0].start + i * 16, 16)
        out[at, halves[0][1]] = acc.astype(BF)
        return carry

    lax.fori_loop(0, shape_a[0] // 16, end_a, 0)

    def end_b(i, carry):
        r = rows_of(i)
        acc = own_b[me[0], me[1], r, :].astype(F32)
        for j in range(3):
            acc = acc + last_b[j, r, :].astype(F32)
        at = pl.ds(pl.multiple_of(halves[1][0].start + i * 16, 16), 16)
        out[at, halves[1][1]] = acc.astype(BF)
        return carry

    lax.fori_loop(0, shape_b[0] // 16, end_b, 0)


def by_rows(rows, width):
    h = rows // 2
    return ((pl.ds(0, h), pl.ds(0, width)), (pl.ds(h, h), pl.ds(0, width)))


def by_columns(rows, width):
    h = width // 2
    return ((pl.ds(0, rows), pl.ds(0, h)), (pl.ds(0, rows), pl.ds(h, h)))


def call(body, name, ident, out_shape, in_specs, out_specs, scratch, sems, near, **kw):
    return pl.pallas_call(
        body,
        name=name,
        out_shape=out_shape,
        in_specs=in_specs,
        out_specs=out_specs,
        scratch_shapes=list(scratch)
        + [
            pltpu.SemaphoreType.DMA((sems,)),
            pltpu.SemaphoreType.DMA((sems,)),
            pltpu.SemaphoreType.DMA((near,)),
        ],
        compiler_params=pltpu.CompilerParams(
            collective_id=ident, has_side_effects=True, vmem_limit_bytes=56 << 20
        ),
        **kw,
    )


def gather_body(
    tok, gain, w_in, w_f, w_og, w_o, gu, dn, cot, b3, bo, bgu, bdn, fi, gf, first, send, recv, near
):
    cp = Copies(send, recv, near)
    p, g = place()
    d = p * 8 + g
    to_p, to_g = lax.rem(d, 16), lax.div(d, 16)
    from_d = 16 * g + p
    target = device(to_p, to_g)
    source = device(lax.div(from_d, 8), lax.rem(from_d, 8))
    same = to_p * 8 + to_g == d
    greet(rings() + [in_group(*st) for st in GROUP], (source, from_d == d, same))
    me = (ax("xlo"), ax("xhi"), ax("z"))
    mine16 = pl.ds(pl.multiple_of(g * 16, 16), 16)
    shards = (w_in, w_f, w_og)
    third = w_in.shape[1] // 8
    locals_ = []
    arrive3, arrive_gu = [], []
    for j, w in enumerate(shards):
        to = b3.at[me + (mine16, pl.ds(j * third, third))]
        for st in GROUP:
            q = in_group(*st)
            k = q["y"] * 2 + q["core"]
            arrive3.append(cp.send(w.at[:, pl.ds(pl.multiple_of(k * third, 128), third)], to, q))
        locals_.append(cp.local(w.at[:, pl.ds(pl.multiple_of(g * third, 128), third)], to))

    shuffles = []
    for src, buf in ((w_o, bo), (dn, bdn)):
        at = (lax.div(to_p, 8), lax.rem(lax.div(to_p, 4), 2), lax.rem(to_p, 4))
        copy = cp.remote(src, buf.at[at], target)
        home = pltpu.make_async_copy(src, buf.at[at], cp.sems[2].at[cp.locals])
        cp.locals += 1

        @pl.when(same)
        def _(home=home):
            home.start()

        @pl.when(jnp.logical_not(same))
        def _(copy=copy):
            copy.start()

        shuffles.append((copy, home))
    to = bgu.at[me + (mine16,)]
    for st in GROUP:
        q = in_group(*st)
        arrive_gu.append(cp.send(gu.at[q["y"] * 2 + q["core"]], to, q))
    locals_.append(cp.local(gu.at[g], to))

    def norm(i, carry):
        r = rows_of(i)
        x = tok[r, :].astype(F32)
        s = lax.rsqrt(jnp.mean(x * x, axis=-1, keepdims=True) + EPS)
        first[r, :] = (x * s * gain[...]).astype(BF)
        return carry

    lax.fori_loop(0, tok.shape[0] // 16, norm, 0)
    chain_fi = group_gather(cp, first, fi)
    next(chain_fi)
    chain_g = group_gather(cp, cot, gf)
    next(chain_g)
    for copy in arrive3 + arrive_gu:
        copy.wait_recv()
    for copy in locals_:
        copy.wait()

    for copy, home in shuffles:

        @pl.when(same)
        def _(home=home):
            home.wait()

        @pl.when(jnp.logical_not(same))
        def _(copy=copy):
            copy.wait()

    rows = b3.shape[3]
    chains = [
        plane_gather(cp, b3, by_rows(rows, b3.shape[4])),
        plane_gather(cp, bo, by_columns(16, bo.shape[4])),
        plane_gather(cp, bgu, by_rows(rows, bgu.shape[4])),
        plane_gather(cp, bdn, by_columns(bdn.shape[3], bdn.shape[4])),
        chain_fi,
        chain_g,
    ]
    run(chains, (0, 1, 2, 3, 0, 1, 2, 3, 4, 0, 1, 5, 2, 3))
    cp.finish()


def silu_slope(v, s):
    return s * (1.0 + v * (1.0 - s))


def row_sums(x):
    ones = jnp.ones((8, x.shape[1]), F32)
    return lax.dot_general(
        ones, x, (((1,), (1,)), ((), ())), precision=HIGH, preferred_element_type=F32
    )[0:1]


def as_column(row, width):
    t = jnp.transpose(jnp.broadcast_to(row, (128, 128)))
    return jnp.concatenate([t] * (width // 128), axis=1)


def chunk_rows(s):
    return pl.ds(pl.multiple_of(s * 128, 128), 128)


def wide(ref, r):
    return jnp.concatenate([ref[j, r, :] for j in range(ref.shape[0])], axis=1)


def put(ref, r, value):
    for j in range(ref.shape[0]):
        ref[j, r, :] = value[:, 128 * j : 128 * (j + 1)]


def share(cp, src, dst, index, peers):
    copies = [cp.send(src, dst.at[index], dev) for dev in peers]
    dst[pl.ds(index, 1)] = src[...][None]
    return copies


def scan_body(
    proj, lb, gain, gated, states, forget, tot, links, carry, prod, entry, mine, rowsum, rows8, send, recv, near
):
    cp = Copies(send, recv, near)
    tiles, rows = states.shape[:2]
    w = 128 * tiles
    steps = rows // 8
    peers_chain = [in_chain(*st) for st in CHAIN]
    peers_group = [in_group(*st) for st in GROUP]
    greet(peers_chain + peers_group)
    low = lb[...]

    def gates(i, c):
        r = rows_of(i, 32)
        f = low + (1.0 - low) * jax.nn.sigmoid(proj[r, w : 2 * w])
        v = proj[r, 0:w]
        put(forget, r, f)
        put(states, r, v * jax.nn.sigmoid(v) * (1.0 - f))
        return c

    lax.fori_loop(0, 8 * steps // 32, gates, 0)

    def step(t, c):
        at = pl.ds(t, 8, stride=steps)
        new = []
        for j, (h, a) in enumerate(c):
            f = forget[j, at, :]
            h = f * h + states[j, at, :]
            a = a * f
            states[j, at, :] = h
            prod[j, at, :] = a
            new.append((h, a))
        return tuple(new)

    start = ((jnp.zeros((8, 128), F32), jnp.ones((8, 128), F32)),) * tiles
    ends = lax.fori_loop(0, steps, step, start, unroll=8)
    h = jnp.concatenate([e[0] for e in ends], axis=1)
    a = jnp.concatenate([e[1] for e in ends], axis=1)
    c = jnp.zeros((1, w), F32)
    q = jnp.ones((1, w), F32)
    cs, qs = [], []
    for s in range(8):
        cs.append(c)
        qs.append(q)
        c = a[s : s + 1] * c + h[s : s + 1]
        q = a[s : s + 1] * q
    mine[...] = jnp.concatenate([q, c, jnp.zeros((6, w), F32)], axis=0)
    k = ax("xhi") * 4 + ax("z")
    for copy in share(cp, mine, links, k, peers_chain):
        copy.wait_recv()
    come = jnp.zeros((1, w), F32)
    for j in range(8):
        new = links[j, 0:1, :] * come + links[j, 1:2, :]
        come = jnp.where(j < k, new, come)
    carry[...] = jnp.broadcast_to(come, (8, w))
    entry[...] = jnp.concatenate(qs, axis=0) * come + jnp.concatenate(cs, axis=0)

    def finish(s, c):
        r = chunk_rows(s)
        st = wide(states, r) + wide(prod, r) * entry[pl.ds(s, 1), :]
        put(states, r, st)
        rowsum[pl.ds(s, 1), :] = row_sums(st * st)
        return c

    lax.fori_loop(0, 8, finish, 0)
    for copy in share(cp, rowsum, rows8, place()[1], peers_group):
        copy.wait_recv()
    total = rows8[0]
    for j in range(1, 8):
        total = total + rows8[j]
    tot[...] = lax.rsqrt(total / (8.0 * w) + EPS)

    def gate(s, c):
        r = chunk_rows(s)
        v = proj[r, 2 * w : 3 * w]
        n = wide(states, r) * as_column(tot[pl.ds(s, 1), :], w)
        gated[r, :] = (n * gain[...] * (v * jax.nn.sigmoid(v))).astype(BF)
        return c

    lax.fori_loop(0, 8, gate, 0)
    cp.finish()


def middle_body(part, tok, gain, mid, full, own, near_, far, block, send, recv, near):
    cp = Copies(send, recv, near)
    greet(ys())
    sums = []
    run([group_sum(cp, part, own, near_, far, sums)], ())

    def norm(i, carry):
        r = rows_of(i)
        x = tok[r, :].astype(F32) + sums[0](r)
        mid[r, :] = x
        s = lax.rsqrt(jnp.mean(x * x, axis=-1, keepdims=True) + EPS)
        block[r, :] = (x * s * gain[...]).astype(BF)
        return carry

    lax.fori_loop(0, mid.shape[0] // 16, norm, 0)
    run([group_gather(cp, block, full)], ())
    cp.finish()


def turn_body(
    part, part_r, mid, cot, gain, result, mixed, full, sums_out, own, near_, far, own_r, near_r, far_r, block, send, recv, near
):
    cp = Copies(send, recv, near)
    greet(ys())
    sums, sums_r = [], []
    chain = group_sum(cp, part, own, near_, far, sums)
    chain_r = group_sum(cp, part_r, own_r, near_r, far_r, sums_r)
    run([chain, chain_r], (0, 0, 1, 1, 0))
    sums_out[...] = jnp.zeros_like(sums_out)

    def back(i, carry):
        r = rows_of(i)
        x = mid[r, :]
        s = lax.rsqrt(jnp.mean(x * x, axis=-1, keepdims=True) + EPS)
        n = x * s
        dy = sums[0](r)
        sums_out[0:1, :] = sums_out[0:1, :] + jnp.sum(dy * n, axis=0, keepdims=True)
        dy = dy * gain[...]
        v = cot[r, :].astype(F32) + s * (dy - n * jnp.mean(dy * n, axis=-1, keepdims=True))
        mixed[r, :] = v
        block[r, :] = v.astype(BF)
        result[r, :] = (x + sums_r[0](r)).astype(BF)
        return carry

    lax.fori_loop(0, mid.shape[0] // 16, back, 0)
    run([group_gather(cp, block, full)], ())
    cp.finish()


def back_body(
    gg, proj, states, forget, tot, links, carry, lb, gain, grads, sums_out, gs, prod, entry, mine, rowsum, rows8, far, send, recv, near
):
    cp = Copies(send, recv, near)
    tiles, rows = states.shape[:2]
    w = 128 * tiles
    steps = rows // 8
    peers_chain = [in_chain(*st) for st in CHAIN]
    peers_group = [in_group(*st) for st in GROUP]
    greet(peers_chain + peers_group)
    low = lb[...]
    sums_out[...] = jnp.zeros_like(sums_out)

    def through(s, c):
        r = chunk_rows(s)
        v = proj[r, 2 * w : 3 * w]
        sig = jax.nn.sigmoid(v)
        n = wide(states, r) * as_column(tot[pl.ds(s, 1), :], w)
        dy = gg[r, :]
        sums_out[0:1, :] = sums_out[0:1, :] + jnp.sum(dy * n * (v * sig), axis=0, keepdims=True)
        grads[r, 2 * w : 3 * w] = (dy * n * gain[...] * silu_slope(v, sig)).astype(BF)
        dy = dy * gain[...] * (v * sig)
        put(gs, r, dy)
        rowsum[pl.ds(s, 1), :] = row_sums(dy * n)
        return c

    lax.fori_loop(0, 8, through, 0)
    for copy in share(cp, rowsum, rows8, place()[1], peers_group):
        copy.wait_recv()
    total = rows8[0]
    for j in range(1, 8):
        total = total + rows8[j]
    def norm(s, c):
        r = chunk_rows(s)
        t = as_column(tot[pl.ds(s, 1), :], w)
        m = as_column(rowsum[pl.ds(s, 1), :], w)
        put(gs, r, t * (wide(gs, r) - wide(states, r) * t * m))
        return c

    cp.finish()
    cp.open = []
    rowsum[...] = total / (8.0 * w)
    lax.fori_loop(0, 8, norm, 0)

    def step(i, c):
        at = pl.ds(steps - 1 - i, 8, stride=steps)
        new = []
        for j, (h, a) in enumerate(c):
            f = forget[j, at, :]
            v = gs[j, at, :] + h
            gs[j, at, :] = v
            prod[j, at, :] = a
            new.append((f * v, a * f))
        return tuple(new)

    start = ((jnp.zeros((8, 128), F32), jnp.ones((8, 128), F32)),) * tiles
    ends = lax.fori_loop(0, steps, step, start, unroll=8)
    h = jnp.concatenate([e[0] for e in ends], axis=1)
    a = jnp.concatenate([e[1] for e in ends], axis=1)
    c = jnp.zeros((1, w), F32)
    q = jnp.ones((1, w), F32)
    cs, qs = [None] * 8, [None] * 8
    for s in range(7, -1, -1):
        cs[s] = c
        qs[s] = q
        c = a[s : s + 1] * c + h[s : s + 1]
        q = a[s : s + 1] * q
    mine[...] = jnp.broadcast_to(c, (8, w))
    k = ax("xhi") * 4 + ax("z")
    for copy in share(cp, mine, far, k, peers_chain):
        copy.wait_recv()
    come = jnp.zeros((1, w), F32)
    for j in range(7, -1, -1):
        new = links[j, 0:1, :] * come + far[j, 0:1, :]
        come = jnp.where(j > k, new, come)
    entry[...] = jnp.concatenate(qs, axis=0) * come + jnp.concatenate(cs, axis=0)

    def last(s, c):
        r = chunk_rows(s)
        v = wide(gs, r) + wide(prod, r) * entry[pl.ds(s, 1), :]
        st = wide(states, r)
        above = pl.ds(jnp.maximum(s * 128 - 1, 0), 1)
        before = jnp.where(s == 0, carry[0:1, :], wide(states, above))
        top = lax.broadcasted_iota(jnp.int32, (128, w), 0) == 0
        prev = jnp.where(top, before, pltpu.roll(st, 1, 0))
        x = proj[r, 0:w]
        sx = jax.nn.sigmoid(x)
        f = wide(forget, r)
        sf = jax.nn.sigmoid(proj[r, w : 2 * w])
        gf = v * (prev - x * sx)
        grads[r, 0:w] = (v * (1.0 - f) * silu_slope(x, sx)).astype(BF)
        grads[r, w : 2 * w] = (gf * (1.0 - low) * sf * (1.0 - sf)).astype(BF)
        sums_out[1:2, :] = sums_out[1:2, :] + jnp.sum(gf * (1.0 - sf), axis=0, keepdims=True)
        return c

    lax.fori_loop(0, 8, last, 0)
    cp.finish()


def sum_body(*refs):
    (part, tok, mixed, gain, ffn_sums, mix_sums, d3, do, dgu, ddn) = refs[:10]
    (gtok, r3, rgu, ro, rdn, totals) = refs[10:16]
    scratch = list(refs[16:-3])
    cp = Copies(*refs[-3:])
    own, near_, far = scratch[:3]
    plane = [scratch[3 + 6 * i : 9 + 6 * i] for i in range(4)]
    o3, ogu, oo, od, va, ga, ta, gb, tb = scratch[27:]
    p, g = place()
    d = p * 8 + g
    from_d = 16 * g + p
    same = from_d == d
    target = device(lax.div(from_d, 8), lax.rem(from_d, 8))
    source = device(lax.rem(d, 16), lax.div(d, 16))
    greet(
        [in_plane(*st) for st in PLANE] + [in_group(*st) for st in GROUP],
        (source, lax.rem(d, 16) * 8 + lax.div(d, 16) == d, same),
    )
    sums = []
    rows = d3.shape[3]
    chain = group_sum(cp, part, own, near_, far, sums)
    chains = [
        plane_sum(cp, dgu, by_rows(rows, dgu.shape[4]), *plane[0], ogu),
        plane_sum(cp, ddn, by_columns(ddn.shape[3], ddn.shape[4]), *plane[1], od),
        plane_sum(cp, d3, by_rows(rows, d3.shape[4]), *plane[2], o3),
        plane_sum(cp, do, by_columns(16, do.shape[4]), *plane[3], oo),
    ]
    next(chain)
    for c in chains:
        next(c)
    next(chain)
    for _ in chain:
        pass
    va[...] = jnp.zeros_like(va)

    def back(i, carry):
        r = rows_of(i)
        x = tok[r, :].astype(F32)
        s = lax.rsqrt(jnp.mean(x * x, axis=-1, keepdims=True) + EPS)
        n = x * s
        dy = sums[0](r)
        va[0:1, :] = va[0:1, :] + jnp.sum(dy * n, axis=0, keepdims=True)
        dy = dy * gain[...]
        gtok[r, :] = mixed[r, :] + s * (dy - n * jnp.mean(dy * n, axis=-1, keepdims=True))
        return carry

    lax.fori_loop(0, gtok.shape[0] // 16, back, 0)
    va[1:2, :] = ffn_sums[0:1, :]
    w = ga.shape[2]
    small = []
    for st in GROUP:
        q = in_group(*st)
        k = q["y"] * 2 + q["core"]
        small.append(cp.send(va.at[:, pl.ds(pl.multiple_of(k * w, 128), w)], ga.at[g], q))
    ga[pl.ds(g, 1)] = va[:, pl.ds(pl.multiple_of(g * w, 128), w)][None]
    for c in chains:
        next(c)
    for copy in small:
        copy.wait_recv()
    acc = ga[0]
    for j in range(1, 8):
        acc = acc + ga[j]
    ta[...] = acc
    ta[2:4, :] = mix_sums[0:2, :]
    for copy in share(cp, ta, gb, p, [in_plane(*st) for st in PLANE]):
        copy.wait_recv()
    acc = gb[0]
    for j in range(1, 16):
        acc = acc + gb[j]
    tb[...] = acc
    small = share(cp, tb, totals, g, [in_group(*st) for st in GROUP])
    for c in chains:
        for _ in c:
            pass
    arrive = []
    near_copies = []
    for src, dst in ((ogu, rgu), (o3, r3)):
        for st in GROUP:
            q = in_group(*st)
            k = q["y"] * 2 + q["core"]
            at = pl.ds(pl.multiple_of(k * 16, 16), 16)
            arrive.append(cp.send(src.at[at, :], dst.at[g], q))
        near_copies.append(cp.local(src.at[pl.ds(pl.multiple_of(g * 16, 16), 16), :], dst.at[g]))
    shuffles = []
    for src, dst in ((oo, ro), (od, rdn)):
        copy = cp.remote(src, dst, target)
        home = pltpu.make_async_copy(src, dst, cp.sems[2].at[cp.locals])
        cp.locals += 1

        @pl.when(same)
        def _(home=home):
            home.start()

        @pl.when(jnp.logical_not(same))
        def _(copy=copy):
            copy.start()

        shuffles.append((copy, home))
    for copy in small + arrive:
        copy.wait_recv()
    for copy in near_copies:
        copy.wait()
    for copy, home in shuffles:

        @pl.when(same)
        def _(home=home):
            home.wait()

        @pl.when(jnp.logical_not(same))
        def _(copy=copy):
            copy.wait()

    cp.finish()


def bound_value(bound_table, layer_idx):
    probabilities = jax.nn.softmax(bound_table, axis=0)
    levels = jnp.arange(bound_table.shape[0], dtype=jnp.int32)[:, None]
    keep = jnp.where((levels >= 1) & (levels <= layer_idx[0]), 1.0, 0.0).astype(F32)
    return jnp.sum(probabilities * keep, axis=0)


def dot(a, b, dims):
    return lax.dot_general(a, b, (dims, ((), ())), preferred_element_type=F32)


NN = ((1,), (0,))
NT = ((1,), (1,))
TN = ((0,), (0,))


def on_device(
    tokens, cotangent, attn_gain, w_input, w_forget, w_outgate, w_out, norm_gain, mlp_gain, w_gate, w_up, w_down, bound_table, layer_idx
):
    n, width = tokens.shape
    rows = w_input.shape[0]
    hidden_width = w_gate.shape[1]
    down = w_down.shape[0]
    padded = -(-down // 16) * 16
    unit = 16 * padded
    w = width // 8
    shape = jax.ShapeDtypeStruct

    def spread(m):
        m = jnp.pad(m.reshape(rows, 128, down), ((0, 0), (0, 0), (0, padded - down)))
        return m.reshape(rows, 8, unit).transpose(1, 0, 2)

    gu = jnp.concatenate([spread(w_gate), spread(w_up)], axis=2)
    dn = jnp.pad(w_down, ((0, padded - down), (0, 0)))
    gains = attn_gain[None, :]
    b3, bo, bgu, bdn, fi, gf = call(
        gather_body,
        "gather",
        0,
        [
            shape((2, 2, 4, 8 * rows, 3 * w), BF),
            shape((2, 2, 4, rows, width), BF),
            shape((2, 2, 4, 8 * rows, 2 * unit), BF),
            shape((2, 2, 4, padded, width), BF),
            shape((8, n, width), BF),
            shape((8, n, width), BF),
        ],
        [VMEM, VMEM] + [ANY] * 7,
        [ANY] * 6,
        [pltpu.VMEM((n, width), BF)],
        110,
        10,
    )(tokens, gains, w_input, w_forget, w_outgate, w_out, gu, dn, cotangent)
    big3 = b3.reshape(width, 3 * w)
    big_out = bo.reshape(w, width)
    big_gu = bgu.reshape(width, 2 * unit)
    big_down = bdn.reshape(unit, width)
    first_full = fi.reshape(8 * n, width)
    g_full = gf.reshape(8 * n, width)

    group = ax("y") * 2 + ax("core")
    lower = bound_value(lax.dynamic_slice_in_dim(bound_table, group * w, w, 1), layer_idx)[None, :]
    mixer_gain = lax.dynamic_slice_in_dim(norm_gain, group * w, w, 0)[None, :]
    proj = dot(first_full, big3, NN)
    gated, states, forget, tot, links, carry = call(
        scan_body,
        "scan",
        1,
        [
            shape((8 * n, w), BF),
            shape((w // 128, 8 * n, 128), F32),
            shape((w // 128, 8 * n, 128), F32),
            shape((8, n), F32),
            shape((8, 8, w), F32),
            shape((8, w), F32),
        ],
        [VMEM] * 3,
        [VMEM] * 6,
        [
            pltpu.VMEM((w // 128, 8 * n, 128), F32),
            pltpu.VMEM((8, w), F32),
            pltpu.VMEM((8, w), F32),
            pltpu.VMEM((8, n), F32),
            pltpu.VMEM((8, 8, n), F32),
        ],
        16,
        2,
    )(proj, lower, mixer_gain)
    mid_part = dot(gated, big_out, NN).astype(BF).reshape(8, n, width)
    sum_scratch = group_sum_scratch(n, width)
    mid, si = call(
        middle_body,
        "middle",
        2,
        [shape((n, width), F32), shape((8, n, width), BF)],
        [ANY, VMEM, VMEM],
        [VMEM, ANY],
        sum_scratch + [pltpu.VMEM((n, width), BF)],
        20,
        8,
    )(mid_part, tokens, mlp_gain[None, :])
    second_full = si.reshape(8 * n, width)
    gate_up = dot(second_full, big_gu, NN)
    gate_proj, up_proj = gate_up[:, :unit], gate_up[:, unit:]
    sig = jax.nn.sigmoid(gate_proj)
    act = gate_proj * sig
    hidden = (act * up_proj).astype(BF)
    result_part = dot(hidden, big_down, NN).astype(BF).reshape(8, n, width)

    grad_hidden = dot(g_full, big_down, NT)
    grad_gate = (grad_hidden * up_proj * silu_slope(gate_proj, sig)).astype(BF)
    grad_up = (grad_hidden * act).astype(BF)
    grad_gu = jnp.concatenate([grad_gate, grad_up], axis=1)
    second_part = dot(grad_gu, big_gu, NT).astype(BF).reshape(8, n, width)
    result, mixed, gb, ffn_sums = call(
        turn_body,
        "turn",
        3,
        [
            shape((n, width), BF),
            shape((n, width), F32),
            shape((8, n, width), BF),
            shape((8, width), F32),
        ],
        [ANY, ANY, VMEM, VMEM, VMEM],
        [VMEM, VMEM, ANY, VMEM],
        sum_scratch + sum_scratch + [pltpu.VMEM((n, width), BF)],
        32,
        12,
    )(second_part, result_part, mid, cotangent, mlp_gain[None, :])
    branch_full = gb.reshape(8 * n, width)
    grad_gated = dot(branch_full, big_out, NT)
    grads3, mix_sums = call(
        back_body,
        "back",
        4,
        [shape((8 * n, 3 * w), BF), shape((8, w), F32)],
        [VMEM] * 9,
        [VMEM] * 2,
        [
            pltpu.VMEM((w // 128, 8 * n, 128), F32),
            pltpu.VMEM((w // 128, 8 * n, 128), F32),
            pltpu.VMEM((8, w), F32),
            pltpu.VMEM((8, w), F32),
            pltpu.VMEM((8, n), F32),
            pltpu.VMEM((8, 8, n), F32),
            pltpu.VMEM((8, 8, w), F32),
        ],
        16,
        2,
    )(grad_gated, proj, states, forget, tot, links, carry, lower, mixer_gain)
    first_part = dot(grads3, big3, NT).astype(BF).reshape(8, n, width)

    d3 = dot(first_full, grads3, TN).astype(BF).reshape(2, 2, 4, 8 * rows, 3 * w)
    do = dot(gated, branch_full, TN).astype(BF).reshape(2, 2, 4, rows, width)
    dgu = dot(second_full, grad_gu, TN).astype(BF).reshape(2, 2, 4, 8 * rows, 2 * unit)
    ddn = dot(hidden, g_full, TN).astype(BF).reshape(2, 2, 4, padded, width)
    plane_scratch = (
        plane_sum_scratch(by_rows(8 * rows, 2 * unit))
        + plane_sum_scratch(by_columns(padded, width))
        + plane_sum_scratch(by_rows(8 * rows, 3 * w))
        + plane_sum_scratch(by_columns(rows, width))
    )
    grad_tokens, r3, rgu, ro, rdn, totals = call(
        sum_body,
        "sums",
        5,
        [
            shape((n, width), F32),
            shape((8, rows, 3 * w), BF),
            shape((8, rows, 2 * unit), BF),
            shape((rows, width), BF),
            shape((padded, width), BF),
            shape((8, 8, w), F32),
        ],
        [ANY, VMEM, VMEM, VMEM, VMEM, VMEM] + [ANY] * 4,
        [VMEM, VMEM, VMEM, VMEM, VMEM, VMEM],
        sum_scratch
        + plane_scratch
        + [
            pltpu.VMEM((8 * rows, 3 * w), BF),
            pltpu.VMEM((8 * rows, 2 * unit), BF),
            pltpu.VMEM((rows, width), BF),
            pltpu.VMEM((padded, width), BF),
            pltpu.VMEM((8, width), F32),
            pltpu.VMEM((8, 8, w), F32),
            pltpu.VMEM((8, w), F32),
            pltpu.VMEM((16, 8, w), F32),
            pltpu.VMEM((8, w), F32),
        ],
        110,
        18,
    )(first_part, tokens, mixed, gains, ffn_sums, mix_sums, d3, do, dgu, ddn)

    def join(m):
        m = m.transpose(1, 0, 2)
        return m.reshape(rows, 8 * m.shape[2]).astype(F32)

    def unspread(m):
        m = m.transpose(1, 0, 2).reshape(rows, 128, padded)[:, :, :down]
        return m.reshape(rows, hidden_width).astype(F32)

    sums = totals.transpose(1, 0, 2).reshape(8, width)
    pullback = jax.vjp(lambda table: bound_value(table, layer_idx), bound_table)[1]
    return (
        result,
        grad_tokens,
        sums[0],
        join(r3[:, :, :w]),
        join(r3[:, :, w : 2 * w]),
        join(r3[:, :, 2 * w :]),
        ro.astype(F32),
        sums[2],
        sums[1],
        unspread(rgu[:, :, :unit]),
        unspread(rgu[:, :, unit:]),
        rdn[:down].astype(F32),
        pullback(sums[3])[0],
    )


def solution(mesh):
    split = Mesh(mesh.devices.reshape(2, 2, 4, 4, 2), AXES)
    cut = P(AXES, None)
    return jax.shard_map(
        on_device,
        mesh=split,
        in_specs=(cut, cut, P(), cut, cut, cut, cut, P(), P(), cut, cut, cut, P(), P()),
        out_specs=(cut, cut, P(), cut, cut, cut, cut, P(), P(), cut, cut, cut, P()),
        check_vma=False,
    )
```

```python
import functools

import jax
import jax.numpy as jnp
from jax import lax
from jax.experimental import pallas as pl
from jax.experimental.pallas import tpu as pltpu
from jax.sharding import Mesh, PartitionSpec as P

EPS = 1e-06
BF = jnp.bfloat16
F32 = jnp.float32
AXES = ("xlo", "xhi", "z", "y", "core")
MESH = pl.DeviceIdType.MESH
ANY = pl.BlockSpec(memory_space=pl.ANY)
VMEM = pl.BlockSpec(memory_space=pltpu.VMEM)
STEPS = (1, 3, 2)
GROUP = [(a, b) for a in range(4) for b in range(2) if a or b]
CHAIN = [(a, b) for a in range(2) for b in range(4) if a or b]
PLANE = [(a, b) for a in range(4) for b in range(4) if a or b]
HIGH = lax.Precision.HIGHEST


def ax(name):
    return lax.axis_index(name)


def ring(axis, s):
    if axis == "x":
        x = lax.rem(ax("xhi") * 2 + ax("xlo") + s, 4)
        return {"xhi": lax.div(x, 2), "xlo": lax.rem(x, 2)}
    return {axis: lax.rem(ax(axis) + s, 4)}


def sibling():
    return {"core": 1 - ax("core")}


def in_group(s, t):
    return {"y": lax.rem(ax("y") + s, 4), "core": lax.rem(ax("core") + t, 2)}


def in_chain(s, t):
    return {"xhi": lax.rem(ax("xhi") + s, 2), "z": lax.rem(ax("z") + t, 4)}


def in_plane(s, t):
    return {**ring("x", s), **ring("z", t)}


def place():
    return ax("xlo") * 8 + ax("xhi") * 4 + ax("z"), ax("y") * 2 + ax("core")


def device(p, g):
    return {
        "xlo": lax.div(p, 8),
        "xhi": lax.rem(lax.div(p, 4), 2),
        "z": lax.rem(p, 4),
        "y": lax.div(g, 2),
        "core": lax.rem(g, 2),
    }


class Copies:
    def __init__(self, send, recv, near):
        self.sems = (send, recv, near)
        self.count = 0
        self.locals = 0
        self.open = []

    def remote(self, src, dst, dev):
        i = self.count
        self.count += 1
        return pltpu.make_async_remote_copy(
            src_ref=src,
            dst_ref=dst,
            send_sem=self.sems[0].at[i],
            recv_sem=self.sems[1].at[i],
            device_id=dev,
            device_id_type=MESH,
        )

    def send(self, src, dst, dev):
        copy = self.remote(src, dst, dev)
        copy.start()
        self.open.append(copy)
        return copy

    def local(self, src, dst):
        copy = pltpu.make_async_copy(src, dst, self.sems[2].at[self.locals])
        self.locals += 1
        copy.start()
        return copy

    def sent(self, copies):
        for copy in copies:
            copy.wait_send()
        gone = {id(copy) for copy in copies}
        self.open = [copy for copy in self.open if id(copy) not in gone]

    def finish(self):
        for copy in self.open:
            copy.wait_send()


def greet(peers, shuffle=None):
    bar = pltpu.get_barrier_semaphore()
    for dev in peers:
        pl.semaphore_signal(bar, inc=1, device_id=dev, device_id_type=MESH)
    count = len(peers)
    if shuffle is not None:
        source, from_me, to_me = shuffle

        @pl.when(jnp.logical_not(from_me))
        def _():
            pl.semaphore_signal(bar, inc=1, device_id=source, device_id_type=MESH)

        count = count + jnp.where(to_me, 0, 1)
    pl.semaphore_wait(bar, count)


def to_group(cp, source, dst):
    g = place()[1]
    there = dst(g)
    copies = []
    for st in GROUP:
        q = in_group(*st)
        copies.append(cp.send(source(q["y"] * 2 + q["core"]), there, q))
    return copies, cp.local(source(g), there)


def settle(copies, home):
    for copy in copies:
        copy.wait_recv()
    home.wait()


class Shuffle:
    def __init__(self, outward):
        p, g = place()
        self.d = p * 8 + g
        row = 16 * g + p
        there = (lax.rem(self.d, 16), lax.div(self.d, 16))
        here = (lax.div(row, 8), lax.rem(row, 8))
        to, come = (there, here) if outward else (here, there)
        self.to = to
        self.target, self.source = device(*to), device(*come)
        self.to_me = to[0] * 8 + to[1] == self.d
        self.from_me = come[0] * 8 + come[1] == self.d
        self.greeting = (self.source, self.from_me, self.to_me)

    def start(self, cp, src, dst):
        copy = cp.remote(src, dst, self.target)
        home = pltpu.make_async_copy(src, dst, cp.sems[2].at[cp.locals])
        cp.locals += 1

        @pl.when(self.to_me)
        def _():
            home.start()

        @pl.when(jnp.logical_not(self.to_me))
        def _():
            copy.start()

        return copy, home

    def wait(self, pair):
        @pl.when(self.to_me)
        def _():
            pair[1].wait()

        @pl.when(jnp.logical_not(self.to_me))
        def _():
            pair[0].wait()


def rings():
    return [ring("x", s) for s in STEPS] + [ring("z", s) for s in STEPS]


def ys():
    return [ring("y", s) for s in STEPS] + [sibling()]


def run(chains, order):
    for i in order:
        next(chains[i], None)
    for chain in chains:
        for _ in chain:
            pass


def rows_of(i, n=16):
    return pl.ds(pl.multiple_of(i * n, n), n)


def group_gather(cp, src, full):
    g = place()[1]
    own = cp.local(src, full.at[g])
    moved = {s: cp.send(src, full.at[g], ring("y", s)) for s in STEPS}
    near = [cp.send(src, full.at[g], sibling())]
    yield
    for s in STEPS:
        moved[s].wait_recv()
        k = 2 * lax.rem(ax("y") + 4 - s, 4) + ax("core")
        near.append(cp.send(full.at[k], full.at[k], sibling()))
    yield
    for copy in near:
        copy.wait_recv()
    own.wait()


def group_sum(cp, part, mine, near, far, out):
    c = ax("core")
    block = {s: 2 * lax.rem(ax("y") + s, 4) for s in range(4)}
    sent = {s: cp.send(part.at[block[s] + 1 - c], near.at[s], sibling()) for s in (2, 1, 3, 0)}
    own = {s: cp.local(part.at[block[s] + c], mine.at[s]) for s in (2, 1, 3, 0)}
    yield
    moved = {}
    for s in (2, 1, 3):
        own[s].wait()
        sent[s].wait_recv()

        def add(i, carry, s=s):
            r = rows_of(i)
            mine[s, r, :] = (mine[s, r, :].astype(F32) + near[s, r, :].astype(F32)).astype(BF)
            return carry

        lax.fori_loop(0, mine.shape[1] // 16, add, 0)
        moved[s] = cp.send(mine.at[s], far.at[s - 1], ring("y", s))
    own[0].wait()
    sent[0].wait_recv()
    yield
    for s in (1, 3, 2):
        moved[s].wait_recv()

    def total(r):
        acc = mine[0, r, :].astype(F32) + near[0, r, :].astype(F32)
        for s in range(3):
            acc = acc + far[s, r, :].astype(F32)
        return acc

    out.append(total)


def group_sum_scratch(rows, width):
    return [
        pltpu.VMEM((4, rows, width), BF),
        pltpu.VMEM((4, rows, width), BF),
        pltpu.VMEM((3, rows, width), BF),
    ]


def plane_gather(cp, buf, halves, block=None):
    me = (ax("xlo"), ax("xhi"), ax("z"))
    home = None if block is None else cp.local(block, buf.at[me])

    def view(h, *at):
        return buf.at[at + halves[h]]

    mine = [view(h, *me) if block is None else block.at[halves[h]] for h in range(2)]
    first = []
    for s in STEPS:
        first.append(cp.send(mine[0], view(0, *me), ring("z", s)))
        first.append(cp.send(mine[1], view(1, *me), ring("x", s)))
    yield
    if home is not None:
        home.wait()
    for copy in first:
        copy.wait_recv()
    column = view(0, me[0], me[1], pl.ds(0, 4))
    row = view(1, pl.ds(0, 2), pl.ds(0, 2), me[2])
    wide = {}
    for s in (1, 3):
        wide["x", s] = cp.send(column, column, ring("x", s))
        wide["z", s] = cp.send(row, row, ring("z", s))
    yield
    last = []
    for s in (1, 3):
        back = ring("x", 4 - s)
        wide["x", s].wait_recv()
        v = view(0, back["xlo"], back["xhi"], pl.ds(0 if s == 1 else 2, 2))
        last.append(cp.send(v, v, ring("x", s)))
        back = ring("z", 4 - s)
        wide["z", s].wait_recv()
        v = view(1, 0 if s == 1 else 1, pl.ds(0, 2), back["z"])
        last.append(cp.send(v, v, ring("z", s)))
    yield
    for copy in last:
        copy.wait_recv()


def half_shapes(halves):
    return [tuple(d.size for d in h) for h in halves]


def plane_sum_scratch(halves):
    a, b = half_shapes(halves)
    return [
        pltpu.VMEM((4,) + a, BF),
        pltpu.VMEM((3, 4) + a, BF),
        pltpu.VMEM((3,) + a, BF),
        pltpu.VMEM((2, 2) + b, BF),
        pltpu.VMEM((3, 2, 2) + b, BF),
        pltpu.VMEM((3,) + b, BF),
    ]


def plane_sum(cp, part, halves, own_a, far_a, last_a, own_b, far_b, last_b, out):
    me = (ax("xlo"), ax("xhi"), ax("z"))
    shape_a, shape_b = half_shapes(halves)

    def view(h, *at):
        return part.at[at + halves[h]]

    near_a = cp.local(view(0, me[0], me[1], pl.ds(0, 4)), own_a)
    near_b = cp.local(view(1, pl.ds(0, 2), pl.ds(0, 2), me[2]), own_b)
    first_a, first_b = [], []
    for j, s in enumerate(STEPS):
        d = ring("x", s)
        first_a.append(cp.send(view(0, d["xlo"], d["xhi"], pl.ds(0, 4)), far_a.at[j], d))
        d = ring("z", s)
        first_b.append(cp.send(view(1, pl.ds(0, 2), pl.ds(0, 2), d["z"]), far_b.at[j], d))
    yield
    near_a.wait()
    for copy in first_a:
        copy.wait_recv()
    for k in range(4):

        def add(i, carry, k=k):
            r = rows_of(i)
            acc = own_a[k, r, :].astype(F32)
            for j in range(3):
                acc = acc + far_a[j, k, r, :].astype(F32)
            own_a[k, r, :] = acc.astype(BF)
            return carry

        lax.fori_loop(0, shape_a[0] // 16, add, 0)
    second = []
    for j, s in enumerate(STEPS):
        d = ring("z", s)
        second.append(cp.send(own_a.at[d["z"]], last_a.at[j], d))
    near_b.wait()
    for copy in first_b:
        copy.wait_recv()
    for k in range(4):

        def add(i, carry, k=k):
            r = rows_of(i)
            acc = own_b[k // 2, k % 2, r, :].astype(F32)
            for j in range(3):
                acc = acc + far_b[j, k // 2, k % 2, r, :].astype(F32)
            own_b[k // 2, k % 2, r, :] = acc.astype(BF)
            return carry

        lax.fori_loop(0, shape_b[0] // 16, add, 0)
    for j, s in enumerate(STEPS):
        d = ring("x", s)
        second.append(cp.send(own_b.at[d["xlo"], d["xhi"]], last_b.at[j], d))
    yield
    for copy in second:
        copy.wait_recv()

    def end_a(i, carry):
        r = rows_of(i)
        acc = own_a[me[2], r, :].astype(F32)
        for j in range(3):
            acc = acc + last_a[j, r, :].astype(F32)
        at = rows_of(i) if halves[0][0].start == 0 else pl.ds(halves[0][0].start + i * 16, 16)
        out[at, halves[0][1]] = acc.astype(BF)
        return carry

    lax.fori_loop(0, shape_a[0] // 16, end_a, 0)

    def end_b(i, carry):
        r = rows_of(i)
        acc = own_b[me[0], me[1], r, :].astype(F32)
        for j in range(3):
            acc = acc + last_b[j, r, :].astype(F32)
        at = pl.ds(pl.multiple_of(halves[1][0].start + i * 16, 16), 16)
        out[at, halves[1][1]] = acc.astype(BF)
        return carry

    lax.fori_loop(0, shape_b[0] // 16, end_b, 0)


def by_rows(rows, width):
    h = rows // 2
    return ((pl.ds(0, h), pl.ds(0, width)), (pl.ds(h, h), pl.ds(0, width)))


def by_columns(rows, width):
    h = width // 2
    return ((pl.ds(0, rows), pl.ds(0, h)), (pl.ds(0, rows), pl.ds(h, h)))


def call(body, name, ident, out_shape, in_specs, out_specs, scratch, sems, near, **kw):
    return pl.pallas_call(
        body,
        name=name,
        out_shape=out_shape,
        in_specs=in_specs,
        out_specs=out_specs,
        scratch_shapes=list(scratch)
        + [
            pltpu.SemaphoreType.DMA((sems,)),
            pltpu.SemaphoreType.DMA((sems,)),
            pltpu.SemaphoreType.DMA((near,)),
        ],
        compiler_params=pltpu.CompilerParams(
            collective_id=ident, has_side_effects=True, vmem_limit_bytes=56 << 20
        ),
        **kw,
    )


def gather_body(tok, gain, w_in, w_f, w_og, w_o, b3, bo, fi, first, send, recv, near):
    cp = Copies(send, recv, near)
    g = place()[1]
    shuffle = Shuffle(True)
    greet(rings() + [in_group(*st) for st in GROUP], shuffle.greeting)
    me = (ax("xlo"), ax("xhi"), ax("z"))
    third = w_in.shape[1] // 8
    arrive = []
    for j, w in enumerate((w_in, w_f, w_og)):
        arrive.append(
            to_group(
                cp,
                lambda k, w=w: w.at[:, pl.ds(pl.multiple_of(k * third, 128), third)],
                lambda k, j=j: b3.at[me + (rows_of(k), pl.ds(j * third, third))],
            )
        )
    q = shuffle.to[0]
    moved = shuffle.start(
        cp, w_o, bo.at[lax.div(q, 8), lax.rem(lax.div(q, 4), 2), lax.rem(q, 4)]
    )

    def norm(i, carry):
        r = rows_of(i)
        x = tok[r, :].astype(F32)
        s = lax.rsqrt(jnp.mean(x * x, axis=-1, keepdims=True) + EPS)
        first[r, :] = (x * s * gain[...]).astype(BF)
        return carry

    lax.fori_loop(0, tok.shape[0] // 16, norm, 0)
    chain = group_gather(cp, first, fi)
    next(chain)
    for pair in arrive:
        settle(*pair)
    shuffle.wait(moved)
    chains = [
        plane_gather(cp, b3, by_rows(*b3.shape[3:])),
        plane_gather(cp, bo, by_columns(*bo.shape[3:])),
        chain,
    ]
    run(chains, (0, 1, 0, 1, 0, 1, 2))
    cp.finish()


def silu_slope(v, s):
    return s * (1.0 + v * (1.0 - s))


def row_sums(x):
    ones = jnp.ones((8, x.shape[1]), F32)
    return lax.dot_general(
        ones, x, (((1,), (1,)), ((), ())), precision=HIGH, preferred_element_type=F32
    )[0:1]


def as_column(row, width):
    t = jnp.transpose(jnp.broadcast_to(row, (128, 128)))
    return jnp.concatenate([t] * (width // 128), axis=1)


def chunk_rows(s):
    return pl.ds(pl.multiple_of(s * 128, 128), 128)


def wide(ref, r):
    return jnp.concatenate([ref[j, r, :] for j in range(ref.shape[0])], axis=1)


def put(ref, r, value):
    for j in range(ref.shape[0]):
        ref[j, r, :] = value[:, 128 * j : 128 * (j + 1)]


def share(cp, src, dst, index, peers):
    copies = [cp.send(src, dst.at[index], dev) for dev in peers]
    dst[pl.ds(index, 1)] = src[...][None]
    return copies


def scan_body(
    proj, lb, gain, gu, dn, cot, gated, states, forget, tot, links, carry, gf, block_gu, block_dn, prod, entry, mine, rowsum, rows8, send, recv, near
):
    cp = Copies(send, recv, near)
    shuffle = Shuffle(True)
    tiles, rows = states.shape[:2]
    w = 128 * tiles
    steps = rows // 8
    peers_chain = [in_chain(*st) for st in CHAIN]
    peers_group = [in_group(*st) for st in GROUP]
    greet(peers_chain + peers_group, shuffle.greeting)
    arrive = to_group(cp, lambda k: gu.at[k], lambda k: block_gu.at[rows_of(k), :])
    moved = shuffle.start(cp, dn, block_dn)
    chain = group_gather(cp, cot, gf)
    next(chain)
    low = lb[...]

    def gates(i, c):
        r = rows_of(i, 32)
        f = low + (1.0 - low) * jax.nn.sigmoid(proj[r, w : 2 * w])
        v = proj[r, 0:w]
        put(forget, r, f)
        put(states, r, v * jax.nn.sigmoid(v) * (1.0 - f))
        return c

    lax.fori_loop(0, 8 * steps // 32, gates, 0)

    def step(t, c):
        at = pl.ds(t, 8, stride=steps)
        new = []
        for j, (h, a) in enumerate(c):
            f = forget[j, at, :]
            h = f * h + states[j, at, :]
            a = a * f
            states[j, at, :] = h
            prod[j, at, :] = a
            new.append((h, a))
        return tuple(new)

    start = ((jnp.zeros((8, 128), F32), jnp.ones((8, 128), F32)),) * tiles
    ends = lax.fori_loop(0, steps, step, start, unroll=8)
    h = jnp.concatenate([e[0] for e in ends], axis=1)
    a = jnp.concatenate([e[1] for e in ends], axis=1)
    c = jnp.zeros((1, w), F32)
    q = jnp.ones((1, w), F32)
    cs, qs = [], []
    for s in range(8):
        cs.append(c)
        qs.append(q)
        c = a[s : s + 1] * c + h[s : s + 1]
        q = a[s : s + 1] * q
    mine[...] = jnp.concatenate([q, c, jnp.zeros((6, w), F32)], axis=0)
    k = ax("xhi") * 4 + ax("z")
    for copy in share(cp, mine, links, k, peers_chain):
        copy.wait_recv()
    come = jnp.zeros((1, w), F32)
    for j in range(8):
        new = links[j, 0:1, :] * come + links[j, 1:2, :]
        come = jnp.where(j < k, new, come)
    carry[...] = jnp.broadcast_to(come, (8, w))
    entry[...] = jnp.concatenate(qs, axis=0) * come + jnp.concatenate(cs, axis=0)

    def finish(s, c):
        r = chunk_rows(s)
        st = wide(states, r) + wide(prod, r) * entry[pl.ds(s, 1), :]
        put(states, r, st)
        rowsum[pl.ds(s, 1), :] = row_sums(st * st)
        return c

    lax.fori_loop(0, 8, finish, 0)
    for copy in share(cp, rowsum, rows8, place()[1], peers_group):
        copy.wait_recv()
    total = rows8[0]
    for j in range(1, 8):
        total = total + rows8[j]
    tot[...] = lax.rsqrt(total / (8.0 * w) + EPS)

    def gate(s, c):
        r = chunk_rows(s)
        v = proj[r, 2 * w : 3 * w]
        n = wide(states, r) * as_column(tot[pl.ds(s, 1), :], w)
        gated[r, :] = (n * gain[...] * (v * jax.nn.sigmoid(v))).astype(BF)
        return c

    lax.fori_loop(0, 8, gate, 0)
    settle(*arrive)
    shuffle.wait(moved)
    for _ in chain:
        pass
    cp.finish()


def middle_body(
    part, tok, gain, block_gu, block_dn, mid, full, bgu, bdn, own, near_, far, block, send, recv, near
):
    cp = Copies(send, recv, near)
    greet(ys() + rings())
    sums = []
    chains = [
        group_sum(cp, part, own, near_, far, sums),
        plane_gather(cp, bgu, by_rows(*bgu.shape[3:]), block_gu),
        plane_gather(cp, bdn, by_columns(*bdn.shape[3:]), block_dn),
    ]
    for i in (0, 1, 2, 0, 1, 2, 0):
        next(chains[i], None)

    def norm(i, carry):
        r = rows_of(i)
        x = tok[r, :].astype(F32) + sums[0](r)
        mid[r, :] = x
        s = lax.rsqrt(jnp.mean(x * x, axis=-1, keepdims=True) + EPS)
        block[r, :] = (x * s * gain[...]).astype(BF)
        return carry

    lax.fori_loop(0, mid.shape[0] // 16, norm, 0)
    chains[0] = group_gather(cp, block, full)
    run(chains, (0, 1, 2, 0))
    cp.finish()


def turn_body(
    part, part_r, mid, cot, gain, dgu, ddn, result, mixed, full, sums_out, block_gu, block_dn, own, near_, far, own_r, near_r, far_r, block, *rest
):
    cp = Copies(*rest[-3:])
    greet(ys() + rings())
    sums, sums_r = [], []
    chain = group_sum(cp, part, own, near_, far, sums)
    chain_r = group_sum(cp, part_r, own_r, near_r, far_r, sums_r)
    planes = [
        plane_sum(cp, dgu, by_rows(*dgu.shape[3:]), *rest[:6], block_gu),
        plane_sum(cp, ddn, by_columns(*ddn.shape[3:]), *rest[6:12], block_dn),
    ]
    next(chain)
    next(planes[0])
    next(planes[1])
    next(chain)
    next(chain_r)
    next(chain_r)
    for _ in chain:
        pass
    for _ in chain_r:
        pass
    sums_out[...] = jnp.zeros_like(sums_out)

    def back(i, carry):
        r = rows_of(i)
        x = mid[r, :]
        s = lax.rsqrt(jnp.mean(x * x, axis=-1, keepdims=True) + EPS)
        n = x * s
        dy = sums[0](r)
        sums_out[0:1, :] = sums_out[0:1, :] + jnp.sum(dy * n, axis=0, keepdims=True)
        dy = dy * gain[...]
        v = cot[r, :].astype(F32) + s * (dy - n * jnp.mean(dy * n, axis=-1, keepdims=True))
        mixed[r, :] = v
        block[r, :] = v.astype(BF)
        result[r, :] = (x + sums_r[0](r)).astype(BF)
        return carry

    lax.fori_loop(0, mid.shape[0] // 16, back, 0)
    run([group_gather(cp, block, full)] + planes, (0, 1, 2, 0))
    cp.finish()


def back_body(
    gg, proj, states, forget, tot, links, carry, lb, gain, block_gu, block_dn, grads, sums_out, rgu, rdn, gs, prod, entry, mine, rowsum, rows8, far, send, recv, near
):
    cp = Copies(send, recv, near)
    shuffle = Shuffle(False)
    tiles, rows = states.shape[:2]
    w = 128 * tiles
    steps = rows // 8
    peers_chain = [in_chain(*st) for st in CHAIN]
    peers_group = [in_group(*st) for st in GROUP]
    greet(peers_chain + peers_group, shuffle.greeting)
    arrive = to_group(cp, lambda k: block_gu.at[rows_of(k), :], lambda k: rgu.at[k])
    moved = shuffle.start(cp, block_dn, rdn)
    low = lb[...]
    sums_out[...] = jnp.zeros_like(sums_out)

    def through(s, c):
        r = chunk_rows(s)
        v = proj[r, 2 * w : 3 * w]
        sig = jax.nn.sigmoid(v)
        n = wide(states, r) * as_column(tot[pl.ds(s, 1), :], w)
        dy = gg[r, :]
        sums_out[0:1, :] = sums_out[0:1, :] + jnp.sum(dy * n * (v * sig), axis=0, keepdims=True)
        grads[r, 2 * w : 3 * w] = (dy * n * gain[...] * silu_slope(v, sig)).astype(BF)
        dy = dy * gain[...] * (v * sig)
        put(gs, r, dy)
        rowsum[pl.ds(s, 1), :] = row_sums(dy * n)
        return c

    lax.fori_loop(0, 8, through, 0)
    small = share(cp, rowsum, rows8, place()[1], peers_group)
    for copy in small:
        copy.wait_recv()
    total = rows8[0]
    for j in range(1, 8):
        total = total + rows8[j]
    def norm(s, c):
        r = chunk_rows(s)
        t = as_column(tot[pl.ds(s, 1), :], w)
        m = as_column(rowsum[pl.ds(s, 1), :], w)
        put(gs, r, t * (wide(gs, r) - wide(states, r) * t * m))
        return c

    cp.sent(small)
    rowsum[...] = total / (8.0 * w)
    lax.fori_loop(0, 8, norm, 0)

    def step(i, c):
        at = pl.ds(steps - 1 - i, 8, stride=steps)
        new = []
        for j, (h, a) in enumerate(c):
            f = forget[j, at, :]
            v = gs[j, at, :] + h
            gs[j, at, :] = v
            prod[j, at, :] = a
            new.append((f * v, a * f))
        return tuple(new)

    start = ((jnp.zeros((8, 128), F32), jnp.ones((8, 128), F32)),) * tiles
    ends = lax.fori_loop(0, steps, step, start, unroll=8)
    h = jnp.concatenate([e[0] for e in ends], axis=1)
    a = jnp.concatenate([e[1] for e in ends], axis=1)
    c = jnp.zeros((1, w), F32)
    q = jnp.ones((1, w), F32)
    cs, qs = [None] * 8, [None] * 8
    for s in range(7, -1, -1):
        cs[s] = c
        qs[s] = q
        c = a[s : s + 1] * c + h[s : s + 1]
        q = a[s : s + 1] * q
    mine[...] = jnp.broadcast_to(c, (8, w))
    k = ax("xhi") * 4 + ax("z")
    for copy in share(cp, mine, far, k, peers_chain):
        copy.wait_recv()
    come = jnp.zeros((1, w), F32)
    for j in range(7, -1, -1):
        new = links[j, 0:1, :] * come + far[j, 0:1, :]
        come = jnp.where(j > k, new, come)
    entry[...] = jnp.concatenate(qs, axis=0) * come + jnp.concatenate(cs, axis=0)

    def last(s, c):
        r = chunk_rows(s)
        v = wide(gs, r) + wide(prod, r) * entry[pl.ds(s, 1), :]
        st = wide(states, r)
        above = pl.ds(jnp.maximum(s * 128 - 1, 0), 1)
        before = jnp.where(s == 0, carry[0:1, :], wide(states, above))
        top = lax.broadcasted_iota(jnp.int32, (128, w), 0) == 0
        prev = jnp.where(top, before, pltpu.roll(st, 1, 0))
        x = proj[r, 0:w]
        sx = jax.nn.sigmoid(x)
        f = wide(forget, r)
        sf = jax.nn.sigmoid(proj[r, w : 2 * w])
        gf = v * (prev - x * sx)
        grads[r, 0:w] = (v * (1.0 - f) * silu_slope(x, sx)).astype(BF)
        grads[r, w : 2 * w] = (gf * (1.0 - low) * sf * (1.0 - sf)).astype(BF)
        sums_out[1:2, :] = sums_out[1:2, :] + jnp.sum(gf * (1.0 - sf), axis=0, keepdims=True)
        return c

    lax.fori_loop(0, 8, last, 0)
    settle(*arrive)
    shuffle.wait(moved)
    cp.finish()


def sum_body(*refs):
    (part, tok, mixed, gain, ffn_sums, mix_sums, d3, do) = refs[:8]
    (gtok, r3, ro, totals) = refs[8:12]
    scratch = list(refs[12:-3])
    cp = Copies(*refs[-3:])
    own, near_, far = scratch[:3]
    o3, oo, va, ga, ta, gb, tb = scratch[15:]
    p, g = place()
    shuffle = Shuffle(False)
    greet(
        [in_plane(*st) for st in PLANE] + [in_group(*st) for st in GROUP], shuffle.greeting
    )
    sums = []
    chain = group_sum(cp, part, own, near_, far, sums)
    chains = [
        plane_sum(cp, d3, by_rows(*d3.shape[3:]), *scratch[3:9], o3),
        plane_sum(cp, do, by_columns(*do.shape[3:]), *scratch[9:15], oo),
    ]
    next(chain)
    for c in chains:
        next(c)
    next(chain)
    for c in chains:
        next(c)
    for _ in chain:
        pass
    va[...] = jnp.zeros_like(va)

    def back(i, carry):
        r = rows_of(i)
        x = tok[r, :].astype(F32)
        s = lax.rsqrt(jnp.mean(x * x, axis=-1, keepdims=True) + EPS)
        n = x * s
        dy = sums[0](r)
        va[0:1, :] = va[0:1, :] + jnp.sum(dy * n, axis=0, keepdims=True)
        dy = dy * gain[...]
        gtok[r, :] = mixed[r, :] + s * (dy - n * jnp.mean(dy * n, axis=-1, keepdims=True))
        return carry

    lax.fori_loop(0, gtok.shape[0] // 16, back, 0)
    va[1:2, :] = ffn_sums[0:1, :]
    w = ga.shape[2]
    small = []
    for st in GROUP:
        q = in_group(*st)
        k = q["y"] * 2 + q["core"]
        small.append(cp.send(va.at[:, pl.ds(pl.multiple_of(k * w, 128), w)], ga.at[g], q))
    ga[pl.ds(g, 1)] = va[:, pl.ds(pl.multiple_of(g * w, 128), w)][None]
    for copy in small:
        copy.wait_recv()
    acc = ga[0]
    for j in range(1, 8):
        acc = acc + ga[j]
    ta[...] = acc
    ta[2:4, :] = mix_sums[0:2, :]
    for copy in share(cp, ta, gb, p, [in_plane(*st) for st in PLANE]):
        copy.wait_recv()
    acc = gb[0]
    for j in range(1, 16):
        acc = acc + gb[j]
    tb[...] = acc
    small = share(cp, tb, totals, g, [in_group(*st) for st in GROUP])
    for c in chains:
        for _ in c:
            pass
    arrive = to_group(cp, lambda k: o3.at[rows_of(k), :], lambda k: r3.at[k])
    moved = shuffle.start(cp, oo, ro)
    for copy in small:
        copy.wait_recv()
    settle(*arrive)
    shuffle.wait(moved)
    cp.finish()


def bound_value(bound_table, layer_idx):
    probabilities = jax.nn.softmax(bound_table, axis=0)
    levels = jnp.arange(bound_table.shape[0], dtype=jnp.int32)[:, None]
    keep = jnp.where((levels >= 1) & (levels <= layer_idx[0]), 1.0, 0.0).astype(F32)
    return jnp.sum(probabilities * keep, axis=0)


def dot(a, b, dims):
    return lax.dot_general(a, b, (dims, ((), ())), preferred_element_type=F32)


NN = ((1,), (0,))
NT = ((1,), (1,))
TN = ((0,), (0,))


def on_device(
    tokens, cotangent, attn_gain, w_input, w_forget, w_outgate, w_out, norm_gain, mlp_gain, w_gate, w_up, w_down, bound_table, layer_idx
):
    n, width = tokens.shape
    rows = w_input.shape[0]
    hidden_width = w_gate.shape[1]
    down = w_down.shape[0]
    padded = -(-down // 16) * 16
    unit = 16 * padded
    w = width // 8
    shape = jax.ShapeDtypeStruct

    def spread(m):
        m = jnp.pad(m.reshape(rows, 128, down), ((0, 0), (0, 0), (0, padded - down)))
        return m.reshape(rows, 8, unit).transpose(1, 0, 2)

    gu = jnp.concatenate([spread(w_gate), spread(w_up)], axis=2)
    dn = jnp.pad(w_down, ((0, padded - down), (0, 0)))
    gains = attn_gain[None, :]
    b3, bo, fi = call(
        gather_body,
        "gather",
        0,
        [
            shape((2, 2, 4, 8 * rows, 3 * w), BF),
            shape((2, 2, 4, rows, width), BF),
            shape((8, n, width), BF),
        ],
        [VMEM, VMEM] + [ANY] * 4,
        [ANY] * 3,
        [pltpu.VMEM((n, width), BF)],
        64,
        8,
    )(tokens, gains, w_input, w_forget, w_outgate, w_out)
    big3 = b3.reshape(width, 3 * w)
    big_out = bo.reshape(w, width)
    first_full = fi.reshape(8 * n, width)

    group = ax("y") * 2 + ax("core")
    lower = bound_value(lax.dynamic_slice_in_dim(bound_table, group * w, w, 1), layer_idx)[None, :]
    mixer_gain = lax.dynamic_slice_in_dim(norm_gain, group * w, w, 0)[None, :]
    proj = dot(first_full, big3, NN)
    gated, states, forget, tot, links, carry, gf, block_gu, block_dn = call(
        scan_body,
        "scan",
        1,
        [
            shape((8 * n, w), BF),
            shape((w // 128, 8 * n, 128), F32),
            shape((w // 128, 8 * n, 128), F32),
            shape((8, n), F32),
            shape((8, 8, w), F32),
            shape((8, w), F32),
            shape((8, n, width), BF),
            shape((8 * rows, 2 * unit), BF),
            shape((padded, width), BF),
        ],
        [VMEM] * 3 + [ANY] * 3,
        [VMEM] * 6 + [ANY] * 3,
        [
            pltpu.VMEM((w // 128, 8 * n, 128), F32),
            pltpu.VMEM((8, w), F32),
            pltpu.VMEM((8, w), F32),
            pltpu.VMEM((8, n), F32),
            pltpu.VMEM((8, 8, n), F32),
        ],
        32,
        4,
    )(proj, lower, mixer_gain, gu, dn, cotangent)
    g_full = gf.reshape(8 * n, width)
    mid_part = dot(gated, big_out, NN).astype(BF).reshape(8, n, width)
    sum_scratch = group_sum_scratch(n, width)
    mid, si, bgu, bdn = call(
        middle_body,
        "middle",
        2,
        [
            shape((n, width), F32),
            shape((8, n, width), BF),
            shape((2, 2, 4, 8 * rows, 2 * unit), BF),
            shape((2, 2, 4, padded, width), BF),
        ],
        [ANY, VMEM, VMEM, ANY, ANY],
        [VMEM, ANY, ANY, ANY],
        sum_scratch + [pltpu.VMEM((n, width), BF)],
        48,
        10,
    )(mid_part, tokens, mlp_gain[None, :], block_gu, block_dn)
    big_gu = bgu.reshape(width, 2 * unit)
    big_down = bdn.reshape(unit, width)
    second_full = si.reshape(8 * n, width)
    gate_up = dot(second_full, big_gu, NN)
    gate_proj, up_proj = gate_up[:, :unit], gate_up[:, unit:]
    sig = jax.nn.sigmoid(gate_proj)
    act = gate_proj * sig
    hidden = (act * up_proj).astype(BF)
    result_part = dot(hidden, big_down, NN).astype(BF).reshape(8, n, width)

    grad_hidden = dot(g_full, big_down, NT)
    grad_gate = (grad_hidden * up_proj * silu_slope(gate_proj, sig)).astype(BF)
    grad_up = (grad_hidden * act).astype(BF)
    grad_gu = jnp.concatenate([grad_gate, grad_up], axis=1)
    second_part = dot(grad_gu, big_gu, NT).astype(BF).reshape(8, n, width)
    dgu = dot(second_full, grad_gu, TN).astype(BF).reshape(2, 2, 4, 8 * rows, 2 * unit)
    ddn = dot(hidden, g_full, TN).astype(BF).reshape(2, 2, 4, padded, width)
    result, mixed, gb, ffn_sums, block_dgu, block_ddn = call(
        turn_body,
        "turn",
        3,
        [
            shape((n, width), BF),
            shape((n, width), F32),
            shape((8, n, width), BF),
            shape((8, width), F32),
            shape((8 * rows, 2 * unit), BF),
            shape((padded, width), BF),
        ],
        [ANY, ANY, VMEM, VMEM, VMEM, ANY, ANY],
        [VMEM, VMEM, ANY, VMEM, VMEM, VMEM],
        sum_scratch
        + sum_scratch
        + [pltpu.VMEM((n, width), BF)]
        + plane_sum_scratch(by_rows(8 * rows, 2 * unit))
        + plane_sum_scratch(by_columns(padded, width)),
        56,
        16,
    )(second_part, result_part, mid, cotangent, mlp_gain[None, :], dgu, ddn)
    branch_full = gb.reshape(8 * n, width)
    grad_gated = dot(branch_full, big_out, NT)
    grads3, mix_sums, rgu, rdn = call(
        back_body,
        "back",
        4,
        [
            shape((8 * n, 3 * w), BF),
            shape((8, w), F32),
            shape((8, rows, 2 * unit), BF),
            shape((padded, width), BF),
        ],
        [VMEM] * 9 + [ANY] * 2,
        [VMEM] * 2 + [ANY] * 2,
        [
            pltpu.VMEM((w // 128, 8 * n, 128), F32),
            pltpu.VMEM((w // 128, 8 * n, 128), F32),
            pltpu.VMEM((8, w), F32),
            pltpu.VMEM((8, w), F32),
            pltpu.VMEM((8, n), F32),
            pltpu.VMEM((8, 8, n), F32),
            pltpu.VMEM((8, 8, w), F32),
        ],
        24,
        4,
    )(grad_gated, proj, states, forget, tot, links, carry, lower, mixer_gain, block_dgu, block_ddn)
    first_part = dot(grads3, big3, NT).astype(BF).reshape(8, n, width)

    d3 = dot(first_full, grads3, TN).astype(BF).reshape(2, 2, 4, 8 * rows, 3 * w)
    do = dot(gated, branch_full, TN).astype(BF).reshape(2, 2, 4, rows, width)
    grad_tokens, r3, ro, totals = call(
        sum_body,
        "sums",
        5,
        [
            shape((n, width), F32),
            shape((8, rows, 3 * w), BF),
            shape((rows, width), BF),
            shape((8, 8, w), F32),
        ],
        [ANY, VMEM, VMEM, VMEM, VMEM, VMEM] + [ANY] * 2,
        [VMEM, VMEM, VMEM, VMEM],
        sum_scratch
        + plane_sum_scratch(by_rows(8 * rows, 3 * w))
        + plane_sum_scratch(by_columns(rows, width))
        + [
            pltpu.VMEM((8 * rows, 3 * w), BF),
            pltpu.VMEM((rows, width), BF),
            pltpu.VMEM((8, width), F32),
            pltpu.VMEM((8, 8, w), F32),
            pltpu.VMEM((8, w), F32),
            pltpu.VMEM((16, 8, w), F32),
            pltpu.VMEM((8, w), F32),
        ],
        80,
        16,
    )(first_part, tokens, mixed, gains, ffn_sums, mix_sums, d3, do)

    def join(m):
        m = m.transpose(1, 0, 2)
        return m.reshape(rows, 8 * m.shape[2]).astype(F32)

    def unspread(m):
        m = m.transpose(1, 0, 2).reshape(rows, 128, padded)[:, :, :down]
        return m.reshape(rows, hidden_width).astype(F32)

    sums = totals.transpose(1, 0, 2).reshape(8, width)
    pullback = jax.vjp(lambda table: bound_value(table, layer_idx), bound_table)[1]
    return (
        result,
        grad_tokens,
        sums[0],
        join(r3[:, :, :w]),
        join(r3[:, :, w : 2 * w]),
        join(r3[:, :, 2 * w :]),
        ro.astype(F32),
        sums[2],
        sums[1],
        unspread(rgu[:, :, :unit]),
        unspread(rgu[:, :, unit:]),
        rdn[:down].astype(F32),
        pullback(sums[3])[0],
    )


def solution(mesh):
    split = Mesh(mesh.devices.reshape(2, 2, 4, 4, 2), AXES)
    cut = P(AXES, None)
    return jax.shard_map(
        on_device,
        mesh=split,
        in_specs=(cut, cut, P(), cut, cut, cut, cut, P(), P(), cut, cut, cut, P(), P()),
        out_specs=(cut, cut, P(), cut, cut, cut, cut, P(), P(), cut, cut, cut, P()),
        check_vma=False,
    )
```

```python
from types import SimpleNamespace

import jax
import jax.numpy as jnp
from jax import lax
from jax.experimental import pallas as pl
from jax.experimental.pallas import tpu as pltpu
from jax.sharding import Mesh, PartitionSpec as P

EPS = 1e-06
BF = jnp.bfloat16
F32 = jnp.float32
AXES = ("xlo", "xhi", "z", "y", "core")
MESH = pl.DeviceIdType.MESH
ANY = pl.BlockSpec(memory_space=pl.ANY)
VMEM = pl.BlockSpec(memory_space=pltpu.VMEM)
STEPS = (1, 3, 2)
GROUP = [(a, b) for a in range(4) for b in range(2) if a or b]
CHAIN = [(a, b) for a in range(2) for b in range(4) if a or b]
PLANE = [(a, b) for a in range(4) for b in range(4) if a or b]
HIGH = lax.Precision.HIGHEST


def ax(name):
    return lax.axis_index(name)


def ring(axis, s):
    if axis == "x":
        x = lax.rem(ax("xhi") * 2 + ax("xlo") + s, 4)
        return {"xhi": lax.div(x, 2), "xlo": lax.rem(x, 2)}
    return {axis: lax.rem(ax(axis) + s, 4)}


def sibling():
    return {"core": 1 - ax("core")}


def in_group(s, t):
    return {"y": lax.rem(ax("y") + s, 4), "core": lax.rem(ax("core") + t, 2)}


def in_chain(s, t):
    return {"xhi": lax.rem(ax("xhi") + s, 2), "z": lax.rem(ax("z") + t, 4)}


def in_plane(s, t):
    return {**ring("x", s), **ring("z", t)}


def place():
    return ax("xlo") * 8 + ax("xhi") * 4 + ax("z"), ax("y") * 2 + ax("core")


def device(p, g):
    return {
        "xlo": lax.div(p, 8),
        "xhi": lax.rem(lax.div(p, 4), 2),
        "z": lax.rem(p, 4),
        "y": lax.div(g, 2),
        "core": lax.rem(g, 2),
    }


class Copies:
    def __init__(self, send, recv, near):
        self.sems = (send, recv, near)
        self.count = 0
        self.locals = 0
        self.open = []

    def remote(self, src, dst, dev):
        i = self.count
        self.count += 1
        return pltpu.make_async_remote_copy(
            src_ref=src,
            dst_ref=dst,
            send_sem=self.sems[0].at[i],
            recv_sem=self.sems[1].at[i],
            device_id=dev,
            device_id_type=MESH,
        )

    def send(self, src, dst, dev):
        copy = self.remote(src, dst, dev)
        copy.start()
        self.open.append(copy)
        return copy

    def local(self, src, dst):
        copy = pltpu.make_async_copy(src, dst, self.sems[2].at[self.locals])
        self.locals += 1
        copy.start()
        return copy

    def sent(self, copies):
        for copy in copies:
            copy.wait_send()
        gone = {id(copy) for copy in copies}
        self.open = [copy for copy in self.open if id(copy) not in gone]

    def finish(self):
        for copy in self.open:
            copy.wait_send()


def greet(peers, shuffle=None):
    bar = pltpu.get_barrier_semaphore()
    for dev in peers:
        pl.semaphore_signal(bar, inc=1, device_id=dev, device_id_type=MESH)
    count = len(peers)
    if shuffle is not None:
        source, from_me, to_me = shuffle

        @pl.when(jnp.logical_not(from_me))
        def _():
            pl.semaphore_signal(bar, inc=1, device_id=source, device_id_type=MESH)

        count = count + jnp.where(to_me, 0, 1)
    pl.semaphore_wait(bar, count)


def to_group(cp, source, dst):
    g = place()[1]
    there = dst(g)
    copies = []
    for st in GROUP:
        q = in_group(*st)
        copies.append(cp.send(source(q["y"] * 2 + q["core"]), there, q))
    return copies, cp.local(source(g), there)


def settle(copies, home):
    for copy in copies:
        copy.wait_recv()
    home.wait()


class Shuffle:
    def __init__(self, outward):
        p, g = place()
        self.d = p * 8 + g
        row = 16 * g + p
        there = (lax.rem(self.d, 16), lax.div(self.d, 16))
        here = (lax.div(row, 8), lax.rem(row, 8))
        to, come = (there, here) if outward else (here, there)
        self.to = to
        self.target, self.source = device(*to), device(*come)
        self.to_me = to[0] * 8 + to[1] == self.d
        self.from_me = come[0] * 8 + come[1] == self.d
        self.greeting = (self.source, self.from_me, self.to_me)

    def start(self, cp, src, dst):
        copy = cp.remote(src, dst, self.target)
        home = pltpu.make_async_copy(src, dst, cp.sems[2].at[cp.locals])
        cp.locals += 1

        @pl.when(self.to_me)
        def _():
            home.start()

        @pl.when(jnp.logical_not(self.to_me))
        def _():
            copy.start()

        return copy, home

    def wait(self, pair):
        @pl.when(self.to_me)
        def _():
            pair[1].wait()

        @pl.when(jnp.logical_not(self.to_me))
        def _():
            pair[0].wait()


def rings():
    return [ring("x", s) for s in STEPS] + [ring("z", s) for s in STEPS]


def ys():
    return [ring("y", s) for s in STEPS] + [sibling()]


def run(chains, order):
    for i in order:
        next(chains[i], None)
    for chain in chains:
        for _ in chain:
            pass


def rows_of(i, n=16):
    return pl.ds(pl.multiple_of(i * n, n), n)


def block_of(k):
    return rows_of(k, 128)


class GroupGather:
    def __init__(self, cp, src, full):
        self.cp, self.full = cp, full
        self.at = full.at[block_of(place()[1])]
        self.moved = {s: cp.send(src, self.at, ring("y", s)) for s in STEPS}
        self.near = {0: cp.send(src, self.at, sibling())}

    def forward(self, s):
        self.moved[s].wait_recv()
        k = 2 * lax.rem(ax("y") + 4 - s, 4) + ax("core")
        at = self.full.at[block_of(k)]
        self.near[s] = self.cp.send(at, at, sibling())

    def ready(self, s):
        self.near[s].wait_recv()

    def rest(self):
        for s in STEPS:
            if s not in self.near:
                self.forward(s)
        for s in (0, 1, 3, 2):
            self.ready(s)


class GroupSum:
    def __init__(self, cp, near, far):
        self.cp, self.near, self.far = cp, near, far
        self.sent, self.moved = {}, {}

    def chip(self, s):
        return 2 * lax.rem(ax("y") + s, 4)

    def give(self, s, src):
        self.sent[s] = self.cp.send(src, self.near.at[s], sibling())

    def add(self, s, mine, at):
        near = self.near
        self.sent[s].wait_recv()

        def step(i, carry):
            r = rows_of(i)
            to = pl.ds(pl.multiple_of(at + i * 16, 16), 16)
            mine[to, :] = (mine[to, :].astype(F32) + near[s, r, :].astype(F32)).astype(BF)
            return carry

        lax.fori_loop(0, 8, step, 0)
        here = mine.at[pl.ds(pl.multiple_of(at, 128), 128)]
        self.moved[s] = self.cp.send(here, self.far.at[s - 1], ring("y", s))

    def total(self, mine, at):
        self.sent[0].wait_recv()
        for s in STEPS:
            self.moved[s].wait_recv()
        self.cp.sent(list(self.moved.values()))
        near, far = self.near, self.far

        def rows(i):
            r = rows_of(i)
            own = mine[pl.ds(pl.multiple_of(at + i * 16, 16), 16), :]
            acc = own.astype(F32) + near[0, r, :].astype(F32)
            for s in range(3):
                acc = acc + far[s, r, :].astype(F32)
            return acc

        return rows


def sum_of(cp, part, mine, near, far):
    total = GroupSum(cp, near, far)
    c = ax("core")
    own = {}
    for s in (2, 1, 3, 0):
        total.give(s, part.at[block_of(total.chip(s) + 1 - c)])
        own[s] = cp.local(part.at[block_of(total.chip(s) + c)], mine.at[pl.ds(128 * s, 128)])
    yield
    for s in (2, 1, 3):
        own[s].wait()
        total.add(s, mine, 128 * s)
    own[0].wait()
    yield
    yield total.total(mine, 0)


def plane_gather(cp, buf, halves, block=None):
    me = (ax("xlo"), ax("xhi"), ax("z"))
    home = None if block is None else cp.local(block, buf.at[me])

    def view(h, *at):
        return buf.at[at + halves[h]]

    mine = [view(h, *me) if block is None else block.at[halves[h]] for h in range(2)]
    first = []
    for s in STEPS:
        first.append(cp.send(mine[0], view(0, *me), ring("z", s)))
        first.append(cp.send(mine[1], view(1, *me), ring("x", s)))
    yield
    if home is not None:
        home.wait()
    for copy in first:
        copy.wait_recv()
    column = view(0, me[0], me[1], pl.ds(0, 4))
    row = view(1, pl.ds(0, 2), pl.ds(0, 2), me[2])
    wide = {}
    for s in (1, 3):
        wide["x", s] = cp.send(column, column, ring("x", s))
        wide["z", s] = cp.send(row, row, ring("z", s))
    yield
    last = []
    for s in (1, 3):
        back = ring("x", 4 - s)
        wide["x", s].wait_recv()
        v = view(0, back["xlo"], back["xhi"], pl.ds(0 if s == 1 else 2, 2))
        last.append(cp.send(v, v, ring("x", s)))
        back = ring("z", 4 - s)
        wide["z", s].wait_recv()
        v = view(1, 0 if s == 1 else 1, pl.ds(0, 2), back["z"])
        last.append(cp.send(v, v, ring("z", s)))
    yield
    for copy in last:
        copy.wait_recv()


def half_shapes(halves):
    return [tuple(d.size for d in h) for h in halves]


def plane_sum_scratch(halves):
    a, b = half_shapes(halves)
    return [
        pltpu.VMEM((4,) + a, BF),
        pltpu.VMEM((3, 4) + a, BF),
        pltpu.VMEM((3,) + a, BF),
        pltpu.VMEM((2, 2) + b, BF),
        pltpu.VMEM((3, 2, 2) + b, BF),
        pltpu.VMEM((3,) + b, BF),
    ]


def plane_sum(cp, part, halves, own_a, far_a, last_a, own_b, far_b, last_b, out):
    me = (ax("xlo"), ax("xhi"), ax("z"))
    shape_a, shape_b = half_shapes(halves)

    def view(h, *at):
        return part.at[at + halves[h]]

    near_a = cp.local(view(0, me[0], me[1], pl.ds(0, 4)), own_a)
    near_b = cp.local(view(1, pl.ds(0, 2), pl.ds(0, 2), me[2]), own_b)
    first_a, first_b = [], []
    for j, s in enumerate(STEPS):
        d = ring("x", s)
        first_a.append(cp.send(view(0, d["xlo"], d["xhi"], pl.ds(0, 4)), far_a.at[j], d))
        d = ring("z", s)
        first_b.append(cp.send(view(1, pl.ds(0, 2), pl.ds(0, 2), d["z"]), far_b.at[j], d))
    yield
    near_a.wait()
    for copy in first_a:
        copy.wait_recv()
    for k in range(4):

        def add(i, carry, k=k):
            r = rows_of(i)
            acc = own_a[k, r, :].astype(F32)
            for j in range(3):
                acc = acc + far_a[j, k, r, :].astype(F32)
            own_a[k, r, :] = acc.astype(BF)
            return carry

        lax.fori_loop(0, shape_a[0] // 16, add, 0)
    second = []
    for j, s in enumerate(STEPS):
        d = ring("z", s)
        second.append(cp.send(own_a.at[d["z"]], last_a.at[j], d))
    near_b.wait()
    for copy in first_b:
        copy.wait_recv()
    for k in range(4):

        def add(i, carry, k=k):
            r = rows_of(i)
            acc = own_b[k // 2, k % 2, r, :].astype(F32)
            for j in range(3):
                acc = acc + far_b[j, k // 2, k % 2, r, :].astype(F32)
            own_b[k // 2, k % 2, r, :] = acc.astype(BF)
            return carry

        lax.fori_loop(0, shape_b[0] // 16, add, 0)
    for j, s in enumerate(STEPS):
        d = ring("x", s)
        second.append(cp.send(own_b.at[d["xlo"], d["xhi"]], last_b.at[j], d))
    yield
    for copy in second:
        copy.wait_recv()

    def end_a(i, carry):
        r = rows_of(i)
        acc = own_a[me[2], r, :].astype(F32)
        for j in range(3):
            acc = acc + last_a[j, r, :].astype(F32)
        at = rows_of(i) if halves[0][0].start == 0 else pl.ds(halves[0][0].start + i * 16, 16)
        out[at, halves[0][1]] = acc.astype(BF)
        return carry

    lax.fori_loop(0, shape_a[0] // 16, end_a, 0)

    def end_b(i, carry):
        r = rows_of(i)
        acc = own_b[me[0], me[1], r, :].astype(F32)
        for j in range(3):
            acc = acc + last_b[j, r, :].astype(F32)
        at = pl.ds(pl.multiple_of(halves[1][0].start + i * 16, 16), 16)
        out[at, halves[1][1]] = acc.astype(BF)
        return carry

    lax.fori_loop(0, shape_b[0] // 16, end_b, 0)


def by_rows(rows, width):
    h = rows // 2
    return ((pl.ds(0, h), pl.ds(0, width)), (pl.ds(h, h), pl.ds(0, width)))


def by_columns(rows, width):
    h = width // 2
    return ((pl.ds(0, rows), pl.ds(0, h)), (pl.ds(0, rows), pl.ds(h, h)))


def scratch(**kw):
    return {k: pltpu.VMEM(*v) for k, v in kw.items()}


def call(body, name, ident, ins, outs, work, sems, near):
    names = list(ins) + list(outs) + list(work)

    def run_body(*refs):
        body(SimpleNamespace(**dict(zip(names, refs[:-3]))), Copies(*refs[-3:]))

    results = pl.pallas_call(
        run_body,
        name=name,
        out_shape=[jax.ShapeDtypeStruct(*v[:2]) for v in outs.values()],
        in_specs=[v[1] for v in ins.values()],
        out_specs=[v[2] for v in outs.values()],
        scratch_shapes=list(work.values())
        + [
            pltpu.SemaphoreType.DMA((sems,)),
            pltpu.SemaphoreType.DMA((sems,)),
            pltpu.SemaphoreType.DMA((near,)),
        ],
        compiler_params=pltpu.CompilerParams(
            collective_id=ident, has_side_effects=True, vmem_limit_bytes=60 << 20
        ),
    )(*[v[0] for v in ins.values()])
    return SimpleNamespace(**dict(zip(outs, results)))


def drain(*chains):
    for chain in chains:
        for _ in chain:
            pass


NN = ((1,), (0,))
NT = ((1,), (1,))
TN = ((0,), (0,))


def dot(a, b, dims):
    return lax.dot_general(a, b, (dims, ((), ())), preferred_element_type=F32)


def gather_body(R, cp):
    g = place()[1]
    shuffle = Shuffle(True)
    greet(rings() + [in_group(*st) for st in GROUP], shuffle.greeting)
    me = (ax("xlo"), ax("xhi"), ax("z"))
    third = R.w_in.shape[1] // 8
    arrive = []
    for j, w in enumerate((R.w_in, R.w_f, R.w_og)):
        arrive.append(
            to_group(
                cp,
                lambda k, w=w: w.at[:, pl.ds(pl.multiple_of(k * third, 128), third)],
                lambda k, j=j: R.b3.at[me + (rows_of(k), pl.ds(j * third, third))],
            )
        )
    q = shuffle.to[0]
    at = (lax.div(q, 8), lax.rem(lax.div(q, 4), 2), lax.rem(q, 4))
    moved = [shuffle.start(cp, R.w_o, R.bo.at[at]), shuffle.start(cp, R.dn, R.bdn.at[at])]
    arrive_gu = to_group(cp, lambda k: R.gu.at[k], lambda k: R.block_gu.at[rows_of(k), :])

    def norm(i, carry):
        r = rows_of(i)
        x = R.tok[r, :].astype(F32)
        s = lax.rsqrt(jnp.mean(x * x, axis=-1, keepdims=True) + EPS)
        R.first[r, :] = (x * s * R.gain[...]).astype(BF)
        return carry

    lax.fori_loop(0, R.tok.shape[0] // 16, norm, 0)
    own = cp.local(R.first, R.fi.at[block_of(g)])
    chain = GroupGather(cp, R.first, R.fi)
    for pair in arrive:
        settle(*pair)
    b3 = plane_gather(cp, R.b3, by_rows(*R.b3.shape[3:]))
    next(b3)
    for pair in moved:
        shuffle.wait(pair)
    others = [
        plane_gather(cp, R.bo, by_columns(*R.bo.shape[3:])),
        plane_gather(cp, R.bdn, by_columns(*R.bdn.shape[3:])),
    ]
    run([b3] + others, (1, 2, 0, 1, 2, 0, 1))
    chain.rest()
    own.wait()
    settle(*arrive_gu)
    cp.finish()


def silu_slope(v, s):
    return s * (1.0 + v * (1.0 - s))


def row_sums(x):
    ones = jnp.ones((8, x.shape[1]), F32)
    return lax.dot_general(
        ones, x, (((1,), (1,)), ((), ())), precision=HIGH, preferred_element_type=F32
    )[0:1]


def as_column(row, width):
    t = jnp.transpose(jnp.broadcast_to(row, (128, 128)))
    return jnp.concatenate([t] * (width // 128), axis=1)


def chunk_rows(s):
    return pl.ds(pl.multiple_of(s * 128, 128), 128)


def wide(ref, r):
    return jnp.concatenate([ref[j, r, :] for j in range(ref.shape[0])], axis=1)


def put(ref, r, value):
    for j in range(ref.shape[0]):
        ref[j, r, :] = value[:, 128 * j : 128 * (j + 1)]


def share(cp, src, dst, index, peers):
    copies = [cp.send(src, dst.at[index], dev) for dev in peers]
    dst[pl.ds(index, 1)] = src[...][None]
    return copies


def links_before(links, k, w):
    come = jnp.zeros((1, w), F32)
    for j in range(8):
        new = links[j, 0:1, :] * come + links[j, 1:2, :]
        come = jnp.where(j < k, new, come)
    return come


def scan_body(R, cp):
    tiles, rows = R.states.shape[:2]
    w = 128 * tiles
    steps = rows // 8
    peers_chain = [in_chain(*st) for st in CHAIN]
    peers_group = [in_group(*st) for st in GROUP]
    greet(peers_chain + peers_group + [ring("x", s) for s in (1, 3)])
    load = [cp.local(R.b3, R.w3), cp.local(R.fi, R.x)]
    load_out = cp.local(R.bo, R.wo)
    own = cp.local(R.cot, R.gf.at[block_of(place()[1])])
    bulk = plane_gather(cp, R.bgu, by_rows(*R.bgu.shape[3:]), R.block_gu)
    next(bulk)
    chain = GroupGather(cp, R.cot, R.gf)
    low = R.lb[...]
    for copy in load:
        copy.wait()

    def project(j):
        for i in range(2):
            r = pl.ds(i * rows // 2, rows // 2)
            at = pl.ds(j * w, w)
            R.proj[r, at] = dot(R.x[r, :], R.w3[:, at], NN)

    project(0)
    project(1)
    next(bulk)

    def gates(i, c):
        r = rows_of(i, 32)
        f = low + (1.0 - low) * jax.nn.sigmoid(R.proj[r, w : 2 * w])
        v = R.proj[r, 0:w]
        put(R.forget, r, f)
        put(R.states, r, v * jax.nn.sigmoid(v) * (1.0 - f))
        return c

    lax.fori_loop(0, rows // 32, gates, 0)

    def step(t, c):
        at = pl.ds(t, 8, stride=steps)
        new = []
        for j, (h, a) in enumerate(c):
            f = R.forget[j, at, :]
            h = f * h + R.states[j, at, :]
            a = a * f
            R.states[j, at, :] = h
            R.prod[j, at, :] = a
            new.append((h, a))
        return tuple(new)

    start = ((jnp.zeros((8, 128), F32), jnp.ones((8, 128), F32)),) * tiles
    ends = lax.fori_loop(0, steps, step, start, unroll=8)
    h = jnp.concatenate([e[0] for e in ends], axis=1)
    a = jnp.concatenate([e[1] for e in ends], axis=1)
    c = jnp.zeros((1, w), F32)
    q = jnp.ones((1, w), F32)
    cs, qs = [], []
    for s in range(8):
        cs.append(c)
        qs.append(q)
        c = a[s : s + 1] * c + h[s : s + 1]
        q = a[s : s + 1] * q
    R.mine[...] = jnp.concatenate([q, c, jnp.zeros((6, w), F32)], axis=0)
    k = ax("xhi") * 4 + ax("z")
    small = share(cp, R.mine, R.links, k, peers_chain)
    project(2)
    for copy in small:
        copy.wait_recv()
    come = links_before(R.links, k, w)
    R.carry[...] = jnp.broadcast_to(come, (8, w))
    R.entry[...] = jnp.concatenate(qs, axis=0) * come + jnp.concatenate(cs, axis=0)

    def finish(s, c):
        r = chunk_rows(s)
        st = wide(R.states, r) + wide(R.prod, r) * R.entry[pl.ds(s, 1), :]
        put(R.states, r, st)
        R.rowsum[pl.ds(s, 1), :] = row_sums(st * st)
        return c

    lax.fori_loop(0, 8, finish, 0)
    small = share(cp, R.rowsum, R.rows8, place()[1], peers_group)
    next(bulk)
    for copy in small:
        copy.wait_recv()
    total = R.rows8[0]
    for j in range(1, 8):
        total = total + R.rows8[j]
    R.tot[...] = lax.rsqrt(total / (8.0 * w) + EPS)

    def gate(s, c):
        r = chunk_rows(s)
        v = R.proj[r, 2 * w : 3 * w]
        n = wide(R.states, r) * as_column(R.tot[pl.ds(s, 1), :], w)
        R.gated[r, :] = (n * R.gain[...] * (v * jax.nn.sigmoid(v))).astype(BF)
        return c

    lax.fori_loop(0, 8, gate, 0)
    load_out.wait()

    def out(i, c):
        at = rows_of(i, 512)
        R.part[:, at] = dot(R.gated[...], R.wo[:, at], NN).astype(BF)
        return c

    lax.fori_loop(0, R.part.shape[1] // 512, out, 0)
    chain.rest()
    own.wait()
    drain(bulk)
    cp.finish()


def feed_body(R, cp):
    y, c = ax("y"), ax("core")
    g = place()[1]
    unit, width = R.wdn.shape
    greet(ys() + rings())
    load = [cp.local(R.bgu, R.wgu), cp.local(R.gf, R.g), cp.local(R.bdn, R.wdn)]
    mixer = sum_of(cp, R.part, R.ps, R.near, R.far)
    next(mixer)
    next(mixer)
    terms = next(mixer)

    def norm(i, carry):
        r = rows_of(i)
        x = R.tok[r, :].astype(F32) + terms(i)
        R.mid[r, :] = x
        s = lax.rsqrt(jnp.mean(x * x, axis=-1, keepdims=True) + EPS)
        R.si[rows_of(g * 8 + i), :] = (x * s * R.gain[...]).astype(BF)
        return carry

    lax.fori_loop(0, 8, norm, 0)
    gather = GroupGather(cp, R.si.at[block_of(g)], R.si)
    second = GroupSum(cp, R.near, R.far)
    for copy in load:
        copy.wait()
    order = (0, 1, 3, 2)
    stores = []

    def forward(yy):
        r = rows_of(yy, 256)

        def tile(j, carry):
            at = rows_of(j, 256)
            up = pl.ds(pl.multiple_of(unit + j * 256, 256), 256)
            x = R.si[r, :]
            v = dot(x, R.wgu[:, at], NN)
            u = dot(x, R.wgu[:, up], NN)
            gh = dot(R.g[r, :], R.wdn[at, :], NT)
            sig = jax.nn.sigmoid(v)
            act = v * sig
            R.hid[r, at] = (act * u).astype(BF)
            R.ggu[r, at] = (gh * u * silu_slope(v, sig)).astype(BF)
            R.ggu[r, up] = (gh * act).astype(BF)
            return carry

        lax.fori_loop(0, unit // 256, tile, 0)

    def backward(yy):
        r = rows_of(yy, 256)

        def tile(j, carry):
            at = rows_of(j, 512)
            R.ps[r, at] = dot(R.ggu[r, :], R.wgu[at, :], NT).astype(BF)
            return carry

        lax.fori_loop(0, width // 512, tile, 0)

    def result(yy, slot):
        r = rows_of(yy, 256)

        def tile(j, carry):
            at = rows_of(j, 512)
            R.pr[slot, :, at] = dot(R.hid[r, :], R.wdn[:, at], NN).astype(BF)
            return carry

        lax.fori_loop(0, width // 512, tile, 0)
        stores.append(cp.local(R.pr.at[slot], R.part_r.at[r]))

    for i, s in enumerate(order):
        yy = lax.rem(y + 4 - s, 4)
        gather.ready(s)
        forward(yy)
        if i < 3:
            gather.forward(order[i + 1])
        if i > 1:
            back = (4 - order[i - 1]) % 4
            second.add(back, R.ps, 128 * (second.chip(back) + c))
        backward(yy)
        second.give((4 - s) % 4, R.ps.at[block_of(2 * yy + 1 - c)])
        if i > 1:
            stores[i - 2].wait()
        result(yy, i % 2)
    second.add(2, R.ps, 128 * (second.chip(2) + c))

    def grad_down(j, carry):
        at = rows_of(j, 512)
        for i in range(2):
            h = unit // 2
            v = dot(R.hid[:, h * i : h * (i + 1)], R.g[:, at], TN)
            R.ddn[i, :, :, :, at] = v.astype(BF).reshape(R.ddn.shape[1:4] + (512,))
        return carry

    lax.fori_loop(0, width // 512, grad_down, 0)
    planes = [plane_sum(cp, R.ddn, by_columns(*R.ddn.shape[3:]), *plane_refs(R, "a"), R.block_ddn)]
    next(planes[0])

    def grad_gate(i, carry):
        at = rows_of(i, 256)
        v = dot(R.si[:, at], R.ggu[:, 0:unit], TN).astype(BF)
        to = (lax.div(i, 4), lax.rem(lax.div(i, 2), 2), pl.ds(2 * lax.rem(i, 2), 2))
        R.dgate[to] = v.reshape(2, 128, unit)
        return carry

    lax.fori_loop(0, width // 256, grad_gate, 0)
    planes.append(plane_sum(cp, R.dgate, by_rows(*R.dgate.shape[3:]), *plane_refs(R, "b"), R.block_dgate))
    next(planes[1])
    terms = second.total(R.ps, 128 * g)
    R.sums[...] = jnp.zeros_like(R.sums)

    def back(i, carry):
        r = rows_of(i)
        x = R.mid[r, :]
        s = lax.rsqrt(jnp.mean(x * x, axis=-1, keepdims=True) + EPS)
        n = x * s
        dy = terms(i)
        R.sums[0:1, :] = R.sums[0:1, :] + jnp.sum(dy * n, axis=0, keepdims=True)
        dy = dy * R.gain[...]
        v = R.cot[r, :].astype(F32) + s * (dy - n * jnp.mean(dy * n, axis=-1, keepdims=True))
        R.mixed[r, :] = v
        R.block[r, :] = v.astype(BF)
        return carry

    lax.fori_loop(0, 8, back, 0)
    own = cp.local(R.block, R.gb.at[block_of(g)])
    branch = GroupGather(cp, R.block, R.gb)
    ups = []
    for copy in stores[2:]:
        copy.wait()

    def grad_up(i):
        at = pl.ds(i * 256, 256)
        v = dot(R.si[:, at], R.ggu[:, unit : 2 * unit], TN).astype(BF)
        if i > 1:
            ups[i - 2].wait()
        R.pu[i % 2] = v
        ups.append(cp.local(R.pu.at[i % 2], R.dup.at[at]))

    for i in range(width // 256):
        grad_up(i)
    for copy in ups[-2:]:
        copy.wait()
    next(planes[0])
    branch.forward(1)
    branch.forward(3)
    next(planes[1])
    branch.rest()
    own.wait()
    drain(*planes)
    cp.finish()


def plane_refs(R, key):
    return [getattr(R, "plane_" + key + str(i)) for i in range(6)]


def plane_work(key, halves):
    return {"plane_" + key + str(i): v for i, v in enumerate(plane_sum_scratch(halves))}


def back_body(R, cp):
    c = ax("core")
    p, g = place()
    tiles, rows = R.states.shape[:2]
    w = 128 * tiles
    steps = rows // 8
    width = R.tok.shape[1]
    shuffle = Shuffle(False)
    peers_chain = [in_chain(*st) for st in CHAIN]
    peers_group = [in_group(*st) for st in GROUP]
    peers_plane = [in_plane(*st) for st in PLANE]
    greet(peers_plane + peers_group, shuffle.greeting)
    load = [cp.local(R.gb, R.gbv), cp.local(R.bo, R.wo)]
    load_last = [cp.local(R.b3, R.w3), cp.local(R.fi, R.x)]
    res = sum_of(cp, R.part_r, R.pr, R.pr_near, R.pr_far)
    next(res)
    up = plane_sum(cp, R.dup, by_rows(*R.dup.shape[3:]), *plane_refs(R, "a"), R.block_dup)
    next(up)
    low = R.lb[...]
    R.sums[...] = jnp.zeros_like(R.sums)
    for copy in load:
        copy.wait()
    for i in range(2):
        r = pl.ds(i * rows // 2, rows // 2)
        R.gg[r, :] = dot(R.gbv[r, :], R.wo[...], NT)

    def through(s, carry):
        r = chunk_rows(s)
        v = R.proj[r, 2 * w : 3 * w]
        sig = jax.nn.sigmoid(v)
        n = wide(R.states, r) * as_column(R.tot[pl.ds(s, 1), :], w)
        dy = R.gg[r, :]
        R.sums[0:1, :] = R.sums[0:1, :] + jnp.sum(dy * n * (v * sig), axis=0, keepdims=True)
        R.grads[r, 2 * w : 3 * w] = (dy * n * R.gain[...] * silu_slope(v, sig)).astype(BF)
        dy = dy * R.gain[...] * (v * sig)
        put(R.gs, r, dy)
        R.rowsum[pl.ds(s, 1), :] = row_sums(dy * n)
        return carry

    lax.fori_loop(0, 8, through, 0)
    small = share(cp, R.rowsum, R.rows8, g, peers_group)
    def grad_out(j, carry):
        at = rows_of(j, 512)
        v = dot(R.gated[...], R.gbv[:, at], TN).astype(BF)
        R.do[:, :, :, :, at] = v.reshape(R.do.shape[:4] + (512,))
        return carry

    lax.fori_loop(0, width // 512, grad_out, 0)
    outs = plane_sum(cp, R.do, by_columns(*R.do.shape[3:]), *plane_refs(R, "b"), R.oo)
    next(outs)
    for copy in small:
        copy.wait_recv()
    total = R.rows8[0]
    for j in range(1, 8):
        total = total + R.rows8[j]
    cp.sent(small)
    R.rowsum[...] = total / (8.0 * w)

    def norm(s, carry):
        r = chunk_rows(s)
        t = as_column(R.tot[pl.ds(s, 1), :], w)
        m = as_column(R.rowsum[pl.ds(s, 1), :], w)
        put(R.gs, r, t * (wide(R.gs, r) - wide(R.states, r) * t * m))
        return carry

    lax.fori_loop(0, 8, norm, 0)

    def step(i, carry):
        at = pl.ds(steps - 1 - i, 8, stride=steps)
        new = []
        for j, (h, a) in enumerate(carry):
            f = R.forget[j, at, :]
            v = R.gs[j, at, :] + h
            R.gs[j, at, :] = v
            R.prod[j, at, :] = a
            new.append((f * v, a * f))
        return tuple(new)

    start = ((jnp.zeros((8, 128), F32), jnp.ones((8, 128), F32)),) * tiles
    ends = lax.fori_loop(0, steps, step, start, unroll=8)
    h = jnp.concatenate([e[0] for e in ends], axis=1)
    a = jnp.concatenate([e[1] for e in ends], axis=1)
    e = jnp.zeros((1, w), F32)
    q = jnp.ones((1, w), F32)
    cs, qs = [None] * 8, [None] * 8
    for s in range(7, -1, -1):
        cs[s] = e
        qs[s] = q
        e = a[s : s + 1] * e + h[s : s + 1]
        q = a[s : s + 1] * q
    R.mine[...] = jnp.broadcast_to(e, (8, w))
    k = ax("xhi") * 4 + ax("z")
    small = share(cp, R.mine, R.chain, k, peers_chain)
    next(res)
    for copy in small:
        copy.wait_recv()
    come = jnp.zeros((1, w), F32)
    for j in range(7, -1, -1):
        new = R.links[j, 0:1, :] * come + R.chain[j, 0:1, :]
        come = jnp.where(j > k, new, come)
    R.entry[...] = jnp.concatenate(qs, axis=0) * come + jnp.concatenate(cs, axis=0)

    def last(s, carry):
        r = chunk_rows(s)
        v = wide(R.gs, r) + wide(R.prod, r) * R.entry[pl.ds(s, 1), :]
        st = wide(R.states, r)
        above = pl.ds(jnp.maximum(s * 128 - 1, 0), 1)
        before = jnp.where(s == 0, R.carry[0:1, :], wide(R.states, above))
        top = lax.broadcasted_iota(jnp.int32, (128, w), 0) == 0
        prev = jnp.where(top, before, pltpu.roll(st, 1, 0))
        x = R.proj[r, 0:w]
        sx = jax.nn.sigmoid(x)
        f = wide(R.forget, r)
        sf = jax.nn.sigmoid(R.proj[r, w : 2 * w])
        gf = v * (prev - x * sx)
        R.grads[r, 0:w] = (v * (1.0 - f) * silu_slope(x, sx)).astype(BF)
        R.grads[r, w : 2 * w] = (gf * (1.0 - low) * sf * (1.0 - sf)).astype(BF)
        R.sums[1:2, :] = R.sums[1:2, :] + jnp.sum(gf * (1.0 - sf), axis=0, keepdims=True)
        return carry

    lax.fori_loop(0, 8, last, 0)
    for copy in load_last:
        copy.wait()
    first = GroupSum(cp, R.near, R.far)
    order = (2, 1, 3, 0)
    for i, s in enumerate(order):
        chip = first.chip(s)
        r = pl.ds(pl.multiple_of(chip * 128, 256), 256)

        def tile(j, carry, r=r):
            at = rows_of(j, 512)
            R.fp[r, at] = dot(R.grads[r, :], R.w3[at, :], NT).astype(BF)
            return carry

        lax.fori_loop(0, width // 512, tile, 0)
        first.give(s, R.fp.at[block_of(chip + 1 - c)])
        if i > 0:
            back = order[i - 1]
            first.add(back, R.fp, 128 * (first.chip(back) + c))

    def grad_three(i, carry):
        at = rows_of(i, 256)
        v = dot(R.x[:, at], R.grads[...], TN).astype(BF)
        to = (lax.div(i, 4), lax.rem(lax.div(i, 2), 2), pl.ds(2 * lax.rem(i, 2), 2))
        R.d3[to] = v.reshape(2, 128, 3 * w)
        return carry

    lax.fori_loop(0, width // 256, grad_three, 0)
    three = plane_sum(cp, R.d3, by_rows(*R.d3.shape[3:]), *plane_refs(R, "c"), R.o3)
    next(three)
    next(up)
    next(outs)
    drain(up, outs)
    arrive = [
        to_group(cp, lambda k: R.block_dgate.at[rows_of(k), :], lambda k: R.rgate.at[k]),
        to_group(cp, lambda k: R.block_dup.at[rows_of(k), :], lambda k: R.rup.at[k]),
    ]
    moved = [shuffle.start(cp, R.block_ddn, R.rdn), shuffle.start(cp, R.oo, R.ro)]
    terms = next(res)

    def finish_result(i, carry):
        r = rows_of(i)
        R.result[r, :] = (R.mid[r, :] + terms(i)).astype(BF)
        return carry

    lax.fori_loop(0, 8, finish_result, 0)
    terms_first = first.total(R.fp, 128 * g)
    R.va[...] = jnp.zeros_like(R.va)

    def back(i, carry):
        r = rows_of(i)
        x = R.tok[r, :].astype(F32)
        s = lax.rsqrt(jnp.mean(x * x, axis=-1, keepdims=True) + EPS)
        n = x * s
        dy = terms_first(i)
        R.va[0:1, :] = R.va[0:1, :] + jnp.sum(dy * n, axis=0, keepdims=True)
        dy = dy * R.attn_gain[...]
        R.gtok[r, :] = R.mixed[r, :] + s * (dy - n * jnp.mean(dy * n, axis=-1, keepdims=True))
        return carry

    lax.fori_loop(0, 8, back, 0)
    R.va[1:2, :] = R.ffn_sums[0:1, :]
    small = []
    for st in GROUP:
        dev = in_group(*st)
        k = dev["y"] * 2 + dev["core"]
        small.append(cp.send(R.va.at[:, rows_of(k, w)], R.ga.at[g], dev))
    R.ga[pl.ds(g, 1)] = R.va[:, rows_of(g, w)][None]
    next(three)
    for copy in small:
        copy.wait_recv()
    acc = R.ga[0]
    for j in range(1, 8):
        acc = acc + R.ga[j]
    R.ta[...] = acc
    R.ta[2:4, :] = R.sums[0:2, :]
    for copy in share(cp, R.ta, R.gather, p, peers_plane):
        copy.wait_recv()
    acc = R.gather[0]
    for j in range(1, 16):
        acc = acc + R.gather[j]
    R.tb[...] = acc
    small = share(cp, R.tb, R.totals, g, peers_group)
    drain(three)
    arrive.append(to_group(cp, lambda k: R.o3.at[rows_of(k), :], lambda k: R.r3.at[k]))
    for copy in small:
        copy.wait_recv()
    for pair in arrive:
        settle(*pair)
    for pair in moved:
        shuffle.wait(pair)
    cp.finish()


def bound_value(bound_table, layer_idx):
    probabilities = jax.nn.softmax(bound_table, axis=0)
    levels = jnp.arange(bound_table.shape[0], dtype=jnp.int32)[:, None]
    keep = jnp.where((levels >= 1) & (levels <= layer_idx[0]), 1.0, 0.0).astype(F32)
    return jnp.sum(probabilities * keep, axis=0)


def on_device(
    tokens, cotangent, attn_gain, w_input, w_forget, w_outgate, w_out, norm_gain, mlp_gain, w_gate, w_up, w_down, bound_table, layer_idx
):
    n, width = tokens.shape
    rows = w_input.shape[0]
    hidden_width = w_gate.shape[1]
    down = w_down.shape[0]
    padded = -(-down // 16) * 16
    unit = 16 * padded
    w = width // 8

    def spread(m):
        m = jnp.pad(m.reshape(rows, 128, down), ((0, 0), (0, 0), (0, padded - down)))
        return m.reshape(rows, 8, unit).transpose(1, 0, 2)

    gu = jnp.concatenate([spread(w_gate), spread(w_up)], axis=2)
    dn = jnp.pad(w_down, ((0, padded - down), (0, 0)))
    gains = attn_gain[None, :]
    full = (8 * n, width)
    block = (n, width)
    gate_blocks = (2, 2, 4, 8 * rows, unit)
    A = call(
        gather_body,
        "gather",
        0,
        dict(
            tok=(tokens, VMEM),
            gain=(gains, VMEM),
            w_in=(w_input, ANY),
            w_f=(w_forget, ANY),
            w_og=(w_outgate, ANY),
            w_o=(w_out, ANY),
            dn=(dn, ANY),
            gu=(gu, ANY),
        ),
        dict(
            b3=((2, 2, 4, 8 * rows, 3 * w), BF, ANY),
            bo=((2, 2, 4, rows, width), BF, ANY),
            bdn=((2, 2, 4, padded, width), BF, ANY),
            fi=(full, BF, ANY),
            block_gu=((8 * rows, 2 * unit), BF, ANY),
        ),
        scratch(first=(block, BF)),
        96,
        10,
    )
    big3 = A.b3.reshape(width, 3 * w)
    big_out = A.bo.reshape(w, width)
    group = ax("y") * 2 + ax("core")
    lower = bound_value(lax.dynamic_slice_in_dim(bound_table, group * w, w, 1), layer_idx)[None, :]
    mixer_gain = lax.dynamic_slice_in_dim(norm_gain, group * w, w, 0)[None, :]
    column = (w // 128, 8 * n, 128)
    B = call(
        scan_body,
        "scan",
        1,
        dict(
            lb=(lower, VMEM),
            gain=(mixer_gain, VMEM),
            b3=(big3, ANY),
            bo=(big_out, ANY),
            fi=(A.fi, ANY),
            block_gu=(A.block_gu, ANY),
            cot=(cotangent, ANY),
        ),
        dict(
            gated=((8 * n, w), BF, VMEM),
            states=(column, F32, VMEM),
            forget=(column, F32, VMEM),
            proj=((8 * n, 3 * w), F32, VMEM),
            tot=((8, n), F32, VMEM),
            links=((8, 8, w), F32, VMEM),
            carry=((8, w), F32, VMEM),
            part=(full, BF, VMEM),
            gf=(full, BF, ANY),
            bgu=((2, 2, 4, 8 * rows, 2 * unit), BF, ANY),
        ),
        scratch(
            w3=((width, 3 * w), BF),
            x=(full, BF),
            wo=((w, width), BF),
            prod=(column, F32),
            entry=((8, w), F32),
            mine=((8, w), F32),
            rowsum=((8, n), F32),
            rows8=((8, 8, n), F32),
        ),
        48,
        8,
    )
    gains_two = mlp_gain[None, :]
    C = call(
        feed_body,
        "feed",
        2,
        dict(
            tok=(tokens, VMEM),
            cot=(cotangent, VMEM),
            gain=(gains_two, VMEM),
            part=(B.part, ANY),
            bgu=(B.bgu.reshape(width, 2 * unit), ANY),
            bdn=(A.bdn.reshape(unit, width), ANY),
            gf=(B.gf, ANY),
        ),
        dict(
            mid=(block, F32, VMEM),
            mixed=(block, F32, VMEM),
            gb=(full, BF, ANY),
            part_r=(full, BF, ANY),
            sums=((8, width), F32, VMEM),
            block_ddn=((padded, width), BF, VMEM),
            block_dgate=((8 * rows, unit), BF, VMEM),
            dup=((width, unit), BF, ANY),
        ),
        scratch(
            wgu=((width, 2 * unit), BF),
            wdn=((unit, width), BF),
            g=(full, BF),
            si=(full, BF),
            hid=((8 * n, unit), BF),
            ggu=((8 * n, 2 * unit), BF),
            ps=(full, BF),
            pr=((2, 2 * n, width), BF),
            near=((4,) + block, BF),
            far=((3,) + block, BF),
            block=(block, BF),
            ddn=((2, 2, 4, padded, width), BF),
            dgate=(gate_blocks, BF),
            pu=((2, 256, unit), BF),
        )
        | plane_work("a", by_columns(padded, width))
        | plane_work("b", by_rows(8 * rows, unit)),
        56,
        30,
    )
    D = call(
        back_body,
        "back",
        3,
        dict(
            tok=(tokens, VMEM),
            mid=(C.mid, VMEM),
            mixed=(C.mixed, VMEM),
            attn_gain=(gains, VMEM),
            lb=(lower, VMEM),
            gain=(mixer_gain, VMEM),
            ffn_sums=(C.sums, VMEM),
            states=(B.states, VMEM),
            forget=(B.forget, VMEM),
            proj=(B.proj, VMEM),
            gated=(B.gated, VMEM),
            tot=(B.tot, VMEM),
            links=(B.links, VMEM),
            carry=(B.carry, VMEM),
            b3=(big3, ANY),
            bo=(big_out, ANY),
            fi=(A.fi, ANY),
            gb=(C.gb, ANY),
            part_r=(C.part_r, ANY),
            dup=(C.dup.reshape(gate_blocks), ANY),
            block_dgate=(C.block_dgate, ANY),
            block_ddn=(C.block_ddn, ANY),
        ),
        dict(
            result=(block, BF, VMEM),
            gtok=(block, F32, VMEM),
            rgate=((8, rows, unit), BF, VMEM),
            rup=((8, rows, unit), BF, VMEM),
            r3=((8, rows, 3 * w), BF, VMEM),
            ro=((rows, width), BF, VMEM),
            rdn=((padded, width), BF, VMEM),
            totals=((8, 8, w), F32, VMEM),
        ),
        scratch(
            gbv=(full, BF),
            wo=((w, width), BF),
            w3=((width, 3 * w), BF),
            x=(full, BF),
            gg=((8 * n, w), F32),
            gs=(column, F32),
            prod=(column, F32),
            grads=((8 * n, 3 * w), BF),
            sums=((8, w), F32),
            entry=((8, w), F32),
            mine=((8, w), F32),
            rowsum=((8, n), F32),
            rows8=((8, 8, n), F32),
            chain=((8, 8, w), F32),
            pr=((4 * n, width), BF),
            pr_near=((4,) + block, BF),
            pr_far=((3,) + block, BF),
            fp=(full, BF),
            near=((4,) + block, BF),
            far=((3,) + block, BF),
            do=((2, 2, 4, rows, width), BF),
            d3=((2, 2, 4, 8 * rows, 3 * w), BF),
            block_dup=((8 * rows, unit), BF),
            o3=((8 * rows, 3 * w), BF),
            oo=((rows, width), BF),
            va=((8, width), F32),
            ga=((8, 8, w), F32),
            ta=((8, w), F32),
            gather=((16, 8, w), F32),
            tb=((8, w), F32),
        )
        | plane_work("a", by_rows(8 * rows, unit))
        | plane_work("b", by_columns(rows, width))
        | plane_work("c", by_rows(8 * rows, 3 * w)),
        150,
        30,
    )

    def join(m):
        m = m.transpose(1, 0, 2)
        return m.reshape(rows, 8 * m.shape[2]).astype(F32)

    def unspread(m):
        m = m.transpose(1, 0, 2).reshape(rows, 128, padded)[:, :, :down]
        return m.reshape(rows, hidden_width).astype(F32)

    sums = D.totals.transpose(1, 0, 2).reshape(8, width)
    pullback = jax.vjp(lambda table: bound_value(table, layer_idx), bound_table)[1]
    return (
        D.result,
        D.gtok,
        sums[0],
        join(D.r3[:, :, :w]),
        join(D.r3[:, :, w : 2 * w]),
        join(D.r3[:, :, 2 * w :]),
        D.ro.astype(F32),
        sums[2],
        sums[1],
        unspread(D.rgate),
        unspread(D.rup),
        D.rdn[:down].astype(F32),
        pullback(sums[3])[0],
    )


def solution(mesh):
    split = Mesh(mesh.devices.reshape(2, 2, 4, 4, 2), AXES)
    cut = P(AXES, None)
    return jax.shard_map(
        on_device,
        mesh=split,
        in_specs=(cut, cut, P(), cut, cut, cut, cut, P(), P(), cut, cut, cut, P(), P()),
        out_specs=(cut, cut, P(), cut, cut, cut, cut, P(), P(), cut, cut, cut, P()),
        check_vma=False,
    )
```

```python
from types import SimpleNamespace

import jax
import jax.numpy as jnp
from jax import lax
from jax.experimental import pallas as pl
from jax.experimental.pallas import tpu as pltpu
from jax.sharding import Mesh, PartitionSpec as P

EPS = 1e-06
BF = jnp.bfloat16
F32 = jnp.float32
AXES = ("xlo", "xhi", "z", "y", "core")
MESH = pl.DeviceIdType.MESH
ANY = pl.BlockSpec(memory_space=pl.ANY)
VMEM = pl.BlockSpec(memory_space=pltpu.VMEM)
STEPS = (1, 3, 2)
GROUP = [(a, b) for a in range(4) for b in range(2) if a or b]
CHAIN = [(a, b) for a in range(2) for b in range(4) if a or b]
PLANE = [(a, b) for a in range(4) for b in range(4) if a or b]
HIGH = lax.Precision.HIGHEST


def ax(name):
    return lax.axis_index(name)


def ring(axis, s):
    if axis == "x":
        x = lax.rem(ax("xhi") * 2 + ax("xlo") + s, 4)
        return {"xhi": lax.div(x, 2), "xlo": lax.rem(x, 2)}
    return {axis: lax.rem(ax(axis) + s, 4)}


def sibling():
    return {"core": 1 - ax("core")}


def in_group(s, t):
    return {"y": lax.rem(ax("y") + s, 4), "core": lax.rem(ax("core") + t, 2)}


def in_chain(s, t):
    return {"xhi": lax.rem(ax("xhi") + s, 2), "z": lax.rem(ax("z") + t, 4)}


def in_plane(s, t):
    return {**ring("x", s), **ring("z", t)}


def place():
    return ax("xlo") * 8 + ax("xhi") * 4 + ax("z"), ax("y") * 2 + ax("core")


def device(p, g):
    return {
        "xlo": lax.div(p, 8),
        "xhi": lax.rem(lax.div(p, 4), 2),
        "z": lax.rem(p, 4),
        "y": lax.div(g, 2),
        "core": lax.rem(g, 2),
    }


class Copies:
    def __init__(self, send, recv, near):
        self.sems = (send, recv, near)
        self.count = 0
        self.locals = 0
        self.open = []

    def remote(self, src, dst, dev):
        i = self.count
        self.count += 1
        assert i < self.sems[0].shape[0]
        return pltpu.make_async_remote_copy(
            src_ref=src,
            dst_ref=dst,
            send_sem=self.sems[0].at[i],
            recv_sem=self.sems[1].at[i],
            device_id=dev,
            device_id_type=MESH,
        )

    def send(self, src, dst, dev):
        copy = self.remote(src, dst, dev)
        copy.start()
        self.open.append(copy)
        return copy

    def near(self, src, dst):
        i = self.locals
        self.locals += 1
        assert i < self.sems[2].shape[0]
        return pltpu.make_async_copy(src, dst, self.sems[2].at[i])

    def local(self, src, dst):
        copy = self.near(src, dst)
        copy.start()
        return copy

    def sent(self, copies):
        for copy in copies:
            copy.wait_send()
        gone = {id(copy) for copy in copies}
        self.open = [copy for copy in self.open if id(copy) not in gone]

    def finish(self):
        for copy in self.open:
            copy.wait_send()


def greet(peers, shuffle=None):
    bar = pltpu.get_barrier_semaphore()
    for dev in peers:
        pl.semaphore_signal(bar, inc=1, device_id=dev, device_id_type=MESH)
    count = len(peers)
    if shuffle is not None:
        source, from_me, to_me = shuffle

        @pl.when(jnp.logical_not(from_me))
        def _():
            pl.semaphore_signal(bar, inc=1, device_id=source, device_id_type=MESH)

        count = count + jnp.where(to_me, 0, 1)
    pl.semaphore_wait(bar, count)


def to_group(cp, source, dst):
    g = place()[1]
    there = dst(g)
    copies = []
    for st in GROUP:
        q = in_group(*st)
        copies.append(cp.send(source(q["y"] * 2 + q["core"]), there, q))
    return copies, cp.local(source(g), there)


def settle(copies, home):
    for copy in copies:
        copy.wait_recv()
    home.wait()


class Shuffle:
    def __init__(self, outward):
        p, g = place()
        self.d = p * 8 + g
        row = 16 * g + p
        there = (lax.rem(self.d, 16), lax.div(self.d, 16))
        here = (lax.div(row, 8), lax.rem(row, 8))
        to, come = (there, here) if outward else (here, there)
        self.to = to
        self.target, self.source = device(*to), device(*come)
        self.to_me = to[0] * 8 + to[1] == self.d
        self.from_me = come[0] * 8 + come[1] == self.d
        self.greeting = (self.source, self.from_me, self.to_me)

    def start(self, cp, src, dst):
        copy = cp.remote(src, dst, self.target)
        home = cp.near(src, dst)

        @pl.when(self.to_me)
        def _():
            home.start()

        @pl.when(jnp.logical_not(self.to_me))
        def _():
            copy.start()

        return copy, home

    def wait(self, pair):
        @pl.when(self.to_me)
        def _():
            pair[1].wait()

        @pl.when(jnp.logical_not(self.to_me))
        def _():
            pair[0].wait()


def rings():
    return [ring("x", s) for s in STEPS] + [ring("z", s) for s in STEPS]


def ys():
    return [ring("y", s) for s in STEPS] + [sibling()]


def run(chains, order):
    for i in order:
        next(chains[i], None)
    for chain in chains:
        for _ in chain:
            pass


def rows_of(i, n=16):
    return pl.ds(pl.multiple_of(i * n, n), n)


def block_of(k):
    return rows_of(k, 128)


class GroupGather:
    def __init__(self, cp, src, full):
        self.cp, self.full = cp, full
        self.at = full.at[block_of(place()[1])]
        self.moved = {s: cp.send(src, self.at, ring("y", s)) for s in STEPS}
        self.near = {0: cp.send(src, self.at, sibling())}

    def forward(self, s):
        self.moved[s].wait_recv()
        k = 2 * lax.rem(ax("y") + 4 - s, 4) + ax("core")
        at = self.full.at[block_of(k)]
        self.near[s] = self.cp.send(at, at, sibling())

    def ready(self, s):
        self.near[s].wait_recv()

    def rest(self):
        for s in STEPS:
            if s not in self.near:
                self.forward(s)
        for s in (0, 1, 3, 2):
            self.ready(s)


class GroupSum:
    def __init__(self, cp, near, far):
        self.cp, self.near, self.far = cp, near, far
        self.sent, self.moved = {}, {}

    def chip(self, s):
        return 2 * lax.rem(ax("y") + s, 4)

    def give(self, s, src):
        self.sent[s] = self.cp.send(src, self.near.at[s], sibling())

    def add(self, s, mine, at):
        near = self.near
        self.sent[s].wait_recv()

        def step(i, carry):
            r = rows_of(i)
            to = pl.ds(pl.multiple_of(at + i * 16, 16), 16)
            mine[to, :] = (mine[to, :].astype(F32) + near[s, r, :].astype(F32)).astype(BF)
            return carry

        lax.fori_loop(0, 8, step, 0)
        here = mine.at[pl.ds(pl.multiple_of(at, 128), 128)]
        self.moved[s] = self.cp.send(here, self.far.at[s - 1], ring("y", s))

    def total(self, mine, at):
        self.sent[0].wait_recv()
        for s in STEPS:
            self.moved[s].wait_recv()
        self.cp.sent(list(self.moved.values()))
        near, far = self.near, self.far

        def rows(i):
            r = rows_of(i)
            own = mine[pl.ds(pl.multiple_of(at + i * 16, 16), 16), :]
            acc = own.astype(F32) + near[0, r, :].astype(F32)
            for s in range(3):
                acc = acc + far[s, r, :].astype(F32)
            return acc

        return rows


def sum_of(cp, part, mine, near, far):
    total = GroupSum(cp, near, far)
    c = ax("core")
    own = {}
    for s in (2, 1, 3, 0):
        total.give(s, part.at[block_of(total.chip(s) + 1 - c)])
        own[s] = cp.local(part.at[block_of(total.chip(s) + c)], mine.at[pl.ds(128 * s, 128)])
    yield
    for s in (2, 1, 3):
        own[s].wait()
        total.add(s, mine, 128 * s)
    own[0].wait()
    yield
    yield total.total(mine, 0)


def plane_gather(cp, buf, halves, block=None):
    me = (ax("xlo"), ax("xhi"), ax("z"))
    home = None if block is None else cp.local(block, buf.at[me])

    def view(h, *at):
        return buf.at[at + halves[h]]

    mine = [view(h, *me) if block is None else block.at[halves[h]] for h in range(2)]
    first = []
    for s in STEPS:
        first.append(cp.send(mine[0], view(0, *me), ring("z", s)))
        first.append(cp.send(mine[1], view(1, *me), ring("x", s)))
    yield
    if home is not None:
        home.wait()
    for copy in first:
        copy.wait_recv()
    column = view(0, me[0], me[1], pl.ds(0, 4))
    row = view(1, pl.ds(0, 2), pl.ds(0, 2), me[2])
    wide = {}
    for s in (1, 3):
        wide["x", s] = cp.send(column, column, ring("x", s))
        wide["z", s] = cp.send(row, row, ring("z", s))
    yield
    last = []
    for s in (1, 3):
        back = ring("x", 4 - s)
        wide["x", s].wait_recv()
        v = view(0, back["xlo"], back["xhi"], pl.ds(0 if s == 1 else 2, 2))
        last.append(cp.send(v, v, ring("x", s)))
        back = ring("z", 4 - s)
        wide["z", s].wait_recv()
        v = view(1, 0 if s == 1 else 1, pl.ds(0, 2), back["z"])
        last.append(cp.send(v, v, ring("z", s)))
    yield
    for copy in last:
        copy.wait_recv()


def plane_first(cp, block, column, row, halves):
    me = (ax("xlo"), ax("xhi"), ax("z"))
    top, bottom = block.at[halves[0]], block.at[halves[1]]
    home = [cp.local(top, column.at[me[2]]), cp.local(bottom, row.at[me[0], me[1]])]
    first = []
    for s in STEPS:
        first.append(cp.send(top, column.at[me[2]], ring("z", s)))
        first.append(cp.send(bottom, row.at[me[0], me[1]], ring("x", s)))
    yield
    for copy in first:
        copy.wait_recv()
    for copy in home:
        copy.wait()


def plane_second(cp, column, row, buf, halves):
    me = (ax("xlo"), ax("xhi"), ax("z"))

    def view(h, *at):
        return buf.at[at + halves[h]]

    here = view(0, me[0], me[1], pl.ds(0, 4))
    across = view(1, pl.ds(0, 2), pl.ds(0, 2), me[2])
    home = [cp.local(column, here), cp.local(row, across)]
    wide = {}
    for s in (1, 3):
        wide["x", s] = cp.send(column, here, ring("x", s))
        wide["z", s] = cp.send(row, across, ring("z", s))
    yield
    last = []
    for s in (1, 3):
        back = ring("x", 4 - s)
        wide["x", s].wait_recv()
        v = view(0, back["xlo"], back["xhi"], pl.ds(0 if s == 1 else 2, 2))
        last.append(cp.send(v, v, ring("x", s)))
        back = ring("z", 4 - s)
        wide["z", s].wait_recv()
        v = view(1, 0 if s == 1 else 1, pl.ds(0, 2), back["z"])
        last.append(cp.send(v, v, ring("z", s)))
    yield
    for copy in last:
        copy.wait_recv()
    for copy in home:
        copy.wait()


def half_shapes(halves):
    return [tuple(d.size for d in h) for h in halves]


def plane_sum_scratch(halves):
    a, b = half_shapes(halves)
    return [
        pltpu.VMEM((4,) + a, BF),
        pltpu.VMEM((3, 4) + a, BF),
        pltpu.VMEM((3,) + a, BF),
        pltpu.VMEM((2, 2) + b, BF),
        pltpu.VMEM((3, 2, 2) + b, BF),
        pltpu.VMEM((3,) + b, BF),
    ]


def plane_sum(cp, part, halves, own_a, far_a, last_a, own_b, far_b, last_b, out):
    me = (ax("xlo"), ax("xhi"), ax("z"))
    shape_a, shape_b = half_shapes(halves)

    def view(h, *at):
        return part.at[at + halves[h]]

    near_a = cp.local(view(0, me[0], me[1], pl.ds(0, 4)), own_a)
    near_b = cp.local(view(1, pl.ds(0, 2), pl.ds(0, 2), me[2]), own_b)
    first_a, first_b = [], []
    for j, s in enumerate(STEPS):
        d = ring("x", s)
        first_a.append(cp.send(view(0, d["xlo"], d["xhi"], pl.ds(0, 4)), far_a.at[j], d))
        d = ring("z", s)
        first_b.append(cp.send(view(1, pl.ds(0, 2), pl.ds(0, 2), d["z"]), far_b.at[j], d))
    yield
    near_a.wait()
    for copy in first_a:
        copy.wait_recv()
    for k in range(4):

        def add(i, carry, k=k):
            r = rows_of(i)
            acc = own_a[k, r, :].astype(F32)
            for j in range(3):
                acc = acc + far_a[j, k, r, :].astype(F32)
            own_a[k, r, :] = acc.astype(BF)
            return carry

        lax.fori_loop(0, shape_a[0] // 16, add, 0)
    second = []
    for j, s in enumerate(STEPS):
        d = ring("z", s)
        second.append(cp.send(own_a.at[d["z"]], last_a.at[j], d))
    near_b.wait()
    for copy in first_b:
        copy.wait_recv()
    for k in range(4):

        def add(i, carry, k=k):
            r = rows_of(i)
            acc = own_b[k // 2, k % 2, r, :].astype(F32)
            for j in range(3):
                acc = acc + far_b[j, k // 2, k % 2, r, :].astype(F32)
            own_b[k // 2, k % 2, r, :] = acc.astype(BF)
            return carry

        lax.fori_loop(0, shape_b[0] // 16, add, 0)
    for j, s in enumerate(STEPS):
        d = ring("x", s)
        second.append(cp.send(own_b.at[d["xlo"], d["xhi"]], last_b.at[j], d))
    yield
    for copy in second:
        copy.wait_recv()

    def end_a(i, carry):
        r = rows_of(i)
        acc = own_a[me[2], r, :].astype(F32)
        for j in range(3):
            acc = acc + last_a[j, r, :].astype(F32)
        at = rows_of(i) if halves[0][0].start == 0 else pl.ds(halves[0][0].start + i * 16, 16)
        out[at, halves[0][1]] = acc.astype(BF)
        return carry

    lax.fori_loop(0, shape_a[0] // 16, end_a, 0)

    def end_b(i, carry):
        r = rows_of(i)
        acc = own_b[me[0], me[1], r, :].astype(F32)
        for j in range(3):
            acc = acc + last_b[j, r, :].astype(F32)
        at = pl.ds(pl.multiple_of(halves[1][0].start + i * 16, 16), 16)
        out[at, halves[1][1]] = acc.astype(BF)
        return carry

    lax.fori_loop(0, shape_b[0] // 16, end_b, 0)


def by_rows(rows, width):
    h = rows // 2
    return ((pl.ds(0, h), pl.ds(0, width)), (pl.ds(h, h), pl.ds(0, width)))


def by_columns(rows, width):
    h = width // 2
    return ((pl.ds(0, rows), pl.ds(0, h)), (pl.ds(0, rows), pl.ds(h, h)))


def scratch(**kw):
    return {k: pltpu.VMEM(*v) for k, v in kw.items()}


def call(body, name, ident, ins, outs, work, sems, near):
    names = list(ins) + list(outs) + list(work)

    def run_body(*refs):
        body(SimpleNamespace(**dict(zip(names, refs[:-3]))), Copies(*refs[-3:]))

    results = pl.pallas_call(
        run_body,
        name=name,
        out_shape=[jax.ShapeDtypeStruct(*v[:2]) for v in outs.values()],
        in_specs=[v[1] for v in ins.values()],
        out_specs=[v[2] for v in outs.values()],
        scratch_shapes=list(work.values())
        + [
            pltpu.SemaphoreType.DMA((sems,)),
            pltpu.SemaphoreType.DMA((sems,)),
            pltpu.SemaphoreType.DMA((near,)),
        ],
        compiler_params=pltpu.CompilerParams(
            collective_id=ident, has_side_effects=True, vmem_limit_bytes=60 << 20
        ),
    )(*[v[0] for v in ins.values()])
    return SimpleNamespace(**dict(zip(outs, results)))


def drain(*chains):
    for chain in chains:
        for _ in chain:
            pass


NN = ((1,), (0,))
NT = ((1,), (1,))
TN = ((0,), (0,))


def dot(a, b, dims):
    return lax.dot_general(a, b, (dims, ((), ())), preferred_element_type=F32)


def gather_body(R, cp):
    g = place()[1]
    shuffle = Shuffle(True)
    greet(rings() + [in_group(*st) for st in GROUP], shuffle.greeting)
    me = (ax("xlo"), ax("xhi"), ax("z"))
    third = R.w_in.shape[1] // 8
    arrive = []
    for j, w in enumerate((R.w_in, R.w_f, R.w_og)):
        arrive.append(
            to_group(
                cp,
                lambda k, w=w: w.at[:, pl.ds(pl.multiple_of(k * third, 128), third)],
                lambda k, j=j: R.b3.at[me + (rows_of(k), pl.ds(j * third, third))],
            )
        )
    q = shuffle.to[0]
    at = (lax.div(q, 8), lax.rem(lax.div(q, 4), 2), lax.rem(q, 4))
    moved = shuffle.start(cp, R.w_o, R.bo.at[at])
    arrive_gu = to_group(cp, lambda k: R.gu.at[k], lambda k: R.block_gu.at[rows_of(k), :])

    def norm(i, carry):
        r = rows_of(i)
        x = R.tok[r, :].astype(F32)
        s = lax.rsqrt(jnp.mean(x * x, axis=-1, keepdims=True) + EPS)
        R.first[r, :] = (x * s * R.gain[...]).astype(BF)
        return carry

    lax.fori_loop(0, R.tok.shape[0] // 16, norm, 0)
    own = cp.local(R.first, R.fi.at[block_of(g)])
    chain = GroupGather(cp, R.first, R.fi)
    for pair in arrive:
        settle(*pair)
    b3 = plane_gather(cp, R.b3, by_rows(*R.b3.shape[3:]))
    next(b3)
    shuffle.wait(moved)
    bo = plane_gather(cp, R.bo, by_columns(*R.bo.shape[3:]))
    next(bo)
    settle(*arrive_gu)
    gu = plane_first(cp, R.block_gu, R.gu_column, R.gu_row, by_rows(*R.block_gu.shape))
    next(gu)
    run([b3, bo, gu], (0, 1, 0, 1, 2))
    chain.rest()
    own.wait()
    cp.finish()


def silu_slope(v, s):
    return s * (1.0 + v * (1.0 - s))


def row_sums(x):
    ones = jnp.ones((8, x.shape[1]), F32)
    return lax.dot_general(
        ones, x, (((1,), (1,)), ((), ())), precision=HIGH, preferred_element_type=F32
    )[0:1]


def as_column(row, width):
    t = jnp.transpose(jnp.broadcast_to(row, (128, 128)))
    return jnp.concatenate([t] * (width // 128), axis=1)


def chunk_rows(s):
    return pl.ds(pl.multiple_of(s * 128, 128), 128)


def wide(ref, r):
    return jnp.concatenate([ref[j, r, :] for j in range(ref.shape[0])], axis=1)


def put(ref, r, value):
    for j in range(ref.shape[0]):
        ref[j, r, :] = value[:, 128 * j : 128 * (j + 1)]


def share(cp, src, dst, index, peers):
    copies = [cp.send(src, dst.at[index], dev) for dev in peers]
    dst[pl.ds(index, 1)] = src[...][None]
    return copies


def links_before(links, k, w):
    come = jnp.zeros((1, w), F32)
    for j in range(8):
        new = links[j, 0:1, :] * come + links[j, 1:2, :]
        come = jnp.where(j < k, new, come)
    return come


def scan_body(R, cp):
    tiles, rows = R.states.shape[:2]
    w = 128 * tiles
    steps = rows // 8
    peers_chain = [in_chain(*st) for st in CHAIN]
    peers_group = [in_group(*st) for st in GROUP]
    greet(peers_chain + peers_group + [ring("x", s) for s in (1, 3)])
    load = [cp.local(R.b3, R.w3), cp.local(R.fi, R.x)]
    load_out = cp.local(R.bo, R.wo)
    own = cp.local(R.cot, R.gf.at[block_of(place()[1])])
    bulk = plane_gather(cp, R.bdn, by_columns(*R.bdn.shape[3:]), R.dn)
    next(bulk)
    chain = GroupGather(cp, R.cot, R.gf)
    low = R.lb[...]
    for copy in load:
        copy.wait()

    def project(j):
        for i in range(2):
            r = pl.ds(i * rows // 2, rows // 2)
            at = pl.ds(j * w, w)
            R.proj[r, at] = dot(R.x[r, :], R.w3[:, at], NN)

    project(0)
    project(1)
    next(bulk)

    def gates(i, c):
        r = rows_of(i, 32)
        f = low + (1.0 - low) * jax.nn.sigmoid(R.proj[r, w : 2 * w])
        v = R.proj[r, 0:w]
        put(R.forget, r, f)
        put(R.states, r, v * jax.nn.sigmoid(v) * (1.0 - f))
        return c

    lax.fori_loop(0, rows // 32, gates, 0)

    def step(t, c):
        at = pl.ds(t, 8, stride=steps)
        new = []
        for j, (h, a) in enumerate(c):
            f = R.forget[j, at, :]
            h = f * h + R.states[j, at, :]
            a = a * f
            R.states[j, at, :] = h
            R.prod[j, at, :] = a
            new.append((h, a))
        return tuple(new)

    start = ((jnp.zeros((8, 128), F32), jnp.ones((8, 128), F32)),) * tiles
    ends = lax.fori_loop(0, steps, step, start, unroll=8)
    h = jnp.concatenate([e[0] for e in ends], axis=1)
    a = jnp.concatenate([e[1] for e in ends], axis=1)
    c = jnp.zeros((1, w), F32)
    q = jnp.ones((1, w), F32)
    cs, qs = [], []
    for s in range(8):
        cs.append(c)
        qs.append(q)
        c = a[s : s + 1] * c + h[s : s + 1]
        q = a[s : s + 1] * q
    R.mine[...] = jnp.concatenate([q, c, jnp.zeros((6, w), F32)], axis=0)
    k = ax("xhi") * 4 + ax("z")
    small = share(cp, R.mine, R.links, k, peers_chain)
    project(2)
    for copy in small:
        copy.wait_recv()
    come = links_before(R.links, k, w)
    R.carry[...] = jnp.broadcast_to(come, (8, w))
    R.entry[...] = jnp.concatenate(qs, axis=0) * come + jnp.concatenate(cs, axis=0)

    def finish(s, c):
        r = chunk_rows(s)
        st = wide(R.states, r) + wide(R.prod, r) * R.entry[pl.ds(s, 1), :]
        put(R.states, r, st)
        R.rowsum[pl.ds(s, 1), :] = row_sums(st * st)
        return c

    lax.fori_loop(0, 8, finish, 0)
    small = share(cp, R.rowsum, R.rows8, place()[1], peers_group)
    next(bulk)
    for copy in small:
        copy.wait_recv()
    total = R.rows8[0]
    for j in range(1, 8):
        total = total + R.rows8[j]
    R.tot[...] = lax.rsqrt(total / (8.0 * w) + EPS)

    def gate(s, c):
        r = chunk_rows(s)
        v = R.proj[r, 2 * w : 3 * w]
        n = wide(R.states, r) * as_column(R.tot[pl.ds(s, 1), :], w)
        R.gated[r, :] = (n * R.gain[...] * (v * jax.nn.sigmoid(v))).astype(BF)
        return c

    lax.fori_loop(0, 8, gate, 0)
    load_out.wait()

    def out(i, c):
        at = rows_of(i, 512)
        R.part[:, at] = dot(R.gated[...], R.wo[:, at], NN).astype(BF)
        return c

    lax.fori_loop(0, R.part.shape[1] // 512, out, 0)
    chain.rest()
    own.wait()
    drain(bulk)
    cp.finish()


def feed_body(R, cp):
    y, c = ax("y"), ax("core")
    g = place()[1]
    unit, width = R.wdn.shape
    greet(ys() + rings())
    weights = plane_second(cp, R.gu_column, R.gu_row, R.wgu, by_rows(*R.wgu.shape[3:]))
    next(weights)
    mixer = sum_of(cp, R.part, R.ps, R.near, R.far)
    next(mixer)
    load = [cp.local(R.gf, R.g), cp.local(R.bdn, R.wdn)]
    next(mixer)
    next(weights)
    terms = next(mixer)

    def norm(i, carry):
        r = rows_of(i)
        x = R.tok[r, :].astype(F32) + terms(i)
        R.mid[r, :] = x
        s = lax.rsqrt(jnp.mean(x * x, axis=-1, keepdims=True) + EPS)
        R.si[rows_of(g * 8 + i), :] = (x * s * R.gain[...]).astype(BF)
        return carry

    lax.fori_loop(0, 8, norm, 0)
    gather = GroupGather(cp, R.si.at[block_of(g)], R.si)
    second = GroupSum(cp, R.near, R.far)
    for copy in load:
        copy.wait()
    drain(weights)
    order = (0, 1, 3, 2)
    stores = []

    def forward(yy):
        r = rows_of(yy, 256)

        def tile(j, carry):
            at = rows_of(j, 256)
            up = pl.ds(pl.multiple_of(unit + j * 256, 256), 256)
            x = R.si[r, :]
            v = dot(x, R.wgu[:, :, :, :, at].reshape(width, 256), NN)
            u = dot(x, R.wgu[:, :, :, :, up].reshape(width, 256), NN)
            gh = dot(R.g[r, :], R.wdn[at, :], NT)
            sig = jax.nn.sigmoid(v)
            act = v * sig
            R.hid[r, at] = (act * u).astype(BF)
            R.ggu[r, at] = (gh * u * silu_slope(v, sig)).astype(BF)
            R.ggu[r, up] = (gh * act).astype(BF)
            return carry

        lax.fori_loop(0, unit // 256, tile, 0)

    def backward(yy):
        r = rows_of(yy, 256)

        def tile(j, carry):
            at = rows_of(j, 512)
            w = R.wgu[lax.div(j, 2), lax.rem(j, 2)].reshape(512, 2 * unit)
            R.ps[r, at] = dot(R.ggu[r, :], w, NT).astype(BF)
            return carry

        lax.fori_loop(0, width // 512, tile, 0)

    def result(yy, slot):
        r = rows_of(yy, 256)

        def tile(j, carry):
            at = rows_of(j, 512)
            R.pr[slot, :, at] = dot(R.hid[r, :], R.wdn[:, at], NN).astype(BF)
            return carry

        lax.fori_loop(0, width // 512, tile, 0)
        stores.append(cp.local(R.pr.at[slot], R.part_r.at[r]))

    for i, s in enumerate(order):
        yy = lax.rem(y + 4 - s, 4)
        gather.ready(s)
        forward(yy)
        if i < 3:
            gather.forward(order[i + 1])
        if i > 1:
            back = (4 - order[i - 1]) % 4
            second.add(back, R.ps, 128 * (second.chip(back) + c))
        backward(yy)
        second.give((4 - s) % 4, R.ps.at[block_of(2 * yy + 1 - c)])
        if i > 1:
            stores[i - 2].wait()
        result(yy, i % 2)
    second.add(2, R.ps, 128 * (second.chip(2) + c))

    def grad_down(j, carry):
        at = rows_of(j, 512)
        for i in range(2):
            h = unit // 2
            v = dot(R.hid[:, h * i : h * (i + 1)], R.g[:, at], TN)
            R.ddn[i, :, :, :, at] = v.astype(BF).reshape(R.ddn.shape[1:4] + (512,))
        return carry

    lax.fori_loop(0, width // 512, grad_down, 0)
    planes = [plane_sum(cp, R.ddn, by_columns(*R.ddn.shape[3:]), *plane_refs(R, "a"), R.block_ddn)]
    next(planes[0])

    def grad_gate(i, carry):
        at = rows_of(i, 256)
        v = dot(R.si[:, at], R.ggu[:, 0:unit], TN).astype(BF)
        to = (lax.div(i, 4), lax.rem(lax.div(i, 2), 2), pl.ds(2 * lax.rem(i, 2), 2))
        R.dgate[to] = v.reshape(2, 128, unit)
        return carry

    lax.fori_loop(0, width // 256, grad_gate, 0)
    planes.append(plane_sum(cp, R.dgate, by_rows(*R.dgate.shape[3:]), *plane_refs(R, "b"), R.block_dgate))
    next(planes[1])
    terms = second.total(R.ps, 128 * g)
    R.sums[...] = jnp.zeros_like(R.sums)

    def back(i, carry):
        r = rows_of(i)
        x = R.mid[r, :]
        s = lax.rsqrt(jnp.mean(x * x, axis=-1, keepdims=True) + EPS)
        n = x * s
        dy = terms(i)
        R.sums[0:1, :] = R.sums[0:1, :] + jnp.sum(dy * n, axis=0, keepdims=True)
        dy = dy * R.gain[...]
        v = R.cot[r, :].astype(F32) + s * (dy - n * jnp.mean(dy * n, axis=-1, keepdims=True))
        R.mixed[r, :] = v
        R.block[r, :] = v.astype(BF)
        return carry

    lax.fori_loop(0, 8, back, 0)
    own = cp.local(R.block, R.gb.at[block_of(g)])
    branch = GroupGather(cp, R.block, R.gb)
    ups = []
    for copy in stores[2:]:
        copy.wait()

    def grad_up(i):
        at = pl.ds(i * 256, 256)
        v = dot(R.si[:, at], R.ggu[:, unit : 2 * unit], TN).astype(BF)
        if i > 1:
            ups[i - 2].wait()
        R.pu[i % 2] = v
        ups.append(cp.local(R.pu.at[i % 2], R.dup.at[at]))

    for i in range(width // 256):
        grad_up(i)
    for copy in ups[-2:]:
        copy.wait()
    next(planes[0])
    branch.forward(1)
    branch.forward(3)
    next(planes[1])
    branch.rest()
    own.wait()
    drain(*planes)
    cp.finish()


def plane_refs(R, key):
    return [getattr(R, "plane_" + key + str(i)) for i in range(6)]


def plane_work(key, halves):
    return {"plane_" + key + str(i): v for i, v in enumerate(plane_sum_scratch(halves))}


def back_body(R, cp):
    c = ax("core")
    p, g = place()
    tiles, rows = R.states.shape[:2]
    w = 128 * tiles
    steps = rows // 8
    width = R.tok.shape[1]
    shuffle = Shuffle(False)
    peers_chain = [in_chain(*st) for st in CHAIN]
    peers_group = [in_group(*st) for st in GROUP]
    peers_plane = [in_plane(*st) for st in PLANE]
    greet(peers_plane + peers_group, shuffle.greeting)
    load = [cp.local(R.gb, R.gbv), cp.local(R.bo, R.wo)]
    load_last = [cp.local(R.b3, R.w3), cp.local(R.fi, R.x)]
    res = sum_of(cp, R.part_r, R.pr, R.pr_near, R.pr_far)
    next(res)
    up = plane_sum(cp, R.dup, by_rows(*R.dup.shape[3:]), *plane_refs(R, "a"), R.block_dup)
    next(up)
    low = R.lb[...]
    R.sums[...] = jnp.zeros_like(R.sums)
    gate_home = to_group(cp, lambda k: R.block_dgate.at[rows_of(k), :], lambda k: R.rgate.at[k])
    for copy in load:
        copy.wait()
    for i in range(2):
        r = pl.ds(i * rows // 2, rows // 2)
        R.gg[r, :] = dot(R.gbv[r, :], R.wo[...], NT)
    next(res)

    def through(s, carry):
        r = chunk_rows(s)
        v = R.proj[r, 2 * w : 3 * w]
        sig = jax.nn.sigmoid(v)
        n = wide(R.states, r) * as_column(R.tot[pl.ds(s, 1), :], w)
        dy = R.gg[r, :]
        R.sums[0:1, :] = R.sums[0:1, :] + jnp.sum(dy * n * (v * sig), axis=0, keepdims=True)
        R.grads[r, 2 * w : 3 * w] = (dy * n * R.gain[...] * silu_slope(v, sig)).astype(BF)
        dy = dy * R.gain[...] * (v * sig)
        put(R.gs, r, dy)
        R.rowsum[pl.ds(s, 1), :] = row_sums(dy * n)
        return carry

    lax.fori_loop(0, 8, through, 0)
    small = share(cp, R.rowsum, R.rows8, g, peers_group)
    def grad_out(j, carry):
        at = rows_of(j, 512)
        v = dot(R.gated[...], R.gbv[:, at], TN).astype(BF)
        R.do[:, :, :, :, at] = v.reshape(R.do.shape[:4] + (512,))
        return carry

    lax.fori_loop(0, width // 512, grad_out, 0)
    outs = plane_sum(cp, R.do, by_columns(*R.do.shape[3:]), *plane_refs(R, "b"), R.oo)
    next(outs)
    for copy in small:
        copy.wait_recv()
    total = R.rows8[0]
    for j in range(1, 8):
        total = total + R.rows8[j]
    cp.sent(small)
    R.rowsum[...] = total / (8.0 * w)

    def norm(s, carry):
        r = chunk_rows(s)
        t = as_column(R.tot[pl.ds(s, 1), :], w)
        m = as_column(R.rowsum[pl.ds(s, 1), :], w)
        put(R.gs, r, t * (wide(R.gs, r) - wide(R.states, r) * t * m))
        return carry

    lax.fori_loop(0, 8, norm, 0)

    def step(i, carry):
        at = pl.ds(steps - 1 - i, 8, stride=steps)
        new = []
        for j, (h, a) in enumerate(carry):
            f = R.forget[j, at, :]
            v = R.gs[j, at, :] + h
            R.gs[j, at, :] = v
            R.prod[j, at, :] = a
            new.append((f * v, a * f))
        return tuple(new)

    start = ((jnp.zeros((8, 128), F32), jnp.ones((8, 128), F32)),) * tiles
    ends = lax.fori_loop(0, steps, step, start, unroll=8)
    h = jnp.concatenate([e[0] for e in ends], axis=1)
    a = jnp.concatenate([e[1] for e in ends], axis=1)
    e = jnp.zeros((1, w), F32)
    q = jnp.ones((1, w), F32)
    cs, qs = [None] * 8, [None] * 8
    for s in range(7, -1, -1):
        cs[s] = e
        qs[s] = q
        e = a[s : s + 1] * e + h[s : s + 1]
        q = a[s : s + 1] * q
    R.mine[...] = jnp.broadcast_to(e, (8, w))
    k = ax("xhi") * 4 + ax("z")
    small = share(cp, R.mine, R.chain, k, peers_chain)
    next(up)
    next(outs)
    for copy in small:
        copy.wait_recv()
    come = jnp.zeros((1, w), F32)
    for j in range(7, -1, -1):
        new = R.links[j, 0:1, :] * come + R.chain[j, 0:1, :]
        come = jnp.where(j > k, new, come)
    R.entry[...] = jnp.concatenate(qs, axis=0) * come + jnp.concatenate(cs, axis=0)

    def last(s, carry):
        r = chunk_rows(s)
        v = wide(R.gs, r) + wide(R.prod, r) * R.entry[pl.ds(s, 1), :]
        st = wide(R.states, r)
        above = pl.ds(jnp.maximum(s * 128 - 1, 0), 1)
        before = jnp.where(s == 0, R.carry[0:1, :], wide(R.states, above))
        top = lax.broadcasted_iota(jnp.int32, (128, w), 0) == 0
        prev = jnp.where(top, before, pltpu.roll(st, 1, 0))
        x = R.proj[r, 0:w]
        sx = jax.nn.sigmoid(x)
        f = wide(R.forget, r)
        sf = jax.nn.sigmoid(R.proj[r, w : 2 * w])
        gf = v * (prev - x * sx)
        R.grads[r, 0:w] = (v * (1.0 - f) * silu_slope(x, sx)).astype(BF)
        R.grads[r, w : 2 * w] = (gf * (1.0 - low) * sf * (1.0 - sf)).astype(BF)
        R.sums[1:2, :] = R.sums[1:2, :] + jnp.sum(gf * (1.0 - sf), axis=0, keepdims=True)
        return carry

    lax.fori_loop(0, 8, last, 0)
    for copy in load_last:
        copy.wait()
    R.va[...] = jnp.zeros_like(R.va)
    R.va[1:2, :] = R.ffn_sums[0:1, :]
    first = GroupSum(cp, R.near, R.far)
    order = (2, 1, 3, 0)
    for i, s in enumerate(order):
        chip = first.chip(s)
        r = pl.ds(pl.multiple_of(chip * 128, 256), 256)

        def tile(j, carry, r=r):
            at = rows_of(j, 512)
            v = dot(R.grads[r, :], R.w3[at, :], NT)
            R.va[0:1, at] = R.va[0:1, at] + jnp.sum(
                v * (R.x[r, at].astype(F32) / R.attn_gain[:, at]), axis=0, keepdims=True
            )
            R.fp[r, at] = v.astype(BF)
            return carry

        lax.fori_loop(0, width // 512, tile, 0)
        first.give(s, R.fp.at[block_of(chip + 1 - c)])
        if i > 0:
            back = order[i - 1]
            first.add(back, R.fp, 128 * (first.chip(back) + c))

    gains = []
    for st in GROUP:
        dev = in_group(*st)
        k = dev["y"] * 2 + dev["core"]
        gains.append(cp.send(R.va.at[:, rows_of(k, w)], R.ga.at[g], dev))
    R.ga[pl.ds(g, 1)] = R.va[:, rows_of(g, w)][None]

    def grad_three(i, carry):
        at = rows_of(i, 256)
        v = dot(R.x[:, at], R.grads[...], TN).astype(BF)
        to = (lax.div(i, 4), lax.rem(lax.div(i, 2), 2), pl.ds(2 * lax.rem(i, 2), 2))
        R.d3[to] = v.reshape(2, 128, 3 * w)
        return carry

    lax.fori_loop(0, width // 256, grad_three, 0)
    three = plane_sum(cp, R.d3, by_rows(*R.d3.shape[3:]), *plane_refs(R, "c"), R.o3)
    next(three)
    drain(up, outs)
    arrive = [
        gate_home,
        to_group(cp, lambda k: R.block_dup.at[rows_of(k), :], lambda k: R.rup.at[k]),
    ]
    moved = shuffle.start(cp, R.oo, R.ro)
    for copy in gains:
        copy.wait_recv()
    acc = R.ga[0]
    for j in range(1, 8):
        acc = acc + R.ga[j]
    R.ta[...] = acc
    R.ta[2:4, :] = R.sums[0:2, :]
    for copy in share(cp, R.ta, R.gather, p, peers_plane):
        copy.wait_recv()
    acc = R.gather[0]
    for j in range(1, 16):
        acc = acc + R.gather[j]
    R.tb[...] = acc
    terms = next(res)

    def finish_result(i, carry):
        r = rows_of(i)
        R.result[r, :] = (R.mid[r, :] + terms(i)).astype(BF)
        return carry

    lax.fori_loop(0, 8, finish_result, 0)
    small = share(cp, R.tb, R.totals, g, peers_group)
    next(three)
    terms_first = first.total(R.fp, 128 * g)

    def back(i, carry):
        r = rows_of(i)
        x = R.tok[r, :].astype(F32)
        s = lax.rsqrt(jnp.mean(x * x, axis=-1, keepdims=True) + EPS)
        n = x * s
        dy = terms_first(i)
        dy = dy * R.attn_gain[...]
        R.gtok[r, :] = R.mixed[r, :] + s * (dy - n * jnp.mean(dy * n, axis=-1, keepdims=True))
        return carry

    lax.fori_loop(0, 8, back, 0)
    drain(three)
    arrive.append(to_group(cp, lambda k: R.o3.at[rows_of(k), :], lambda k: R.r3.at[k]))
    for copy in small:
        copy.wait_recv()
    for pair in arrive:
        settle(*pair)
    shuffle.wait(moved)
    cp.finish()


def bound_value(bound_table, layer_idx):
    probabilities = jax.nn.softmax(bound_table, axis=0)
    levels = jnp.arange(bound_table.shape[0], dtype=jnp.int32)[:, None]
    keep = jnp.where((levels >= 1) & (levels <= layer_idx[0]), 1.0, 0.0).astype(F32)
    return jnp.sum(probabilities * keep, axis=0)


def on_device(
    tokens, cotangent, attn_gain, w_input, w_forget, w_outgate, w_out, norm_gain, mlp_gain, w_gate, w_up, w_down, bound_table, layer_idx
):
    n, width = tokens.shape
    rows = w_input.shape[0]
    hidden_width = w_gate.shape[1]
    down = w_down.shape[0]
    padded = -(-down // 16) * 16
    unit = 16 * padded
    w = width // 8

    def spread(m):
        m = m.reshape(rows, 16, 8, down)
        m = jnp.pad(m, ((0, 0), (0, 0), (0, 0), (0, padded - down)))
        return m.transpose(2, 0, 1, 3).reshape(8, rows, unit)

    gu = jnp.concatenate([spread(w_gate), spread(w_up)], axis=2)
    dn = jnp.pad(w_down, ((0, padded - down), (0, 0)))
    gains = attn_gain[None, :]
    full = (8 * n, width)
    block = (n, width)
    gate_blocks = (2, 2, 4, 8 * rows, unit)
    A = call(
        gather_body,
        "gather",
        0,
        dict(
            tok=(tokens, VMEM),
            gain=(gains, VMEM),
            w_in=(w_input, VMEM),
            w_f=(w_forget, VMEM),
            w_og=(w_outgate, VMEM),
            w_o=(w_out, VMEM),
            gu=(gu, VMEM),
        ),
        dict(
            b3=((2, 2, 4, 8 * rows, 3 * w), BF, ANY),
            bo=((2, 2, 4, rows, width), BF, ANY),
            fi=(full, BF, ANY),
            gu_column=((4, 4 * rows, 2 * unit), BF, ANY),
            gu_row=((2, 2, 4 * rows, 2 * unit), BF, ANY),
        ),
        scratch(first=(block, BF), block_gu=((8 * rows, 2 * unit), BF)),
        96,
        10,
    )
    big3 = A.b3.reshape(width, 3 * w)
    big_out = A.bo.reshape(w, width)
    group = ax("y") * 2 + ax("core")
    lower = bound_value(lax.dynamic_slice_in_dim(bound_table, group * w, w, 1), layer_idx)[None, :]
    mixer_gain = lax.dynamic_slice_in_dim(norm_gain, group * w, w, 0)[None, :]
    column = (w // 128, 8 * n, 128)
    B = call(
        scan_body,
        "scan",
        1,
        dict(
            lb=(lower, VMEM),
            gain=(mixer_gain, VMEM),
            b3=(big3, ANY),
            bo=(big_out, ANY),
            fi=(A.fi, ANY),
            dn=(dn, VMEM),
            cot=(cotangent, VMEM),
        ),
        dict(
            gated=((8 * n, w), BF, VMEM),
            states=(column, F32, VMEM),
            forget=(column, F32, VMEM),
            proj=((8 * n, 3 * w), F32, VMEM),
            tot=((8, n), F32, VMEM),
            links=((8, 8, w), F32, VMEM),
            carry=((8, w), F32, VMEM),
            part=(full, BF, VMEM),
            gf=(full, BF, ANY),
            bdn=((2, 2, 4, padded, width), BF, ANY),
        ),
        scratch(
            w3=((width, 3 * w), BF),
            x=(full, BF),
            wo=((w, width), BF),
            prod=(column, F32),
            entry=((8, w), F32),
            mine=((8, w), F32),
            rowsum=((8, n), F32),
            rows8=((8, 8, n), F32),
        ),
        48,
        8,
    )
    gains_two = mlp_gain[None, :]
    C = call(
        feed_body,
        "feed",
        2,
        dict(
            tok=(tokens, VMEM),
            cot=(cotangent, VMEM),
            gain=(gains_two, VMEM),
            part=(B.part, ANY),
            gu_column=(A.gu_column, ANY),
            gu_row=(A.gu_row, ANY),
            bdn=(B.bdn.reshape(unit, width), ANY),
            gf=(B.gf, ANY),
        ),
        dict(
            mid=(block, F32, VMEM),
            mixed=(block, F32, VMEM),
            gb=(full, BF, ANY),
            part_r=(full, BF, ANY),
            sums=((8, width), F32, VMEM),
            block_ddn=((padded, width), BF, VMEM),
            block_dgate=((8 * rows, unit), BF, VMEM),
            dup=((width, unit), BF, ANY),
        ),
        scratch(
            wgu=((2, 2, 4, 8 * rows, 2 * unit), BF),
            wdn=((unit, width), BF),
            g=(full, BF),
            si=(full, BF),
            hid=((8 * n, unit), BF),
            ggu=((8 * n, 2 * unit), BF),
            ps=(full, BF),
            pr=((2, 2 * n, width), BF),
            near=((4,) + block, BF),
            far=((3,) + block, BF),
            block=(block, BF),
            ddn=((2, 2, 4, padded, width), BF),
            dgate=(gate_blocks, BF),
            pu=((2, 256, unit), BF),
        )
        | plane_work("a", by_columns(padded, width))
        | plane_work("b", by_rows(8 * rows, unit)),
        72,
        30,
    )
    D = call(
        back_body,
        "back",
        3,
        dict(
            tok=(tokens, VMEM),
            mid=(C.mid, VMEM),
            mixed=(C.mixed, VMEM),
            attn_gain=(gains, VMEM),
            lb=(lower, VMEM),
            gain=(mixer_gain, VMEM),
            ffn_sums=(C.sums, VMEM),
            states=(B.states, VMEM),
            forget=(B.forget, VMEM),
            proj=(B.proj, VMEM),
            gated=(B.gated, VMEM),
            tot=(B.tot, VMEM),
            links=(B.links, VMEM),
            carry=(B.carry, VMEM),
            b3=(big3, ANY),
            bo=(big_out, ANY),
            fi=(A.fi, ANY),
            gb=(C.gb, ANY),
            part_r=(C.part_r, ANY),
            dup=(C.dup.reshape(gate_blocks), ANY),
            block_dgate=(C.block_dgate, ANY),
        ),
        dict(
            result=(block, BF, VMEM),
            gtok=(block, F32, VMEM),
            rgate=((8, rows, unit), BF, VMEM),
            rup=((8, rows, unit), BF, VMEM),
            r3=((8, rows, 3 * w), BF, VMEM),
            ro=((rows, width), BF, VMEM),
            totals=((8, 8, w), F32, VMEM),
        ),
        scratch(
            gbv=(full, BF),
            wo=((w, width), BF),
            w3=((width, 3 * w), BF),
            x=(full, BF),
            gg=((8 * n, w), F32),
            gs=(column, F32),
            prod=(column, F32),
            grads=((8 * n, 3 * w), BF),
            sums=((8, w), F32),
            entry=((8, w), F32),
            mine=((8, w), F32),
            rowsum=((8, n), F32),
            rows8=((8, 8, n), F32),
            chain=((8, 8, w), F32),
            pr=((4 * n, width), BF),
            pr_near=((4,) + block, BF),
            pr_far=((3,) + block, BF),
            fp=(full, BF),
            near=((4,) + block, BF),
            far=((3,) + block, BF),
            do=((2, 2, 4, rows, width), BF),
            d3=((2, 2, 4, 8 * rows, 3 * w), BF),
            block_dup=((8 * rows, unit), BF),
            o3=((8 * rows, 3 * w), BF),
            oo=((rows, width), BF),
            va=((8, width), F32),
            ga=((8, 8, w), F32),
            ta=((8, w), F32),
            gather=((16, 8, w), F32),
            tb=((8, w), F32),
        )
        | plane_work("a", by_rows(8 * rows, unit))
        | plane_work("b", by_columns(rows, width))
        | plane_work("c", by_rows(8 * rows, 3 * w)),
        150,
        30,
    )

    def join(m):
        m = m.transpose(1, 0, 2)
        return m.reshape(rows, 8 * m.shape[2]).astype(F32)

    def unspread(m):
        m = m.reshape(8, rows, 16, padded)[:, :, :, :down].transpose(1, 2, 0, 3)
        return m.reshape(rows, hidden_width).astype(F32)

    sums = D.totals.transpose(1, 0, 2).reshape(8, width)
    pullback = jax.vjp(lambda table: bound_value(table, layer_idx), bound_table)[1]
    return (
        D.result,
        D.gtok,
        sums[0],
        join(D.r3[:, :, :w]),
        join(D.r3[:, :, w : 2 * w]),
        join(D.r3[:, :, 2 * w :]),
        D.ro.astype(F32),
        sums[2],
        sums[1],
        unspread(D.rgate),
        unspread(D.rup),
        C.block_ddn[:down].astype(F32),
        pullback(sums[3])[0],
    )


def solution(mesh):
    split = Mesh(mesh.devices.reshape(2, 2, 4, 4, 2), AXES)
    cut = P(AXES, None)
    return jax.shard_map(
        on_device,
        mesh=split,
        in_specs=(cut, cut, P(), cut, cut, cut, cut, P(), P(), cut, cut, cut, P(), P()),
        out_specs=(cut, cut, P(), cut, cut, cut, cut, P(), P(), cut, cut, cut, P()),
        check_vma=False,
    )
```

```python
from types import SimpleNamespace

import jax
import jax.numpy as jnp
from jax import lax
from jax.experimental import pallas as pl
from jax.experimental.pallas import tpu as pltpu
from jax.sharding import Mesh, PartitionSpec as P

EPS = 1e-06
BF = jnp.bfloat16
F32 = jnp.float32
AXES = ("xlo", "xhi", "z", "y", "core")
MESH = pl.DeviceIdType.MESH
ANY = pl.BlockSpec(memory_space=pl.ANY)
VMEM = pl.BlockSpec(memory_space=pltpu.VMEM)
STEPS = (1, 3, 2)
GROUP = [(a, b) for a in range(4) for b in range(2) if a or b]
CHAIN = [(a, b) for a in range(2) for b in range(4) if a or b]
PLANE = [(a, b) for a in range(4) for b in range(4) if a or b]
HIGH = lax.Precision.HIGHEST


def ax(name):
    return lax.axis_index(name)


def ring(axis, s):
    if axis == "x":
        x = lax.rem(ax("xhi") * 2 + ax("xlo") + s, 4)
        return {"xhi": lax.div(x, 2), "xlo": lax.rem(x, 2)}
    return {axis: lax.rem(ax(axis) + s, 4)}


def sibling():
    return {"core": 1 - ax("core")}


def in_group(s, t):
    return {"y": lax.rem(ax("y") + s, 4), "core": lax.rem(ax("core") + t, 2)}


def in_chain(s, t):
    return {"xhi": lax.rem(ax("xhi") + s, 2), "z": lax.rem(ax("z") + t, 4)}


def in_plane(s, t):
    return {**ring("x", s), **ring("z", t)}


def place():
    return ax("xlo") * 8 + ax("xhi") * 4 + ax("z"), ax("y") * 2 + ax("core")


def device(p, g):
    return {
        "xlo": lax.div(p, 8),
        "xhi": lax.rem(lax.div(p, 4), 2),
        "z": lax.rem(p, 4),
        "y": lax.div(g, 2),
        "core": lax.rem(g, 2),
    }


class Copies:
    def __init__(self, send, recv, near):
        self.sems = (send, recv, near)
        self.count = 0
        self.locals = 0
        self.open = []

    def remote(self, src, dst, dev):
        i = self.count
        self.count += 1
        assert i < self.sems[0].shape[0]
        return pltpu.make_async_remote_copy(
            src_ref=src,
            dst_ref=dst,
            send_sem=self.sems[0].at[i],
            recv_sem=self.sems[1].at[i],
            device_id=dev,
            device_id_type=MESH,
        )

    def send(self, src, dst, dev):
        copy = self.remote(src, dst, dev)
        copy.start()
        self.open.append(copy)
        return copy

    def near(self, src, dst):
        i = self.locals
        self.locals += 1
        assert i < self.sems[2].shape[0]
        return pltpu.make_async_copy(src, dst, self.sems[2].at[i])

    def local(self, src, dst):
        copy = self.near(src, dst)
        copy.start()
        return copy

    def sent(self, copies):
        for copy in copies:
            copy.wait_send()
        gone = {id(copy) for copy in copies}
        self.open = [copy for copy in self.open if id(copy) not in gone]

    def finish(self):
        for copy in self.open:
            copy.wait_send()


def greet(peers, shuffle=None):
    bar = pltpu.get_barrier_semaphore()
    for dev in peers:
        pl.semaphore_signal(bar, inc=1, device_id=dev, device_id_type=MESH)
    count = len(peers)
    if shuffle is not None:
        source, from_me, to_me = shuffle

        @pl.when(jnp.logical_not(from_me))
        def _():
            pl.semaphore_signal(bar, inc=1, device_id=source, device_id_type=MESH)

        count = count + jnp.where(to_me, 0, 1)
    pl.semaphore_wait(bar, count)


def to_group(cp, source, dst):
    g = place()[1]
    there = dst(g)
    copies = []
    for st in GROUP:
        q = in_group(*st)
        copies.append(cp.send(source(q["y"] * 2 + q["core"]), there, q))
    return copies, cp.local(source(g), there)


def settle(copies, home):
    for copy in copies:
        copy.wait_recv()
    home.wait()


class Shuffle:
    def __init__(self, outward):
        p, g = place()
        self.d = p * 8 + g
        row = 16 * g + p
        there = (lax.rem(self.d, 16), lax.div(self.d, 16))
        here = (lax.div(row, 8), lax.rem(row, 8))
        to, come = (there, here) if outward else (here, there)
        self.to = to
        self.target, self.source = device(*to), device(*come)
        self.to_me = to[0] * 8 + to[1] == self.d
        self.from_me = come[0] * 8 + come[1] == self.d
        self.greeting = (self.source, self.from_me, self.to_me)

    def start(self, cp, src, dst):
        copy = cp.remote(src, dst, self.target)
        home = cp.near(src, dst)

        @pl.when(self.to_me)
        def _():
            home.start()

        @pl.when(jnp.logical_not(self.to_me))
        def _():
            copy.start()

        return copy, home

    def wait(self, pair):
        @pl.when(self.to_me)
        def _():
            pair[1].wait()

        @pl.when(jnp.logical_not(self.to_me))
        def _():
            pair[0].wait()


def rings():
    return [ring("x", s) for s in STEPS] + [ring("z", s) for s in STEPS]


def ys():
    return [ring("y", s) for s in STEPS] + [sibling()]


def run(chains, order):
    for i in order:
        next(chains[i], None)
    for chain in chains:
        for _ in chain:
            pass


def rows_of(i, n=16):
    return pl.ds(pl.multiple_of(i * n, n), n)


def block_of(k):
    return rows_of(k, 128)


class GroupGather:
    def __init__(self, cp, src, full):
        self.cp, self.full = cp, full
        k = place()[1]
        self.half = {}
        for first in (0, 1):
            for s in (1, 3):
                h = first if s == 1 else 1 - first
                self.half[s, h] = cp.send(
                    src.at[pl.ds(64 * h, 64)], full.at[self.rows(k, h)], ring("y", s)
                )
        self.near = {0: cp.send(src, full.at[block_of(k)], sibling())}
        self.done = set()

    def rows(self, k, h):
        return pl.ds(pl.multiple_of(k * 128 + 64 * h, 64), 64)

    def chip(self, s):
        return 2 * lax.rem(ax("y") + 4 - s, 4) + ax("core")

    def arrived(self, s, h):
        if (s, h) not in self.done:
            self.done.add((s, h))
            self.half[s, h].wait_recv()

    def relay(self):
        for s, h in ((1, 0), (3, 1)):
            self.arrived(s, h)
            at = self.full.at[self.rows(self.chip(s), h)]
            self.half[2, h] = self.cp.send(at, at, ring("y", s))

    def forward(self, s):
        if (2, 0) not in self.half:
            self.relay()
        self.arrived(s, 0)
        self.arrived(s, 1)
        at = self.full.at[block_of(self.chip(s))]
        self.near[s] = self.cp.send(at, at, sibling())

    def ready(self, s):
        self.near[s].wait_recv()

    def rest(self):
        for s in STEPS:
            if s not in self.near:
                self.forward(s)
        for s in (0, 1, 3, 2):
            self.ready(s)


class GroupSum:
    def __init__(self, cp, near, far):
        self.cp, self.near, self.far = cp, near, far
        self.sent, self.moved = {}, {}

    def chip(self, s):
        return 2 * lax.rem(ax("y") + s, 4)

    def give(self, s, src):
        self.sent[s] = self.cp.send(src, self.near.at[s], sibling())

    def add(self, s, mine, at):
        near = self.near
        self.sent[s].wait_recv()

        def step(i, carry):
            r = rows_of(i)
            to = pl.ds(pl.multiple_of(at + i * 16, 16), 16)
            mine[to, :] = (mine[to, :].astype(F32) + near[s, r, :].astype(F32)).astype(BF)
            return carry

        lax.fori_loop(0, 8, step, 0)
        here = mine.at[pl.ds(pl.multiple_of(at, 128), 128)]
        self.moved[s] = self.cp.send(here, self.far.at[s - 1], ring("y", s))

    def total(self, mine, at):
        self.sent[0].wait_recv()
        for s in STEPS:
            self.moved[s].wait_recv()
        self.cp.sent(list(self.moved.values()))
        near, far = self.near, self.far

        def rows(i):
            r = rows_of(i)
            own = mine[pl.ds(pl.multiple_of(at + i * 16, 16), 16), :]
            acc = own.astype(F32) + near[0, r, :].astype(F32)
            for s in range(3):
                acc = acc + far[s, r, :].astype(F32)
            return acc

        return rows


class RelaySum(GroupSum):
    def piece(self, mine, at, h):
        return mine.at[pl.ds(pl.multiple_of(at + 64 * h, 64), 64)]

    def plus(self, mine, at, term, n):
        def step(i, carry):
            to = pl.ds(pl.multiple_of(at + i * 16, 16), 16)
            mine[to, :] = (mine[to, :].astype(F32) + term(rows_of(i)).astype(F32)).astype(BF)
            return carry

        lax.fori_loop(0, n // 16, step, 0)

    def to(self, s, slot, h, mine, at):
        return self.cp.send(
            self.piece(mine, at, h), self.far.at[slot, pl.ds(64 * h, 64)], ring("y", s)
        )

    def add(self, s, mine, at):
        near = self.near
        self.sent[s].wait_recv()
        self.plus(mine, at, lambda r: near[s, r, :], 128)
        if s == 2:
            self.hop = [self.to(1, 2, 0, mine, at), self.to(3, 2, 1, mine, at)]
        elif s == 1:
            self.moved[1, 1] = self.to(1, 0, 1, mine, at)
        else:
            self.moved[3, 0] = self.to(3, 1, 0, mine, at)

    def relay(self, mine, at_next, at_last):
        far = self.far
        self.hop[0].wait_recv()
        self.plus(mine, at_next, lambda r: far[2, r, :], 64)
        self.moved[1, 0] = self.to(1, 0, 0, mine, at_next)
        self.hop[1].wait_recv()
        up = lambda r: far[2, pl.ds(pl.multiple_of(64 + r.start, 16), 16), :]
        self.plus(mine, at_last + 64, up, 64)
        self.moved[3, 1] = self.to(3, 1, 1, mine, at_last)

    def total(self, mine, at):
        self.sent[0].wait_recv()
        for key in ((1, 1), (3, 0), (1, 0), (3, 1)):
            self.moved[key].wait_recv()
        self.cp.sent(self.hop + list(self.moved.values()))
        near, far = self.near, self.far

        def rows(i):
            r = rows_of(i)
            own = mine[pl.ds(pl.multiple_of(at + i * 16, 16), 16), :]
            acc = own.astype(F32) + near[0, r, :].astype(F32)
            return acc + (far[0, r, :].astype(F32) + far[1, r, :].astype(F32))

        return rows


def sum_of(cp, part, mine, near, far):
    total = RelaySum(cp, near, far)
    c = ax("core")
    own = {}
    for s in (2, 1, 3, 0):
        total.give(s, part.at[block_of(total.chip(s) + 1 - c)])
        own[s] = cp.local(part.at[block_of(total.chip(s) + c)], mine.at[pl.ds(128 * s, 128)])
    yield
    for s in (2, 1, 3):
        own[s].wait()
        total.add(s, mine, 128 * s)
    own[0].wait()
    yield
    total.relay(mine, 128, 384)
    yield
    yield total.total(mine, 0)


def plane_gather(cp, buf, halves, block=None):
    me = (ax("xlo"), ax("xhi"), ax("z"))
    home = None if block is None else cp.local(block, buf.at[me])

    def view(h, *at):
        return buf.at[at + halves[h]]

    mine = [view(h, *me) if block is None else block.at[halves[h]] for h in range(2)]
    first = []
    for s in STEPS:
        first.append(cp.send(mine[0], view(0, *me), ring("z", s)))
        first.append(cp.send(mine[1], view(1, *me), ring("x", s)))
    yield
    if home is not None:
        home.wait()
    for copy in first:
        copy.wait_recv()
    column = view(0, me[0], me[1], pl.ds(0, 4))
    row = view(1, pl.ds(0, 2), pl.ds(0, 2), me[2])
    wide = {}
    for s in (1, 3):
        wide["x", s] = cp.send(column, column, ring("x", s))
        wide["z", s] = cp.send(row, row, ring("z", s))
    yield
    last = []
    for s in (1, 3):
        back = ring("x", 4 - s)
        wide["x", s].wait_recv()
        v = view(0, back["xlo"], back["xhi"], pl.ds(0 if s == 1 else 2, 2))
        last.append(cp.send(v, v, ring("x", s)))
        back = ring("z", 4 - s)
        wide["z", s].wait_recv()
        v = view(1, 0 if s == 1 else 1, pl.ds(0, 2), back["z"])
        last.append(cp.send(v, v, ring("z", s)))
    yield
    for copy in last:
        copy.wait_recv()


def plane_first(cp, block, column, row, halves):
    me = (ax("xlo"), ax("xhi"), ax("z"))
    top, bottom = block.at[halves[0]], block.at[halves[1]]
    home = [cp.local(top, column.at[me[2]]), cp.local(bottom, row.at[me[0], me[1]])]
    first = []
    for s in STEPS:
        first.append(cp.send(top, column.at[me[2]], ring("z", s)))
        first.append(cp.send(bottom, row.at[me[0], me[1]], ring("x", s)))
    yield
    for copy in first:
        copy.wait_recv()
    for copy in home:
        copy.wait()


def plane_second(cp, column, row, buf, halves):
    me = (ax("xlo"), ax("xhi"), ax("z"))

    def view(h, *at):
        return buf.at[at + halves[h]]

    here = view(0, me[0], me[1], pl.ds(0, 4))
    across = view(1, pl.ds(0, 2), pl.ds(0, 2), me[2])
    home = [cp.local(column, here), cp.local(row, across)]
    wide = {}
    for s in (1, 3):
        wide["x", s] = cp.send(column, here, ring("x", s))
        wide["z", s] = cp.send(row, across, ring("z", s))
    yield
    last = []
    for s in (1, 3):
        back = ring("x", 4 - s)
        wide["x", s].wait_recv()
        v = view(0, back["xlo"], back["xhi"], pl.ds(0 if s == 1 else 2, 2))
        last.append(cp.send(v, v, ring("x", s)))
        back = ring("z", 4 - s)
        wide["z", s].wait_recv()
        v = view(1, 0 if s == 1 else 1, pl.ds(0, 2), back["z"])
        last.append(cp.send(v, v, ring("z", s)))
    yield
    for copy in last:
        copy.wait_recv()
    for copy in home:
        copy.wait()


def half_shapes(halves):
    return [tuple(d.size for d in h) for h in halves]


def plane_sum_scratch(halves):
    a, b = half_shapes(halves)
    return [
        pltpu.VMEM((4,) + a, BF),
        pltpu.VMEM((3, 4) + a, BF),
        pltpu.VMEM((3,) + a, BF),
        pltpu.VMEM((2, 2) + b, BF),
        pltpu.VMEM((3, 2, 2) + b, BF),
        pltpu.VMEM((3,) + b, BF),
    ]


def plane_sum(cp, part, halves, own_a, far_a, last_a, own_b, far_b, last_b, out):
    me = (ax("xlo"), ax("xhi"), ax("z"))
    shape_a, shape_b = half_shapes(halves)

    def view(h, *at):
        return part.at[at + halves[h]]

    near_a = cp.local(view(0, me[0], me[1], pl.ds(0, 4)), own_a)
    near_b = cp.local(view(1, pl.ds(0, 2), pl.ds(0, 2), me[2]), own_b)
    first_a, first_b = [], []
    for j, s in enumerate(STEPS):
        d = ring("x", s)
        first_a.append(cp.send(view(0, d["xlo"], d["xhi"], pl.ds(0, 4)), far_a.at[j], d))
        d = ring("z", s)
        first_b.append(cp.send(view(1, pl.ds(0, 2), pl.ds(0, 2), d["z"]), far_b.at[j], d))
    yield
    near_a.wait()
    for copy in first_a:
        copy.wait_recv()
    for k in range(4):

        def add(i, carry, k=k):
            r = rows_of(i)
            acc = own_a[k, r, :].astype(F32)
            for j in range(3):
                acc = acc + far_a[j, k, r, :].astype(F32)
            own_a[k, r, :] = acc.astype(BF)
            return carry

        lax.fori_loop(0, shape_a[0] // 16, add, 0)
    second = []
    for j, s in enumerate(STEPS):
        d = ring("z", s)
        second.append(cp.send(own_a.at[d["z"]], last_a.at[j], d))
    near_b.wait()
    for copy in first_b:
        copy.wait_recv()
    for k in range(4):

        def add(i, carry, k=k):
            r = rows_of(i)
            acc = own_b[k // 2, k % 2, r, :].astype(F32)
            for j in range(3):
                acc = acc + far_b[j, k // 2, k % 2, r, :].astype(F32)
            own_b[k // 2, k % 2, r, :] = acc.astype(BF)
            return carry

        lax.fori_loop(0, shape_b[0] // 16, add, 0)
    for j, s in enumerate(STEPS):
        d = ring("x", s)
        second.append(cp.send(own_b.at[d["xlo"], d["xhi"]], last_b.at[j], d))
    yield
    for copy in second:
        copy.wait_recv()

    def end_a(i, carry):
        r = rows_of(i)
        acc = own_a[me[2], r, :].astype(F32)
        for j in range(3):
            acc = acc + last_a[j, r, :].astype(F32)
        at = rows_of(i) if halves[0][0].start == 0 else pl.ds(halves[0][0].start + i * 16, 16)
        out[at, halves[0][1]] = acc.astype(BF)
        return carry

    lax.fori_loop(0, shape_a[0] // 16, end_a, 0)

    def end_b(i, carry):
        r = rows_of(i)
        acc = own_b[me[0], me[1], r, :].astype(F32)
        for j in range(3):
            acc = acc + last_b[j, r, :].astype(F32)
        at = pl.ds(pl.multiple_of(halves[1][0].start + i * 16, 16), 16)
        out[at, halves[1][1]] = acc.astype(BF)
        return carry

    lax.fori_loop(0, shape_b[0] // 16, end_b, 0)


def by_rows(rows, width):
    h = rows // 2
    return ((pl.ds(0, h), pl.ds(0, width)), (pl.ds(h, h), pl.ds(0, width)))


def by_columns(rows, width):
    h = width // 2
    return ((pl.ds(0, rows), pl.ds(0, h)), (pl.ds(0, rows), pl.ds(h, h)))


def scratch(**kw):
    return {k: pltpu.VMEM(*v) for k, v in kw.items()}


def call(body, name, ident, ins, outs, work, sems, near):
    names = list(ins) + list(outs) + list(work)

    def run_body(*refs):
        body(SimpleNamespace(**dict(zip(names, refs[:-3]))), Copies(*refs[-3:]))

    results = pl.pallas_call(
        run_body,
        name=name,
        out_shape=[jax.ShapeDtypeStruct(*v[:2]) for v in outs.values()],
        in_specs=[v[1] for v in ins.values()],
        out_specs=[v[2] for v in outs.values()],
        scratch_shapes=list(work.values())
        + [
            pltpu.SemaphoreType.DMA((sems,)),
            pltpu.SemaphoreType.DMA((sems,)),
            pltpu.SemaphoreType.DMA((near,)),
        ],
        compiler_params=pltpu.CompilerParams(
            collective_id=ident, has_side_effects=True, vmem_limit_bytes=60 << 20
        ),
    )(*[v[0] for v in ins.values()])
    return SimpleNamespace(**dict(zip(outs, results)))


def drain(*chains):
    for chain in chains:
        for _ in chain:
            pass


NN = ((1,), (0,))
NT = ((1,), (1,))
TN = ((0,), (0,))


def dot(a, b, dims):
    return lax.dot_general(a, b, (dims, ((), ())), preferred_element_type=F32)


def gather_body(R, cp):
    g = place()[1]
    shuffle = Shuffle(True)
    greet(rings() + [in_group(*st) for st in GROUP], shuffle.greeting)
    me = (ax("xlo"), ax("xhi"), ax("z"))
    third = R.w_in.shape[1] // 8
    arrive = []
    for j, w in enumerate((R.w_in, R.w_f, R.w_og)):
        arrive.append(
            to_group(
                cp,
                lambda k, w=w: w.at[:, pl.ds(pl.multiple_of(k * third, 128), third)],
                lambda k, j=j: R.b3.at[me + (rows_of(k), pl.ds(j * third, third))],
            )
        )
    q = shuffle.to[0]
    at = (lax.div(q, 8), lax.rem(lax.div(q, 4), 2), lax.rem(q, 4))
    moved = shuffle.start(cp, R.w_o, R.bo.at[at])
    arrive_gu = to_group(cp, lambda k: R.gu.at[k], lambda k: R.block_gu.at[rows_of(k), :])

    def norm(i, carry):
        r = rows_of(i)
        x = R.tok[r, :].astype(F32)
        s = lax.rsqrt(jnp.mean(x * x, axis=-1, keepdims=True) + EPS)
        R.first[r, :] = (x * s * R.gain[...]).astype(BF)
        return carry

    lax.fori_loop(0, R.tok.shape[0] // 16, norm, 0)
    own = cp.local(R.first, R.fi.at[block_of(g)])
    chain = GroupGather(cp, R.first, R.fi)
    for pair in arrive:
        settle(*pair)
    b3 = plane_gather(cp, R.b3, by_rows(*R.b3.shape[3:]))
    next(b3)
    shuffle.wait(moved)
    bo = plane_gather(cp, R.bo, by_columns(*R.bo.shape[3:]))
    next(bo)
    next(b3)
    next(bo)
    settle(*arrive_gu)
    gu = plane_first(cp, R.block_gu, R.gu_column, R.gu_row, by_rows(*R.block_gu.shape))
    next(gu)
    chain.relay()
    run([b3, bo, gu], (0, 1, 2))
    chain.rest()
    own.wait()
    cp.finish()


def silu_slope(v, s):
    return s * (1.0 + v * (1.0 - s))


def row_sums(x):
    ones = jnp.ones((8, x.shape[1]), F32)
    return lax.dot_general(
        ones, x, (((1,), (1,)), ((), ())), precision=HIGH, preferred_element_type=F32
    )[0:1]


def as_column(row, width):
    t = jnp.transpose(jnp.broadcast_to(row, (128, 128)))
    return jnp.concatenate([t] * (width // 128), axis=1)


def chunk_rows(s):
    return pl.ds(pl.multiple_of(s * 128, 128), 128)


def wide(ref, r):
    return jnp.concatenate([ref[j, r, :] for j in range(ref.shape[0])], axis=1)


def put(ref, r, value):
    for j in range(ref.shape[0]):
        ref[j, r, :] = value[:, 128 * j : 128 * (j + 1)]


def share(cp, src, dst, index, peers):
    copies = [cp.send(src, dst.at[index], dev) for dev in peers]
    dst[pl.ds(index, 1)] = src[...][None]
    return copies


def links_before(links, k, w):
    come = jnp.zeros((1, w), F32)
    for j in range(8):
        new = links[j, 0:1, :] * come + links[j, 1:2, :]
        come = jnp.where(j < k, new, come)
    return come


def scan_body(R, cp):
    tiles, rows = R.states.shape[:2]
    w = 128 * tiles
    steps = rows // 8
    peers_chain = [in_chain(*st) for st in CHAIN]
    peers_group = [in_group(*st) for st in GROUP]
    greet(peers_chain + peers_group + [ring("x", s) for s in (1, 3)])
    load = [cp.local(R.b3, R.w3), cp.local(R.fi, R.x)]
    load_out = cp.local(R.bo, R.wo)
    own = cp.local(R.cot, R.gf.at[block_of(place()[1])])
    bulk = plane_gather(cp, R.bdn, by_columns(*R.bdn.shape[3:]), R.dn)
    next(bulk)
    chain = GroupGather(cp, R.cot, R.gf)
    low = R.lb[...]
    for copy in load:
        copy.wait()

    def project(j):
        for i in range(2):
            r = pl.ds(i * rows // 2, rows // 2)
            at = pl.ds(j * w, w)
            R.proj[r, at] = dot(R.x[r, :], R.w3[:, at], NN)

    project(0)
    project(1)
    next(bulk)
    chain.relay()

    def gates(i, c):
        r = rows_of(i, 32)
        f = low + (1.0 - low) * jax.nn.sigmoid(R.proj[r, w : 2 * w])
        v = R.proj[r, 0:w]
        put(R.forget, r, f)
        put(R.states, r, v * jax.nn.sigmoid(v) * (1.0 - f))
        return c

    lax.fori_loop(0, rows // 32, gates, 0)
    keep = [cp.local(R.forget, R.forget_out)]

    def step(t, c):
        at = pl.ds(t, 8, stride=steps)
        new = []
        for j, (h, a) in enumerate(c):
            f = R.forget[j, at, :]
            h = f * h + R.states[j, at, :]
            a = a * f
            R.states[j, at, :] = h
            R.prod[j, at, :] = a
            new.append((h, a))
        return tuple(new)

    start = ((jnp.zeros((8, 128), F32), jnp.ones((8, 128), F32)),) * tiles
    ends = lax.fori_loop(0, steps, step, start, unroll=8)
    h = jnp.concatenate([e[0] for e in ends], axis=1)
    a = jnp.concatenate([e[1] for e in ends], axis=1)
    c = jnp.zeros((1, w), F32)
    q = jnp.ones((1, w), F32)
    cs, qs = [], []
    for s in range(8):
        cs.append(c)
        qs.append(q)
        c = a[s : s + 1] * c + h[s : s + 1]
        q = a[s : s + 1] * q
    R.mine[...] = jnp.concatenate([q, c, jnp.zeros((6, w), F32)], axis=0)
    k = ax("xhi") * 4 + ax("z")
    small = share(cp, R.mine, R.links, k, peers_chain)
    project(2)
    keep.append(cp.local(R.proj, R.proj_out))
    for copy in small:
        copy.wait_recv()
    come = links_before(R.links, k, w)
    R.carry[...] = jnp.broadcast_to(come, (8, w))
    R.entry[...] = jnp.concatenate(qs, axis=0) * come + jnp.concatenate(cs, axis=0)

    def finish(s, c):
        r = chunk_rows(s)
        st = wide(R.states, r) + wide(R.prod, r) * R.entry[pl.ds(s, 1), :]
        put(R.states, r, st)
        R.rowsum[pl.ds(s, 1), :] = row_sums(st * st)
        return c

    lax.fori_loop(0, 8, finish, 0)
    keep.append(cp.local(R.states, R.states_out))
    small = share(cp, R.rowsum, R.rows8, place()[1], peers_group)
    next(bulk)
    for copy in small:
        copy.wait_recv()
    total = R.rows8[0]
    for j in range(1, 8):
        total = total + R.rows8[j]
    R.tot[...] = lax.rsqrt(total / (8.0 * w) + EPS)

    def gate(s, c):
        r = chunk_rows(s)
        v = R.proj[r, 2 * w : 3 * w]
        n = wide(R.states, r) * as_column(R.tot[pl.ds(s, 1), :], w)
        R.gated[r, :] = (n * R.gain[...] * (v * jax.nn.sigmoid(v))).astype(BF)
        return c

    lax.fori_loop(0, 8, gate, 0)
    keep.append(cp.local(R.gated, R.gated_out))
    load_out.wait()
    for i in range(4):
        r = pl.ds(i * rows // 4, rows // 4)

        def out(j, c, r=r):
            at = rows_of(j, 512)
            R.part[r, at] = dot(R.gated[r, :], R.wo[:, at], NN).astype(BF)
            return c

        lax.fori_loop(0, R.part.shape[1] // 512, out, 0)
        keep.append(cp.local(R.part.at[r], R.part_out.at[r]))
    chain.rest()
    for copy in keep:
        copy.wait()
    own.wait()
    drain(bulk)
    cp.finish()


def feed_body(R, cp):
    y, c = ax("y"), ax("core")
    g = place()[1]
    unit, width = R.wdn.shape
    greet(ys() + rings())
    weights = plane_second(cp, R.gu_column, R.gu_row, R.wgu, by_rows(*R.wgu.shape[3:]))
    next(weights)
    mixer = sum_of(cp, R.part, R.ps, R.near, R.far)
    next(mixer)
    load = [cp.local(R.gf, R.g), cp.local(R.bdn, R.wdn)]
    next(mixer)
    next(mixer)
    next(weights)
    terms = next(mixer)

    def norm(i, carry):
        r = rows_of(i)
        x = R.tok[r, :].astype(F32) + terms(i)
        R.mid[r, :] = x
        s = lax.rsqrt(jnp.mean(x * x, axis=-1, keepdims=True) + EPS)
        R.si[rows_of(g * 8 + i), :] = (x * s * R.gain[...]).astype(BF)
        return carry

    lax.fori_loop(0, 8, norm, 0)
    gather = GroupGather(cp, R.si.at[block_of(g)], R.si)
    second = GroupSum(cp, R.near, R.far)
    for copy in load:
        copy.wait()
    drain(weights)
    order = (0, 1, 3, 2)
    stores = []

    def forward(yy):
        r = rows_of(yy, 256)

        def tile(j, carry):
            at = rows_of(j, 256)
            up = pl.ds(pl.multiple_of(unit + j * 256, 256), 256)
            x = R.si[r, :]
            v = dot(x, R.wgu[:, :, :, :, at].reshape(width, 256), NN)
            u = dot(x, R.wgu[:, :, :, :, up].reshape(width, 256), NN)
            gh = dot(R.g[r, :], R.wdn[at, :], NT)
            sig = jax.nn.sigmoid(v)
            act = v * sig
            R.hid[r, at] = (act * u).astype(BF)
            R.ggu[r, at] = (gh * u * silu_slope(v, sig)).astype(BF)
            R.ggu[r, up] = (gh * act).astype(BF)
            return carry

        lax.fori_loop(0, unit // 256, tile, 0)

    def backward(yy):
        r = rows_of(yy, 256)

        def tile(j, carry):
            at = rows_of(j, 512)
            w = R.wgu[lax.div(j, 2), lax.rem(j, 2)].reshape(512, 2 * unit)
            R.ps[r, at] = dot(R.ggu[r, :], w, NT).astype(BF)
            return carry

        lax.fori_loop(0, width // 512, tile, 0)

    def result(yy, slot):
        r = rows_of(yy, 256)

        def tile(j, carry):
            at = rows_of(j, 512)
            R.pr[slot, :, at] = dot(R.hid[r, :], R.wdn[:, at], NN).astype(BF)
            return carry

        lax.fori_loop(0, width // 512, tile, 0)
        stores.append(cp.local(R.pr.at[slot], R.part_r.at[r]))

    for i, s in enumerate(order):
        yy = lax.rem(y + 4 - s, 4)
        gather.ready(s)
        forward(yy)
        if i < 3:
            gather.forward(order[i + 1])
        if i > 1:
            back = (4 - order[i - 1]) % 4
            second.add(back, R.ps, 128 * (second.chip(back) + c))
        backward(yy)
        second.give((4 - s) % 4, R.ps.at[block_of(2 * yy + 1 - c)])
        if i > 1:
            stores[i - 2].wait()
        result(yy, i % 2)
    second.add(2, R.ps, 128 * (second.chip(2) + c))

    def grad_down(j, carry):
        at = rows_of(j, 512)
        for i in range(2):
            h = unit // 2
            v = dot(R.hid[:, h * i : h * (i + 1)], R.g[:, at], TN)
            R.ddn[i, :, :, :, at] = v.astype(BF).reshape(R.ddn.shape[1:4] + (512,))
        return carry

    lax.fori_loop(0, width // 512, grad_down, 0)
    planes = [plane_sum(cp, R.ddn, by_columns(*R.ddn.shape[3:]), *plane_refs(R, "a"), R.block_ddn)]
    next(planes[0])

    def grad_gate(i, carry):
        at = rows_of(i, 256)
        v = dot(R.si[:, at], R.ggu[:, 0:unit], TN).astype(BF)
        to = (lax.div(i, 4), lax.rem(lax.div(i, 2), 2), pl.ds(2 * lax.rem(i, 2), 2))
        R.dgate[to] = v.reshape(2, 128, unit)
        return carry

    lax.fori_loop(0, width // 256, grad_gate, 0)
    planes.append(plane_sum(cp, R.dgate, by_rows(*R.dgate.shape[3:]), *plane_refs(R, "b"), R.block_dgate))
    next(planes[1])
    terms = second.total(R.ps, 128 * g)
    R.sums[...] = jnp.zeros_like(R.sums)

    def back(i, carry):
        r = rows_of(i)
        x = R.mid[r, :]
        s = lax.rsqrt(jnp.mean(x * x, axis=-1, keepdims=True) + EPS)
        n = x * s
        dy = terms(i)
        R.sums[0:1, :] = R.sums[0:1, :] + jnp.sum(dy * n, axis=0, keepdims=True)
        dy = dy * R.gain[...]
        v = R.cot[r, :].astype(F32) + s * (dy - n * jnp.mean(dy * n, axis=-1, keepdims=True))
        R.mixed[r, :] = v
        R.block[r, :] = v.astype(BF)
        return carry

    lax.fori_loop(0, 8, back, 0)
    own = cp.local(R.block, R.gb.at[block_of(g)])
    branch = GroupGather(cp, R.block, R.gb)
    ups = []
    for copy in stores[2:]:
        copy.wait()

    def grad_up(i):
        at = pl.ds(i * 256, 256)
        v = dot(R.si[:, at], R.ggu[:, unit : 2 * unit], TN).astype(BF)
        if i > 1:
            ups[i - 2].wait()
        R.pu[i % 2] = v
        ups.append(cp.local(R.pu.at[i % 2], R.dup.at[at]))

    for i in range(width // 256):
        grad_up(i)
    branch.relay()
    for copy in ups[-2:]:
        copy.wait()
    next(planes[0])
    branch.forward(1)
    branch.forward(3)
    next(planes[1])
    branch.rest()
    own.wait()
    drain(*planes)
    cp.finish()


def plane_refs(R, key):
    return [getattr(R, "plane_" + key + str(i)) for i in range(6)]


def plane_work(key, halves):
    return {"plane_" + key + str(i): v for i, v in enumerate(plane_sum_scratch(halves))}


def grad_weights(R, start, dst):
    n = dst.shape[4]

    def tile(i, carry):
        at = rows_of(i, 256)
        v = dot(R.x[:, at], R.grads[:, start : start + n], TN).astype(BF)
        to = (lax.div(i, 4), lax.rem(lax.div(i, 2), 2), pl.ds(2 * lax.rem(i, 2), 2))
        dst[to] = v.reshape(2, 128, n)
        return carry

    lax.fori_loop(0, R.x.shape[1] // 256, tile, 0)


def back_body(R, cp):
    c = ax("core")
    p, g = place()
    tiles, rows = R.states.shape[:2]
    w = 128 * tiles
    steps = rows // 8
    width = R.tok.shape[1]
    shuffle = Shuffle(False)
    peers_chain = [in_chain(*st) for st in CHAIN]
    peers_group = [in_group(*st) for st in GROUP]
    peers_plane = [in_plane(*st) for st in PLANE]
    load = [cp.local(R.gb, R.gbv), cp.local(R.bo, R.wo)]
    load_scan = [
        cp.local(R.states_in, R.states),
        cp.local(R.proj_in, R.proj),
        cp.local(R.forget_in, R.forget),
        cp.local(R.gated_in, R.gated),
    ]
    load_x = cp.local(R.fi, R.x)
    load_last = [cp.local(R.b3, R.w3), cp.local(R.mid_in, R.mid), cp.local(R.mixed_in, R.mixed)]
    greet(peers_plane + peers_group, shuffle.greeting)
    res = sum_of(cp, R.part_r, R.pr, R.pr_near, R.pr_far)
    next(res)
    up = plane_sum(cp, R.dup, by_rows(*R.dup.shape[3:]), *plane_refs(R, "a"), R.block_dup)
    next(up)
    low = R.lb[...]
    R.sums[...] = jnp.zeros_like(R.sums)
    gate_home = to_group(cp, lambda k: R.block_dgate.at[rows_of(k), :], lambda k: R.rgate.at[k])
    for copy in load:
        copy.wait()
    for i in range(2):
        r = pl.ds(i * rows // 2, rows // 2)
        R.gg[r, :] = dot(R.gbv[r, :], R.wo[...], NT)
    next(res)
    for copy in load_scan:
        copy.wait()

    def through(s, carry):
        r = chunk_rows(s)
        v = R.proj[r, 2 * w : 3 * w]
        sig = jax.nn.sigmoid(v)
        n = wide(R.states, r) * as_column(R.tot[pl.ds(s, 1), :], w)
        dy = R.gg[r, :]
        R.sums[0:1, :] = R.sums[0:1, :] + jnp.sum(dy * n * (v * sig), axis=0, keepdims=True)
        R.grads[r, 2 * w : 3 * w] = (dy * n * R.gain[...] * silu_slope(v, sig)).astype(BF)
        dy = dy * R.gain[...] * (v * sig)
        put(R.gs, r, dy)
        R.rowsum[pl.ds(s, 1), :] = row_sums(dy * n)
        return carry

    lax.fori_loop(0, 8, through, 0)
    small = share(cp, R.rowsum, R.rows8, g, peers_group)
    next(res)
    def grad_out(j, carry):
        at = rows_of(j, 512)
        v = dot(R.gated[...], R.gbv[:, at], TN).astype(BF)
        R.do[:, :, :, :, at] = v.reshape(R.do.shape[:4] + (512,))
        return carry

    lax.fori_loop(0, width // 512, grad_out, 0)
    outs = plane_sum(cp, R.do, by_columns(*R.do.shape[3:]), *plane_refs(R, "b"), R.oo)
    next(outs)
    load_x.wait()
    grad_weights(R, 2 * w, R.d1)
    one = plane_sum(cp, R.d1, by_rows(*R.d1.shape[3:]), *plane_refs(R, "d"), R.o1)
    next(one)
    for copy in small:
        copy.wait_recv()
    total = R.rows8[0]
    for j in range(1, 8):
        total = total + R.rows8[j]
    cp.sent(small)
    R.rowsum[...] = total / (8.0 * w)

    def norm(s, carry):
        r = chunk_rows(s)
        t = as_column(R.tot[pl.ds(s, 1), :], w)
        m = as_column(R.rowsum[pl.ds(s, 1), :], w)
        put(R.gs, r, t * (wide(R.gs, r) - wide(R.states, r) * t * m))
        return carry

    lax.fori_loop(0, 8, norm, 0)

    def step(i, carry):
        at = pl.ds(steps - 1 - i, 8, stride=steps)
        new = []
        for j, (h, a) in enumerate(carry):
            f = R.forget[j, at, :]
            v = R.gs[j, at, :] + h
            R.gs[j, at, :] = v
            R.prod[j, at, :] = a
            new.append((f * v, a * f))
        return tuple(new)

    start = ((jnp.zeros((8, 128), F32), jnp.ones((8, 128), F32)),) * tiles
    ends = lax.fori_loop(0, steps, step, start, unroll=8)
    h = jnp.concatenate([e[0] for e in ends], axis=1)
    a = jnp.concatenate([e[1] for e in ends], axis=1)
    e = jnp.zeros((1, w), F32)
    q = jnp.ones((1, w), F32)
    cs, qs = [None] * 8, [None] * 8
    for s in range(7, -1, -1):
        cs[s] = e
        qs[s] = q
        e = a[s : s + 1] * e + h[s : s + 1]
        q = a[s : s + 1] * q
    R.mine[...] = jnp.broadcast_to(e, (8, w))
    k = ax("xhi") * 4 + ax("z")
    small = share(cp, R.mine, R.chain, k, peers_chain)
    next(up)
    next(outs)
    for copy in small:
        copy.wait_recv()
    come = jnp.zeros((1, w), F32)
    for j in range(7, -1, -1):
        new = R.links[j, 0:1, :] * come + R.chain[j, 0:1, :]
        come = jnp.where(j > k, new, come)
    R.entry[...] = jnp.concatenate(qs, axis=0) * come + jnp.concatenate(cs, axis=0)

    def last(s, carry):
        r = chunk_rows(s)
        v = wide(R.gs, r) + wide(R.prod, r) * R.entry[pl.ds(s, 1), :]
        st = wide(R.states, r)
        above = pl.ds(jnp.maximum(s * 128 - 1, 0), 1)
        before = jnp.where(s == 0, R.carry[0:1, :], wide(R.states, above))
        top = lax.broadcasted_iota(jnp.int32, (128, w), 0) == 0
        prev = jnp.where(top, before, pltpu.roll(st, 1, 0))
        x = R.proj[r, 0:w]
        sx = jax.nn.sigmoid(x)
        f = wide(R.forget, r)
        sf = jax.nn.sigmoid(R.proj[r, w : 2 * w])
        gf = v * (prev - x * sx)
        R.grads[r, 0:w] = (v * (1.0 - f) * silu_slope(x, sx)).astype(BF)
        R.grads[r, w : 2 * w] = (gf * (1.0 - low) * sf * (1.0 - sf)).astype(BF)
        R.sums[1:2, :] = R.sums[1:2, :] + jnp.sum(gf * (1.0 - sf), axis=0, keepdims=True)
        return carry

    lax.fori_loop(0, 8, last, 0)
    for copy in load_last:
        copy.wait()
    grad_weights(R, 0, R.d2)
    two = plane_sum(cp, R.d2, by_rows(*R.d2.shape[3:]), *plane_refs(R, "c"), R.o2)
    next(two)
    next(one)
    R.va[...] = jnp.zeros_like(R.va)
    R.va[1:2, :] = R.ffn_sums[0:1, :]
    first = RelaySum(cp, R.near, R.far)
    order = (2, 1, 3, 0)
    for i, s in enumerate(order):
        chip = first.chip(s)
        r = pl.ds(pl.multiple_of(chip * 128, 256), 256)

        def tile(j, carry, r=r):
            at = rows_of(j, 512)
            v = dot(R.grads[r, :], R.w3[at, :], NT)
            R.va[0:1, at] = R.va[0:1, at] + jnp.sum(
                v * (R.x[r, at].astype(F32) / R.attn_gain[:, at]), axis=0, keepdims=True
            )
            R.fp[r, at] = v.astype(BF)
            return carry

        lax.fori_loop(0, width // 512, tile, 0)
        first.give(s, R.fp.at[block_of(chip + 1 - c)])
        if i > 0:
            back = order[i - 1]
            first.add(back, R.fp, 128 * (first.chip(back) + c))
    first.relay(R.fp, 128 * (first.chip(1) + c), 128 * (first.chip(3) + c))

    gains = []
    for st in GROUP:
        dev = in_group(*st)
        k = dev["y"] * 2 + dev["core"]
        gains.append(cp.send(R.va.at[:, rows_of(k, w)], R.ga.at[g], dev))
    R.ga[pl.ds(g, 1)] = R.va[:, rows_of(g, w)][None]

    drain(up, outs, one)
    arrive = [
        gate_home,
        to_group(cp, lambda k: R.o1.at[rows_of(k), :], lambda k: R.r1.at[k]),
        to_group(cp, lambda k: R.block_dup.at[rows_of(k), :], lambda k: R.rup.at[k]),
    ]
    moved = shuffle.start(cp, R.oo, R.ro)
    for copy in gains:
        copy.wait_recv()
    acc = R.ga[0]
    for j in range(1, 8):
        acc = acc + R.ga[j]
    R.ta[...] = acc
    R.ta[2:4, :] = R.sums[0:2, :]
    for copy in share(cp, R.ta, R.gather, p, peers_plane):
        copy.wait_recv()
    acc = R.gather[0]
    for j in range(1, 16):
        acc = acc + R.gather[j]
    R.tb[...] = acc
    terms = next(res)

    def finish_result(i, carry):
        r = rows_of(i)
        R.result[r, :] = (R.mid[r, :] + terms(i)).astype(BF)
        return carry

    lax.fori_loop(0, 8, finish_result, 0)
    small = share(cp, R.tb, R.totals, g, peers_group)
    next(two)
    terms_first = first.total(R.fp, 128 * g)

    def back(i, carry):
        r = rows_of(i)
        x = R.tok[r, :].astype(F32)
        s = lax.rsqrt(jnp.mean(x * x, axis=-1, keepdims=True) + EPS)
        n = x * s
        dy = terms_first(i)
        dy = dy * R.attn_gain[...]
        R.gtok[r, :] = R.mixed[r, :] + s * (dy - n * jnp.mean(dy * n, axis=-1, keepdims=True))
        return carry

    lax.fori_loop(0, 8, back, 0)
    drain(two)
    arrive.append(to_group(cp, lambda k: R.o2.at[rows_of(k), :], lambda k: R.r2.at[k]))
    for copy in small:
        copy.wait_recv()
    for pair in arrive:
        settle(*pair)
    shuffle.wait(moved)
    cp.finish()


def bound_value(bound_table, layer_idx):
    probabilities = jax.nn.softmax(bound_table, axis=0)
    levels = jnp.arange(bound_table.shape[0], dtype=jnp.int32)[:, None]
    keep = jnp.where((levels >= 1) & (levels <= layer_idx[0]), 1.0, 0.0).astype(F32)
    return jnp.sum(probabilities * keep, axis=0)


def on_device(
    tokens, cotangent, attn_gain, w_input, w_forget, w_outgate, w_out, norm_gain, mlp_gain, w_gate, w_up, w_down, bound_table, layer_idx
):
    n, width = tokens.shape
    rows = w_input.shape[0]
    hidden_width = w_gate.shape[1]
    down = w_down.shape[0]
    padded = -(-down // 16) * 16
    unit = 16 * padded
    w = width // 8

    def spread(m):
        m = m.reshape(rows, 16, 8, down)
        m = jnp.pad(m, ((0, 0), (0, 0), (0, 0), (0, padded - down)))
        return m.transpose(2, 0, 1, 3).reshape(8, rows, unit)

    gu = jnp.concatenate([spread(w_gate), spread(w_up)], axis=2)
    dn = jnp.pad(w_down, ((0, padded - down), (0, 0)))
    gains = attn_gain[None, :]
    full = (8 * n, width)
    block = (n, width)
    gate_blocks = (2, 2, 4, 8 * rows, unit)
    A = call(
        gather_body,
        "gather",
        0,
        dict(
            tok=(tokens, VMEM),
            gain=(gains, VMEM),
            w_in=(w_input, VMEM),
            w_f=(w_forget, VMEM),
            w_og=(w_outgate, VMEM),
            w_o=(w_out, VMEM),
            gu=(gu, VMEM),
        ),
        dict(
            b3=((2, 2, 4, 8 * rows, 3 * w), BF, ANY),
            bo=((2, 2, 4, rows, width), BF, ANY),
            fi=(full, BF, ANY),
            gu_column=((4, 4 * rows, 2 * unit), BF, ANY),
            gu_row=((2, 2, 4 * rows, 2 * unit), BF, ANY),
        ),
        scratch(first=(block, BF), block_gu=((8 * rows, 2 * unit), BF)),
        96,
        10,
    )
    big3 = A.b3.reshape(width, 3 * w)
    big_out = A.bo.reshape(w, width)
    group = ax("y") * 2 + ax("core")
    lower = bound_value(lax.dynamic_slice_in_dim(bound_table, group * w, w, 1), layer_idx)[None, :]
    mixer_gain = lax.dynamic_slice_in_dim(norm_gain, group * w, w, 0)[None, :]
    column = (w // 128, 8 * n, 128)
    B = call(
        scan_body,
        "scan",
        1,
        dict(
            lb=(lower, VMEM),
            gain=(mixer_gain, VMEM),
            b3=(big3, ANY),
            bo=(big_out, ANY),
            fi=(A.fi, ANY),
            dn=(dn, VMEM),
            cot=(cotangent, VMEM),
        ),
        dict(
            gated_out=((8 * n, w), BF, ANY),
            states_out=(column, F32, ANY),
            forget_out=(column, F32, ANY),
            proj_out=((8 * n, 3 * w), F32, ANY),
            tot=((8, n), F32, VMEM),
            links=((8, 8, w), F32, VMEM),
            carry=((8, w), F32, VMEM),
            part_out=(full, BF, ANY),
            gf=(full, BF, ANY),
            bdn=((2, 2, 4, padded, width), BF, ANY),
        ),
        scratch(
            gated=((8 * n, w), BF),
            states=(column, F32),
            forget=(column, F32),
            proj=((8 * n, 3 * w), F32),
            part=(full, BF),
            w3=((width, 3 * w), BF),
            x=(full, BF),
            wo=((w, width), BF),
            prod=(column, F32),
            entry=((8, w), F32),
            mine=((8, w), F32),
            rowsum=((8, n), F32),
            rows8=((8, 8, n), F32),
        ),
        48,
        16,
    )
    gains_two = mlp_gain[None, :]
    C = call(
        feed_body,
        "feed",
        2,
        dict(
            tok=(tokens, VMEM),
            cot=(cotangent, VMEM),
            gain=(gains_two, VMEM),
            part=(B.part_out, ANY),
            gu_column=(A.gu_column, ANY),
            gu_row=(A.gu_row, ANY),
            bdn=(B.bdn.reshape(unit, width), ANY),
            gf=(B.gf, ANY),
        ),
        dict(
            mid=(block, F32, VMEM),
            mixed=(block, F32, VMEM),
            gb=(full, BF, ANY),
            part_r=(full, BF, ANY),
            sums=((8, width), F32, VMEM),
            block_ddn=((padded, width), BF, VMEM),
            block_dgate=((8 * rows, unit), BF, VMEM),
            dup=((width, unit), BF, ANY),
        ),
        scratch(
            wgu=((2, 2, 4, 8 * rows, 2 * unit), BF),
            wdn=((unit, width), BF),
            g=(full, BF),
            si=(full, BF),
            hid=((8 * n, unit), BF),
            ggu=((8 * n, 2 * unit), BF),
            ps=(full, BF),
            pr=((2, 2 * n, width), BF),
            near=((4,) + block, BF),
            far=((3,) + block, BF),
            block=(block, BF),
            ddn=((2, 2, 4, padded, width), BF),
            dgate=(gate_blocks, BF),
            pu=((2, 256, unit), BF),
        )
        | plane_work("a", by_columns(padded, width))
        | plane_work("b", by_rows(8 * rows, unit)),
        72,
        30,
    )
    D = call(
        back_body,
        "back",
        3,
        dict(
            tok=(tokens, VMEM),
            mid_in=(C.mid, ANY),
            mixed_in=(C.mixed, ANY),
            attn_gain=(gains, VMEM),
            lb=(lower, VMEM),
            gain=(mixer_gain, VMEM),
            ffn_sums=(C.sums, VMEM),
            states_in=(B.states_out, ANY),
            forget_in=(B.forget_out, ANY),
            proj_in=(B.proj_out, ANY),
            gated_in=(B.gated_out, ANY),
            tot=(B.tot, VMEM),
            links=(B.links, VMEM),
            carry=(B.carry, VMEM),
            b3=(big3, ANY),
            bo=(big_out, ANY),
            fi=(A.fi, ANY),
            gb=(C.gb, ANY),
            part_r=(C.part_r, ANY),
            dup=(C.dup.reshape(gate_blocks), ANY),
            block_dgate=(C.block_dgate, ANY),
        ),
        dict(
            result=(block, BF, VMEM),
            gtok=(block, F32, VMEM),
            rgate=((8, rows, unit), BF, VMEM),
            rup=((8, rows, unit), BF, VMEM),
            r1=((8, rows, w), BF, VMEM),
            r2=((8, rows, 2 * w), BF, VMEM),
            ro=((rows, width), BF, VMEM),
            totals=((8, 8, w), F32, VMEM),
        ),
        scratch(
            states=(column, F32),
            forget=(column, F32),
            proj=((8 * n, 3 * w), F32),
            gated=((8 * n, w), BF),
            mid=(block, F32),
            mixed=(block, F32),
            gbv=(full, BF),
            wo=((w, width), BF),
            w3=((width, 3 * w), BF),
            x=(full, BF),
            gg=((8 * n, w), F32),
            gs=(column, F32),
            prod=(column, F32),
            grads=((8 * n, 3 * w), BF),
            sums=((8, w), F32),
            entry=((8, w), F32),
            mine=((8, w), F32),
            rowsum=((8, n), F32),
            rows8=((8, 8, n), F32),
            chain=((8, 8, w), F32),
            pr=((4 * n, width), BF),
            pr_near=((4,) + block, BF),
            pr_far=((3,) + block, BF),
            fp=(full, BF),
            near=((4,) + block, BF),
            far=((3,) + block, BF),
            do=((2, 2, 4, rows, width), BF),
            d1=((2, 2, 4, 8 * rows, w), BF),
            d2=((2, 2, 4, 8 * rows, 2 * w), BF),
            block_dup=((8 * rows, unit), BF),
            o1=((8 * rows, w), BF),
            o2=((8 * rows, 2 * w), BF),
            oo=((rows, width), BF),
            va=((8, width), F32),
            ga=((8, 8, w), F32),
            ta=((8, w), F32),
            gather=((16, 8, w), F32),
            tb=((8, w), F32),
        )
        | plane_work("a", by_rows(8 * rows, unit))
        | plane_work("b", by_columns(rows, width))
        | plane_work("c", by_rows(8 * rows, 2 * w))
        | plane_work("d", by_rows(8 * rows, w)),
        160,
        30,
    )

    def join(m):
        m = m.transpose(1, 0, 2)
        return m.reshape(rows, 8 * m.shape[2]).astype(F32)

    def unspread(m):
        m = m.reshape(8, rows, 16, padded)[:, :, :, :down].transpose(1, 2, 0, 3)
        return m.reshape(rows, hidden_width).astype(F32)

    sums = D.totals.transpose(1, 0, 2).reshape(8, width)
    pullback = jax.vjp(lambda table: bound_value(table, layer_idx), bound_table)[1]
    return (
        D.result,
        D.gtok,
        sums[0],
        join(D.r2[:, :, :w]),
        join(D.r2[:, :, w:]),
        join(D.r1),
        D.ro.astype(F32),
        sums[2],
        sums[1],
        unspread(D.rgate),
        unspread(D.rup),
        C.block_ddn[:down].astype(F32),
        pullback(sums[3])[0],
    )


def solution(mesh):
    split = Mesh(mesh.devices.reshape(2, 2, 4, 4, 2), AXES)
    cut = P(AXES, None)
    return jax.shard_map(
        on_device,
        mesh=split,
        in_specs=(cut, cut, P(), cut, cut, cut, cut, P(), P(), cut, cut, cut, P(), P()),
        out_specs=(cut, cut, P(), cut, cut, cut, cut, P(), P(), cut, cut, cut, P()),
        check_vma=False,
    )
```

```python
from types import SimpleNamespace

import jax
import jax.numpy as jnp
from jax import lax
from jax.experimental import pallas as pl
from jax.experimental.pallas import tpu as pltpu
from jax.sharding import Mesh, PartitionSpec as P

EPS = 1e-06
BF = jnp.bfloat16
F32 = jnp.float32
AXES = ("xlo", "xhi", "z", "y", "core")
MESH = pl.DeviceIdType.MESH
ANY = pl.BlockSpec(memory_space=pl.ANY)
VMEM = pl.BlockSpec(memory_space=pltpu.VMEM)
STEPS = (1, 3, 2)
GROUP = [(a, b) for a in range(4) for b in range(2) if a or b]
CHAIN = [(a, b) for a in range(2) for b in range(4) if a or b]
PLANE = [(a, b) for a in range(4) for b in range(4) if a or b]
HIGH = lax.Precision.HIGHEST


def ax(name):
    return lax.axis_index(name)


def ring(axis, s):
    if axis == "x":
        x = lax.rem(ax("xhi") * 2 + ax("xlo") + s, 4)
        return {"xhi": lax.div(x, 2), "xlo": lax.rem(x, 2)}
    return {axis: lax.rem(ax(axis) + s, 4)}


def sibling():
    return {"core": 1 - ax("core")}


def in_group(s, t):
    return {"y": lax.rem(ax("y") + s, 4), "core": lax.rem(ax("core") + t, 2)}


def in_chain(s, t):
    return {"xhi": lax.rem(ax("xhi") + s, 2), "z": lax.rem(ax("z") + t, 4)}


def in_plane(s, t):
    return {**ring("x", s), **ring("z", t)}


def place():
    return ax("xlo") * 8 + ax("xhi") * 4 + ax("z"), ax("y") * 2 + ax("core")


def device(p, g):
    return {
        "xlo": lax.div(p, 8),
        "xhi": lax.rem(lax.div(p, 4), 2),
        "z": lax.rem(p, 4),
        "y": lax.div(g, 2),
        "core": lax.rem(g, 2),
    }


class Copies:
    def __init__(self, send, recv, near):
        self.sems = (send, recv, near)
        self.count = 0
        self.locals = 0
        self.open = []

    def remote(self, src, dst, dev):
        i = self.count
        self.count += 1
        assert i < self.sems[0].shape[0]
        return pltpu.make_async_remote_copy(
            src_ref=src,
            dst_ref=dst,
            send_sem=self.sems[0].at[i],
            recv_sem=self.sems[1].at[i],
            device_id=dev,
            device_id_type=MESH,
        )

    def send(self, src, dst, dev):
        copy = self.remote(src, dst, dev)
        copy.start()
        self.open.append(copy)
        return copy

    def near(self, src, dst):
        i = self.locals
        self.locals += 1
        assert i < self.sems[2].shape[0]
        return pltpu.make_async_copy(src, dst, self.sems[2].at[i])

    def local(self, src, dst):
        copy = self.near(src, dst)
        copy.start()
        return copy

    def sent(self, copies):
        for copy in copies:
            copy.wait_send()
        gone = {id(copy) for copy in copies}
        self.open = [copy for copy in self.open if id(copy) not in gone]

    def finish(self):
        for copy in self.open:
            copy.wait_send()


def hail(peers, shuffle=None):
    bar = pltpu.get_barrier_semaphore()
    for dev in peers:
        pl.semaphore_signal(bar, inc=1, device_id=dev, device_id_type=MESH)
    count = len(peers)
    if shuffle is not None:
        source, from_me, to_me = shuffle

        @pl.when(jnp.logical_not(from_me))
        def _():
            pl.semaphore_signal(bar, inc=1, device_id=source, device_id_type=MESH)

        count = count + jnp.where(to_me, 0, 1)
    return lambda: pl.semaphore_wait(bar, count)


def greet(peers):
    hail(peers)()


def to_group(cp, source, dst):
    g = place()[1]
    there = dst(g)
    copies = []
    for st in GROUP:
        q = in_group(*st)
        copies.append(cp.send(source(q["y"] * 2 + q["core"]), there, q))
    return copies, cp.local(source(g), there)


def settle(copies, home):
    for copy in copies:
        copy.wait_recv()
    home.wait()


class Shuffle:
    def __init__(self, outward):
        p, g = place()
        self.d = p * 8 + g
        row = 16 * g + p
        there = (lax.rem(self.d, 16), lax.div(self.d, 16))
        here = (lax.div(row, 8), lax.rem(row, 8))
        to, come = (there, here) if outward else (here, there)
        self.to = to
        self.target, self.source = device(*to), device(*come)
        self.to_me = to[0] * 8 + to[1] == self.d
        self.from_me = come[0] * 8 + come[1] == self.d
        self.greeting = (self.source, self.from_me, self.to_me)

    def start(self, cp, src, dst):
        copy = cp.remote(src, dst, self.target)
        home = cp.near(src, dst)

        @pl.when(self.to_me)
        def _():
            home.start()

        @pl.when(jnp.logical_not(self.to_me))
        def _():
            copy.start()

        return copy, home

    def wait(self, pair):
        @pl.when(self.to_me)
        def _():
            pair[1].wait()

        @pl.when(jnp.logical_not(self.to_me))
        def _():
            pair[0].wait()


def rings():
    return [ring("x", s) for s in STEPS] + [ring("z", s) for s in STEPS]


def ys():
    return [ring("y", s) for s in STEPS] + [sibling()]


def run(chains, order):
    for i in order:
        next(chains[i], None)
    for chain in chains:
        for _ in chain:
            pass


def rows_of(i, n=16):
    return pl.ds(pl.multiple_of(i * n, n), n)


def block_of(k):
    return rows_of(k, 128)


class GroupGather:
    def __init__(self, cp, src, full):
        self.cp, self.full = cp, full
        k = place()[1]
        self.half = {}
        for first in (0, 1):
            for s in (1, 3):
                h = first if s == 1 else 1 - first
                self.half[s, h] = cp.send(
                    src.at[pl.ds(64 * h, 64)], full.at[self.rows(k, h)], ring("y", s)
                )
        self.near = {0: cp.send(src, full.at[block_of(k)], sibling())}
        self.done = set()

    def rows(self, k, h):
        return pl.ds(pl.multiple_of(k * 128 + 64 * h, 64), 64)

    def chip(self, s):
        return 2 * lax.rem(ax("y") + 4 - s, 4) + ax("core")

    def arrived(self, s, h):
        if (s, h) not in self.done:
            self.done.add((s, h))
            self.half[s, h].wait_recv()

    def relay(self):
        for s, h in ((1, 0), (3, 1)):
            self.arrived(s, h)
            at = self.full.at[self.rows(self.chip(s), h)]
            self.half[2, h] = self.cp.send(at, at, ring("y", s))

    def forward(self, s):
        if (2, 0) not in self.half:
            self.relay()
        self.arrived(s, 0)
        self.arrived(s, 1)
        at = self.full.at[block_of(self.chip(s))]
        self.near[s] = self.cp.send(at, at, sibling())

    def ready(self, s):
        self.near[s].wait_recv()

    def rest(self):
        for s in STEPS:
            if s not in self.near:
                self.forward(s)
        for s in (0, 1, 3, 2):
            self.ready(s)


class GroupSum:
    def __init__(self, cp, near, far):
        self.cp, self.near, self.far = cp, near, far
        self.sent, self.moved = {}, {}

    def chip(self, s):
        return 2 * lax.rem(ax("y") + s, 4)

    def give(self, s, src):
        self.sent[s] = self.cp.send(src, self.near.at[s], sibling())

    def add(self, s, mine, at):
        near = self.near
        self.sent[s].wait_recv()

        def step(i, carry):
            r = rows_of(i)
            to = pl.ds(pl.multiple_of(at + i * 16, 16), 16)
            mine[to, :] = (mine[to, :].astype(F32) + near[s, r, :].astype(F32)).astype(BF)
            return carry

        lax.fori_loop(0, 8, step, 0)
        here = mine.at[pl.ds(pl.multiple_of(at, 128), 128)]
        self.moved[s] = self.cp.send(here, self.far.at[s - 1], ring("y", s))

    def total(self, mine, at):
        self.sent[0].wait_recv()
        for s in STEPS:
            self.moved[s].wait_recv()
        self.cp.sent(list(self.moved.values()))
        near, far = self.near, self.far

        def rows(i):
            r = rows_of(i)
            own = mine[pl.ds(pl.multiple_of(at + i * 16, 16), 16), :]
            acc = own.astype(F32) + near[0, r, :].astype(F32)
            for s in range(3):
                acc = acc + far[s, r, :].astype(F32)
            return acc

        return rows


class RelaySum(GroupSum):
    def piece(self, mine, at, h):
        return mine.at[pl.ds(pl.multiple_of(at + 64 * h, 64), 64)]

    def plus(self, mine, at, term, n):
        def step(i, carry):
            to = pl.ds(pl.multiple_of(at + i * 16, 16), 16)
            mine[to, :] = (mine[to, :].astype(F32) + term(rows_of(i)).astype(F32)).astype(BF)
            return carry

        lax.fori_loop(0, n // 16, step, 0)

    def to(self, s, slot, h, mine, at):
        return self.cp.send(
            self.piece(mine, at, h), self.far.at[slot, pl.ds(64 * h, 64)], ring("y", s)
        )

    def add(self, s, mine, at):
        near = self.near
        self.sent[s].wait_recv()
        self.plus(mine, at, lambda r: near[s, r, :], 128)
        if s == 2:
            self.hop = [self.to(1, 2, 0, mine, at), self.to(3, 2, 1, mine, at)]
        elif s == 1:
            self.moved[1, 1] = self.to(1, 0, 1, mine, at)
        else:
            self.moved[3, 0] = self.to(3, 1, 0, mine, at)

    def relay(self, mine, at_next, at_last):
        far = self.far
        self.hop[0].wait_recv()
        self.plus(mine, at_next, lambda r: far[2, r, :], 64)
        self.moved[1, 0] = self.to(1, 0, 0, mine, at_next)
        self.hop[1].wait_recv()
        up = lambda r: far[2, pl.ds(pl.multiple_of(64 + r.start, 16), 16), :]
        self.plus(mine, at_last + 64, up, 64)
        self.moved[3, 1] = self.to(3, 1, 1, mine, at_last)

    def total(self, mine, at):
        self.sent[0].wait_recv()
        for key in ((1, 1), (3, 0), (1, 0), (3, 1)):
            self.moved[key].wait_recv()
        self.cp.sent(self.hop + list(self.moved.values()))
        near, far = self.near, self.far

        def rows(i):
            r = rows_of(i)
            own = mine[pl.ds(pl.multiple_of(at + i * 16, 16), 16), :]
            acc = own.astype(F32) + near[0, r, :].astype(F32)
            return acc + (far[0, r, :].astype(F32) + far[1, r, :].astype(F32))

        return rows


def sum_of(cp, part, mine, near, far):
    total = RelaySum(cp, near, far)
    c = ax("core")
    own = {}
    for s in (2, 1, 3, 0):
        total.give(s, part.at[block_of(total.chip(s) + 1 - c)])
        own[s] = cp.local(part.at[block_of(total.chip(s) + c)], mine.at[pl.ds(128 * s, 128)])
    yield
    for s in (2, 1, 3):
        own[s].wait()
        total.add(s, mine, 128 * s)
    own[0].wait()
    yield
    total.relay(mine, 128, 384)
    yield
    yield total.total(mine, 0)


def plane_gather(cp, buf, halves, block=None):
    me = (ax("xlo"), ax("xhi"), ax("z"))
    home = None if block is None else cp.local(block, buf.at[me])

    def view(h, *at):
        return buf.at[at + halves[h]]

    mine = [view(h, *me) if block is None else block.at[halves[h]] for h in range(2)]
    first = []
    for s in STEPS:
        first.append(cp.send(mine[0], view(0, *me), ring("z", s)))
        first.append(cp.send(mine[1], view(1, *me), ring("x", s)))
    yield
    if home is not None:
        home.wait()
    for copy in first:
        copy.wait_recv()
    column = view(0, me[0], me[1], pl.ds(0, 4))
    row = view(1, pl.ds(0, 2), pl.ds(0, 2), me[2])
    wide = {}
    for s in (1, 3):
        wide["x", s] = cp.send(column, column, ring("x", s))
        wide["z", s] = cp.send(row, row, ring("z", s))
    yield
    last = []
    for s in (1, 3):
        back = ring("x", 4 - s)
        wide["x", s].wait_recv()
        v = view(0, back["xlo"], back["xhi"], pl.ds(0 if s == 1 else 2, 2))
        last.append(cp.send(v, v, ring("x", s)))
        back = ring("z", 4 - s)
        wide["z", s].wait_recv()
        v = view(1, 0 if s == 1 else 1, pl.ds(0, 2), back["z"])
        last.append(cp.send(v, v, ring("z", s)))
    yield
    for copy in last:
        copy.wait_recv()


def plane_first(cp, block, column, row, halves):
    me = (ax("xlo"), ax("xhi"), ax("z"))
    top, bottom = [block.at[h] for h in halves]
    home = [cp.local(top, column.at[me[2]]), cp.local(bottom, row.at[me[0], me[1]])]
    first = []
    for s in STEPS:
        first.append(cp.send(top, column.at[me[2]], ring("z", s)))
        first.append(cp.send(bottom, row.at[me[0], me[1]], ring("x", s)))
    yield
    for copy in first:
        copy.wait_recv()
    for copy in home:
        copy.wait()


def plane_second(cp, column, row, buf, halves):
    me = (ax("xlo"), ax("xhi"), ax("z"))

    def view(h, *at):
        return buf.at[at + halves[h]]

    here = view(0, me[0], me[1], pl.ds(0, 4))
    across = view(1, pl.ds(0, 2), pl.ds(0, 2), me[2])
    home = [cp.local(column, here), cp.local(row, across)]
    wide = {}
    for s in (1, 3):
        wide["x", s] = cp.send(column, here, ring("x", s))
        wide["z", s] = cp.send(row, across, ring("z", s))
    yield
    last = []
    for s in (1, 3):
        back = ring("x", 4 - s)
        wide["x", s].wait_recv()
        v = view(0, back["xlo"], back["xhi"], pl.ds(0 if s == 1 else 2, 2))
        last.append(cp.send(v, v, ring("x", s)))
        back = ring("z", 4 - s)
        wide["z", s].wait_recv()
        v = view(1, 0 if s == 1 else 1, pl.ds(0, 2), back["z"])
        last.append(cp.send(v, v, ring("z", s)))
    yield
    for copy in last:
        copy.wait_recv()
    for copy in home:
        copy.wait()


def half_shapes(halves):
    return [tuple(d.size for d in h) for h in halves]


def plane_sum_scratch(halves):
    a, b = half_shapes(halves)
    return [
        pltpu.VMEM((4,) + a, BF),
        pltpu.VMEM((3, 4) + a, BF),
        pltpu.VMEM((3,) + a, BF),
        pltpu.VMEM((2, 2) + b, BF),
        pltpu.VMEM((3, 2, 2) + b, BF),
        pltpu.VMEM((3,) + b, BF),
    ]


def plane_sum(cp, part, halves, own_a, far_a, last_a, own_b, far_b, last_b, out):
    me = (ax("xlo"), ax("xhi"), ax("z"))
    shape_a, shape_b = half_shapes(halves)

    def view(h, *at):
        return part.at[at + halves[h]]

    near_a = cp.local(view(0, me[0], me[1], pl.ds(0, 4)), own_a)
    near_b = cp.local(view(1, pl.ds(0, 2), pl.ds(0, 2), me[2]), own_b)
    first_a, first_b = [], []
    for j, s in enumerate(STEPS):
        d = ring("x", s)
        first_a.append(cp.send(view(0, d["xlo"], d["xhi"], pl.ds(0, 4)), far_a.at[j], d))
        d = ring("z", s)
        first_b.append(cp.send(view(1, pl.ds(0, 2), pl.ds(0, 2), d["z"]), far_b.at[j], d))
    yield
    near_a.wait()
    for copy in first_a:
        copy.wait_recv()
    for k in range(4):

        def add(i, carry, k=k):
            r = rows_of(i)
            acc = own_a[k, r, :].astype(F32)
            for j in range(3):
                acc = acc + far_a[j, k, r, :].astype(F32)
            own_a[k, r, :] = acc.astype(BF)
            return carry

        lax.fori_loop(0, shape_a[0] // 16, add, 0)
    second = []
    for j, s in enumerate(STEPS):
        d = ring("z", s)
        second.append(cp.send(own_a.at[d["z"]], last_a.at[j], d))
    near_b.wait()
    for copy in first_b:
        copy.wait_recv()
    for k in range(4):

        def add(i, carry, k=k):
            r = rows_of(i)
            acc = own_b[k // 2, k % 2, r, :].astype(F32)
            for j in range(3):
                acc = acc + far_b[j, k // 2, k % 2, r, :].astype(F32)
            own_b[k // 2, k % 2, r, :] = acc.astype(BF)
            return carry

        lax.fori_loop(0, shape_b[0] // 16, add, 0)
    for j, s in enumerate(STEPS):
        d = ring("x", s)
        second.append(cp.send(own_b.at[d["xlo"], d["xhi"]], last_b.at[j], d))
    yield
    for copy in second:
        copy.wait_recv()

    def end_a(i, carry):
        r = rows_of(i)
        acc = own_a[me[2], r, :].astype(F32)
        for j in range(3):
            acc = acc + last_a[j, r, :].astype(F32)
        at = rows_of(i) if halves[0][0].start == 0 else pl.ds(halves[0][0].start + i * 16, 16)
        out[at, halves[0][1]] = acc.astype(BF)
        return carry

    lax.fori_loop(0, shape_a[0] // 16, end_a, 0)

    def end_b(i, carry):
        r = rows_of(i)
        acc = own_b[me[0], me[1], r, :].astype(F32)
        for j in range(3):
            acc = acc + last_b[j, r, :].astype(F32)
        at = pl.ds(pl.multiple_of(halves[1][0].start + i * 16, 16), 16)
        out[at, halves[1][1]] = acc.astype(BF)
        return carry

    lax.fori_loop(0, shape_b[0] // 16, end_b, 0)


def by_rows(rows, width):
    h = rows // 2
    return ((pl.ds(0, h), pl.ds(0, width)), (pl.ds(h, h), pl.ds(0, width)))


def by_columns(rows, width):
    h = width // 2
    return ((pl.ds(0, rows), pl.ds(0, h)), (pl.ds(0, rows), pl.ds(h, h)))


def scratch(**kw):
    return {k: pltpu.VMEM(*v) for k, v in kw.items()}


def call(body, name, ident, ins, outs, work, sems, near):
    names = list(ins) + list(outs) + list(work)

    def run_body(*refs):
        body(SimpleNamespace(**dict(zip(names, refs[:-3]))), Copies(*refs[-3:]))

    results = pl.pallas_call(
        run_body,
        name=name,
        out_shape=[jax.ShapeDtypeStruct(*v[:2]) for v in outs.values()],
        in_specs=[v[1] for v in ins.values()],
        out_specs=[v[2] for v in outs.values()],
        scratch_shapes=list(work.values())
        + [
            pltpu.SemaphoreType.DMA((sems,)),
            pltpu.SemaphoreType.DMA((sems,)),
            pltpu.SemaphoreType.DMA((near,)),
        ],
        compiler_params=pltpu.CompilerParams(
            collective_id=ident, has_side_effects=True, vmem_limit_bytes=60 << 20
        ),
    )(*[v[0] for v in ins.values()])
    return SimpleNamespace(**dict(zip(outs, results)))


def drain(*chains):
    for chain in chains:
        for _ in chain:
            pass


NN = ((1,), (0,))
NT = ((1,), (1,))
TN = ((0,), (0,))


def dot(a, b, dims):
    return lax.dot_general(a, b, (dims, ((), ())), preferred_element_type=F32)


def spread(m, out, start, down, padded):
    x = m[...].astype(F32)
    none = jnp.zeros((m.shape[0], padded - down), F32)
    for k in range(8):
        runs = []
        for p in range(16):
            at = (8 * p + k) * down
            runs += [x[:, at : at + down], none]
        out[k, :, start : start + 16 * padded] = jnp.concatenate(runs, axis=1).astype(BF)


def unspread(m, out, down, padded):
    for k in range(8):
        for p in range(16):
            at = (8 * p + k) * down
            out[:, at : at + down] = m[k, :, padded * p : padded * p + down].astype(F32)


def gather_body(R, cp):
    g = place()[1]
    shuffle = Shuffle(True)
    meet = hail(rings() + [in_group(*st) for st in GROUP], shuffle.greeting)

    def norm(i, carry):
        r = rows_of(i)
        x = R.tok[r, :].astype(F32)
        s = lax.rsqrt(jnp.mean(x * x, axis=-1, keepdims=True) + EPS)
        R.first[r, :] = (x * s * R.gain[...]).astype(BF)
        return carry

    lax.fori_loop(0, R.tok.shape[0] // 16, norm, 0)
    meet()
    me = (ax("xlo"), ax("xhi"), ax("z"))
    third = R.w_in.shape[1] // 8
    arrive = []
    for j, w in enumerate((R.w_in, R.w_f, R.w_og)):
        arrive.append(
            to_group(
                cp,
                lambda k, w=w: w.at[:, pl.ds(pl.multiple_of(k * third, 128), third)],
                lambda k, j=j: R.b3.at[me + (rows_of(k), pl.ds(j * third, third))],
            )
        )
    q = shuffle.to[0]
    at = (lax.div(q, 8), lax.rem(lax.div(q, 4), 2), lax.rem(q, 4))
    moved = shuffle.start(cp, R.w_o, R.bo.at[at])
    dn = plane_first(cp, R.dn, R.dn_column, R.dn_row, by_columns(*R.dn.shape))
    next(dn)
    own = cp.local(R.first, R.fi.at[block_of(g)])
    chain = GroupGather(cp, R.first, R.fi)
    for pair in arrive:
        settle(*pair)
    b3 = plane_gather(cp, R.b3, by_rows(*R.b3.shape[3:]))
    next(b3)
    shuffle.wait(moved)
    bo = plane_gather(cp, R.bo, by_columns(*R.bo.shape[3:]))
    next(bo)
    next(b3)
    next(bo)
    chain.relay()
    run([b3, bo, dn], (2, 0, 1))
    chain.rest()
    own.wait()
    cp.finish()


def silu_slope(v, s):
    return s * (1.0 + v * (1.0 - s))


def row_sums(x):
    ones = jnp.ones((8, x.shape[1]), F32)
    return lax.dot_general(
        ones, x, (((1,), (1,)), ((), ())), precision=HIGH, preferred_element_type=F32
    )[0:1]


def as_column(row, width):
    t = jnp.transpose(jnp.broadcast_to(row, (128, 128)))
    return jnp.concatenate([t] * (width // 128), axis=1)


def chunk_rows(s):
    return pl.ds(pl.multiple_of(s * 128, 128), 128)


def wide(ref, r):
    return jnp.concatenate([ref[j, r, :] for j in range(ref.shape[0])], axis=1)


def put(ref, r, value):
    for j in range(ref.shape[0]):
        ref[j, r, :] = value[:, 128 * j : 128 * (j + 1)]


def share(cp, src, dst, index, peers):
    copies = [cp.send(src, dst.at[index], dev) for dev in peers]
    dst[pl.ds(index, 1)] = src[...][None]
    return copies


def levels(table, layer):
    e = jnp.exp(table - jnp.max(table, axis=0, keepdims=True))
    level = lax.broadcasted_iota(jnp.int32, table.shape, 0)
    counts = jnp.where((level >= 1) & (level <= layer), 1.0, 0.0)
    return e / jnp.sum(e, axis=0, keepdims=True), counts


def links_before(links, k, w):
    come = jnp.zeros((1, w), F32)
    for j in range(8):
        new = links[j, 0:1, :] * come + links[j, 1:2, :]
        come = jnp.where(j < k, new, come)
    return come


def scan_body(R, cp):
    tiles, rows = R.states.shape[:2]
    w = 128 * tiles
    steps = rows // 8
    peers_chain = [in_chain(*st) for st in CHAIN]
    peers_group = [in_group(*st) for st in GROUP]
    load = [cp.local(R.b3, R.w3), cp.local(R.fi, R.x)]
    load_out = cp.local(R.bo, R.wo)
    meet = hail(peers_chain + peers_group + [ring("x", s) for s in (1, 3)])
    mine = rows_of(place()[1], w)
    prob, keep_mask = levels(R.table[:, mine], R.layer[...])
    low = jnp.sum(prob * keep_mask, axis=0, keepdims=True)
    R.lb[...] = jnp.broadcast_to(low, (8, w))
    gain = R.gain[:, mine]
    unit = R.gu.shape[2] // 2
    down = R.w_gate.shape[1] // 128
    spread(R.w_gate, R.gu, 0, down, unit // 16)
    spread(R.w_up, R.gu, unit, down, unit // 16)
    meet()
    arrive_gu = to_group(cp, lambda k: R.gu.at[k], lambda k: R.block_gu.at[rows_of(k), :])
    own = cp.local(R.cot, R.gf.at[block_of(place()[1])])
    bulk = plane_second(cp, R.dn_column, R.dn_row, R.bdn, by_columns(*R.bdn.shape[3:]))
    next(bulk)
    chain = GroupGather(cp, R.cot, R.gf)
    for copy in load:
        copy.wait()

    def project(j):
        for i in range(2):
            r = pl.ds(i * rows // 2, rows // 2)
            at = pl.ds(j * w, w)
            R.proj[r, at] = dot(R.x[r, :], R.w3[:, at], NN)

    project(0)
    project(1)
    settle(*arrive_gu)
    gate_up = plane_first(cp, R.block_gu, R.gu_column, R.gu_row, by_rows(*R.block_gu.shape))
    next(gate_up)
    next(bulk)
    chain.relay()

    def gates(i, c):
        r = rows_of(i, 32)
        f = low + (1.0 - low) * jax.nn.sigmoid(R.proj[r, w : 2 * w])
        v = R.proj[r, 0:w]
        put(R.forget, r, f)
        put(R.states, r, v * jax.nn.sigmoid(v) * (1.0 - f))
        return c

    lax.fori_loop(0, rows // 32, gates, 0)
    keep = [cp.local(R.forget, R.forget_out)]

    def step(t, c):
        at = pl.ds(t, 8, stride=steps)
        new = []
        for j, (h, a) in enumerate(c):
            f = R.forget[j, at, :]
            h = f * h + R.states[j, at, :]
            a = a * f
            R.states[j, at, :] = h
            R.prod[j, at, :] = a
            new.append((h, a))
        return tuple(new)

    start = ((jnp.zeros((8, 128), F32), jnp.ones((8, 128), F32)),) * tiles
    ends = lax.fori_loop(0, steps, step, start, unroll=8)
    h = jnp.concatenate([e[0] for e in ends], axis=1)
    a = jnp.concatenate([e[1] for e in ends], axis=1)
    c = jnp.zeros((1, w), F32)
    q = jnp.ones((1, w), F32)
    cs, qs = [], []
    for s in range(8):
        cs.append(c)
        qs.append(q)
        c = a[s : s + 1] * c + h[s : s + 1]
        q = a[s : s + 1] * q
    R.mine[...] = jnp.concatenate([q, c, jnp.zeros((6, w), F32)], axis=0)
    k = ax("xhi") * 4 + ax("z")
    small = share(cp, R.mine, R.links, k, peers_chain)
    project(2)
    keep.append(cp.local(R.proj, R.proj_out))
    for copy in small:
        copy.wait_recv()
    come = links_before(R.links, k, w)
    R.carry[...] = jnp.broadcast_to(come, (8, w))
    R.entry[...] = jnp.concatenate(qs, axis=0) * come + jnp.concatenate(cs, axis=0)

    def finish(s, c):
        r = chunk_rows(s)
        st = wide(R.states, r) + wide(R.prod, r) * R.entry[pl.ds(s, 1), :]
        put(R.states, r, st)
        R.rowsum[pl.ds(s, 1), :] = row_sums(st * st)
        return c

    lax.fori_loop(0, 8, finish, 0)
    keep.append(cp.local(R.states, R.states_out))
    small = share(cp, R.rowsum, R.rows8, place()[1], peers_group)
    for copy in small:
        copy.wait_recv()
    total = R.rows8[0]
    for j in range(1, 8):
        total = total + R.rows8[j]
    R.tot[...] = lax.rsqrt(total / (8.0 * w) + EPS)

    def gate(s, c):
        r = chunk_rows(s)
        v = R.proj[r, 2 * w : 3 * w]
        n = wide(R.states, r) * as_column(R.tot[pl.ds(s, 1), :], w)
        R.gated[r, :] = (n * gain * (v * jax.nn.sigmoid(v))).astype(BF)
        return c

    lax.fori_loop(0, 8, gate, 0)
    keep.append(cp.local(R.gated, R.gated_out))
    load_out.wait()
    for i in range(4):
        r = pl.ds(i * rows // 4, rows // 4)

        def out(j, c, r=r):
            at = rows_of(j, 512)
            R.part[r, at] = dot(R.gated[r, :], R.wo[:, at], NN).astype(BF)
            return c

        lax.fori_loop(0, R.part.shape[1] // 512, out, 0)
        keep.append(cp.local(R.part.at[r], R.part_out.at[r]))
    chain.rest()
    for copy in keep:
        copy.wait()
    own.wait()
    drain(bulk, gate_up)
    cp.finish()


def feed_body(R, cp):
    y, c = ax("y"), ax("core")
    g = place()[1]
    unit, width = R.wdn.shape
    greet(ys() + rings())
    weights = plane_second(cp, R.gu_column, R.gu_row, R.wgu, by_rows(*R.wgu.shape[3:]))
    next(weights)
    mixer = sum_of(cp, R.part, R.ps, R.near, R.far)
    next(mixer)
    load = [cp.local(R.gf, R.g), cp.local(R.bdn, R.wdn)]
    next(mixer)
    next(mixer)
    next(weights)
    terms = next(mixer)

    def norm(i, carry):
        r = rows_of(i)
        x = R.tok[r, :].astype(F32) + terms(i)
        R.mid[r, :] = x
        s = lax.rsqrt(jnp.mean(x * x, axis=-1, keepdims=True) + EPS)
        R.si[rows_of(g * 8 + i), :] = (x * s * R.gain[...]).astype(BF)
        return carry

    lax.fori_loop(0, 8, norm, 0)
    gather = GroupGather(cp, R.si.at[block_of(g)], R.si)
    second = GroupSum(cp, R.near, R.far)
    for copy in load:
        copy.wait()
    drain(weights)
    order = (0, 1, 3, 2)
    stores = []

    def forward(yy):
        r = rows_of(yy, 256)

        def tile(j, carry):
            at = rows_of(j, 256)
            up = pl.ds(pl.multiple_of(unit + j * 256, 256), 256)
            x = R.si[r, :]
            v = dot(x, R.wgu[:, :, :, :, at].reshape(width, 256), NN)
            u = dot(x, R.wgu[:, :, :, :, up].reshape(width, 256), NN)
            gh = dot(R.g[r, :], R.wdn[at, :], NT)
            sig = jax.nn.sigmoid(v)
            act = v * sig
            R.hid[r, at] = (act * u).astype(BF)
            R.ggu[r, at] = (gh * u * silu_slope(v, sig)).astype(BF)
            R.ggu[r, up] = (gh * act).astype(BF)
            return carry

        lax.fori_loop(0, unit // 256, tile, 0)

    def backward(yy):
        r = rows_of(yy, 256)

        def tile(j, carry):
            at = rows_of(j, 512)
            w = R.wgu[lax.div(j, 2), lax.rem(j, 2)].reshape(512, 2 * unit)
            R.ps[r, at] = dot(R.ggu[r, :], w, NT).astype(BF)
            return carry

        lax.fori_loop(0, width // 512, tile, 0)

    def result(yy, slot):
        r = rows_of(yy, 256)

        def tile(j, carry):
            at = rows_of(j, 512)
            R.pr[slot, :, at] = dot(R.hid[r, :], R.wdn[:, at], NN).astype(BF)
            return carry

        lax.fori_loop(0, width // 512, tile, 0)
        stores.append(cp.local(R.pr.at[slot], R.part_r.at[r]))

    for i, s in enumerate(order):
        yy = lax.rem(y + 4 - s, 4)
        gather.ready(s)
        forward(yy)
        if i < 3:
            gather.forward(order[i + 1])
        if i > 1:
            back = (4 - order[i - 1]) % 4
            second.add(back, R.ps, 128 * (second.chip(back) + c))
        backward(yy)
        second.give((4 - s) % 4, R.ps.at[block_of(2 * yy + 1 - c)])
        if i > 1:
            stores[i - 2].wait()
        result(yy, i % 2)
    second.add(2, R.ps, 128 * (second.chip(2) + c))

    def grad_down(j, carry):
        at = rows_of(j, 512)
        for i in range(2):
            h = unit // 2
            v = dot(R.hid[:, h * i : h * (i + 1)], R.g[:, at], TN)
            R.ddn[i, :, :, :, at] = v.astype(BF).reshape(R.ddn.shape[1:4] + (512,))
        return carry

    lax.fori_loop(0, width // 512, grad_down, 0)
    planes = [plane_sum(cp, R.ddn, by_columns(*R.ddn.shape[3:]), *plane_refs(R, "a"), R.block_ddn)]
    next(planes[0])

    def grad_gate(i, carry):
        at = rows_of(i, 256)
        v = dot(R.si[:, at], R.ggu[:, 0:unit], TN).astype(BF)
        to = (lax.div(i, 4), lax.rem(lax.div(i, 2), 2), pl.ds(2 * lax.rem(i, 2), 2))
        R.dgate[to] = v.reshape(2, 128, unit)
        return carry

    lax.fori_loop(0, width // 256, grad_gate, 0)
    planes.append(plane_sum(cp, R.dgate, by_rows(*R.dgate.shape[3:]), *plane_refs(R, "b"), R.block_dgate))
    next(planes[1])
    terms = second.total(R.ps, 128 * g)
    R.sums[...] = jnp.zeros_like(R.sums)

    def back(i, carry):
        r = rows_of(i)
        x = R.mid[r, :]
        s = lax.rsqrt(jnp.mean(x * x, axis=-1, keepdims=True) + EPS)
        n = x * s
        dy = terms(i)
        R.sums[0:1, :] = R.sums[0:1, :] + jnp.sum(dy * n, axis=0, keepdims=True)
        dy = dy * R.gain[...]
        v = R.cot[r, :].astype(F32) + s * (dy - n * jnp.mean(dy * n, axis=-1, keepdims=True))
        R.mixed[r, :] = v
        R.block[r, :] = v.astype(BF)
        return carry

    lax.fori_loop(0, 8, back, 0)
    own = cp.local(R.block, R.gb.at[block_of(g)])
    branch = GroupGather(cp, R.block, R.gb)
    ups = []
    for copy in stores[2:]:
        copy.wait()

    def grad_up(i):
        at = pl.ds(i * 256, 256)
        v = dot(R.si[:, at], R.ggu[:, unit : 2 * unit], TN).astype(BF)
        if i > 1:
            ups[i - 2].wait()
        R.pu[i % 2] = v
        ups.append(cp.local(R.pu.at[i % 2], R.dup.at[at]))

    for i in range(width // 256):
        grad_up(i)
    branch.relay()
    for copy in ups[-2:]:
        copy.wait()
    next(planes[0])
    branch.forward(1)
    branch.forward(3)
    next(planes[1])
    branch.rest()
    own.wait()
    drain(*planes)
    cp.finish()


def plane_refs(R, key):
    return [getattr(R, "plane_" + key + str(i)) for i in range(6)]


def plane_work(key, halves):
    return {"plane_" + key + str(i): v for i, v in enumerate(plane_sum_scratch(halves))}


def grad_weights(R, start, dst):
    n = dst.shape[4]

    def tile(i, carry):
        at = rows_of(i, 256)
        v = dot(R.x[:, at], R.grads[:, start : start + n], TN).astype(BF)
        to = (lax.div(i, 4), lax.rem(lax.div(i, 2), 2), pl.ds(2 * lax.rem(i, 2), 2))
        dst[to] = v.reshape(2, 128, n)
        return carry

    lax.fori_loop(0, R.x.shape[1] // 256, tile, 0)


def back_body(R, cp):
    c = ax("core")
    p, g = place()
    tiles, rows = R.states.shape[:2]
    w = 128 * tiles
    steps = rows // 8
    width = R.tok.shape[1]
    shuffle = Shuffle(False)
    peers_chain = [in_chain(*st) for st in CHAIN]
    peers_group = [in_group(*st) for st in GROUP]
    peers_plane = [in_plane(*st) for st in PLANE]
    load = [cp.local(R.gb, R.gbv), cp.local(R.bo, R.wo)]
    load_scan = [
        cp.local(R.states_in, R.states),
        cp.local(R.proj_in, R.proj),
        cp.local(R.forget_in, R.forget),
        cp.local(R.gated_in, R.gated),
    ]
    load_x = cp.local(R.fi, R.x)
    load_last = [cp.local(R.b3, R.w3), cp.local(R.mid_in, R.mid), cp.local(R.mixed_in, R.mixed)]
    hail(peers_plane + peers_group, shuffle.greeting)()
    gain = R.gain[:, rows_of(g, w)]
    res = sum_of(cp, R.part_r, R.pr, R.pr_near, R.pr_far)
    next(res)
    up = plane_sum(cp, R.dup, by_rows(*R.dup.shape[3:]), *plane_refs(R, "a"), R.block_dup)
    next(up)
    low = R.lb[0:1, :]
    R.sums[...] = jnp.zeros_like(R.sums)
    gate_home = to_group(cp, lambda k: R.block_dgate.at[rows_of(k), :], lambda k: R.rgate.at[k])
    for copy in load:
        copy.wait()
    for i in range(2):
        r = pl.ds(i * rows // 2, rows // 2)
        R.gg[r, :] = dot(R.gbv[r, :], R.wo[...], NT)
    next(res)
    for copy in load_scan:
        copy.wait()

    def through(s, carry):
        r = chunk_rows(s)
        v = R.proj[r, 2 * w : 3 * w]
        sig = jax.nn.sigmoid(v)
        n = wide(R.states, r) * as_column(R.tot[pl.ds(s, 1), :], w)
        dy = R.gg[r, :]
        R.sums[0:1, :] = R.sums[0:1, :] + jnp.sum(dy * n * (v * sig), axis=0, keepdims=True)
        R.grads[r, 2 * w : 3 * w] = (dy * n * gain * silu_slope(v, sig)).astype(BF)
        dy = dy * gain * (v * sig)
        put(R.gs, r, dy)
        R.rowsum[pl.ds(s, 1), :] = row_sums(dy * n)
        return carry

    lax.fori_loop(0, 8, through, 0)
    small = share(cp, R.rowsum, R.rows8, g, peers_group)
    next(res)
    def grad_out(j, carry):
        at = rows_of(j, 512)
        v = dot(R.gated[...], R.gbv[:, at], TN).astype(BF)
        R.do[:, :, :, :, at] = v.reshape(R.do.shape[:4] + (512,))
        return carry

    lax.fori_loop(0, width // 512, grad_out, 0)
    outs = plane_sum(cp, R.do, by_columns(*R.do.shape[3:]), *plane_refs(R, "b"), R.oo)
    next(outs)
    load_x.wait()
    grad_weights(R, 2 * w, R.d1)
    one = plane_sum(cp, R.d1, by_rows(*R.d1.shape[3:]), *plane_refs(R, "d"), R.o1)
    next(one)
    for copy in small:
        copy.wait_recv()
    total = R.rows8[0]
    for j in range(1, 8):
        total = total + R.rows8[j]
    cp.sent(small)
    R.rowsum[...] = total / (8.0 * w)

    def norm(s, carry):
        r = chunk_rows(s)
        t = as_column(R.tot[pl.ds(s, 1), :], w)
        m = as_column(R.rowsum[pl.ds(s, 1), :], w)
        put(R.gs, r, t * (wide(R.gs, r) - wide(R.states, r) * t * m))
        return carry

    lax.fori_loop(0, 8, norm, 0)

    def step(i, carry):
        at = pl.ds(steps - 1 - i, 8, stride=steps)
        new = []
        for j, (h, a) in enumerate(carry):
            f = R.forget[j, at, :]
            v = R.gs[j, at, :] + h
            R.gs[j, at, :] = v
            R.prod[j, at, :] = a
            new.append((f * v, a * f))
        return tuple(new)

    start = ((jnp.zeros((8, 128), F32), jnp.ones((8, 128), F32)),) * tiles
    ends = lax.fori_loop(0, steps, step, start, unroll=8)
    h = jnp.concatenate([e[0] for e in ends], axis=1)
    a = jnp.concatenate([e[1] for e in ends], axis=1)
    e = jnp.zeros((1, w), F32)
    q = jnp.ones((1, w), F32)
    cs, qs = [None] * 8, [None] * 8
    for s in range(7, -1, -1):
        cs[s] = e
        qs[s] = q
        e = a[s : s + 1] * e + h[s : s + 1]
        q = a[s : s + 1] * q
    R.mine[...] = jnp.broadcast_to(e, (8, w))
    k = ax("xhi") * 4 + ax("z")
    small = share(cp, R.mine, R.chain, k, peers_chain)
    next(up)
    next(outs)
    for copy in small:
        copy.wait_recv()
    come = jnp.zeros((1, w), F32)
    for j in range(7, -1, -1):
        new = R.links[j, 0:1, :] * come + R.chain[j, 0:1, :]
        come = jnp.where(j > k, new, come)
    R.entry[...] = jnp.concatenate(qs, axis=0) * come + jnp.concatenate(cs, axis=0)

    def last(s, carry):
        r = chunk_rows(s)
        v = wide(R.gs, r) + wide(R.prod, r) * R.entry[pl.ds(s, 1), :]
        st = wide(R.states, r)
        above = pl.ds(jnp.maximum(s * 128 - 1, 0), 1)
        before = jnp.where(s == 0, R.carry[0:1, :], wide(R.states, above))
        top = lax.broadcasted_iota(jnp.int32, (128, w), 0) == 0
        prev = jnp.where(top, before, pltpu.roll(st, 1, 0))
        x = R.proj[r, 0:w]
        sx = jax.nn.sigmoid(x)
        f = wide(R.forget, r)
        sf = jax.nn.sigmoid(R.proj[r, w : 2 * w])
        gf = v * (prev - x * sx)
        R.grads[r, 0:w] = (v * (1.0 - f) * silu_slope(x, sx)).astype(BF)
        R.grads[r, w : 2 * w] = (gf * (1.0 - low) * sf * (1.0 - sf)).astype(BF)
        R.sums[1:2, :] = R.sums[1:2, :] + jnp.sum(gf * (1.0 - sf), axis=0, keepdims=True)
        return carry

    lax.fori_loop(0, 8, last, 0)
    for copy in load_last:
        copy.wait()
    grad_weights(R, 0, R.d2)
    two = plane_sum(cp, R.d2, by_rows(*R.d2.shape[3:]), *plane_refs(R, "c"), R.o2)
    next(two)
    next(one)
    R.va[...] = jnp.zeros_like(R.va)
    R.va[1:2, :] = R.ffn_sums[0:1, :]
    first = RelaySum(cp, R.near, R.far)
    order = (2, 1, 3, 0)
    for i, s in enumerate(order):
        chip = first.chip(s)
        r = pl.ds(pl.multiple_of(chip * 128, 256), 256)

        def tile(j, carry, r=r):
            at = rows_of(j, 512)
            v = dot(R.grads[r, :], R.w3[at, :], NT)
            R.va[0:1, at] = R.va[0:1, at] + jnp.sum(
                v * (R.x[r, at].astype(F32) / R.attn_gain[:, at]), axis=0, keepdims=True
            )
            R.fp[r, at] = v.astype(BF)
            return carry

        lax.fori_loop(0, width // 512, tile, 0)
        first.give(s, R.fp.at[block_of(chip + 1 - c)])
        if i > 0:
            back = order[i - 1]
            first.add(back, R.fp, 128 * (first.chip(back) + c))
    first.relay(R.fp, 128 * (first.chip(1) + c), 128 * (first.chip(3) + c))

    gains = []
    for st in GROUP:
        dev = in_group(*st)
        k = dev["y"] * 2 + dev["core"]
        gains.append(cp.send(R.va.at[:, rows_of(k, w)], R.ga.at[g], dev))
    R.ga[pl.ds(g, 1)] = R.va[:, rows_of(g, w)][None]

    drain(up, outs, one)
    arrive = [
        gate_home,
        to_group(cp, lambda k: R.o1.at[rows_of(k), :], lambda k: R.r1.at[k]),
        to_group(cp, lambda k: R.block_dup.at[rows_of(k), :], lambda k: R.rup.at[k]),
    ]
    moved = shuffle.start(cp, R.oo, R.ro)
    for copy in gains:
        copy.wait_recv()
    acc = R.ga[0]
    for j in range(1, 8):
        acc = acc + R.ga[j]
    R.ta[...] = acc
    R.ta[2:4, :] = R.sums[0:2, :]
    for copy in share(cp, R.ta, R.gather, p, peers_plane):
        copy.wait_recv()
    acc = R.gather[0]
    for j in range(1, 16):
        acc = acc + R.gather[j]
    R.tb[...] = acc
    terms = next(res)

    def finish_result(i, carry):
        r = rows_of(i)
        R.result[r, :] = (R.mid[r, :] + terms(i)).astype(BF)
        return carry

    lax.fori_loop(0, 8, finish_result, 0)
    small = share(cp, R.tb, R.totals, g, peers_group)
    next(two)
    terms_first = first.total(R.fp, 128 * g)

    def back(i, carry):
        r = rows_of(i)
        x = R.tok[r, :].astype(F32)
        s = lax.rsqrt(jnp.mean(x * x, axis=-1, keepdims=True) + EPS)
        n = x * s
        dy = terms_first(i)
        dy = dy * R.attn_gain[...]
        R.gtok[r, :] = R.mixed[r, :] + s * (dy - n * jnp.mean(dy * n, axis=-1, keepdims=True))
        return carry

    lax.fori_loop(0, 8, back, 0)
    for pair in arrive:
        settle(*pair)
    unit = R.rgate.shape[2]
    down = R.g_gate.shape[1] // 128
    unspread(R.rgate, R.g_gate, down, unit // 16)
    unspread(R.rup, R.g_up, down, unit // 16)
    for copy in small:
        copy.wait_recv()
    for j in range(8):
        at = pl.ds(j * w, w)
        R.gains[:, at] = R.totals[j]
        R.g_og[:, at] = R.r1[j].astype(F32)
    prob, counts = levels(R.table[...], R.layer[...])
    bound = jnp.sum(prob * counts, axis=0, keepdims=True)
    R.g_table[...] = R.gains[3:4, :] * prob * (counts - bound)
    shuffle.wait(moved)
    R.g_out[...] = R.ro[...].astype(F32)
    drain(two)
    settle(*to_group(cp, lambda k: R.o2.at[rows_of(k), :], lambda k: R.r2.at[k]))
    for j in range(8):
        at = pl.ds(j * w, w)
        R.g_in[:, at] = R.r2[j, :, 0:w].astype(F32)
        R.g_forget[:, at] = R.r2[j, :, w : 2 * w].astype(F32)
    cp.finish()


def write_body(*refs):
    count = (len(refs) - 3) // 2
    ins, outs, sem = refs[:count], refs[count:-1], refs[-1]
    copies = []
    for i in range(count - 2):
        copies.append(pltpu.make_async_copy(ins[i], outs[i], sem.at[i]))
        copies[-1].start()
    for i, row in enumerate((0, 2, 1)):
        outs[count - 1 + i][...] = ins[count - 2][row : row + 1, :]
    outs[count - 2][...] = ins[count - 1][...].astype(F32)[0 : outs[count - 2].shape[0]]
    for copy in copies:
        copy.wait()


def on_device(
    tokens, cotangent, attn_gain, w_input, w_forget, w_outgate, w_out, norm_gain, mlp_gain, w_gate, w_up, w_down, bound_table, layer_idx
):
    n, width = tokens.shape
    rows = w_input.shape[0]
    hidden_width = w_gate.shape[1]
    down = w_down.shape[0]
    padded = -(-down // 16) * 16
    unit = 16 * padded
    w = width // 8

    dn = jnp.pad(w_down, ((0, padded - down), (0, 0)))
    gains = attn_gain[None, :]
    full = (8 * n, width)
    block = (n, width)
    gate_blocks = (2, 2, 4, 8 * rows, unit)
    A = call(
        gather_body,
        "gather",
        0,
        dict(
            tok=(tokens, VMEM),
            gain=(gains, VMEM),
            w_in=(w_input, VMEM),
            w_f=(w_forget, VMEM),
            w_og=(w_outgate, VMEM),
            w_o=(w_out, VMEM),
            dn=(dn, VMEM),
        ),
        dict(
            b3=((2, 2, 4, 8 * rows, 3 * w), BF, ANY),
            bo=((2, 2, 4, rows, width), BF, ANY),
            fi=(full, BF, ANY),
            dn_column=((4, padded, width // 2), BF, ANY),
            dn_row=((2, 2, padded, width // 2), BF, ANY),
        ),
        scratch(first=(block, BF)),
        96,
        10,
    )
    big3 = A.b3.reshape(width, 3 * w)
    big_out = A.bo.reshape(w, width)
    column = (w // 128, 8 * n, 128)
    B = call(
        scan_body,
        "scan",
        1,
        dict(
            table=(bound_table, VMEM),
            layer=(layer_idx[None, :], VMEM),
            gain=(norm_gain[None, :], VMEM),
            b3=(big3, ANY),
            bo=(big_out, ANY),
            fi=(A.fi, ANY),
            dn_column=(A.dn_column, VMEM),
            dn_row=(A.dn_row, VMEM),
            w_gate=(w_gate, VMEM),
            w_up=(w_up, VMEM),
            cot=(cotangent, VMEM),
        ),
        dict(
            gated_out=((8 * n, w), BF, ANY),
            states_out=(column, F32, ANY),
            forget_out=(column, F32, ANY),
            proj_out=((8 * n, 3 * w), F32, ANY),
            tot=((8, n), F32, VMEM),
            links=((8, 8, w), F32, VMEM),
            carry=((8, w), F32, VMEM),
            lb=((8, w), F32, VMEM),
            part_out=(full, BF, ANY),
            gf=(full, BF, ANY),
            bdn=((2, 2, 4, padded, width), BF, ANY),
            gu_column=((4, 4 * rows, 2 * unit), BF, ANY),
            gu_row=((2, 2, 4 * rows, 2 * unit), BF, ANY),
        ),
        scratch(
            gu=((8, rows, 2 * unit), BF),
            block_gu=((8 * rows, 2 * unit), BF),
            gated=((8 * n, w), BF),
            states=(column, F32),
            forget=(column, F32),
            proj=((8 * n, 3 * w), F32),
            part=(full, BF),
            w3=((width, 3 * w), BF),
            x=(full, BF),
            wo=((w, width), BF),
            prod=(column, F32),
            entry=((8, w), F32),
            mine=((8, w), F32),
            rowsum=((8, n), F32),
            rows8=((8, 8, n), F32),
        ),
        64,
        24,
    )
    gains_two = mlp_gain[None, :]
    C = call(
        feed_body,
        "feed",
        2,
        dict(
            tok=(tokens, VMEM),
            cot=(cotangent, VMEM),
            gain=(gains_two, VMEM),
            part=(B.part_out, ANY),
            gu_column=(B.gu_column, ANY),
            gu_row=(B.gu_row, ANY),
            bdn=(B.bdn.reshape(unit, width), ANY),
            gf=(B.gf, ANY),
        ),
        dict(
            mid=(block, F32, VMEM),
            mixed=(block, F32, VMEM),
            gb=(full, BF, ANY),
            part_r=(full, BF, ANY),
            sums=((8, width), F32, VMEM),
            block_ddn=((padded, width), BF, VMEM),
            block_dgate=((8 * rows, unit), BF, VMEM),
            dup=((width, unit), BF, ANY),
        ),
        scratch(
            wgu=((2, 2, 4, 8 * rows, 2 * unit), BF),
            wdn=((unit, width), BF),
            g=(full, BF),
            si=(full, BF),
            hid=((8 * n, unit), BF),
            ggu=((8 * n, 2 * unit), BF),
            ps=(full, BF),
            pr=((2, 2 * n, width), BF),
            near=((4,) + block, BF),
            far=((3,) + block, BF),
            block=(block, BF),
            ddn=((2, 2, 4, padded, width), BF),
            dgate=(gate_blocks, BF),
            pu=((2, 256, unit), BF),
        )
        | plane_work("a", by_columns(padded, width))
        | plane_work("b", by_rows(8 * rows, unit)),
        72,
        30,
    )
    D = call(
        back_body,
        "back",
        3,
        dict(
            tok=(tokens, VMEM),
            mid_in=(C.mid, ANY),
            mixed_in=(C.mixed, ANY),
            attn_gain=(gains, VMEM),
            lb=(B.lb, VMEM),
            table=(bound_table, VMEM),
            layer=(layer_idx[None, :], VMEM),
            gain=(norm_gain[None, :], VMEM),
            ffn_sums=(C.sums, VMEM),
            states_in=(B.states_out, ANY),
            forget_in=(B.forget_out, ANY),
            proj_in=(B.proj_out, ANY),
            gated_in=(B.gated_out, ANY),
            tot=(B.tot, VMEM),
            links=(B.links, VMEM),
            carry=(B.carry, VMEM),
            b3=(big3, ANY),
            bo=(big_out, ANY),
            fi=(A.fi, ANY),
            gb=(C.gb, ANY),
            part_r=(C.part_r, ANY),
            dup=(C.dup.reshape(gate_blocks), ANY),
            block_dgate=(C.block_dgate, ANY),
        ),
        dict(
            result=(block, BF, VMEM),
            gtok=(block, F32, VMEM),
            g_in=((rows, width), F32, VMEM),
            g_forget=((rows, width), F32, VMEM),
            g_og=((rows, width), F32, VMEM),
            g_out=((rows, width), F32, VMEM),
            g_gate=((rows, hidden_width), F32, VMEM),
            g_up=((rows, hidden_width), F32, VMEM),
            g_table=(bound_table.shape, F32, VMEM),
            gains=((8, width), F32, VMEM),
        ),
        scratch(
            rgate=((8, rows, unit), BF),
            rup=((8, rows, unit), BF),
            r1=((8, rows, w), BF),
            r2=((8, rows, 2 * w), BF),
            ro=((rows, width), BF),
            totals=((8, 8, w), F32),
            states=(column, F32),
            forget=(column, F32),
            proj=((8 * n, 3 * w), F32),
            gated=((8 * n, w), BF),
            mid=(block, F32),
            mixed=(block, F32),
            gbv=(full, BF),
            wo=((w, width), BF),
            w3=((width, 3 * w), BF),
            x=(full, BF),
            gg=((8 * n, w), F32),
            gs=(column, F32),
            prod=(column, F32),
            grads=((8 * n, 3 * w), BF),
            sums=((8, w), F32),
            entry=((8, w), F32),
            mine=((8, w), F32),
            rowsum=((8, n), F32),
            rows8=((8, 8, n), F32),
            chain=((8, 8, w), F32),
            pr=((4 * n, width), BF),
            pr_near=((4,) + block, BF),
            pr_far=((3,) + block, BF),
            fp=(full, BF),
            near=((4,) + block, BF),
            far=((3,) + block, BF),
            do=((2, 2, 4, rows, width), BF),
            d1=((2, 2, 4, 8 * rows, w), BF),
            d2=((2, 2, 4, 8 * rows, 2 * w), BF),
            block_dup=((8 * rows, unit), BF),
            o1=((8 * rows, w), BF),
            o2=((8 * rows, 2 * w), BF),
            oo=((rows, width), BF),
            va=((8, width), F32),
            ga=((8, 8, w), F32),
            ta=((8, w), F32),
            gather=((16, 8, w), F32),
            tb=((8, w), F32),
        )
        | plane_work("a", by_rows(8 * rows, unit))
        | plane_work("b", by_columns(rows, width))
        | plane_work("c", by_rows(8 * rows, 2 * w))
        | plane_work("d", by_rows(8 * rows, w)),
        160,
        30,
    )

    moved = (D.result, D.gtok, D.g_in, D.g_forget, D.g_og, D.g_out, D.g_gate, D.g_up, D.g_table)
    like = [jax.ShapeDtypeStruct(m.shape, m.dtype) for m in moved]
    row = jax.ShapeDtypeStruct((1, width), F32)
    last = pl.pallas_call(
        write_body,
        name="write",
        out_shape=like + [jax.ShapeDtypeStruct((down, width), F32), row, row, row],
        in_specs=[ANY] * len(moved) + [VMEM] * 2,
        out_specs=[VMEM] * (len(moved) + 4),
        scratch_shapes=[pltpu.SemaphoreType.DMA((len(moved),))],
        compiler_params=pltpu.CompilerParams(vmem_limit_bytes=60 << 20),
    )(*moved, D.gains, C.block_ddn)
    result, grad_tokens, g_in, g_forget, g_og, g_out, g_gate, g_up, g_table, g_down = last[:10]
    attn, norm, mlp = [m[0] for m in last[10:]]
    return (
        result,
        grad_tokens,
        attn,
        g_in,
        g_forget,
        g_og,
        g_out,
        norm,
        mlp,
        g_gate,
        g_up,
        g_down,
        g_table,
    )


def solution(mesh):
    split = Mesh(mesh.devices.reshape(2, 2, 4, 4, 2), AXES)
    cut = P(AXES, None)
    return jax.shard_map(
        on_device,
        mesh=split,
        in_specs=(cut, cut, P(), cut, cut, cut, cut, P(), P(), cut, cut, cut, P(), P()),
        out_specs=(cut, cut, P(), cut, cut, cut, cut, P(), P(), cut, cut, cut, P()),
        check_vma=False,
    )
```

```python
from types import SimpleNamespace

import jax
import jax.numpy as jnp
from jax import lax
from jax.experimental import pallas as pl
from jax.experimental.pallas import tpu as pltpu
from jax.sharding import Mesh, PartitionSpec as P

EPS = 1e-06
BF = jnp.bfloat16
F32 = jnp.float32
AXES = ("xlo", "xhi", "z", "y", "core")
MESH = pl.DeviceIdType.MESH
ANY = pl.BlockSpec(memory_space=pl.ANY)
VMEM = pl.BlockSpec(memory_space=pltpu.VMEM)
STEPS = (1, 3, 2)
GROUP = [(a, b) for a in range(4) for b in range(2) if a or b]
CHAIN = [(a, b) for a in range(2) for b in range(4) if a or b]
PLANE = [(a, b) for a in range(4) for b in range(4) if a or b]
HIGH = lax.Precision.HIGHEST


def ax(name):
    return lax.axis_index(name)


def ring(axis, s):
    if axis == "x":
        x = lax.rem(ax("xhi") * 2 + ax("xlo") + s, 4)
        return {"xhi": lax.div(x, 2), "xlo": lax.rem(x, 2)}
    return {axis: lax.rem(ax(axis) + s, 4)}


def sibling():
    return {"core": 1 - ax("core")}


def in_group(s, t):
    return {"y": lax.rem(ax("y") + s, 4), "core": lax.rem(ax("core") + t, 2)}


def in_chain(s, t):
    return {"xhi": lax.rem(ax("xhi") + s, 2), "z": lax.rem(ax("z") + t, 4)}


def in_plane(s, t):
    return {**ring("x", s), **ring("z", t)}


def place():
    return ax("xlo") * 8 + ax("xhi") * 4 + ax("z"), ax("y") * 2 + ax("core")


def device(p, g):
    return {
        "xlo": lax.div(p, 8),
        "xhi": lax.rem(lax.div(p, 4), 2),
        "z": lax.rem(p, 4),
        "y": lax.div(g, 2),
        "core": lax.rem(g, 2),
    }


class Copies:
    def __init__(self, send, recv, near):
        self.sems = (send, recv, near)
        self.count = 0
        self.locals = 0
        self.open = []

    def remote(self, src, dst, dev):
        i = self.count
        self.count += 1
        assert i < self.sems[0].shape[0]
        return pltpu.make_async_remote_copy(
            src_ref=src,
            dst_ref=dst,
            send_sem=self.sems[0].at[i],
            recv_sem=self.sems[1].at[i],
            device_id=dev,
            device_id_type=MESH,
        )

    def send(self, src, dst, dev):
        copy = self.remote(src, dst, dev)
        copy.start()
        self.open.append(copy)
        return copy

    def near(self, src, dst):
        i = self.locals
        self.locals += 1
        assert i < self.sems[2].shape[0]
        return pltpu.make_async_copy(src, dst, self.sems[2].at[i])

    def local(self, src, dst):
        copy = self.near(src, dst)
        copy.start()
        return copy

    def sent(self, copies):
        for copy in copies:
            copy.wait_send()
        gone = {id(copy) for copy in copies}
        self.open = [copy for copy in self.open if id(copy) not in gone]

    def finish(self):
        for copy in self.open:
            copy.wait_send()


def hail(peers, shuffle=None):
    bar = pltpu.get_barrier_semaphore()
    for dev in peers:
        pl.semaphore_signal(bar, inc=1, device_id=dev, device_id_type=MESH)
    count = len(peers)
    if shuffle is not None:
        source, from_me, to_me = shuffle

        @pl.when(jnp.logical_not(from_me))
        def _():
            pl.semaphore_signal(bar, inc=1, device_id=source, device_id_type=MESH)

        count = count + jnp.where(to_me, 0, 1)
    return lambda: pl.semaphore_wait(bar, count)


def greet(peers):
    hail(peers)()


def to_group(cp, source, dst):
    g = place()[1]
    there = dst(g)
    copies = []
    for st in GROUP:
        q = in_group(*st)
        copies.append(cp.send(source(q["y"] * 2 + q["core"]), there, q))
    return copies, cp.local(source(g), there)


def settle(copies, home):
    for copy in copies:
        copy.wait_recv()
    home.wait()


class Shuffle:
    def __init__(self, outward):
        p, g = place()
        self.d = p * 8 + g
        row = 16 * g + p
        there = (lax.rem(self.d, 16), lax.div(self.d, 16))
        here = (lax.div(row, 8), lax.rem(row, 8))
        to, come = (there, here) if outward else (here, there)
        self.to = to
        self.target, self.source = device(*to), device(*come)
        self.to_me = to[0] * 8 + to[1] == self.d
        self.from_me = come[0] * 8 + come[1] == self.d
        self.greeting = (self.source, self.from_me, self.to_me)

    def start(self, cp, src, dst):
        copy = cp.remote(src, dst, self.target)
        home = cp.near(src, dst)

        @pl.when(self.to_me)
        def _():
            home.start()

        @pl.when(jnp.logical_not(self.to_me))
        def _():
            copy.start()

        return copy, home

    def wait(self, pair):
        @pl.when(self.to_me)
        def _():
            pair[1].wait()

        @pl.when(jnp.logical_not(self.to_me))
        def _():
            pair[0].wait()


def rings():
    return [ring("x", s) for s in STEPS] + [ring("z", s) for s in STEPS]


def ys():
    return [ring("y", s) for s in STEPS] + [sibling()]


def run(chains, order):
    for i in order:
        next(chains[i], None)
    for chain in chains:
        for _ in chain:
            pass


def rows_of(i, n=16):
    return pl.ds(pl.multiple_of(i * n, n), n)


def block_of(k):
    return rows_of(k, 128)


class GroupGather:
    def __init__(self, cp, src, full):
        self.cp, self.full = cp, full
        k = place()[1]
        self.half = {}
        for first in (0, 1):
            for s in (1, 3):
                h = first if s == 1 else 1 - first
                self.half[s, h] = cp.send(
                    src.at[pl.ds(64 * h, 64)], full.at[self.rows(k, h)], ring("y", s)
                )
        self.near = {0: cp.send(src, full.at[block_of(k)], sibling())}
        self.done = set()

    def rows(self, k, h):
        return pl.ds(pl.multiple_of(k * 128 + 64 * h, 64), 64)

    def chip(self, s):
        return 2 * lax.rem(ax("y") + 4 - s, 4) + ax("core")

    def arrived(self, s, h):
        if (s, h) not in self.done:
            self.done.add((s, h))
            self.half[s, h].wait_recv()

    def relay(self):
        for s, h in ((1, 0), (3, 1)):
            self.arrived(s, h)
            at = self.full.at[self.rows(self.chip(s), h)]
            self.half[2, h] = self.cp.send(at, at, ring("y", s))

    def forward(self, s):
        if (2, 0) not in self.half:
            self.relay()
        self.arrived(s, 0)
        self.arrived(s, 1)
        at = self.full.at[block_of(self.chip(s))]
        self.near[s] = self.cp.send(at, at, sibling())

    def ready(self, s):
        self.near[s].wait_recv()

    def rest(self):
        for s in STEPS:
            if s not in self.near:
                self.forward(s)
        for s in (0, 1, 3, 2):
            self.ready(s)


class GroupSum:
    def __init__(self, cp, near, far):
        self.cp, self.near, self.far = cp, near, far
        self.sent, self.moved = {}, {}

    def chip(self, s):
        return 2 * lax.rem(ax("y") + s, 4)

    def give(self, s, src):
        self.sent[s] = self.cp.send(src, self.near.at[s], sibling())

    def add(self, s, mine, at):
        near = self.near
        self.sent[s].wait_recv()

        def step(i, carry):
            r = rows_of(i)
            to = pl.ds(pl.multiple_of(at + i * 16, 16), 16)
            mine[to, :] = (mine[to, :].astype(F32) + near[s, r, :].astype(F32)).astype(BF)
            return carry

        lax.fori_loop(0, 8, step, 0)
        here = mine.at[pl.ds(pl.multiple_of(at, 128), 128)]
        self.moved[s] = self.cp.send(here, self.far.at[s - 1], ring("y", s))

    def total(self, mine, at):
        self.sent[0].wait_recv()
        for s in STEPS:
            self.moved[s].wait_recv()
        self.cp.sent(list(self.moved.values()))
        near, far = self.near, self.far

        def rows(i):
            r = rows_of(i)
            own = mine[pl.ds(pl.multiple_of(at + i * 16, 16), 16), :]
            acc = own.astype(F32) + near[0, r, :].astype(F32)
            for s in range(3):
                acc = acc + far[s, r, :].astype(F32)
            return acc

        return rows


class RelaySum(GroupSum):
    def piece(self, mine, at, h):
        return mine.at[pl.ds(pl.multiple_of(at + 64 * h, 64), 64)]

    def plus(self, mine, at, term, n):
        def step(i, carry):
            to = pl.ds(pl.multiple_of(at + i * 16, 16), 16)
            mine[to, :] = (mine[to, :].astype(F32) + term(rows_of(i)).astype(F32)).astype(BF)
            return carry

        lax.fori_loop(0, n // 16, step, 0)

    def to(self, s, slot, h, mine, at):
        return self.cp.send(
            self.piece(mine, at, h), self.far.at[slot, pl.ds(64 * h, 64)], ring("y", s)
        )

    def add(self, s, mine, at):
        near = self.near
        self.sent[s].wait_recv()
        self.plus(mine, at, lambda r: near[s, r, :], 128)
        if s == 2:
            self.hop = [self.to(1, 2, 0, mine, at), self.to(3, 2, 1, mine, at)]
        elif s == 1:
            self.moved[1, 1] = self.to(1, 0, 1, mine, at)
        else:
            self.moved[3, 0] = self.to(3, 1, 0, mine, at)

    def relay(self, mine, at_next, at_last):
        far = self.far
        self.hop[0].wait_recv()
        self.plus(mine, at_next, lambda r: far[2, r, :], 64)
        self.moved[1, 0] = self.to(1, 0, 0, mine, at_next)
        self.hop[1].wait_recv()
        up = lambda r: far[2, pl.ds(pl.multiple_of(64 + r.start, 16), 16), :]
        self.plus(mine, at_last + 64, up, 64)
        self.moved[3, 1] = self.to(3, 1, 1, mine, at_last)

    def total(self, mine, at):
        self.sent[0].wait_recv()
        for key in ((1, 1), (3, 0), (1, 0), (3, 1)):
            self.moved[key].wait_recv()
        self.cp.sent(self.hop + list(self.moved.values()))
        near, far = self.near, self.far

        def rows(i):
            r = rows_of(i)
            own = mine[pl.ds(pl.multiple_of(at + i * 16, 16), 16), :]
            acc = own.astype(F32) + near[0, r, :].astype(F32)
            return acc + (far[0, r, :].astype(F32) + far[1, r, :].astype(F32))

        return rows


def sum_of(cp, part, mine, near, far):
    total = RelaySum(cp, near, far)
    c = ax("core")
    own = {}
    for s in (2, 1, 3, 0):
        total.give(s, part.at[block_of(total.chip(s) + 1 - c)])
        own[s] = cp.local(part.at[block_of(total.chip(s) + c)], mine.at[pl.ds(128 * s, 128)])
    yield
    for s in (2, 1, 3):
        own[s].wait()
        total.add(s, mine, 128 * s)
    own[0].wait()
    yield
    total.relay(mine, 128, 384)
    yield
    yield total.total(mine, 0)


def plane_gather(cp, buf, halves, block=None):
    me = (ax("xlo"), ax("xhi"), ax("z"))
    home = None if block is None else cp.local(block, buf.at[me])

    def view(h, *at):
        return buf.at[at + halves[h]]

    mine = [view(h, *me) if block is None else block.at[halves[h]] for h in range(2)]
    first = []
    for s in STEPS:
        first.append(cp.send(mine[0], view(0, *me), ring("z", s)))
        first.append(cp.send(mine[1], view(1, *me), ring("x", s)))
    yield
    if home is not None:
        home.wait()
    for copy in first:
        copy.wait_recv()
    column = view(0, me[0], me[1], pl.ds(0, 4))
    row = view(1, pl.ds(0, 2), pl.ds(0, 2), me[2])
    wide = {}
    for s in (1, 3):
        wide["x", s] = cp.send(column, column, ring("x", s))
        wide["z", s] = cp.send(row, row, ring("z", s))
    yield
    last = []
    for s in (1, 3):
        back = ring("x", 4 - s)
        wide["x", s].wait_recv()
        v = view(0, back["xlo"], back["xhi"], pl.ds(0 if s == 1 else 2, 2))
        last.append(cp.send(v, v, ring("x", s)))
        back = ring("z", 4 - s)
        wide["z", s].wait_recv()
        v = view(1, 0 if s == 1 else 1, pl.ds(0, 2), back["z"])
        last.append(cp.send(v, v, ring("z", s)))
    yield
    for copy in last:
        copy.wait_recv()


def plane_first(cp, block, column, row, halves):
    me = (ax("xlo"), ax("xhi"), ax("z"))
    top, bottom = [block.at[h] for h in halves]
    home = [cp.local(top, column.at[me[2]]), cp.local(bottom, row.at[me[0], me[1]])]
    first = []
    for s in STEPS:
        first.append(cp.send(top, column.at[me[2]], ring("z", s)))
        first.append(cp.send(bottom, row.at[me[0], me[1]], ring("x", s)))
    yield
    for copy in first:
        copy.wait_recv()
    for copy in home:
        copy.wait()


def plane_second(cp, column, row, buf, halves):
    me = (ax("xlo"), ax("xhi"), ax("z"))

    def view(h, *at):
        return buf.at[at + halves[h]]

    here = view(0, me[0], me[1], pl.ds(0, 4))
    across = view(1, pl.ds(0, 2), pl.ds(0, 2), me[2])
    home = [cp.local(column, here), cp.local(row, across)]
    wide = {}
    for s in (1, 3):
        wide["x", s] = cp.send(column, here, ring("x", s))
        wide["z", s] = cp.send(row, across, ring("z", s))
    yield
    last = []
    for s in (1, 3):
        back = ring("x", 4 - s)
        wide["x", s].wait_recv()
        v = view(0, back["xlo"], back["xhi"], pl.ds(0 if s == 1 else 2, 2))
        last.append(cp.send(v, v, ring("x", s)))
        back = ring("z", 4 - s)
        wide["z", s].wait_recv()
        v = view(1, 0 if s == 1 else 1, pl.ds(0, 2), back["z"])
        last.append(cp.send(v, v, ring("z", s)))
    yield
    for copy in last:
        copy.wait_recv()
    for copy in home:
        copy.wait()


def half_shapes(halves):
    return [tuple(d.size for d in h) for h in halves]


def plane_sum_scratch(halves):
    a, b = half_shapes(halves)
    return [
        pltpu.VMEM((4,) + a, BF),
        pltpu.VMEM((3, 4) + a, BF),
        pltpu.VMEM((3,) + a, BF),
        pltpu.VMEM((2, 2) + b, BF),
        pltpu.VMEM((3, 2, 2) + b, BF),
        pltpu.VMEM((3,) + b, BF),
    ]


def plane_sum(cp, part, halves, own_a, far_a, last_a, own_b, far_b, last_b, out):
    me = (ax("xlo"), ax("xhi"), ax("z"))
    shape_a, shape_b = half_shapes(halves)

    def view(h, *at):
        return part.at[at + halves[h]]

    near_a = cp.local(view(0, me[0], me[1], pl.ds(0, 4)), own_a)
    near_b = cp.local(view(1, pl.ds(0, 2), pl.ds(0, 2), me[2]), own_b)
    first_a, first_b = [], []
    for j, s in enumerate(STEPS):
        d = ring("x", s)
        first_a.append(cp.send(view(0, d["xlo"], d["xhi"], pl.ds(0, 4)), far_a.at[j], d))
        d = ring("z", s)
        first_b.append(cp.send(view(1, pl.ds(0, 2), pl.ds(0, 2), d["z"]), far_b.at[j], d))
    yield
    near_a.wait()
    for copy in first_a:
        copy.wait_recv()
    for k in range(4):

        def add(i, carry, k=k):
            r = rows_of(i)
            acc = own_a[k, r, :].astype(F32)
            for j in range(3):
                acc = acc + far_a[j, k, r, :].astype(F32)
            own_a[k, r, :] = acc.astype(BF)
            return carry

        lax.fori_loop(0, shape_a[0] // 16, add, 0)
    second = []
    for j, s in enumerate(STEPS):
        d = ring("z", s)
        second.append(cp.send(own_a.at[d["z"]], last_a.at[j], d))
    near_b.wait()
    for copy in first_b:
        copy.wait_recv()
    for k in range(4):

        def add(i, carry, k=k):
            r = rows_of(i)
            acc = own_b[k // 2, k % 2, r, :].astype(F32)
            for j in range(3):
                acc = acc + far_b[j, k // 2, k % 2, r, :].astype(F32)
            own_b[k // 2, k % 2, r, :] = acc.astype(BF)
            return carry

        lax.fori_loop(0, shape_b[0] // 16, add, 0)
    for j, s in enumerate(STEPS):
        d = ring("x", s)
        second.append(cp.send(own_b.at[d["xlo"], d["xhi"]], last_b.at[j], d))
    yield
    for copy in second:
        copy.wait_recv()

    def end_a(i, carry):
        r = rows_of(i)
        acc = own_a[me[2], r, :].astype(F32)
        for j in range(3):
            acc = acc + last_a[j, r, :].astype(F32)
        at = rows_of(i) if halves[0][0].start == 0 else pl.ds(halves[0][0].start + i * 16, 16)
        out[at, halves[0][1]] = acc.astype(BF)
        return carry

    lax.fori_loop(0, shape_a[0] // 16, end_a, 0)

    def end_b(i, carry):
        r = rows_of(i)
        acc = own_b[me[0], me[1], r, :].astype(F32)
        for j in range(3):
            acc = acc + last_b[j, r, :].astype(F32)
        at = pl.ds(pl.multiple_of(halves[1][0].start + i * 16, 16), 16)
        out[at, halves[1][1]] = acc.astype(BF)
        return carry

    lax.fori_loop(0, shape_b[0] // 16, end_b, 0)


def by_rows(rows, width):
    h = rows // 2
    return ((pl.ds(0, h), pl.ds(0, width)), (pl.ds(h, h), pl.ds(0, width)))


def by_columns(rows, width):
    h = width // 2
    return ((pl.ds(0, rows), pl.ds(0, h)), (pl.ds(0, rows), pl.ds(h, h)))


def scratch(**kw):
    return {k: pltpu.VMEM(*v) for k, v in kw.items()}


def call(body, name, ident, ins, outs, work, sems, near):
    names = list(ins) + list(outs) + list(work)

    def run_body(*refs):
        body(SimpleNamespace(**dict(zip(names, refs[:-3]))), Copies(*refs[-3:]))

    results = pl.pallas_call(
        run_body,
        name=name,
        out_shape=[jax.ShapeDtypeStruct(*v[:2]) for v in outs.values()],
        in_specs=[v[1] for v in ins.values()],
        out_specs=[v[2] for v in outs.values()],
        scratch_shapes=list(work.values())
        + [
            pltpu.SemaphoreType.DMA((sems,)),
            pltpu.SemaphoreType.DMA((sems,)),
            pltpu.SemaphoreType.DMA((near,)),
        ],
        compiler_params=pltpu.CompilerParams(
            collective_id=ident, has_side_effects=True, vmem_limit_bytes=60 << 20
        ),
    )(*[v[0] for v in ins.values()])
    return SimpleNamespace(**dict(zip(outs, results)))


def drain(*chains):
    for chain in chains:
        for _ in chain:
            pass


NN = ((1,), (0,))
NT = ((1,), (1,))
TN = ((0,), (0,))


def dot(a, b, dims):
    return lax.dot_general(a, b, (dims, ((), ())), preferred_element_type=F32)


def spread(m, out, start, down, padded):
    x = m[...].astype(F32)
    none = jnp.zeros((m.shape[0], padded - down), F32)
    for k in range(8):
        runs = []
        for p in range(16):
            at = (8 * p + k) * down
            runs += [x[:, at : at + down], none]
        out[k, :, start : start + 16 * padded] = jnp.concatenate(runs, axis=1).astype(BF)


def unspread(m, out, down, padded):
    for k in range(8):
        for p in range(16):
            at = (8 * p + k) * down
            out[:, at : at + down] = m[k, :, padded * p : padded * p + down].astype(F32)


def gather_body(R, cp):
    g = place()[1]
    shuffle = Shuffle(True)
    meet = hail(rings() + [in_group(*st) for st in GROUP], shuffle.greeting)

    def norm(i, carry):
        r = rows_of(i)
        x = R.tok[r, :].astype(F32)
        s = lax.rsqrt(jnp.mean(x * x, axis=-1, keepdims=True) + EPS)
        R.first[r, :] = (x * s * R.gain[...]).astype(BF)
        return carry

    lax.fori_loop(0, R.tok.shape[0] // 16, norm, 0)
    meet()
    me = (ax("xlo"), ax("xhi"), ax("z"))
    third = R.w_in.shape[1] // 8
    arrive = []
    for j, w in enumerate((R.w_in, R.w_f, R.w_og)):
        arrive.append(
            to_group(
                cp,
                lambda k, w=w: w.at[:, pl.ds(pl.multiple_of(k * third, 128), third)],
                lambda k, j=j: R.b3.at[me + (rows_of(k), pl.ds(j * third, third))],
            )
        )
    q = shuffle.to[0]
    at = (lax.div(q, 8), lax.rem(lax.div(q, 4), 2), lax.rem(q, 4))
    moved = shuffle.start(cp, R.w_o, R.bo.at[at])
    dn = plane_first(cp, R.dn, R.dn_column, R.dn_row, by_columns(*R.dn.shape))
    next(dn)
    own = cp.local(R.first, R.fi.at[block_of(g)])
    chain = GroupGather(cp, R.first, R.fi)
    for pair in arrive:
        settle(*pair)
    b3 = plane_gather(cp, R.b3, by_rows(*R.b3.shape[3:]))
    next(b3)
    shuffle.wait(moved)
    bo = plane_gather(cp, R.bo, by_columns(*R.bo.shape[3:]))
    next(bo)
    next(b3)
    next(bo)
    chain.relay()
    run([b3, bo, dn], (2, 0, 1))
    chain.rest()
    own.wait()
    cp.finish()


def silu_slope(v, s):
    return s * (1.0 + v * (1.0 - s))


def row_sums(x):
    ones = jnp.ones((8, x.shape[1]), F32)
    return lax.dot_general(
        ones, x, (((1,), (1,)), ((), ())), precision=HIGH, preferred_element_type=F32
    )[0:1]


def as_column(row, width):
    t = jnp.transpose(jnp.broadcast_to(row, (128, 128)))
    return jnp.concatenate([t] * (width // 128), axis=1)


def chunk_rows(s):
    return pl.ds(pl.multiple_of(s * 128, 128), 128)


def wide(ref, r):
    return jnp.concatenate([ref[j, r, :] for j in range(ref.shape[0])], axis=1)


def put(ref, r, value):
    for j in range(ref.shape[0]):
        ref[j, r, :] = value[:, 128 * j : 128 * (j + 1)]


def share(cp, src, dst, index, peers):
    copies = [cp.send(src, dst.at[index], dev) for dev in peers]
    dst[pl.ds(index, 1)] = src[...][None]
    return copies


def levels(table, layer):
    e = jnp.exp(table - jnp.max(table, axis=0, keepdims=True))
    level = lax.broadcasted_iota(jnp.int32, table.shape, 0)
    counts = jnp.where((level >= 1) & (level <= layer), 1.0, 0.0)
    return e / jnp.sum(e, axis=0, keepdims=True), counts


def links_before(links, k, w):
    come = jnp.zeros((1, w), F32)
    for j in range(8):
        new = links[j, 0:1, :] * come + links[j, 1:2, :]
        come = jnp.where(j < k, new, come)
    return come


def scan_body(R, cp):
    tiles, rows = R.states.shape[:2]
    w = 128 * tiles
    steps = rows // 8
    peers_chain = [in_chain(*st) for st in CHAIN]
    peers_group = [in_group(*st) for st in GROUP]
    load = [cp.local(R.b3, R.w3), cp.local(R.fi, R.x)]
    load_out = cp.local(R.bo, R.wo)
    meet = hail(peers_chain + peers_group + [ring("x", s) for s in (1, 3)])
    mine = rows_of(place()[1], w)
    prob, keep_mask = levels(R.table[:, mine], R.layer[...])
    low = jnp.sum(prob * keep_mask, axis=0, keepdims=True)
    R.lb[...] = jnp.broadcast_to(low, (8, w))
    gain = R.gain[:, mine]
    unit = R.gu.shape[2] // 2
    down = R.w_gate.shape[1] // 128
    spread(R.w_gate, R.gu, 0, down, unit // 16)
    spread(R.w_up, R.gu, unit, down, unit // 16)
    meet()
    arrive_gu = to_group(cp, lambda k: R.gu.at[k], lambda k: R.block_gu.at[rows_of(k), :])
    own = cp.local(R.cot, R.gf.at[block_of(place()[1])])
    bulk = plane_second(cp, R.dn_column, R.dn_row, R.bdn, by_columns(*R.bdn.shape[3:]))
    next(bulk)
    chain = GroupGather(cp, R.cot, R.gf)
    for copy in load:
        copy.wait()

    def project(j):
        for i in range(2):
            r = pl.ds(i * rows // 2, rows // 2)
            at = pl.ds(j * w, w)
            R.proj[r, at] = dot(R.x[r, :], R.w3[:, at], NN)

    project(0)
    project(1)
    settle(*arrive_gu)
    gate_up = plane_first(cp, R.block_gu, R.gu_column, R.gu_row, by_rows(*R.block_gu.shape))
    next(gate_up)
    next(bulk)
    chain.relay()

    def gates(i, c):
        r = rows_of(i, 32)
        f = low + (1.0 - low) * jax.nn.sigmoid(R.proj[r, w : 2 * w])
        v = R.proj[r, 0:w]
        put(R.forget, r, f)
        put(R.states, r, v * jax.nn.sigmoid(v) * (1.0 - f))
        return c

    lax.fori_loop(0, rows // 32, gates, 0)
    keep = [cp.local(R.forget, R.forget_out)]

    def step(t, c):
        at = pl.ds(t, 8, stride=steps)
        new = []
        for j, (h, a) in enumerate(c):
            f = R.forget[j, at, :]
            h = f * h + R.states[j, at, :]
            a = a * f
            R.states[j, at, :] = h
            R.prod[j, at, :] = a
            new.append((h, a))
        return tuple(new)

    start = ((jnp.zeros((8, 128), F32), jnp.ones((8, 128), F32)),) * tiles
    ends = lax.fori_loop(0, steps, step, start, unroll=8)
    h = jnp.concatenate([e[0] for e in ends], axis=1)
    a = jnp.concatenate([e[1] for e in ends], axis=1)
    c = jnp.zeros((1, w), F32)
    q = jnp.ones((1, w), F32)
    cs, qs = [], []
    for s in range(8):
        cs.append(c)
        qs.append(q)
        c = a[s : s + 1] * c + h[s : s + 1]
        q = a[s : s + 1] * q
    R.mine[...] = jnp.concatenate([q, c, jnp.zeros((6, w), F32)], axis=0)
    k = ax("xhi") * 4 + ax("z")
    small = share(cp, R.mine, R.links, k, peers_chain)
    project(2)
    keep.append(cp.local(R.proj, R.proj_out))
    for copy in small:
        copy.wait_recv()
    come = links_before(R.links, k, w)
    R.carry[...] = jnp.broadcast_to(come, (8, w))
    R.entry[...] = jnp.concatenate(qs, axis=0) * come + jnp.concatenate(cs, axis=0)

    def finish(s, c):
        r = chunk_rows(s)
        st = wide(R.states, r) + wide(R.prod, r) * R.entry[pl.ds(s, 1), :]
        put(R.states, r, st)
        R.rowsum[pl.ds(s, 1), :] = row_sums(st * st)
        return c

    lax.fori_loop(0, 8, finish, 0)
    keep.append(cp.local(R.states, R.states_out))
    small = share(cp, R.rowsum, R.rows8, place()[1], peers_group)
    for copy in small:
        copy.wait_recv()
    total = R.rows8[0]
    for j in range(1, 8):
        total = total + R.rows8[j]
    R.tot[...] = lax.rsqrt(total / (8.0 * w) + EPS)

    def gate(s, c):
        r = chunk_rows(s)
        v = R.proj[r, 2 * w : 3 * w]
        n = wide(R.states, r) * as_column(R.tot[pl.ds(s, 1), :], w)
        R.gated[r, :] = (n * gain * (v * jax.nn.sigmoid(v))).astype(BF)
        return c

    lax.fori_loop(0, 8, gate, 0)
    keep.append(cp.local(R.gated, R.gated_out))
    load_out.wait()
    for i in range(4):
        r = pl.ds(i * rows // 4, rows // 4)

        def out(j, c, r=r):
            at = rows_of(j, 512)
            R.part[r, at] = dot(R.gated[r, :], R.wo[:, at], NN).astype(BF)
            return c

        lax.fori_loop(0, R.part.shape[1] // 512, out, 0)
        keep.append(cp.local(R.part.at[r], R.part_out.at[r]))
    chain.rest()
    for copy in keep:
        copy.wait()
    own.wait()
    drain(bulk, gate_up)
    cp.finish()


def feed_body(R, cp):
    y, c = ax("y"), ax("core")
    g = place()[1]
    unit, width = R.wdn.shape
    greet(ys() + rings())
    weights = plane_second(cp, R.gu_column, R.gu_row, R.wgu, by_rows(*R.wgu.shape[3:]))
    next(weights)
    mixer = sum_of(cp, R.part, R.ps, R.near, R.far)
    next(mixer)
    load = [cp.local(R.gf, R.g), cp.local(R.bdn, R.wdn)]
    next(mixer)
    next(mixer)
    next(weights)
    terms = next(mixer)

    def norm(i, carry):
        r = rows_of(i)
        x = R.tok[r, :].astype(F32) + terms(i)
        R.mid[r, :] = x
        s = lax.rsqrt(jnp.mean(x * x, axis=-1, keepdims=True) + EPS)
        R.si[rows_of(g * 8 + i), :] = (x * s * R.gain[...]).astype(BF)
        return carry

    lax.fori_loop(0, 8, norm, 0)
    gather = GroupGather(cp, R.si.at[block_of(g)], R.si)
    second = GroupSum(cp, R.near, R.far)
    for copy in load:
        copy.wait()
    drain(weights)
    order = (0, 1, 3, 2)
    stores = []

    def forward(yy):
        r = rows_of(yy, 256)

        def tile(j, carry):
            at = rows_of(j, 256)
            up = pl.ds(pl.multiple_of(unit + j * 256, 256), 256)
            x = R.si[r, :]
            v = dot(x, R.wgu[:, :, :, :, at].reshape(width, 256), NN)
            u = dot(x, R.wgu[:, :, :, :, up].reshape(width, 256), NN)
            gh = dot(R.g[r, :], R.wdn[at, :], NT)
            sig = jax.nn.sigmoid(v)
            act = v * sig
            R.hid[r, at] = (act * u).astype(BF)
            R.ggu[r, at] = (gh * u * silu_slope(v, sig)).astype(BF)
            R.ggu[r, up] = (gh * act).astype(BF)
            return carry

        lax.fori_loop(0, unit // 256, tile, 0)

    def backward(yy):
        r = rows_of(yy, 256)

        def tile(j, carry):
            at = rows_of(j, 512)
            w = R.wgu[lax.div(j, 2), lax.rem(j, 2)].reshape(512, 2 * unit)
            R.ps[r, at] = dot(R.ggu[r, :], w, NT).astype(BF)
            return carry

        lax.fori_loop(0, width // 512, tile, 0)

    def result(yy, slot):
        r = rows_of(yy, 256)

        def tile(j, carry):
            at = rows_of(j, 512)
            R.pr[slot, :, at] = dot(R.hid[r, :], R.wdn[:, at], NN).astype(BF)
            return carry

        lax.fori_loop(0, width // 512, tile, 0)
        stores.append(cp.local(R.pr.at[slot], R.part_r.at[r]))

    for i, s in enumerate(order):
        yy = lax.rem(y + 4 - s, 4)
        gather.ready(s)
        forward(yy)
        if i > 1:
            back = (4 - order[i - 1]) % 4
            second.add(back, R.ps, 128 * (second.chip(back) + c))
        backward(yy)
        second.give((4 - s) % 4, R.ps.at[block_of(2 * yy + 1 - c)])
        if i > 1:
            stores[i - 2].wait()
        result(yy, i % 2)
        for ahead in ((1, 3), (2,), (), ())[i]:
            gather.forward(ahead)
    second.add(2, R.ps, 128 * (second.chip(2) + c))

    def grad_down(j, carry):
        at = rows_of(j, 512)
        for i in range(2):
            h = unit // 2
            v = dot(R.hid[:, h * i : h * (i + 1)], R.g[:, at], TN)
            R.ddn[i, :, :, :, at] = v.astype(BF).reshape(R.ddn.shape[1:4] + (512,))
        return carry

    lax.fori_loop(0, width // 512, grad_down, 0)
    planes = [plane_sum(cp, R.ddn, by_columns(*R.ddn.shape[3:]), *plane_refs(R, "a"), R.block_ddn)]
    next(planes[0])

    def grad_gate(i, carry):
        at = rows_of(i, 256)
        v = dot(R.si[:, at], R.ggu[:, 0:unit], TN).astype(BF)
        to = (lax.div(i, 4), lax.rem(lax.div(i, 2), 2), pl.ds(2 * lax.rem(i, 2), 2))
        R.dgate[to] = v.reshape(2, 128, unit)
        return carry

    lax.fori_loop(0, width // 256, grad_gate, 0)
    planes.append(plane_sum(cp, R.dgate, by_rows(*R.dgate.shape[3:]), *plane_refs(R, "b"), R.block_dgate))
    next(planes[1])
    terms = second.total(R.ps, 128 * g)
    R.sums[...] = jnp.zeros_like(R.sums)

    def back(i, carry):
        r = rows_of(i)
        x = R.mid[r, :]
        s = lax.rsqrt(jnp.mean(x * x, axis=-1, keepdims=True) + EPS)
        n = x * s
        dy = terms(i)
        R.sums[0:1, :] = R.sums[0:1, :] + jnp.sum(dy * n, axis=0, keepdims=True)
        dy = dy * R.gain[...]
        v = R.cot[r, :].astype(F32) + s * (dy - n * jnp.mean(dy * n, axis=-1, keepdims=True))
        R.mixed[r, :] = v
        R.block[r, :] = v.astype(BF)
        return carry

    lax.fori_loop(0, 8, back, 0)
    own = cp.local(R.block, R.gb.at[block_of(g)])
    branch = GroupGather(cp, R.block, R.gb)
    ups = []
    for copy in stores[2:]:
        copy.wait()

    def grad_up(i):
        at = pl.ds(i * 256, 256)
        v = dot(R.si[:, at], R.ggu[:, unit : 2 * unit], TN).astype(BF)
        if i > 1:
            ups[i - 2].wait()
        R.pu[i % 2] = v
        ups.append(cp.local(R.pu.at[i % 2], R.dup.at[at]))

    for i in range(width // 256):
        grad_up(i)
    branch.relay()
    for copy in ups[-2:]:
        copy.wait()
    next(planes[0])
    branch.forward(1)
    branch.forward(3)
    next(planes[1])
    branch.rest()
    own.wait()
    drain(*planes)
    cp.finish()


def plane_refs(R, key):
    return [getattr(R, "plane_" + key + str(i)) for i in range(6)]


def plane_work(key, halves):
    return {"plane_" + key + str(i): v for i, v in enumerate(plane_sum_scratch(halves))}


def grad_weights(R, start, dst):
    n = dst.shape[4]

    def tile(i, carry):
        at = rows_of(i, 256)
        v = dot(R.x[:, at], R.grads[:, start : start + n], TN).astype(BF)
        to = (lax.div(i, 4), lax.rem(lax.div(i, 2), 2), pl.ds(2 * lax.rem(i, 2), 2))
        dst[to] = v.reshape(2, 128, n)
        return carry

    lax.fori_loop(0, R.x.shape[1] // 256, tile, 0)


def back_body(R, cp):
    c = ax("core")
    p, g = place()
    tiles, rows = R.states.shape[:2]
    w = 128 * tiles
    steps = rows // 8
    width = R.tok.shape[1]
    shuffle = Shuffle(False)
    peers_chain = [in_chain(*st) for st in CHAIN]
    peers_group = [in_group(*st) for st in GROUP]
    peers_plane = [in_plane(*st) for st in PLANE]
    load = [cp.local(R.gb, R.gbv), cp.local(R.bo, R.wo)]
    load_scan = [
        cp.local(R.states_in, R.states),
        cp.local(R.proj_in, R.proj),
        cp.local(R.forget_in, R.forget),
        cp.local(R.gated_in, R.gated),
    ]
    load_x = cp.local(R.fi, R.x)
    load_last = [cp.local(R.b3, R.w3), cp.local(R.mid_in, R.mid), cp.local(R.mixed_in, R.mixed)]
    hail(peers_plane + peers_group, shuffle.greeting)()
    gain = R.gain[:, rows_of(g, w)]
    res = sum_of(cp, R.part_r, R.pr, R.pr_near, R.pr_far)
    next(res)
    up = plane_sum(cp, R.dup, by_rows(*R.dup.shape[3:]), *plane_refs(R, "a"), R.block_dup)
    next(up)
    low = R.lb[0:1, :]
    R.sums[...] = jnp.zeros_like(R.sums)
    gate_home = to_group(cp, lambda k: R.block_dgate.at[rows_of(k), :], lambda k: R.rgate.at[k])
    for copy in load:
        copy.wait()
    for i in range(2):
        r = pl.ds(i * rows // 2, rows // 2)
        R.gg[r, :] = dot(R.gbv[r, :], R.wo[...], NT)
    next(res)
    for copy in load_scan:
        copy.wait()

    def through(s, carry):
        r = chunk_rows(s)
        v = R.proj[r, 2 * w : 3 * w]
        sig = jax.nn.sigmoid(v)
        n = wide(R.states, r) * as_column(R.tot[pl.ds(s, 1), :], w)
        dy = R.gg[r, :]
        R.sums[0:1, :] = R.sums[0:1, :] + jnp.sum(dy * n * (v * sig), axis=0, keepdims=True)
        R.grads[r, 2 * w : 3 * w] = (dy * n * gain * silu_slope(v, sig)).astype(BF)
        dy = dy * gain * (v * sig)
        put(R.gs, r, dy)
        R.rowsum[pl.ds(s, 1), :] = row_sums(dy * n)
        return carry

    lax.fori_loop(0, 8, through, 0)
    small = share(cp, R.rowsum, R.rows8, g, peers_group)
    next(res)
    def grad_out(j, carry):
        at = rows_of(j, 512)
        v = dot(R.gated[...], R.gbv[:, at], TN).astype(BF)
        R.do[:, :, :, :, at] = v.reshape(R.do.shape[:4] + (512,))
        return carry

    lax.fori_loop(0, width // 512, grad_out, 0)
    outs = plane_sum(cp, R.do, by_columns(*R.do.shape[3:]), *plane_refs(R, "b"), R.oo)
    next(outs)
    for copy in small:
        copy.wait_recv()
    total = R.rows8[0]
    for j in range(1, 8):
        total = total + R.rows8[j]
    cp.sent(small)
    R.rowsum[...] = total / (8.0 * w)

    def norm(s, carry):
        r = chunk_rows(s)
        t = as_column(R.tot[pl.ds(s, 1), :], w)
        m = as_column(R.rowsum[pl.ds(s, 1), :], w)
        put(R.gs, r, t * (wide(R.gs, r) - wide(R.states, r) * t * m))
        return carry

    lax.fori_loop(0, 8, norm, 0)

    def step(i, carry):
        at = pl.ds(steps - 1 - i, 8, stride=steps)
        new = []
        for j, (h, a) in enumerate(carry):
            f = R.forget[j, at, :]
            v = R.gs[j, at, :] + h
            R.gs[j, at, :] = v
            R.prod[j, at, :] = a
            new.append((f * v, a * f))
        return tuple(new)

    start = ((jnp.zeros((8, 128), F32), jnp.ones((8, 128), F32)),) * tiles
    ends = lax.fori_loop(0, steps, step, start, unroll=8)
    h = jnp.concatenate([e[0] for e in ends], axis=1)
    a = jnp.concatenate([e[1] for e in ends], axis=1)
    e = jnp.zeros((1, w), F32)
    q = jnp.ones((1, w), F32)
    cs, qs = [None] * 8, [None] * 8
    for s in range(7, -1, -1):
        cs[s] = e
        qs[s] = q
        e = a[s : s + 1] * e + h[s : s + 1]
        q = a[s : s + 1] * q
    R.mine[...] = jnp.broadcast_to(e, (8, w))
    k = ax("xhi") * 4 + ax("z")
    small = share(cp, R.mine, R.chain, k, peers_chain)
    load_x.wait()
    grad_weights(R, 2 * w, R.d1)
    one = plane_sum(cp, R.d1, by_rows(*R.d1.shape[3:]), *plane_refs(R, "d"), R.o1)
    next(one)
    next(up)
    next(outs)
    for copy in small:
        copy.wait_recv()
    come = jnp.zeros((1, w), F32)
    for j in range(7, -1, -1):
        new = R.links[j, 0:1, :] * come + R.chain[j, 0:1, :]
        come = jnp.where(j > k, new, come)
    R.entry[...] = jnp.concatenate(qs, axis=0) * come + jnp.concatenate(cs, axis=0)

    def last(s, carry):
        r = chunk_rows(s)
        v = wide(R.gs, r) + wide(R.prod, r) * R.entry[pl.ds(s, 1), :]
        st = wide(R.states, r)
        above = pl.ds(jnp.maximum(s * 128 - 1, 0), 1)
        before = jnp.where(s == 0, R.carry[0:1, :], wide(R.states, above))
        top = lax.broadcasted_iota(jnp.int32, (128, w), 0) == 0
        prev = jnp.where(top, before, pltpu.roll(st, 1, 0))
        x = R.proj[r, 0:w]
        sx = jax.nn.sigmoid(x)
        f = wide(R.forget, r)
        sf = jax.nn.sigmoid(R.proj[r, w : 2 * w])
        gf = v * (prev - x * sx)
        R.grads[r, 0:w] = (v * (1.0 - f) * silu_slope(x, sx)).astype(BF)
        R.grads[r, w : 2 * w] = (gf * (1.0 - low) * sf * (1.0 - sf)).astype(BF)
        R.sums[1:2, :] = R.sums[1:2, :] + jnp.sum(gf * (1.0 - sf), axis=0, keepdims=True)
        return carry

    lax.fori_loop(0, 8, last, 0)
    for copy in load_last:
        copy.wait()
    R.va[...] = jnp.zeros_like(R.va)
    R.va[1:2, :] = R.ffn_sums[0:1, :]
    first = RelaySum(cp, R.near, R.far)
    order = (2, 1, 3, 0)
    for i, s in enumerate(order):
        chip = first.chip(s)
        r = pl.ds(pl.multiple_of(chip * 128, 256), 256)

        def tile(j, carry, r=r):
            at = rows_of(j, 512)
            v = dot(R.grads[r, :], R.w3[at, :], NT)
            R.va[0:1, at] = R.va[0:1, at] + jnp.sum(
                v * (R.x[r, at].astype(F32) / R.attn_gain[:, at]), axis=0, keepdims=True
            )
            R.fp[r, at] = v.astype(BF)
            return carry

        lax.fori_loop(0, width // 512, tile, 0)
        first.give(s, R.fp.at[block_of(chip + 1 - c)])
        if i > 0:
            back = order[i - 1]
            first.add(back, R.fp, 128 * (first.chip(back) + c))
    grad_weights(R, 0, R.d2)
    two = plane_sum(cp, R.d2, by_rows(*R.d2.shape[3:]), *plane_refs(R, "c"), R.o2)
    next(two)
    next(one)
    first.relay(R.fp, 128 * (first.chip(1) + c), 128 * (first.chip(3) + c))

    gains = []
    for st in GROUP:
        dev = in_group(*st)
        k = dev["y"] * 2 + dev["core"]
        gains.append(cp.send(R.va.at[:, rows_of(k, w)], R.ga.at[g], dev))
    R.ga[pl.ds(g, 1)] = R.va[:, rows_of(g, w)][None]

    drain(up, outs, one)
    arrive = [
        gate_home,
        to_group(cp, lambda k: R.o1.at[rows_of(k), :], lambda k: R.r1.at[k]),
        to_group(cp, lambda k: R.block_dup.at[rows_of(k), :], lambda k: R.rup.at[k]),
    ]
    moved = shuffle.start(cp, R.oo, R.ro)
    for copy in gains:
        copy.wait_recv()
    acc = R.ga[0]
    for j in range(1, 8):
        acc = acc + R.ga[j]
    R.ta[...] = acc
    R.ta[2:4, :] = R.sums[0:2, :]
    for copy in share(cp, R.ta, R.gather, p, peers_plane):
        copy.wait_recv()
    acc = R.gather[0]
    for j in range(1, 16):
        acc = acc + R.gather[j]
    R.tb[...] = acc
    terms = next(res)

    def finish_result(i, carry):
        r = rows_of(i)
        R.result[r, :] = (R.mid[r, :] + terms(i)).astype(BF)
        return carry

    lax.fori_loop(0, 8, finish_result, 0)
    small = share(cp, R.tb, R.totals, g, peers_group)
    next(two)
    terms_first = first.total(R.fp, 128 * g)

    def back(i, carry):
        r = rows_of(i)
        x = R.tok[r, :].astype(F32)
        s = lax.rsqrt(jnp.mean(x * x, axis=-1, keepdims=True) + EPS)
        n = x * s
        dy = terms_first(i)
        dy = dy * R.attn_gain[...]
        R.gtok[r, :] = R.mixed[r, :] + s * (dy - n * jnp.mean(dy * n, axis=-1, keepdims=True))
        return carry

    lax.fori_loop(0, 8, back, 0)
    for pair in arrive:
        settle(*pair)
    unit = R.rgate.shape[2]
    down = R.g_gate.shape[1] // 128
    unspread(R.rgate, R.g_gate, down, unit // 16)
    unspread(R.rup, R.g_up, down, unit // 16)
    for copy in small:
        copy.wait_recv()
    for j in range(8):
        at = pl.ds(j * w, w)
        R.gains[:, at] = R.totals[j]
        R.g_og[:, at] = R.r1[j].astype(F32)
    prob, counts = levels(R.table[...], R.layer[...])
    bound = jnp.sum(prob * counts, axis=0, keepdims=True)
    R.g_table[...] = R.gains[3:4, :] * prob * (counts - bound)
    shuffle.wait(moved)
    R.g_out[...] = R.ro[...].astype(F32)
    drain(two)
    settle(*to_group(cp, lambda k: R.o2.at[rows_of(k), :], lambda k: R.r2.at[k]))
    for j in range(8):
        at = pl.ds(j * w, w)
        R.g_in[:, at] = R.r2[j, :, 0:w].astype(F32)
        R.g_forget[:, at] = R.r2[j, :, w : 2 * w].astype(F32)
    cp.finish()


def write_body(*refs):
    count = (len(refs) - 3) // 2
    ins, outs, sem = refs[:count], refs[count:-1], refs[-1]
    copies = []
    for i in range(count - 2):
        copies.append(pltpu.make_async_copy(ins[i], outs[i], sem.at[i]))
        copies[-1].start()
    for i, row in enumerate((0, 2, 1)):
        outs[count - 1 + i][...] = ins[count - 2][row : row + 1, :]
    outs[count - 2][...] = ins[count - 1][...].astype(F32)[0 : outs[count - 2].shape[0]]
    for copy in copies:
        copy.wait()


def on_device(
    tokens, cotangent, attn_gain, w_input, w_forget, w_outgate, w_out, norm_gain, mlp_gain, w_gate, w_up, w_down, bound_table, layer_idx
):
    n, width = tokens.shape
    rows = w_input.shape[0]
    hidden_width = w_gate.shape[1]
    down = w_down.shape[0]
    padded = -(-down // 16) * 16
    unit = 16 * padded
    w = width // 8

    dn = jnp.pad(w_down, ((0, padded - down), (0, 0)))
    gains = attn_gain[None, :]
    full = (8 * n, width)
    block = (n, width)
    gate_blocks = (2, 2, 4, 8 * rows, unit)
    A = call(
        gather_body,
        "gather",
        0,
        dict(
            tok=(tokens, VMEM),
            gain=(gains, VMEM),
            w_in=(w_input, VMEM),
            w_f=(w_forget, VMEM),
            w_og=(w_outgate, VMEM),
            w_o=(w_out, VMEM),
            dn=(dn, VMEM),
        ),
        dict(
            b3=((2, 2, 4, 8 * rows, 3 * w), BF, ANY),
            bo=((2, 2, 4, rows, width), BF, ANY),
            fi=(full, BF, ANY),
            dn_column=((4, padded, width // 2), BF, ANY),
            dn_row=((2, 2, padded, width // 2), BF, ANY),
        ),
        scratch(first=(block, BF)),
        96,
        10,
    )
    big3 = A.b3.reshape(width, 3 * w)
    big_out = A.bo.reshape(w, width)
    column = (w // 128, 8 * n, 128)
    B = call(
        scan_body,
        "scan",
        1,
        dict(
            table=(bound_table, VMEM),
            layer=(layer_idx[None, :], VMEM),
            gain=(norm_gain[None, :], VMEM),
            b3=(big3, ANY),
            bo=(big_out, ANY),
            fi=(A.fi, ANY),
            dn_column=(A.dn_column, VMEM),
            dn_row=(A.dn_row, VMEM),
            w_gate=(w_gate, VMEM),
            w_up=(w_up, VMEM),
            cot=(cotangent, VMEM),
        ),
        dict(
            gated_out=((8 * n, w), BF, ANY),
            states_out=(column, F32, ANY),
            forget_out=(column, F32, ANY),
            proj_out=((8 * n, 3 * w), F32, ANY),
            tot=((8, n), F32, VMEM),
            links=((8, 8, w), F32, VMEM),
            carry=((8, w), F32, VMEM),
            lb=((8, w), F32, VMEM),
            part_out=(full, BF, ANY),
            gf=(full, BF, ANY),
            bdn=((2, 2, 4, padded, width), BF, ANY),
            gu_column=((4, 4 * rows, 2 * unit), BF, ANY),
            gu_row=((2, 2, 4 * rows, 2 * unit), BF, ANY),
        ),
        scratch(
            gu=((8, rows, 2 * unit), BF),
            block_gu=((8 * rows, 2 * unit), BF),
            gated=((8 * n, w), BF),
            states=(column, F32),
            forget=(column, F32),
            proj=((8 * n, 3 * w), F32),
            part=(full, BF),
            w3=((width, 3 * w), BF),
            x=(full, BF),
            wo=((w, width), BF),
            prod=(column, F32),
            entry=((8, w), F32),
            mine=((8, w), F32),
            rowsum=((8, n), F32),
            rows8=((8, 8, n), F32),
        ),
        64,
        24,
    )
    gains_two = mlp_gain[None, :]
    C = call(
        feed_body,
        "feed",
        2,
        dict(
            tok=(tokens, VMEM),
            cot=(cotangent, VMEM),
            gain=(gains_two, VMEM),
            part=(B.part_out, ANY),
            gu_column=(B.gu_column, ANY),
            gu_row=(B.gu_row, ANY),
            bdn=(B.bdn.reshape(unit, width), ANY),
            gf=(B.gf, ANY),
        ),
        dict(
            mid=(block, F32, VMEM),
            mixed=(block, F32, VMEM),
            gb=(full, BF, ANY),
            part_r=(full, BF, ANY),
            sums=((8, width), F32, VMEM),
            block_ddn=((padded, width), BF, VMEM),
            block_dgate=((8 * rows, unit), BF, VMEM),
            dup=((width, unit), BF, ANY),
        ),
        scratch(
            wgu=((2, 2, 4, 8 * rows, 2 * unit), BF),
            wdn=((unit, width), BF),
            g=(full, BF),
            si=(full, BF),
            hid=((8 * n, unit), BF),
            ggu=((8 * n, 2 * unit), BF),
            ps=(full, BF),
            pr=((2, 2 * n, width), BF),
            near=((4,) + block, BF),
            far=((3,) + block, BF),
            block=(block, BF),
            ddn=((2, 2, 4, padded, width), BF),
            dgate=(gate_blocks, BF),
            pu=((2, 256, unit), BF),
        )
        | plane_work("a", by_columns(padded, width))
        | plane_work("b", by_rows(8 * rows, unit)),
        72,
        30,
    )
    D = call(
        back_body,
        "back",
        3,
        dict(
            tok=(tokens, VMEM),
            mid_in=(C.mid, ANY),
            mixed_in=(C.mixed, ANY),
            attn_gain=(gains, VMEM),
            lb=(B.lb, VMEM),
            table=(bound_table, VMEM),
            layer=(layer_idx[None, :], VMEM),
            gain=(norm_gain[None, :], VMEM),
            ffn_sums=(C.sums, VMEM),
            states_in=(B.states_out, ANY),
            forget_in=(B.forget_out, ANY),
            proj_in=(B.proj_out, ANY),
            gated_in=(B.gated_out, ANY),
            tot=(B.tot, VMEM),
            links=(B.links, VMEM),
            carry=(B.carry, VMEM),
            b3=(big3, ANY),
            bo=(big_out, ANY),
            fi=(A.fi, ANY),
            gb=(C.gb, ANY),
            part_r=(C.part_r, ANY),
            dup=(C.dup.reshape(gate_blocks), ANY),
            block_dgate=(C.block_dgate, ANY),
        ),
        dict(
            result=(block, BF, VMEM),
            gtok=(block, F32, VMEM),
            g_in=((rows, width), F32, VMEM),
            g_forget=((rows, width), F32, VMEM),
            g_og=((rows, width), F32, VMEM),
            g_out=((rows, width), F32, VMEM),
            g_gate=((rows, hidden_width), F32, VMEM),
            g_up=((rows, hidden_width), F32, VMEM),
            g_table=(bound_table.shape, F32, VMEM),
            gains=((8, width), F32, VMEM),
        ),
        scratch(
            rgate=((8, rows, unit), BF),
            rup=((8, rows, unit), BF),
            r1=((8, rows, w), BF),
            r2=((8, rows, 2 * w), BF),
            ro=((rows, width), BF),
            totals=((8, 8, w), F32),
            states=(column, F32),
            forget=(column, F32),
            proj=((8 * n, 3 * w), F32),
            gated=((8 * n, w), BF),
            mid=(block, F32),
            mixed=(block, F32),
            gbv=(full, BF),
            wo=((w, width), BF),
            w3=((width, 3 * w), BF),
            x=(full, BF),
            gg=((8 * n, w), F32),
            gs=(column, F32),
            prod=(column, F32),
            grads=((8 * n, 3 * w), BF),
            sums=((8, w), F32),
            entry=((8, w), F32),
            mine=((8, w), F32),
            rowsum=((8, n), F32),
            rows8=((8, 8, n), F32),
            chain=((8, 8, w), F32),
            pr=((4 * n, width), BF),
            pr_near=((4,) + block, BF),
            pr_far=((3,) + block, BF),
            fp=(full, BF),
            near=((4,) + block, BF),
            far=((3,) + block, BF),
            do=((2, 2, 4, rows, width), BF),
            d1=((2, 2, 4, 8 * rows, w), BF),
            d2=((2, 2, 4, 8 * rows, 2 * w), BF),
            block_dup=((8 * rows, unit), BF),
            o1=((8 * rows, w), BF),
            o2=((8 * rows, 2 * w), BF),
            oo=((rows, width), BF),
            va=((8, width), F32),
            ga=((8, 8, w), F32),
            ta=((8, w), F32),
            gather=((16, 8, w), F32),
            tb=((8, w), F32),
        )
        | plane_work("a", by_rows(8 * rows, unit))
        | plane_work("b", by_columns(rows, width))
        | plane_work("c", by_rows(8 * rows, 2 * w))
        | plane_work("d", by_rows(8 * rows, w)),
        160,
        30,
    )

    moved = (D.result, D.gtok, D.g_in, D.g_forget, D.g_og, D.g_out, D.g_gate, D.g_up, D.g_table)
    like = [jax.ShapeDtypeStruct(m.shape, m.dtype) for m in moved]
    row = jax.ShapeDtypeStruct((1, width), F32)
    last = pl.pallas_call(
        write_body,
        name="write",
        out_shape=like + [jax.ShapeDtypeStruct((down, width), F32), row, row, row],
        in_specs=[ANY] * len(moved) + [VMEM] * 2,
        out_specs=[VMEM] * (len(moved) + 4),
        scratch_shapes=[pltpu.SemaphoreType.DMA((len(moved),))],
        compiler_params=pltpu.CompilerParams(vmem_limit_bytes=60 << 20),
    )(*moved, D.gains, C.block_ddn)
    result, grad_tokens, g_in, g_forget, g_og, g_out, g_gate, g_up, g_table, g_down = last[:10]
    attn, norm, mlp = [m[0] for m in last[10:]]
    return (
        result,
        grad_tokens,
        attn,
        g_in,
        g_forget,
        g_og,
        g_out,
        norm,
        mlp,
        g_gate,
        g_up,
        g_down,
        g_table,
    )


def solution(mesh):
    split = Mesh(mesh.devices.reshape(2, 2, 4, 4, 2), AXES)
    cut = P(AXES, None)
    return jax.shard_map(
        on_device,
        mesh=split,
        in_specs=(cut, cut, P(), cut, cut, cut, cut, P(), P(), cut, cut, cut, P(), P()),
        out_specs=(cut, cut, P(), cut, cut, cut, cut, P(), P(), cut, cut, cut, P()),
        check_vma=False,
    )
```

```python
from types import SimpleNamespace

import jax
import jax.numpy as jnp
from jax import lax
from jax.experimental import pallas as pl
from jax.experimental.pallas import tpu as pltpu
from jax.sharding import Mesh, PartitionSpec as P

EPS = 1e-06
BF = jnp.bfloat16
F32 = jnp.float32
AXES = ("xlo", "xhi", "z", "y", "core")
MESH = pl.DeviceIdType.MESH
ANY = pl.BlockSpec(memory_space=pl.ANY)
VMEM = pl.BlockSpec(memory_space=pltpu.VMEM)
STEPS = (1, 3, 2)
GROUP = [(a, b) for a in range(4) for b in range(2) if a or b]
CHAIN = [(a, b) for a in range(2) for b in range(4) if a or b]
PLANE = [(a, b) for a in range(4) for b in range(4) if a or b]
HIGH = lax.Precision.HIGHEST


def ax(name):
    return lax.axis_index(name)


def ring(axis, s):
    if axis == "x":
        x = lax.rem(ax("xhi") * 2 + ax("xlo") + s, 4)
        return {"xhi": lax.div(x, 2), "xlo": lax.rem(x, 2)}
    return {axis: lax.rem(ax(axis) + s, 4)}


def sibling():
    return {"core": 1 - ax("core")}


def in_group(s, t):
    return {"y": lax.rem(ax("y") + s, 4), "core": lax.rem(ax("core") + t, 2)}


def in_chain(s, t):
    return {"xhi": lax.rem(ax("xhi") + s, 2), "z": lax.rem(ax("z") + t, 4)}


def in_plane(s, t):
    return {**ring("x", s), **ring("z", t)}


def place():
    return ax("xlo") * 8 + ax("xhi") * 4 + ax("z"), ax("y") * 2 + ax("core")


def device(p, g):
    return {
        "xlo": lax.div(p, 8),
        "xhi": lax.rem(lax.div(p, 4), 2),
        "z": lax.rem(p, 4),
        "y": lax.div(g, 2),
        "core": lax.rem(g, 2),
    }


class Copies:
    def __init__(self, send, recv, near):
        self.sems = (send, recv, near)
        self.count = 0
        self.locals = 0
        self.open = []

    def remote(self, src, dst, dev):
        i = self.count
        self.count += 1
        assert i < self.sems[0].shape[0]
        return pltpu.make_async_remote_copy(
            src_ref=src,
            dst_ref=dst,
            send_sem=self.sems[0].at[i],
            recv_sem=self.sems[1].at[i],
            device_id=dev,
            device_id_type=MESH,
        )

    def send(self, src, dst, dev):
        copy = self.remote(src, dst, dev)
        copy.start()
        self.open.append(copy)
        return copy

    def near(self, src, dst):
        i = self.locals
        self.locals += 1
        assert i < self.sems[2].shape[0]
        return pltpu.make_async_copy(src, dst, self.sems[2].at[i])

    def local(self, src, dst):
        copy = self.near(src, dst)
        copy.start()
        return copy

    def sent(self, copies):
        for copy in copies:
            copy.wait_send()
        gone = {id(copy) for copy in copies}
        self.open = [copy for copy in self.open if id(copy) not in gone]

    def finish(self):
        for copy in self.open:
            copy.wait_send()


def hail(peers, shuffle=None):
    bar = pltpu.get_barrier_semaphore()
    for dev in peers:
        pl.semaphore_signal(bar, inc=1, device_id=dev, device_id_type=MESH)
    count = len(peers)
    if shuffle is not None:
        source, from_me, to_me = shuffle

        @pl.when(jnp.logical_not(from_me))
        def _():
            pl.semaphore_signal(bar, inc=1, device_id=source, device_id_type=MESH)

        count = count + jnp.where(to_me, 0, 1)
    return lambda: pl.semaphore_wait(bar, count)


def greet(peers):
    hail(peers)()


def to_group(cp, source, dst):
    g = place()[1]
    there = dst(g)
    copies = []
    for st in GROUP:
        q = in_group(*st)
        copies.append(cp.send(source(q["y"] * 2 + q["core"]), there, q))
    return copies, cp.local(source(g), there)


def settle(copies, home):
    for copy in copies:
        copy.wait_recv()
    home.wait()


class Shuffle:
    def __init__(self, outward):
        p, g = place()
        self.d = p * 8 + g
        row = 16 * g + p
        there = (lax.rem(self.d, 16), lax.div(self.d, 16))
        here = (lax.div(row, 8), lax.rem(row, 8))
        to, come = (there, here) if outward else (here, there)
        self.to = to
        self.target, self.source = device(*to), device(*come)
        self.to_me = to[0] * 8 + to[1] == self.d
        self.from_me = come[0] * 8 + come[1] == self.d
        self.greeting = (self.source, self.from_me, self.to_me)

    def start(self, cp, src, dst):
        copy = cp.remote(src, dst, self.target)
        home = cp.near(src, dst)

        @pl.when(self.to_me)
        def _():
            home.start()

        @pl.when(jnp.logical_not(self.to_me))
        def _():
            copy.start()

        return copy, home

    def wait(self, pair):
        @pl.when(self.to_me)
        def _():
            pair[1].wait()

        @pl.when(jnp.logical_not(self.to_me))
        def _():
            pair[0].wait()


def rings():
    return [ring("x", s) for s in STEPS] + [ring("z", s) for s in STEPS]


def ys():
    return [ring("y", s) for s in STEPS] + [sibling()]


def run(chains, order):
    for i in order:
        next(chains[i], None)
    for chain in chains:
        for _ in chain:
            pass


def rows_of(i, n=16):
    return pl.ds(pl.multiple_of(i * n, n), n)


def block_of(k):
    return rows_of(k, 128)


class GroupGather:
    def __init__(self, cp, src, full):
        self.cp, self.full = cp, full
        k = place()[1]
        self.half = {}
        for first in (0, 1):
            for s in (1, 3):
                h = first if s == 1 else 1 - first
                self.half[s, h] = cp.send(
                    src.at[pl.ds(64 * h, 64)], full.at[self.rows(k, h)], ring("y", s)
                )
        self.near = {0: cp.send(src, full.at[block_of(k)], sibling())}
        self.done = set()

    def rows(self, k, h):
        return pl.ds(pl.multiple_of(k * 128 + 64 * h, 64), 64)

    def chip(self, s):
        return 2 * lax.rem(ax("y") + 4 - s, 4) + ax("core")

    def arrived(self, s, h):
        if (s, h) not in self.done:
            self.done.add((s, h))
            self.half[s, h].wait_recv()

    def relay(self):
        for s, h in ((1, 0), (3, 1)):
            self.arrived(s, h)
            at = self.full.at[self.rows(self.chip(s), h)]
            self.half[2, h] = self.cp.send(at, at, ring("y", s))

    def forward(self, s):
        if (2, 0) not in self.half:
            self.relay()
        self.arrived(s, 0)
        self.arrived(s, 1)
        at = self.full.at[block_of(self.chip(s))]
        self.near[s] = self.cp.send(at, at, sibling())

    def ready(self, s):
        self.near[s].wait_recv()

    def rest(self):
        for s in STEPS:
            if s not in self.near:
                self.forward(s)
        for s in (0, 1, 3, 2):
            self.ready(s)


class GroupSum:
    def __init__(self, cp, near, far):
        self.cp, self.near, self.far = cp, near, far
        self.sent, self.moved = {}, {}

    def chip(self, s):
        return 2 * lax.rem(ax("y") + s, 4)

    def give(self, s, src):
        self.sent[s] = self.cp.send(src, self.near.at[s], sibling())

    def add(self, s, mine, at):
        near = self.near
        self.sent[s].wait_recv()

        def step(i, carry):
            r = rows_of(i)
            to = pl.ds(pl.multiple_of(at + i * 16, 16), 16)
            mine[to, :] = (mine[to, :].astype(F32) + near[s, r, :].astype(F32)).astype(BF)
            return carry

        lax.fori_loop(0, 8, step, 0)
        here = mine.at[pl.ds(pl.multiple_of(at, 128), 128)]
        self.moved[s] = self.cp.send(here, self.far.at[s - 1], ring("y", s))

    def total(self, mine, at):
        self.sent[0].wait_recv()
        for s in STEPS:
            self.moved[s].wait_recv()
        self.cp.sent(list(self.moved.values()))
        near, far = self.near, self.far

        def rows(i):
            r = rows_of(i)
            own = mine[pl.ds(pl.multiple_of(at + i * 16, 16), 16), :]
            acc = own.astype(F32) + near[0, r, :].astype(F32)
            for s in range(3):
                acc = acc + far[s, r, :].astype(F32)
            return acc

        return rows


class RelaySum(GroupSum):
    def piece(self, mine, at, h):
        return mine.at[pl.ds(pl.multiple_of(at + 64 * h, 64), 64)]

    def plus(self, mine, at, term, n):
        def step(i, carry):
            to = pl.ds(pl.multiple_of(at + i * 16, 16), 16)
            mine[to, :] = (mine[to, :].astype(F32) + term(rows_of(i)).astype(F32)).astype(BF)
            return carry

        lax.fori_loop(0, n // 16, step, 0)

    def to(self, s, slot, h, mine, at):
        return self.cp.send(
            self.piece(mine, at, h), self.far.at[slot, pl.ds(64 * h, 64)], ring("y", s)
        )

    def add(self, s, mine, at):
        near = self.near
        self.sent[s].wait_recv()
        self.plus(mine, at, lambda r: near[s, r, :], 128)
        if s == 2:
            self.hop = [self.to(1, 2, 0, mine, at), self.to(3, 2, 1, mine, at)]
        elif s == 1:
            self.moved[1, 1] = self.to(1, 0, 1, mine, at)
        else:
            self.moved[3, 0] = self.to(3, 1, 0, mine, at)

    def relay(self, mine, at_next, at_last):
        far = self.far
        self.hop[0].wait_recv()
        self.plus(mine, at_next, lambda r: far[2, r, :], 64)
        self.moved[1, 0] = self.to(1, 0, 0, mine, at_next)
        self.hop[1].wait_recv()
        up = lambda r: far[2, pl.ds(pl.multiple_of(64 + r.start, 16), 16), :]
        self.plus(mine, at_last + 64, up, 64)
        self.moved[3, 1] = self.to(3, 1, 1, mine, at_last)

    def total(self, mine, at):
        self.sent[0].wait_recv()
        for key in ((1, 1), (3, 0), (1, 0), (3, 1)):
            self.moved[key].wait_recv()
        self.cp.sent(self.hop + list(self.moved.values()))
        near, far = self.near, self.far

        def rows(i):
            r = rows_of(i)
            own = mine[pl.ds(pl.multiple_of(at + i * 16, 16), 16), :]
            acc = own.astype(F32) + near[0, r, :].astype(F32)
            return acc + (far[0, r, :].astype(F32) + far[1, r, :].astype(F32))

        return rows


def sum_of(cp, part, mine, near, far):
    total = RelaySum(cp, near, far)
    c = ax("core")
    own = {}
    for s in (2, 1, 3, 0):
        total.give(s, part.at[block_of(total.chip(s) + 1 - c)])
        own[s] = cp.local(part.at[block_of(total.chip(s) + c)], mine.at[pl.ds(128 * s, 128)])
    yield
    for s in (2, 1, 3):
        own[s].wait()
        total.add(s, mine, 128 * s)
    own[0].wait()
    yield
    total.relay(mine, 128, 384)
    yield
    yield total.total(mine, 0)


def plane_gather(cp, buf, halves, block=None):
    me = (ax("xlo"), ax("xhi"), ax("z"))
    home = None if block is None else cp.local(block, buf.at[me])

    def view(h, *at):
        return buf.at[at + halves[h]]

    mine = [view(h, *me) if block is None else block.at[halves[h]] for h in range(2)]
    first = []
    for s in STEPS:
        first.append(cp.send(mine[0], view(0, *me), ring("z", s)))
        first.append(cp.send(mine[1], view(1, *me), ring("x", s)))
    yield
    if home is not None:
        home.wait()
    for copy in first:
        copy.wait_recv()
    column = view(0, me[0], me[1], pl.ds(0, 4))
    row = view(1, pl.ds(0, 2), pl.ds(0, 2), me[2])
    wide = {}
    for s in (1, 3):
        wide["x", s] = cp.send(column, column, ring("x", s))
        wide["z", s] = cp.send(row, row, ring("z", s))
    yield
    last = []
    for s in (1, 3):
        back = ring("x", 4 - s)
        wide["x", s].wait_recv()
        v = view(0, back["xlo"], back["xhi"], pl.ds(0 if s == 1 else 2, 2))
        last.append(cp.send(v, v, ring("x", s)))
        back = ring("z", 4 - s)
        wide["z", s].wait_recv()
        v = view(1, 0 if s == 1 else 1, pl.ds(0, 2), back["z"])
        last.append(cp.send(v, v, ring("z", s)))
    yield
    for copy in last:
        copy.wait_recv()


def plane_first(cp, block, column, row, halves):
    me = (ax("xlo"), ax("xhi"), ax("z"))
    top, bottom = [block.at[h] for h in halves]
    home = [cp.local(top, column.at[me[2]]), cp.local(bottom, row.at[me[0], me[1]])]
    first = []
    for s in STEPS:
        first.append(cp.send(top, column.at[me[2]], ring("z", s)))
        first.append(cp.send(bottom, row.at[me[0], me[1]], ring("x", s)))
    yield
    for copy in first:
        copy.wait_recv()
    for copy in home:
        copy.wait()


def plane_second(cp, column, row, buf, halves):
    me = (ax("xlo"), ax("xhi"), ax("z"))

    def view(h, *at):
        return buf.at[at + halves[h]]

    here = view(0, me[0], me[1], pl.ds(0, 4))
    across = view(1, pl.ds(0, 2), pl.ds(0, 2), me[2])
    home = [cp.local(column, here), cp.local(row, across)]
    wide = {}
    for s in (1, 3):
        wide["x", s] = cp.send(column, here, ring("x", s))
        wide["z", s] = cp.send(row, across, ring("z", s))
    yield
    last = []
    for s in (1, 3):
        back = ring("x", 4 - s)
        wide["x", s].wait_recv()
        v = view(0, back["xlo"], back["xhi"], pl.ds(0 if s == 1 else 2, 2))
        last.append(cp.send(v, v, ring("x", s)))
        back = ring("z", 4 - s)
        wide["z", s].wait_recv()
        v = view(1, 0 if s == 1 else 1, pl.ds(0, 2), back["z"])
        last.append(cp.send(v, v, ring("z", s)))
    yield
    for copy in last:
        copy.wait_recv()
    for copy in home:
        copy.wait()


def half_shapes(halves):
    return [tuple(d.size for d in h) for h in halves]


def plane_sum_scratch(halves):
    a, b = half_shapes(halves)
    return [
        pltpu.VMEM((4,) + a, BF),
        pltpu.VMEM((3, 4) + a, BF),
        pltpu.VMEM((3,) + a, BF),
        pltpu.VMEM((2, 2) + b, BF),
        pltpu.VMEM((3, 2, 2) + b, BF),
        pltpu.VMEM((3,) + b, BF),
    ]


def plane_sum(cp, part, halves, own_a, far_a, last_a, own_b, far_b, last_b, out):
    me = (ax("xlo"), ax("xhi"), ax("z"))
    shape_a, shape_b = half_shapes(halves)

    def view(h, *at):
        return part.at[at + halves[h]]

    near_a = cp.local(view(0, me[0], me[1], pl.ds(0, 4)), own_a)
    near_b = cp.local(view(1, pl.ds(0, 2), pl.ds(0, 2), me[2]), own_b)
    first_a, first_b = [], []
    for j, s in enumerate(STEPS):
        d = ring("x", s)
        first_a.append(cp.send(view(0, d["xlo"], d["xhi"], pl.ds(0, 4)), far_a.at[j], d))
        d = ring("z", s)
        first_b.append(cp.send(view(1, pl.ds(0, 2), pl.ds(0, 2), d["z"]), far_b.at[j], d))
    yield
    near_a.wait()
    for copy in first_a:
        copy.wait_recv()
    for k in range(4):

        def add(i, carry, k=k):
            r = rows_of(i)
            acc = own_a[k, r, :].astype(F32)
            for j in range(3):
                acc = acc + far_a[j, k, r, :].astype(F32)
            own_a[k, r, :] = acc.astype(BF)
            return carry

        lax.fori_loop(0, shape_a[0] // 16, add, 0)
    second = []
    for j, s in enumerate(STEPS):
        d = ring("z", s)
        second.append(cp.send(own_a.at[d["z"]], last_a.at[j], d))
    near_b.wait()
    for copy in first_b:
        copy.wait_recv()
    for k in range(4):

        def add(i, carry, k=k):
            r = rows_of(i)
            acc = own_b[k // 2, k % 2, r, :].astype(F32)
            for j in range(3):
                acc = acc + far_b[j, k // 2, k % 2, r, :].astype(F32)
            own_b[k // 2, k % 2, r, :] = acc.astype(BF)
            return carry

        lax.fori_loop(0, shape_b[0] // 16, add, 0)
    for j, s in enumerate(STEPS):
        d = ring("x", s)
        second.append(cp.send(own_b.at[d["xlo"], d["xhi"]], last_b.at[j], d))
    yield
    for copy in second:
        copy.wait_recv()

    def end_a(i, carry):
        r = rows_of(i)
        acc = own_a[me[2], r, :].astype(F32)
        for j in range(3):
            acc = acc + last_a[j, r, :].astype(F32)
        at = rows_of(i) if halves[0][0].start == 0 else pl.ds(halves[0][0].start + i * 16, 16)
        out[at, halves[0][1]] = acc.astype(BF)
        return carry

    lax.fori_loop(0, shape_a[0] // 16, end_a, 0)

    def end_b(i, carry):
        r = rows_of(i)
        acc = own_b[me[0], me[1], r, :].astype(F32)
        for j in range(3):
            acc = acc + last_b[j, r, :].astype(F32)
        at = pl.ds(pl.multiple_of(halves[1][0].start + i * 16, 16), 16)
        out[at, halves[1][1]] = acc.astype(BF)
        return carry

    lax.fori_loop(0, shape_b[0] // 16, end_b, 0)


def by_rows(rows, width):
    h = rows // 2
    return ((pl.ds(0, h), pl.ds(0, width)), (pl.ds(h, h), pl.ds(0, width)))


def by_columns(rows, width):
    h = width // 2
    return ((pl.ds(0, rows), pl.ds(0, h)), (pl.ds(0, rows), pl.ds(h, h)))


def scratch(**kw):
    return {k: pltpu.VMEM(*v) for k, v in kw.items()}


def call(body, name, ident, ins, outs, work, sems, near):
    names = list(ins) + list(outs) + list(work)

    def run_body(*refs):
        body(SimpleNamespace(**dict(zip(names, refs[:-3]))), Copies(*refs[-3:]))

    results = pl.pallas_call(
        run_body,
        name=name,
        out_shape=[jax.ShapeDtypeStruct(*v[:2]) for v in outs.values()],
        in_specs=[v[1] for v in ins.values()],
        out_specs=[v[2] for v in outs.values()],
        scratch_shapes=list(work.values())
        + [
            pltpu.SemaphoreType.DMA((sems,)),
            pltpu.SemaphoreType.DMA((sems,)),
            pltpu.SemaphoreType.DMA((near,)),
        ],
        compiler_params=pltpu.CompilerParams(
            collective_id=ident, has_side_effects=True, vmem_limit_bytes=60 << 20
        ),
    )(*[v[0] for v in ins.values()])
    return SimpleNamespace(**dict(zip(outs, results)))


def drain(*chains):
    for chain in chains:
        for _ in chain:
            pass


NN = ((1,), (0,))
NT = ((1,), (1,))
TN = ((0,), (0,))


def dot(a, b, dims):
    return lax.dot_general(a, b, (dims, ((), ())), preferred_element_type=F32)


def spread(m, out, start, down, padded):
    x = m[...].astype(F32)
    none = jnp.zeros((m.shape[0], padded - down), F32)
    for k in range(8):
        runs = []
        for p in range(16):
            at = (8 * p + k) * down
            runs += [x[:, at : at + down], none]
        out[k, :, start : start + 16 * padded] = jnp.concatenate(runs, axis=1).astype(BF)


def unspread(m, out, down, padded):
    for k in range(8):
        for p in range(16):
            at = (8 * p + k) * down
            out[:, at : at + down] = m[k, :, padded * p : padded * p + down].astype(F32)


def gather_body(R, cp):
    g = place()[1]
    shuffle = Shuffle(True)
    meet = hail(rings() + [in_group(*st) for st in GROUP], shuffle.greeting)

    def norm(i, carry):
        r = rows_of(i)
        x = R.tok[r, :].astype(F32)
        s = lax.rsqrt(jnp.mean(x * x, axis=-1, keepdims=True) + EPS)
        R.first[r, :] = (x * s * R.gain[...]).astype(BF)
        return carry

    lax.fori_loop(0, R.tok.shape[0] // 16, norm, 0)
    last = jnp.zeros((R.dn_pad.shape[0] - R.dn.shape[0], R.dn.shape[1]), F32)
    R.dn_pad[...] = jnp.concatenate([R.dn[...].astype(F32), last], axis=0).astype(BF)
    meet()
    me = (ax("xlo"), ax("xhi"), ax("z"))
    third = R.w_in.shape[1] // 8
    arrive = []
    for j, w in enumerate((R.w_in, R.w_f, R.w_og)):
        arrive.append(
            to_group(
                cp,
                lambda k, w=w: w.at[:, pl.ds(pl.multiple_of(k * third, 128), third)],
                lambda k, j=j: R.b3.at[me + (rows_of(k), pl.ds(j * third, third))],
            )
        )
    q = shuffle.to[0]
    at = (lax.div(q, 8), lax.rem(lax.div(q, 4), 2), lax.rem(q, 4))
    moved = shuffle.start(cp, R.w_o, R.bo.at[at])
    dn = plane_first(cp, R.dn_pad, R.dn_column, R.dn_row, by_columns(*R.dn_pad.shape))
    next(dn)
    own = cp.local(R.first, R.fi.at[block_of(g)])
    chain = GroupGather(cp, R.first, R.fi)
    for pair in arrive:
        settle(*pair)
    b3 = plane_gather(cp, R.b3, by_rows(*R.b3.shape[3:]))
    next(b3)
    shuffle.wait(moved)
    bo = plane_gather(cp, R.bo, by_columns(*R.bo.shape[3:]))
    next(bo)
    next(b3)
    next(bo)
    chain.relay()
    run([b3, bo, dn], (2, 0, 1))
    chain.rest()
    own.wait()
    cp.finish()


def silu_slope(v, s):
    return s * (1.0 + v * (1.0 - s))


def row_sums(x):
    ones = jnp.ones((8, x.shape[1]), F32)
    return lax.dot_general(
        ones, x, (((1,), (1,)), ((), ())), precision=HIGH, preferred_element_type=F32
    )[0:1]


def as_column(row, width):
    t = jnp.transpose(jnp.broadcast_to(row, (128, 128)))
    return jnp.concatenate([t] * (width // 128), axis=1)


def chunk_rows(s):
    return pl.ds(pl.multiple_of(s * 128, 128), 128)


def wide(ref, r):
    return jnp.concatenate([ref[j, r, :] for j in range(ref.shape[0])], axis=1)


def put(ref, r, value):
    for j in range(ref.shape[0]):
        ref[j, r, :] = value[:, 128 * j : 128 * (j + 1)]


def share(cp, src, dst, index, peers):
    copies = [cp.send(src, dst.at[index], dev) for dev in peers]
    dst[pl.ds(index, 1)] = src[...][None]
    return copies


def levels(table, layer):
    e = jnp.exp(table - jnp.max(table, axis=0, keepdims=True))
    level = lax.broadcasted_iota(jnp.int32, table.shape, 0)
    counts = jnp.where((level >= 1) & (level <= layer), 1.0, 0.0)
    return e / jnp.sum(e, axis=0, keepdims=True), counts


def links_before(links, k, w):
    come = jnp.zeros((1, w), F32)
    for j in range(8):
        new = links[j, 0:1, :] * come + links[j, 1:2, :]
        come = jnp.where(j < k, new, come)
    return come


def scan_body(R, cp):
    tiles, rows = R.states.shape[:2]
    w = 128 * tiles
    steps = rows // 8
    peers_chain = [in_chain(*st) for st in CHAIN]
    peers_group = [in_group(*st) for st in GROUP]
    load = [cp.local(R.b3, R.w3), cp.local(R.fi, R.x)]
    load_out = cp.local(R.bo, R.wo)
    meet = hail(peers_chain + peers_group + [ring("x", s) for s in (1, 3)])
    mine = rows_of(place()[1], w)
    prob, keep_mask = levels(R.table[:, mine], R.layer[...])
    low = jnp.sum(prob * keep_mask, axis=0, keepdims=True)
    R.lb[...] = jnp.broadcast_to(low, (8, w))
    gain = R.gain[:, mine]
    unit = R.gu.shape[2] // 2
    down = R.w_gate.shape[1] // 128
    spread(R.w_gate, R.gu, 0, down, unit // 16)
    spread(R.w_up, R.gu, unit, down, unit // 16)
    meet()
    arrive_gu = to_group(cp, lambda k: R.gu.at[k], lambda k: R.block_gu.at[rows_of(k), :])
    own = cp.local(R.cot, R.gf.at[block_of(place()[1])])
    bulk = plane_second(cp, R.dn_column, R.dn_row, R.bdn, by_columns(*R.bdn.shape[3:]))
    next(bulk)
    chain = GroupGather(cp, R.cot, R.gf)
    for copy in load:
        copy.wait()

    def project(j):
        for i in range(2):
            r = pl.ds(i * rows // 2, rows // 2)
            at = pl.ds(j * w, w)
            R.proj[r, at] = dot(R.x[r, :], R.w3[:, at], NN)

    project(0)
    project(1)
    settle(*arrive_gu)
    gate_up = plane_first(cp, R.block_gu, R.gu_column, R.gu_row, by_rows(*R.block_gu.shape))
    next(gate_up)
    next(bulk)
    chain.relay()

    def gates(i, c):
        r = rows_of(i, 32)
        f = low + (1.0 - low) * jax.nn.sigmoid(R.proj[r, w : 2 * w])
        v = R.proj[r, 0:w]
        put(R.forget, r, f)
        put(R.states, r, v * jax.nn.sigmoid(v) * (1.0 - f))
        return c

    lax.fori_loop(0, rows // 32, gates, 0)
    keep = [cp.local(R.forget, R.forget_out)]

    def step(t, c):
        at = pl.ds(t, 8, stride=steps)
        new = []
        for j, (h, a) in enumerate(c):
            f = R.forget[j, at, :]
            h = f * h + R.states[j, at, :]
            a = a * f
            R.states[j, at, :] = h
            R.prod[j, at, :] = a
            new.append((h, a))
        return tuple(new)

    start = ((jnp.zeros((8, 128), F32), jnp.ones((8, 128), F32)),) * tiles
    ends = lax.fori_loop(0, steps, step, start, unroll=8)
    h = jnp.concatenate([e[0] for e in ends], axis=1)
    a = jnp.concatenate([e[1] for e in ends], axis=1)
    c = jnp.zeros((1, w), F32)
    q = jnp.ones((1, w), F32)
    cs, qs = [], []
    for s in range(8):
        cs.append(c)
        qs.append(q)
        c = a[s : s + 1] * c + h[s : s + 1]
        q = a[s : s + 1] * q
    R.mine[...] = jnp.concatenate([q, c, jnp.zeros((6, w), F32)], axis=0)
    k = ax("xhi") * 4 + ax("z")
    small = share(cp, R.mine, R.links, k, peers_chain)
    project(2)
    keep.append(cp.local(R.proj, R.proj_out))
    for copy in small:
        copy.wait_recv()
    come = links_before(R.links, k, w)
    R.carry[...] = jnp.broadcast_to(come, (8, w))
    R.entry[...] = jnp.concatenate(qs, axis=0) * come + jnp.concatenate(cs, axis=0)

    def finish(s, c):
        r = chunk_rows(s)
        st = wide(R.states, r) + wide(R.prod, r) * R.entry[pl.ds(s, 1), :]
        put(R.states, r, st)
        R.rowsum[pl.ds(s, 1), :] = row_sums(st * st)
        return c

    lax.fori_loop(0, 8, finish, 0)
    keep.append(cp.local(R.states, R.states_out))
    small = share(cp, R.rowsum, R.rows8, place()[1], peers_group)
    for copy in small:
        copy.wait_recv()
    total = R.rows8[0]
    for j in range(1, 8):
        total = total + R.rows8[j]
    R.tot[...] = lax.rsqrt(total / (8.0 * w) + EPS)

    def gate(s, c):
        r = chunk_rows(s)
        v = R.proj[r, 2 * w : 3 * w]
        n = wide(R.states, r) * as_column(R.tot[pl.ds(s, 1), :], w)
        R.gated[r, :] = (n * gain * (v * jax.nn.sigmoid(v))).astype(BF)
        return c

    lax.fori_loop(0, 8, gate, 0)
    keep.append(cp.local(R.gated, R.gated_out))
    load_out.wait()
    for i in range(4):
        r = pl.ds(i * rows // 4, rows // 4)

        def out(j, c, r=r):
            at = rows_of(j, 512)
            R.part[r, at] = dot(R.gated[r, :], R.wo[:, at], NN).astype(BF)
            return c

        lax.fori_loop(0, R.part.shape[1] // 512, out, 0)
        keep.append(cp.local(R.part.at[r], R.part_out.at[r]))
    chain.rest()
    for copy in keep:
        copy.wait()
    own.wait()
    drain(bulk, gate_up)
    cp.finish()


def feed_body(R, cp):
    y, c = ax("y"), ax("core")
    g = place()[1]
    unit, width = R.wdn.shape
    greet(ys() + rings())
    weights = plane_second(cp, R.gu_column, R.gu_row, R.wgu, by_rows(*R.wgu.shape[3:]))
    next(weights)
    mixer = sum_of(cp, R.part, R.ps, R.near, R.far)
    next(mixer)
    load = [cp.local(R.gf, R.g), cp.local(R.bdn, R.wdn)]
    next(mixer)
    next(mixer)
    next(weights)
    terms = next(mixer)

    def norm(i, carry):
        r = rows_of(i)
        x = R.tok[r, :].astype(F32) + terms(i)
        R.mid[r, :] = x
        s = lax.rsqrt(jnp.mean(x * x, axis=-1, keepdims=True) + EPS)
        R.si[rows_of(g * 8 + i), :] = (x * s * R.gain[...]).astype(BF)
        return carry

    lax.fori_loop(0, 8, norm, 0)
    gather = GroupGather(cp, R.si.at[block_of(g)], R.si)
    second = GroupSum(cp, R.near, R.far)
    for copy in load:
        copy.wait()
    drain(weights)
    order = (0, 1, 3, 2)
    stores = []

    def forward(yy):
        r = rows_of(yy, 256)

        def tile(j, carry):
            at = rows_of(j, 256)
            up = pl.ds(pl.multiple_of(unit + j * 256, 256), 256)
            x = R.si[r, :]
            v = dot(x, R.wgu[:, :, :, :, at].reshape(width, 256), NN)
            u = dot(x, R.wgu[:, :, :, :, up].reshape(width, 256), NN)
            gh = dot(R.g[r, :], R.wdn[at, :], NT)
            sig = jax.nn.sigmoid(v)
            act = v * sig
            R.hid[r, at] = (act * u).astype(BF)
            R.ggu[r, at] = (gh * u * silu_slope(v, sig)).astype(BF)
            R.ggu[r, up] = (gh * act).astype(BF)
            return carry

        lax.fori_loop(0, unit // 256, tile, 0)

    def backward(yy):
        r = rows_of(yy, 256)

        def tile(j, carry):
            at = rows_of(j, 512)
            w = R.wgu[lax.div(j, 2), lax.rem(j, 2)].reshape(512, 2 * unit)
            R.ps[r, at] = dot(R.ggu[r, :], w, NT).astype(BF)
            return carry

        lax.fori_loop(0, width // 512, tile, 0)

    def result(yy, slot):
        r = rows_of(yy, 256)

        def tile(j, carry):
            at = rows_of(j, 512)
            R.pr[slot, :, at] = dot(R.hid[r, :], R.wdn[:, at], NN).astype(BF)
            return carry

        lax.fori_loop(0, width // 512, tile, 0)
        stores.append(cp.local(R.pr.at[slot], R.part_r.at[r]))

    for i, s in enumerate(order):
        yy = lax.rem(y + 4 - s, 4)
        gather.ready(s)
        forward(yy)
        if i > 1:
            back = (4 - order[i - 1]) % 4
            second.add(back, R.ps, 128 * (second.chip(back) + c))
        backward(yy)
        second.give((4 - s) % 4, R.ps.at[block_of(2 * yy + 1 - c)])
        if i > 1:
            stores[i - 2].wait()
        result(yy, i % 2)
        for ahead in ((1, 3), (2,), (), ())[i]:
            gather.forward(ahead)
    second.add(2, R.ps, 128 * (second.chip(2) + c))

    def grad_down(j, carry):
        at = rows_of(j, 512)
        for i in range(2):
            h = unit // 2
            v = dot(R.hid[:, h * i : h * (i + 1)], R.g[:, at], TN)
            R.ddn[i, :, :, :, at] = v.astype(BF).reshape(R.ddn.shape[1:4] + (512,))
        return carry

    lax.fori_loop(0, width // 512, grad_down, 0)
    planes = [plane_sum(cp, R.ddn, by_columns(*R.ddn.shape[3:]), *plane_refs(R, "a"), R.block_ddn)]
    next(planes[0])

    def grad_gate(i, carry):
        at = rows_of(i, 256)
        v = dot(R.si[:, at], R.ggu[:, 0:unit], TN).astype(BF)
        to = (lax.div(i, 4), lax.rem(lax.div(i, 2), 2), pl.ds(2 * lax.rem(i, 2), 2))
        R.dgate[to] = v.reshape(2, 128, unit)
        return carry

    lax.fori_loop(0, width // 256, grad_gate, 0)
    planes.append(plane_sum(cp, R.dgate, by_rows(*R.dgate.shape[3:]), *plane_refs(R, "b"), R.block_dgate))
    next(planes[1])
    terms = second.total(R.ps, 128 * g)
    R.sums[...] = jnp.zeros_like(R.sums)

    def back(i, carry):
        r = rows_of(i)
        x = R.mid[r, :]
        s = lax.rsqrt(jnp.mean(x * x, axis=-1, keepdims=True) + EPS)
        n = x * s
        dy = terms(i)
        R.sums[0:1, :] = R.sums[0:1, :] + jnp.sum(dy * n, axis=0, keepdims=True)
        dy = dy * R.gain[...]
        v = R.cot[r, :].astype(F32) + s * (dy - n * jnp.mean(dy * n, axis=-1, keepdims=True))
        R.mixed[r, :] = v
        R.block[r, :] = v.astype(BF)
        return carry

    lax.fori_loop(0, 8, back, 0)
    own = cp.local(R.block, R.gb.at[block_of(g)])
    branch = GroupGather(cp, R.block, R.gb)
    ups = []
    for copy in stores[2:]:
        copy.wait()

    def grad_up(i):
        at = pl.ds(i * 256, 256)
        v = dot(R.si[:, at], R.ggu[:, unit : 2 * unit], TN).astype(BF)
        if i > 1:
            ups[i - 2].wait()
        R.pu[i % 2] = v
        ups.append(cp.local(R.pu.at[i % 2], R.dup.at[at]))

    for i in range(width // 256):
        grad_up(i)
    branch.relay()
    for copy in ups[-2:]:
        copy.wait()
    next(planes[0])
    branch.forward(1)
    branch.forward(3)
    next(planes[1])
    branch.rest()
    own.wait()
    drain(*planes)
    cp.finish()


def plane_refs(R, key):
    return [getattr(R, "plane_" + key + str(i)) for i in range(6)]


def plane_work(key, halves):
    return {"plane_" + key + str(i): v for i, v in enumerate(plane_sum_scratch(halves))}


def grad_weights(R, start, dst):
    n = dst.shape[4]

    def tile(i, carry):
        at = rows_of(i, 256)
        v = dot(R.x[:, at], R.grads[:, start : start + n], TN).astype(BF)
        to = (lax.div(i, 4), lax.rem(lax.div(i, 2), 2), pl.ds(2 * lax.rem(i, 2), 2))
        dst[to] = v.reshape(2, 128, n)
        return carry

    lax.fori_loop(0, R.x.shape[1] // 256, tile, 0)


def back_body(R, cp):
    c = ax("core")
    p, g = place()
    tiles, rows = R.states.shape[:2]
    w = 128 * tiles
    steps = rows // 8
    width = R.tok.shape[1]
    shuffle = Shuffle(False)
    peers_chain = [in_chain(*st) for st in CHAIN]
    peers_group = [in_group(*st) for st in GROUP]
    peers_plane = [in_plane(*st) for st in PLANE]
    load = [cp.local(R.gb, R.gbv), cp.local(R.bo, R.wo)]
    load_scan = [
        cp.local(R.states_in, R.states),
        cp.local(R.proj_in, R.proj),
        cp.local(R.forget_in, R.forget),
        cp.local(R.gated_in, R.gated),
    ]
    load_x = cp.local(R.fi, R.x)
    load_last = [cp.local(R.b3, R.w3), cp.local(R.mid_in, R.mid), cp.local(R.mixed_in, R.mixed)]
    hail(peers_plane + peers_group, shuffle.greeting)()
    gain = R.gain[:, rows_of(g, w)]
    res = sum_of(cp, R.part_r, R.pr, R.pr_near, R.pr_far)
    next(res)
    up = plane_sum(cp, R.dup, by_rows(*R.dup.shape[3:]), *plane_refs(R, "a"), R.block_dup)
    next(up)
    low = R.lb[0:1, :]
    R.sums[...] = jnp.zeros_like(R.sums)
    gate_home = to_group(cp, lambda k: R.block_dgate.at[rows_of(k), :], lambda k: R.rgate.at[k])
    for copy in load:
        copy.wait()
    for i in range(2):
        r = pl.ds(i * rows // 2, rows // 2)
        R.gg[r, :] = dot(R.gbv[r, :], R.wo[...], NT)
    next(res)
    for copy in load_scan:
        copy.wait()

    def through(s, carry):
        r = chunk_rows(s)
        v = R.proj[r, 2 * w : 3 * w]
        sig = jax.nn.sigmoid(v)
        n = wide(R.states, r) * as_column(R.tot[pl.ds(s, 1), :], w)
        dy = R.gg[r, :]
        R.sums[0:1, :] = R.sums[0:1, :] + jnp.sum(dy * n * (v * sig), axis=0, keepdims=True)
        R.grads[r, 2 * w : 3 * w] = (dy * n * gain * silu_slope(v, sig)).astype(BF)
        dy = dy * gain * (v * sig)
        put(R.gs, r, dy)
        R.rowsum[pl.ds(s, 1), :] = row_sums(dy * n)
        return carry

    lax.fori_loop(0, 8, through, 0)
    small = share(cp, R.rowsum, R.rows8, g, peers_group)
    next(res)
    def grad_out(j, carry):
        at = rows_of(j, 512)
        v = dot(R.gated[...], R.gbv[:, at], TN).astype(BF)
        R.do[:, :, :, :, at] = v.reshape(R.do.shape[:4] + (512,))
        return carry

    lax.fori_loop(0, width // 512, grad_out, 0)
    outs = plane_sum(cp, R.do, by_columns(*R.do.shape[3:]), *plane_refs(R, "b"), R.oo)
    next(outs)
    for copy in small:
        copy.wait_recv()
    total = R.rows8[0]
    for j in range(1, 8):
        total = total + R.rows8[j]
    cp.sent(small)
    R.rowsum[...] = total / (8.0 * w)

    def norm(s, carry):
        r = chunk_rows(s)
        t = as_column(R.tot[pl.ds(s, 1), :], w)
        m = as_column(R.rowsum[pl.ds(s, 1), :], w)
        put(R.gs, r, t * (wide(R.gs, r) - wide(R.states, r) * t * m))
        return carry

    lax.fori_loop(0, 8, norm, 0)

    def step(i, carry):
        at = pl.ds(steps - 1 - i, 8, stride=steps)
        new = []
        for j, (h, a) in enumerate(carry):
            f = R.forget[j, at, :]
            v = R.gs[j, at, :] + h
            R.gs[j, at, :] = v
            R.prod[j, at, :] = a
            new.append((f * v, a * f))
        return tuple(new)

    start = ((jnp.zeros((8, 128), F32), jnp.ones((8, 128), F32)),) * tiles
    ends = lax.fori_loop(0, steps, step, start, unroll=8)
    h = jnp.concatenate([e[0] for e in ends], axis=1)
    a = jnp.concatenate([e[1] for e in ends], axis=1)
    e = jnp.zeros((1, w), F32)
    q = jnp.ones((1, w), F32)
    cs, qs = [None] * 8, [None] * 8
    for s in range(7, -1, -1):
        cs[s] = e
        qs[s] = q
        e = a[s : s + 1] * e + h[s : s + 1]
        q = a[s : s + 1] * q
    R.mine[...] = jnp.broadcast_to(e, (8, w))
    k = ax("xhi") * 4 + ax("z")
    small = share(cp, R.mine, R.chain, k, peers_chain)
    load_x.wait()
    grad_weights(R, 2 * w, R.d1)
    one = plane_sum(cp, R.d1, by_rows(*R.d1.shape[3:]), *plane_refs(R, "d"), R.o1)
    next(one)
    next(up)
    next(outs)
    for copy in small:
        copy.wait_recv()
    come = jnp.zeros((1, w), F32)
    for j in range(7, -1, -1):
        new = R.links[j, 0:1, :] * come + R.chain[j, 0:1, :]
        come = jnp.where(j > k, new, come)
    R.entry[...] = jnp.concatenate(qs, axis=0) * come + jnp.concatenate(cs, axis=0)

    def last(s, carry):
        r = chunk_rows(s)
        v = wide(R.gs, r) + wide(R.prod, r) * R.entry[pl.ds(s, 1), :]
        st = wide(R.states, r)
        above = pl.ds(jnp.maximum(s * 128 - 1, 0), 1)
        before = jnp.where(s == 0, R.carry[0:1, :], wide(R.states, above))
        top = lax.broadcasted_iota(jnp.int32, (128, w), 0) == 0
        prev = jnp.where(top, before, pltpu.roll(st, 1, 0))
        x = R.proj[r, 0:w]
        sx = jax.nn.sigmoid(x)
        f = wide(R.forget, r)
        sf = jax.nn.sigmoid(R.proj[r, w : 2 * w])
        gf = v * (prev - x * sx)
        R.grads[r, 0:w] = (v * (1.0 - f) * silu_slope(x, sx)).astype(BF)
        R.grads[r, w : 2 * w] = (gf * (1.0 - low) * sf * (1.0 - sf)).astype(BF)
        R.sums[1:2, :] = R.sums[1:2, :] + jnp.sum(gf * (1.0 - sf), axis=0, keepdims=True)
        return carry

    lax.fori_loop(0, 8, last, 0)
    for copy in load_last:
        copy.wait()
    R.va[...] = jnp.zeros_like(R.va)
    R.va[1:2, :] = R.ffn_sums[0:1, :]
    first = RelaySum(cp, R.near, R.far)
    order = (2, 1, 3, 0)
    for i, s in enumerate(order):
        chip = first.chip(s)
        r = pl.ds(pl.multiple_of(chip * 128, 256), 256)

        def tile(j, carry, r=r):
            at = rows_of(j, 512)
            v = dot(R.grads[r, :], R.w3[at, :], NT)
            R.va[0:1, at] = R.va[0:1, at] + jnp.sum(
                v * (R.x[r, at].astype(F32) / R.attn_gain[:, at]), axis=0, keepdims=True
            )
            R.fp[r, at] = v.astype(BF)
            return carry

        lax.fori_loop(0, width // 512, tile, 0)
        first.give(s, R.fp.at[block_of(chip + 1 - c)])
        if i > 0:
            back = order[i - 1]
            first.add(back, R.fp, 128 * (first.chip(back) + c))
    grad_weights(R, 0, R.d2)
    two = plane_sum(cp, R.d2, by_rows(*R.d2.shape[3:]), *plane_refs(R, "c"), R.o2)
    next(two)
    next(one)
    first.relay(R.fp, 128 * (first.chip(1) + c), 128 * (first.chip(3) + c))

    gains = []
    for st in GROUP:
        dev = in_group(*st)
        k = dev["y"] * 2 + dev["core"]
        gains.append(cp.send(R.va.at[:, rows_of(k, w)], R.ga.at[g], dev))
    R.ga[pl.ds(g, 1)] = R.va[:, rows_of(g, w)][None]

    drain(up, outs, one)
    arrive = [
        gate_home,
        to_group(cp, lambda k: R.o1.at[rows_of(k), :], lambda k: R.r1.at[k]),
        to_group(cp, lambda k: R.block_dup.at[rows_of(k), :], lambda k: R.rup.at[k]),
    ]
    moved = shuffle.start(cp, R.oo, R.ro)
    for copy in gains:
        copy.wait_recv()
    acc = R.ga[0]
    for j in range(1, 8):
        acc = acc + R.ga[j]
    R.ta[...] = acc
    R.ta[2:4, :] = R.sums[0:2, :]
    for copy in share(cp, R.ta, R.gather, p, peers_plane):
        copy.wait_recv()
    acc = R.gather[0]
    for j in range(1, 16):
        acc = acc + R.gather[j]
    R.tb[...] = acc
    terms = next(res)

    def finish_result(i, carry):
        r = rows_of(i)
        R.result[r, :] = (R.mid[r, :] + terms(i)).astype(BF)
        return carry

    lax.fori_loop(0, 8, finish_result, 0)
    small = share(cp, R.tb, R.totals, g, peers_group)
    next(two)
    terms_first = first.total(R.fp, 128 * g)

    def back(i, carry):
        r = rows_of(i)
        x = R.tok[r, :].astype(F32)
        s = lax.rsqrt(jnp.mean(x * x, axis=-1, keepdims=True) + EPS)
        n = x * s
        dy = terms_first(i)
        dy = dy * R.attn_gain[...]
        R.gtok[r, :] = R.mixed[r, :] + s * (dy - n * jnp.mean(dy * n, axis=-1, keepdims=True))
        return carry

    lax.fori_loop(0, 8, back, 0)
    for pair in arrive:
        settle(*pair)
    unit = R.rgate.shape[2]
    down = R.g_gate.shape[1] // 128
    unspread(R.rgate, R.g_gate, down, unit // 16)
    unspread(R.rup, R.g_up, down, unit // 16)
    for copy in small:
        copy.wait_recv()
    for j in range(8):
        at = pl.ds(j * w, w)
        R.gains[:, at] = R.totals[j]
        R.g_og[:, at] = R.r1[j].astype(F32)
    prob, counts = levels(R.table[...], R.layer[...])
    bound = jnp.sum(prob * counts, axis=0, keepdims=True)
    R.g_table[...] = R.gains[3:4, :] * prob * (counts - bound)
    shuffle.wait(moved)
    R.g_out[...] = R.ro[...].astype(F32)
    drain(two)
    settle(*to_group(cp, lambda k: R.o2.at[rows_of(k), :], lambda k: R.r2.at[k]))
    for j in range(8):
        at = pl.ds(j * w, w)
        R.g_in[:, at] = R.r2[j, :, 0:w].astype(F32)
        R.g_forget[:, at] = R.r2[j, :, w : 2 * w].astype(F32)
    cp.finish()


def write_body(*refs):
    count = (len(refs) - 3) // 2
    ins, outs, sem = refs[:count], refs[count:-1], refs[-1]
    copies = []
    for i in range(count - 2):
        copies.append(pltpu.make_async_copy(ins[i], outs[i], sem.at[i]))
        copies[-1].start()
    for i, row in enumerate((0, 2, 1)):
        outs[count - 1 + i][...] = ins[count - 2][row : row + 1, :]
    outs[count - 2][...] = ins[count - 1][...].astype(F32)[0 : outs[count - 2].shape[0]]
    for copy in copies:
        copy.wait()


def on_device(
    tokens, cotangent, attn_gain, w_input, w_forget, w_outgate, w_out, norm_gain, mlp_gain, w_gate, w_up, w_down, bound_table, layer_idx
):
    n, width = tokens.shape
    rows = w_input.shape[0]
    hidden_width = w_gate.shape[1]
    down = w_down.shape[0]
    padded = -(-down // 16) * 16
    unit = 16 * padded
    w = width // 8

    gains = attn_gain[None, :]
    full = (8 * n, width)
    block = (n, width)
    gate_blocks = (2, 2, 4, 8 * rows, unit)
    A = call(
        gather_body,
        "gather",
        0,
        dict(
            tok=(tokens, VMEM),
            gain=(gains, VMEM),
            w_in=(w_input, VMEM),
            w_f=(w_forget, VMEM),
            w_og=(w_outgate, VMEM),
            w_o=(w_out, VMEM),
            dn=(w_down, VMEM),
        ),
        dict(
            b3=((2, 2, 4, 8 * rows, 3 * w), BF, ANY),
            bo=((2, 2, 4, rows, width), BF, ANY),
            fi=(full, BF, ANY),
            dn_column=((4, padded, width // 2), BF, ANY),
            dn_row=((2, 2, padded, width // 2), BF, ANY),
        ),
        scratch(first=(block, BF), dn_pad=((padded, width), BF)),
        96,
        10,
    )
    big3 = A.b3.reshape(width, 3 * w)
    big_out = A.bo.reshape(w, width)
    column = (w // 128, 8 * n, 128)
    B = call(
        scan_body,
        "scan",
        1,
        dict(
            table=(bound_table, VMEM),
            layer=(layer_idx[None, :], VMEM),
            gain=(norm_gain[None, :], VMEM),
            b3=(big3, ANY),
            bo=(big_out, ANY),
            fi=(A.fi, ANY),
            dn_column=(A.dn_column, VMEM),
            dn_row=(A.dn_row, VMEM),
            w_gate=(w_gate, VMEM),
            w_up=(w_up, VMEM),
            cot=(cotangent, VMEM),
        ),
        dict(
            gated_out=((8 * n, w), BF, ANY),
            states_out=(column, F32, ANY),
            forget_out=(column, F32, ANY),
            proj_out=((8 * n, 3 * w), F32, ANY),
            tot=((8, n), F32, VMEM),
            links=((8, 8, w), F32, VMEM),
            carry=((8, w), F32, VMEM),
            lb=((8, w), F32, VMEM),
            part_out=(full, BF, ANY),
            gf=(full, BF, ANY),
            bdn=((2, 2, 4, padded, width), BF, ANY),
            gu_column=((4, 4 * rows, 2 * unit), BF, ANY),
            gu_row=((2, 2, 4 * rows, 2 * unit), BF, ANY),
        ),
        scratch(
            gu=((8, rows, 2 * unit), BF),
            block_gu=((8 * rows, 2 * unit), BF),
            gated=((8 * n, w), BF),
            states=(column, F32),
            forget=(column, F32),
            proj=((8 * n, 3 * w), F32),
            part=(full, BF),
            w3=((width, 3 * w), BF),
            x=(full, BF),
            wo=((w, width), BF),
            prod=(column, F32),
            entry=((8, w), F32),
            mine=((8, w), F32),
            rowsum=((8, n), F32),
            rows8=((8, 8, n), F32),
        ),
        64,
        24,
    )
    gains_two = mlp_gain[None, :]
    C = call(
        feed_body,
        "feed",
        2,
        dict(
            tok=(tokens, VMEM),
            cot=(cotangent, VMEM),
            gain=(gains_two, VMEM),
            part=(B.part_out, ANY),
            gu_column=(B.gu_column, ANY),
            gu_row=(B.gu_row, ANY),
            bdn=(B.bdn.reshape(unit, width), ANY),
            gf=(B.gf, ANY),
        ),
        dict(
            mid=(block, F32, VMEM),
            mixed=(block, F32, VMEM),
            gb=(full, BF, ANY),
            part_r=(full, BF, ANY),
            sums=((8, width), F32, VMEM),
            block_ddn=((padded, width), BF, VMEM),
            block_dgate=((8 * rows, unit), BF, VMEM),
            dup=((width, unit), BF, ANY),
        ),
        scratch(
            wgu=((2, 2, 4, 8 * rows, 2 * unit), BF),
            wdn=((unit, width), BF),
            g=(full, BF),
            si=(full, BF),
            hid=((8 * n, unit), BF),
            ggu=((8 * n, 2 * unit), BF),
            ps=(full, BF),
            pr=((2, 2 * n, width), BF),
            near=((4,) + block, BF),
            far=((3,) + block, BF),
            block=(block, BF),
            ddn=((2, 2, 4, padded, width), BF),
            dgate=(gate_blocks, BF),
            pu=((2, 256, unit), BF),
        )
        | plane_work("a", by_columns(padded, width))
        | plane_work("b", by_rows(8 * rows, unit)),
        72,
        30,
    )
    D = call(
        back_body,
        "back",
        3,
        dict(
            tok=(tokens, VMEM),
            mid_in=(C.mid, ANY),
            mixed_in=(C.mixed, ANY),
            attn_gain=(gains, VMEM),
            lb=(B.lb, VMEM),
            table=(bound_table, VMEM),
            layer=(layer_idx[None, :], VMEM),
            gain=(norm_gain[None, :], VMEM),
            ffn_sums=(C.sums, VMEM),
            states_in=(B.states_out, ANY),
            forget_in=(B.forget_out, ANY),
            proj_in=(B.proj_out, ANY),
            gated_in=(B.gated_out, ANY),
            tot=(B.tot, VMEM),
            links=(B.links, VMEM),
            carry=(B.carry, VMEM),
            b3=(big3, ANY),
            bo=(big_out, ANY),
            fi=(A.fi, ANY),
            gb=(C.gb, ANY),
            part_r=(C.part_r, ANY),
            dup=(C.dup.reshape(gate_blocks), ANY),
            block_dgate=(C.block_dgate, ANY),
        ),
        dict(
            result=(block, BF, VMEM),
            gtok=(block, F32, VMEM),
            g_in=((rows, width), F32, VMEM),
            g_forget=((rows, width), F32, VMEM),
            g_og=((rows, width), F32, VMEM),
            g_out=((rows, width), F32, VMEM),
            g_gate=((rows, hidden_width), F32, VMEM),
            g_up=((rows, hidden_width), F32, VMEM),
            g_table=(bound_table.shape, F32, VMEM),
            gains=((8, width), F32, VMEM),
        ),
        scratch(
            rgate=((8, rows, unit), BF),
            rup=((8, rows, unit), BF),
            r1=((8, rows, w), BF),
            r2=((8, rows, 2 * w), BF),
            ro=((rows, width), BF),
            totals=((8, 8, w), F32),
            states=(column, F32),
            forget=(column, F32),
            proj=((8 * n, 3 * w), F32),
            gated=((8 * n, w), BF),
            mid=(block, F32),
            mixed=(block, F32),
            gbv=(full, BF),
            wo=((w, width), BF),
            w3=((width, 3 * w), BF),
            x=(full, BF),
            gg=((8 * n, w), F32),
            gs=(column, F32),
            prod=(column, F32),
            grads=((8 * n, 3 * w), BF),
            sums=((8, w), F32),
            entry=((8, w), F32),
            mine=((8, w), F32),
            rowsum=((8, n), F32),
            rows8=((8, 8, n), F32),
            chain=((8, 8, w), F32),
            pr=((4 * n, width), BF),
            pr_near=((4,) + block, BF),
            pr_far=((3,) + block, BF),
            fp=(full, BF),
            near=((4,) + block, BF),
            far=((3,) + block, BF),
            do=((2, 2, 4, rows, width), BF),
            d1=((2, 2, 4, 8 * rows, w), BF),
            d2=((2, 2, 4, 8 * rows, 2 * w), BF),
            block_dup=((8 * rows, unit), BF),
            o1=((8 * rows, w), BF),
            o2=((8 * rows, 2 * w), BF),
            oo=((rows, width), BF),
            va=((8, width), F32),
            ga=((8, 8, w), F32),
            ta=((8, w), F32),
            gather=((16, 8, w), F32),
            tb=((8, w), F32),
        )
        | plane_work("a", by_rows(8 * rows, unit))
        | plane_work("b", by_columns(rows, width))
        | plane_work("c", by_rows(8 * rows, 2 * w))
        | plane_work("d", by_rows(8 * rows, w)),
        160,
        30,
    )

    moved = (D.result, D.gtok, D.g_in, D.g_forget, D.g_og, D.g_out, D.g_gate, D.g_up, D.g_table)
    like = [jax.ShapeDtypeStruct(m.shape, m.dtype) for m in moved]
    row = jax.ShapeDtypeStruct((1, width), F32)
    last = pl.pallas_call(
        write_body,
        name="write",
        out_shape=like + [jax.ShapeDtypeStruct((down, width), F32), row, row, row],
        in_specs=[ANY] * len(moved) + [VMEM] * 2,
        out_specs=[VMEM] * (len(moved) + 4),
        scratch_shapes=[pltpu.SemaphoreType.DMA((len(moved),))],
        compiler_params=pltpu.CompilerParams(vmem_limit_bytes=60 << 20),
    )(*moved, D.gains, C.block_ddn)
    result, grad_tokens, g_in, g_forget, g_og, g_out, g_gate, g_up, g_table, g_down = last[:10]
    attn, norm, mlp = [m[0] for m in last[10:]]
    return (
        result,
        grad_tokens,
        attn,
        g_in,
        g_forget,
        g_og,
        g_out,
        norm,
        mlp,
        g_gate,
        g_up,
        g_down,
        g_table,
    )


def solution(mesh):
    split = Mesh(mesh.devices.reshape(2, 2, 4, 4, 2), AXES)
    cut = P(AXES, None)
    return jax.shard_map(
        on_device,
        mesh=split,
        in_specs=(cut, cut, P(), cut, cut, cut, cut, P(), P(), cut, cut, cut, P(), P()),
        out_specs=(cut, cut, P(), cut, cut, cut, cut, P(), P(), cut, cut, cut, P()),
        check_vma=False,
    )
```
